32 devices in a mesh: groups: 2 (over y), dom: 16 (over z, x, core).
Axes of the slice: x: 2, y: 2, z: 4, core: 2. Of those that a mesh axis runs over, the one named last changes fastest.
Arguments:
- nodes: bfloat16 [4096, 512], P(('groups', 'dom')), parts along dimension 0, may hold values from -6 to 6
- edges: bfloat16 [24576, 512], P(('groups', 'dom')), parts along dimension 0, may hold values from -6 to 6
- inner_pairs: int32 [8192, 2], P(('groups', 'dom')), parts along dimension 0, may hold values from 0 to 127
- cut_local: int32 [4096], P(('groups', 'dom')), parts along dimension 0, may hold values from 0 to 127
- cut_dest: int32 [4096, 1], P(('groups', 'dom')), parts along dimension 0, may hold values from 0 to 15; in each aligned block of 128 rows (0 to 127, 128 to 255, ...) at most 16 rows name the same one
- cut_remote: int32 [4096], P(('groups', 'dom')), parts along dimension 0, may hold values from 0 to 127
- w_edge_in: bfloat16 [1536, 512], replicated, may hold values from -0.15625 to 0.15625
- w_edge_out: bfloat16 [512, 512], replicated, may hold values from -0.25 to 0.25
- w_node_in: bfloat16 [1024, 512], replicated, may hold values from -0.1875 to 0.1875
- w_node_out: bfloat16 [512, 512], replicated, may hold values from -0.25 to 0.25
- ct_nodes: bfloat16 [4096, 512], P(('groups', 'dom')), parts along dimension 0, may hold values from -6 to 6
- ct_edges: bfloat16 [24576, 512], P(('groups', 'dom')), parts along dimension 0, may hold values from -6 to 6
Outputs:
- new_nodes: bfloat16 [4096, 512], P(('groups', 'dom')), parts along dimension 0
- new_edges: bfloat16 [24576, 512], P(('groups', 'dom')), parts along dimension 0
- grad_nodes: float32 [4096, 512], P(('groups', 'dom')), parts along dimension 0
- grad_edges: float32 [24576, 512], P(('groups', 'dom')), parts along dimension 0
- grad_edge_in: bfloat16 [3072, 512], P('groups'), parts along dimension 0
- grad_edge_out: bfloat16 [1024, 512], P('groups'), parts along dimension 0
- grad_node_in: bfloat16 [2048, 512], P('groups'), parts along dimension 0
- grad_node_out: bfloat16 [1024, 512], P('groups'), parts along dimension 0
The draws below stay inside these ranges and needn't reach their ends.
There are 2 independent parts, one for each index of `groups`. The reference program is written for one: setup_inputs(seed, part) draws one part's arguments, and reference() takes and returns one part's arrays. A program takes and returns all parts, laid end to end along the dimension named above; an argument that names none is the same for every part. Nothing has to cross between parts.
Inputs may be any that keep to these rules, and one draw needn't show every extreme that they name: `cut_dest`: among the cut pairs of one device, at most 16 name any one device, and in every draw some device's pairs name some device exactly 16 times.
All inputs are finite; a program needn't handle non-finite values.
Results may differ from the reference program's by a relative error of at most 0.0085.
Values may be sent and summed in bfloat16 or wider, within the bound.
No kernel may reach another device: no remote copies, remote signals or barrier semaphores. Data moves between devices by JAX's collectives and lax.ppermute only.
A program may use at most 128 MiB of HBM per device.

```python
import math
import jax
import jax.numpy as jnp
import numpy as np
from jax import lax

LATENT = 512
NODE_DEV = 128
INNER_DEV = 256
CUT_DEV = 128
DOMAINS = 16
SLOT = 16
NODES = 2048
EDGES = 12288
INNERS = 4096
CUTS = 2048
N_DOM = 16


def plant(values, stream_key, low, top_value):
    index_at = [jax.random.randint(jax.random.fold_in(stream_key, axis), (), 0, length) for axis, length in enumerate(values.shape)]
    main_axis = values.shape.index(max(values.shape))
    neighbour = index_at[:main_axis] + [(index_at[main_axis] + 1) % values.shape[main_axis]] + index_at[main_axis + 1:]
    return values.at[tuple(index_at)].set(low).at[tuple(neighbour)].set(top_value)


def steps_of(stream_key, shape, pieces, low, high):
    loudness, own = 1.0, jax.random.fold_in(stream_key, 6)
    for axis_at, shards_of in pieces:
        heights = jnp.exp(jax.random.uniform(jax.random.fold_in(own, axis_at), (shards_of,), jnp.float32, low / len(pieces), high / len(pieces)))
        loudness = loudness * jnp.repeat(heights, shape[axis_at] // shards_of).reshape([-1 if axis == axis_at else 1 for axis in range(len(shape))])
    return loudness


def shared_out(stream_key, own, number, rows, count, top, reach, skew):
    order = jax.random.permutation(stream_key, count)
    crowded, common = portions_of(count, rows * top, reach, skew, True), portions_of(count, rows * top, reach, skew, False)
    places = jnp.arange(count)

    def named(sizes, rotation):
        used = int((sizes > 0).sum())
        fixed = max(1, used // 4)
        passed = fixed + (places - fixed + rotation * (used - fixed)) % max(1, count - fixed)
        return jnp.zeros((count,), jnp.int32).at[order[jnp.where(places < fixed, places, passed)]].set(jnp.asarray(sizes, jnp.int32))

    sizes = jnp.where(number % 4 == 0, named(crowded, number // 4), named(common, number - number // 4 - 1))
    mixed = jax.random.permutation(jax.random.fold_in(own, 3), count)
    source_of, receiver = mixed[0:count // 2 * 2:2], mixed[1:count // 2 * 2:2]
    room = jnp.minimum(sizes[source_of] - 1, reach - sizes[receiver]) // 2
    room = jnp.where((source_of == order[0]) | (receiver == order[0]) | (sizes[receiver] == 0), 0, jnp.maximum(room, 0))
    passed = jax.random.randint(jax.random.fold_in(own, 4), (count // 2,), 0, 1 << 20) % (room + 1)
    sizes = sizes.at[source_of].add(-passed).at[receiver].add(passed)
    members = jnp.searchsorted(jnp.cumsum(sizes), jnp.arange(rows * top), side="right").astype(jnp.int32)
    listing = members.reshape(top, rows).T
    listing = listing[jax.random.permutation(jax.random.fold_in(own, 1), rows)]
    rotation = jax.random.randint(jax.random.fold_in(own, 2), (rows, 1), 0, top)
    return jnp.take_along_axis(listing, (jnp.arange(top)[None, :] + rotation) % top, axis=1)


def portions_of(number_of, total, limit, lean, full):
    portions = [(1 << 20) // math.isqrt(standing ** lean) + 1 for standing in range(1, number_of + 1)]
    largest = limit if full else min(limit, max(-(-total // number_of), total * portions[0] // sum(portions)))
    least = 1 if total - largest >= number_of - 1 else 0
    holding, surplus = [largest] + [least] * (number_of - 1), total - largest - least * (number_of - 1)
    while surplus > 0:
        movable = [i for i in range(1, number_of) if holding[i] < largest] or [i for i in range(1, number_of) if holding[i] < limit]
        whole, budget = sum([portions[i] for i in movable]), surplus
        for i in movable:
            more = min(limit - holding[i], max(1, budget * portions[i] // whole), surplus)
            holding[i] = holding[i] + more
            surplus = surplus - more
    return np.array(holding)


def normal_values(stream_key, shape, width, reach, split=(), kind=jnp.bfloat16):
    entries = jax.random.normal(stream_key, shape, jnp.float32) * width
    if len(split) > 0:
        entries = steps_of(stream_key, shape, split, -0.22, 0.18) * entries
    return jnp.clip(entries, min=-reach, max=reach).astype(kind)


def setup_inputs(seed: int = 0, part: int = 0) -> dict:
    streams_of = jax.random.split(jax.random.key(seed), 13)
    part_keys = jax.random.split(jax.random.fold_in(streams_of[12], part), 13)
    nodes = normal_values(part_keys[0], (NODES, LATENT), 1.0, 6.0, ((0, 16),))
    edges = normal_values(part_keys[1], (EDGES, LATENT), 1.0, 6.0, ((0, 16),))
    inner_pairs = plant(jax.random.randint(part_keys[2], (INNERS, 2), 0, NODE_DEV), jax.random.fold_in(part_keys[2], 1), 0, NODE_DEV - 1).astype(jnp.int32)
    cut_local = plant(jax.random.randint(part_keys[3], (CUTS,), 0, NODE_DEV), jax.random.fold_in(part_keys[3], 1), 0, NODE_DEV - 1).astype(jnp.int32)
    cut_dest_keys = jax.random.split(jax.random.fold_in(part_keys[4], 1), CUTS // CUT_DEV)
    cut_dest_turns = jax.random.permutation(jax.random.fold_in(part_keys[4], 3), CUTS // CUT_DEV)
    cut_dest = jax.vmap(lambda own, number: shared_out(jax.random.fold_in(part_keys[4], 2), own, number, CUT_DEV, DOMAINS, 1, SLOT, 2))(cut_dest_keys, cut_dest_turns).reshape((CUTS, 1))
    cut_remote = plant(jax.random.randint(part_keys[5], (CUTS,), 0, NODE_DEV), jax.random.fold_in(part_keys[5], 1), 0, NODE_DEV - 1).astype(jnp.int32)
    w_edge_in = normal_values(streams_of[6], (3 * LATENT, LATENT), (3 * LATENT) ** -0.5, 0.15625)
    w_edge_out = normal_values(streams_of[7], (LATENT, LATENT), LATENT ** -0.5, 0.25)
    w_node_in = normal_values(streams_of[8], (2 * LATENT, LATENT), (2 * LATENT) ** -0.5, 0.1875)
    w_node_out = normal_values(streams_of[9], (LATENT, LATENT), LATENT ** -0.5, 0.25)
    ct_nodes = normal_values(part_keys[10], (NODES, LATENT), 1.0, 6.0, ((0, 16),))
    ct_edges = normal_values(part_keys[11], (EDGES, LATENT), 1.0, 6.0, ((0, 16),))
    return dict(nodes=nodes, edges=edges, inner_pairs=inner_pairs, cut_local=cut_local, cut_dest=cut_dest, cut_remote=cut_remote, w_edge_in=w_edge_in, w_edge_out=w_edge_out, w_node_in=w_node_in, w_node_out=w_node_out, ct_nodes=ct_nodes, ct_edges=ct_edges)


def layer_norm(values):
    row_mean = lax.optimization_barrier(jnp.mean(values, axis=-1, keepdims=True))
    centered = values - row_mean
    inv_scale = lax.rsqrt(lax.optimization_barrier(jnp.mean(centered * centered, axis=-1, keepdims=True)) + 1e-05)
    return (centered * inv_scale, inv_scale)

def mlp_forward(inputs, w_first, w_second):
    pre_hidden = jnp.dot(inputs, w_first, preferred_element_type=jnp.float32)
    hidden = jax.nn.silu(pre_hidden).astype(jnp.bfloat16)
    pre_out = jnp.dot(hidden, w_second, preferred_element_type=jnp.float32)
    normed, _ = layer_norm(pre_out)
    return (normed, hidden, pre_hidden, pre_out)

def mlp_backward(inputs, hidden, pre_hidden, pre_out, w_first, w_second, upstream):
    normed, inv_scale = layer_norm(pre_out)
    centered_grad = upstream - lax.optimization_barrier(jnp.mean(upstream, axis=-1, keepdims=True)) - normed * lax.optimization_barrier(jnp.mean(upstream * normed, axis=-1, keepdims=True))
    grad_out = (inv_scale * centered_grad).astype(jnp.bfloat16)
    grad_second = lax.dot_general(hidden, grad_out, (((0,), (0,)), ((), ())), preferred_element_type=jnp.float32)
    grad_hidden = lax.dot_general(grad_out, w_second, (((1,), (1,)), ((), ())), preferred_element_type=jnp.float32)
    sigmoid_val = jax.nn.sigmoid(pre_hidden)
    grad_pre = (grad_hidden * sigmoid_val * (1.0 + pre_hidden * (1.0 - sigmoid_val))).astype(jnp.bfloat16)
    grad_first = lax.dot_general(inputs, grad_pre, (((0,), (0,)), ((), ())), preferred_element_type=jnp.float32)
    grad_inputs = lax.dot_general(grad_pre, w_first, (((1,), (1,)), ((), ())), preferred_element_type=jnp.float32)
    return (grad_inputs, grad_first, grad_second)

def reference(nodes, edges, inner_pairs, cut_local, cut_dest, cut_remote, w_edge_in, w_edge_out, w_node_in, w_node_out, ct_nodes, ct_edges):
    latent = nodes.shape[1]
    inner_base = jnp.arange(INNERS, dtype=jnp.int32) // INNER_DEV * NODE_DEV
    cut_base = jnp.arange(CUTS, dtype=jnp.int32) // CUT_DEV * NODE_DEV
    inner_first = (inner_base + inner_pairs[:, 0]).reshape(N_DOM, INNER_DEV)
    inner_second = (inner_base + inner_pairs[:, 1]).reshape(N_DOM, INNER_DEV)
    cut_first = (cut_base + cut_local).reshape(N_DOM, CUT_DEV)
    cut_second = (cut_dest[:, 0] * NODE_DEV + cut_remote).reshape(N_DOM, CUT_DEV)
    first_ids = jnp.concatenate([inner_first, cut_first], axis=1).reshape(-1)
    second_ids = jnp.concatenate([inner_second, cut_second], axis=1).reshape(-1)
    senders = jnp.stack([first_ids, second_ids], axis=1).reshape(-1)
    receivers = jnp.stack([second_ids, first_ids], axis=1).reshape(-1)
    edge_input = jnp.concatenate([edges, nodes[senders], nodes[receivers]], axis=1)
    edge_out, edge_hidden, edge_pre_hidden, edge_pre_out = mlp_forward(edge_input, w_edge_in, w_edge_out)
    message = edge_out.astype(jnp.bfloat16)
    new_edges = (edges.astype(jnp.float32) + message.astype(jnp.float32)).astype(jnp.bfloat16)
    aggregate = jax.ops.segment_sum(message.astype(jnp.float32), receivers, NODES).astype(jnp.bfloat16)
    node_input = jnp.concatenate([nodes, aggregate], axis=1)
    node_out, node_hidden, node_pre_hidden, node_pre_out = mlp_forward(node_input, w_node_in, w_node_out)
    new_nodes = (nodes.astype(jnp.float32) + node_out).astype(jnp.bfloat16)
    ct_node_f = ct_nodes.astype(jnp.float32)
    ct_edge_f = ct_edges.astype(jnp.float32)
    grad_node_input, grad_node_in, grad_node_out = mlp_backward(node_input, node_hidden, node_pre_hidden, node_pre_out, w_node_in, w_node_out, ct_node_f)
    grad_aggregate = grad_node_input[:, latent:].astype(jnp.bfloat16)
    grad_message = ct_edge_f + grad_aggregate[receivers].astype(jnp.float32)
    grad_edge_input, grad_edge_in, grad_edge_out = mlp_backward(edge_input, edge_hidden, edge_pre_hidden, edge_pre_out, w_edge_in, w_edge_out, grad_message)
    grad_edges = ct_edge_f + grad_edge_input[:, :latent]
    grad_nodes = ct_node_f + grad_node_input[:, :latent]
    grad_nodes = grad_nodes + jax.ops.segment_sum(grad_edge_input[:, latent:2 * latent], senders, NODES)
    grad_nodes = grad_nodes + jax.ops.segment_sum(grad_edge_input[:, 2 * latent:], receivers, NODES)
    return (new_nodes, new_edges, grad_nodes, grad_edges, grad_edge_in.astype(jnp.bfloat16), grad_edge_out.astype(jnp.bfloat16), grad_node_in.astype(jnp.bfloat16), grad_node_out.astype(jnp.bfloat16))
```

```python
import jax
import jax.numpy as jnp
from jax import lax
from jax.sharding import PartitionSpec as P


def layer_norm(values):
    row_mean = jnp.mean(values, axis=-1, keepdims=True)
    centered = values - row_mean
    inv_scale = lax.rsqrt(jnp.mean(centered * centered, axis=-1, keepdims=True) + 1e-05)
    return (centered * inv_scale, inv_scale)


def mlp_forward(inputs, w_first, w_second):
    pre_hidden = jnp.dot(inputs, w_first, preferred_element_type=jnp.float32)
    hidden = jax.nn.silu(pre_hidden).astype(jnp.bfloat16)
    pre_out = jnp.dot(hidden, w_second, preferred_element_type=jnp.float32)
    normed, _ = layer_norm(pre_out)
    return (normed, hidden, pre_hidden, pre_out)


def mlp_backward(inputs, hidden, pre_hidden, pre_out, w_first, w_second, upstream):
    normed, inv_scale = layer_norm(pre_out)
    centered_grad = (
        upstream
        - jnp.mean(upstream, axis=-1, keepdims=True)
        - normed * jnp.mean(upstream * normed, axis=-1, keepdims=True)
    )
    grad_out = (inv_scale * centered_grad).astype(jnp.bfloat16)
    grad_second = lax.dot_general(
        hidden, grad_out, (((0,), (0,)), ((), ())), preferred_element_type=jnp.float32
    )
    grad_hidden = lax.dot_general(
        grad_out, w_second, (((1,), (1,)), ((), ())), preferred_element_type=jnp.float32
    )
    sigmoid_val = jax.nn.sigmoid(pre_hidden)
    grad_pre = (grad_hidden * sigmoid_val * (1.0 + pre_hidden * (1.0 - sigmoid_val))).astype(
        jnp.bfloat16
    )
    grad_first = lax.dot_general(
        inputs, grad_pre, (((0,), (0,)), ((), ())), preferred_element_type=jnp.float32
    )
    grad_inputs = lax.dot_general(
        grad_pre, w_first, (((1,), (1,)), ((), ())), preferred_element_type=jnp.float32
    )
    return (grad_inputs, grad_first, grad_second)


def edge_inputs(edge_rows, first_rows, second_rows):
    latent = first_rows.shape[1]
    senders = jnp.stack([first_rows, second_rows], axis=1).reshape(-1, latent)
    receivers = jnp.stack([second_rows, first_rows], axis=1).reshape(-1, latent)
    return jnp.concatenate([edge_rows, senders, receivers], axis=1)


def agg_targets_order(inner_a, inner_b, cut_local, asked_flat):
    return jnp.concatenate([inner_a, inner_b, cut_local, asked_flat], axis=0)


def shards(
    nodes,
    edges,
    inner_pairs,
    cut_local,
    cut_dest,
    cut_remote,
    w_edge_in,
    w_edge_out,
    w_node_in,
    w_node_out,
    ct_nodes,
    ct_edges,
):
    domains = lax.axis_size("dom")
    node_rows = nodes.shape[0]
    latent = nodes.shape[1]
    inner_count = inner_pairs.shape[0]
    cut_count = cut_local.shape[0]
    slot_count = max(2, 2 * cut_count // domains)
    total_slots = domains * slot_count
    target_dev = cut_dest[:, 0]
    dest_marks = (target_dev[:, None] == jnp.arange(domains, dtype=jnp.int32)[None, :]).astype(
        jnp.int32
    )
    before = jnp.cumsum(dest_marks, axis=0) - dest_marks
    slot_rank = jnp.sum(before * dest_marks, axis=1)
    position = target_dev * slot_count + slot_rank
    slot_node = jnp.zeros((total_slots,), jnp.int32).at[position].set(cut_remote)
    slot_pair = (
        jnp.zeros((total_slots,), jnp.int32)
        .at[position]
        .set(jnp.arange(cut_count, dtype=jnp.int32))
    )
    slot_used = jnp.zeros((total_slots,), jnp.int32).at[position].set(1)
    asked_ids = lax.all_to_all(
        slot_node.reshape(domains, slot_count), "dom", split_axis=0, concat_axis=0, tiled=True
    )
    fetched, asked_ids = (
        lax.all_to_all(nodes[asked_ids], "dom", split_axis=0, concat_axis=0, tiled=True),
        asked_ids,
    )
    asked_flat = asked_ids.reshape(-1)
    far_rows = fetched.reshape(total_slots, latent)[position]
    inner_a = inner_pairs[:, 0]
    inner_b = inner_pairs[:, 1]
    inner_input = edge_inputs(edges[: 2 * inner_count], nodes[inner_a], nodes[inner_b])
    cut_input = edge_inputs(edges[2 * inner_count :], nodes[cut_local], far_rows)
    edge_input = jnp.concatenate([inner_input, cut_input], axis=0)
    edge_out, edge_hidden, edge_pre_hidden, edge_pre_out = mlp_forward(
        edge_input, w_edge_in, w_edge_out
    )
    message = edge_out.astype(jnp.bfloat16)
    new_edges = (edges.astype(jnp.float32) + message.astype(jnp.float32)).astype(jnp.bfloat16)
    message_pairs = message.reshape(inner_count + cut_count, 2, latent)
    outgoing = jnp.where(
        slot_used[:, None] > 0,
        message_pairs[inner_count:, 0][slot_pair],
        jnp.zeros((), jnp.bfloat16),
    )
    incoming = lax.all_to_all(
        outgoing.reshape(domains, slot_count, latent),
        "dom",
        split_axis=0,
        concat_axis=0,
        tiled=True,
    ).reshape(total_slots, latent)
    agg_values = jnp.concatenate(
        [
            message_pairs[:inner_count, 0],
            message_pairs[:inner_count, 1],
            message_pairs[inner_count:, 1],
            incoming,
        ],
        axis=0,
    )
    agg_targets = jnp.concatenate([inner_b, inner_a, cut_local, asked_flat], axis=0)
    onehot = (jnp.arange(node_rows, dtype=jnp.int32)[:, None] == agg_targets[None, :]).astype(
        jnp.bfloat16
    )
    aggregate = jnp.dot(onehot, agg_values, preferred_element_type=jnp.float32).astype(jnp.bfloat16)
    node_input = jnp.concatenate([nodes, aggregate], axis=1)
    node_out, node_hidden, node_pre_hidden, node_pre_out = mlp_forward(
        node_input, w_node_in, w_node_out
    )
    new_nodes = (nodes.astype(jnp.float32) + node_out).astype(jnp.bfloat16)
    ct_node_f = ct_nodes.astype(jnp.float32)
    ct_edge_f = ct_edges.astype(jnp.float32)
    grad_node_input, grad_node_in, grad_node_out = mlp_backward(
        node_input, node_hidden, node_pre_hidden, node_pre_out, w_node_in, w_node_out, ct_node_f
    )
    grad_aggregate = grad_node_input[:, latent:].astype(jnp.bfloat16)
    far_grads = lax.all_to_all(
        grad_aggregate[asked_ids], "dom", split_axis=0, concat_axis=0, tiled=True
    ).reshape(total_slots, latent)[position]
    toward_second = jnp.concatenate([grad_aggregate[inner_b], far_grads], axis=0)
    toward_first = jnp.concatenate([grad_aggregate[inner_a], grad_aggregate[cut_local]], axis=0)
    receiver_grads = jnp.stack([toward_second, toward_first], axis=1).reshape(-1, latent)
    grad_message = ct_edge_f + receiver_grads.astype(jnp.float32)
    grad_edge_input, grad_edge_in, grad_edge_out = mlp_backward(
        edge_input, edge_hidden, edge_pre_hidden, edge_pre_out, w_edge_in, w_edge_out, grad_message
    )
    node_total = lax.psum(
        jnp.concatenate([grad_node_in, grad_node_out], axis=0).astype(jnp.bfloat16), "dom"
    )
    edge_part = lax.psum_scatter(
        jnp.concatenate([grad_edge_in, grad_edge_out], axis=0).astype(jnp.bfloat16),
        "dom",
        scatter_dimension=0,
        tiled=True,
    )
    edge_total = lax.all_gather(edge_part, "dom", axis=0, tiled=True)
    grad_edge_in, grad_edge_out = edge_total[: 3 * latent], edge_total[3 * latent :]
    grad_node_in, grad_node_out = node_total[: 2 * latent], node_total[2 * latent :]
    grad_edges = ct_edge_f + grad_edge_input[:, :latent]
    send_grads = grad_edge_input[:, latent : 2 * latent].reshape(inner_count + cut_count, 2, latent)
    recv_grads = grad_edge_input[:, 2 * latent :].reshape(inner_count + cut_count, 2, latent)
    first_grads = send_grads[:, 0] + recv_grads[:, 1]
    used_rows = slot_used[:, None] > 0
    both_grads = jnp.stack([recv_grads[inner_count:, 0], send_grads[inner_count:, 1]], axis=1)
    outgoing_grads = jnp.where(used_rows[:, :, None], both_grads[slot_pair], 0.0)
    returned_pairs = lax.all_to_all(
        outgoing_grads.reshape(domains, slot_count, 2, latent).astype(jnp.bfloat16),
        "dom",
        split_axis=0,
        concat_axis=0,
        tiled=True,
    ).astype(jnp.float32)
    returned = (returned_pairs[:, :, 0] + returned_pairs[:, :, 1]).reshape(total_slots, latent)
    inner_second_grads = recv_grads[:inner_count, 0] + send_grads[:inner_count, 1]
    grad_values = jnp.concatenate(
        [first_grads[:inner_count], inner_second_grads, first_grads[inner_count:], returned], axis=0
    )
    grad_nodes = (
        ct_node_f
        + grad_node_input[:, :latent]
        + jax.ops.segment_sum(
            grad_values, agg_targets_order(inner_a, inner_b, cut_local, asked_flat), node_rows
        )
    )
    return (
        new_nodes,
        new_edges,
        grad_nodes,
        grad_edges,
        grad_edge_in.astype(jnp.bfloat16),
        grad_edge_out.astype(jnp.bfloat16),
        grad_node_in.astype(jnp.bfloat16),
        grad_node_out.astype(jnp.bfloat16),
    )


def solution(mesh):
    placed = (
        P(("groups", "dom"), None),
        P(("groups", "dom"), None),
        P(("groups", "dom"), None),
        P(("groups", "dom")),
        P(("groups", "dom"), None),
        P(("groups", "dom")),
        P(),
        P(),
        P(),
        P(),
        P(("groups", "dom"), None),
        P(("groups", "dom"), None),
    )
    return jax.shard_map(
        shards,
        mesh=mesh,
        in_specs=placed,
        out_specs=(
            P(("groups", "dom"), None),
            P(("groups", "dom"), None),
            P(("groups", "dom"), None),
            P(("groups", "dom"), None),
            P("groups", None),
            P("groups", None),
            P("groups", None),
            P("groups", None),
        ),
        check_vma=False,
    )
```

```python
import jax
import jax.numpy as jnp
from jax import lax
from jax.sharding import PartitionSpec as P


def layer_norm(values):
    row_mean = jnp.mean(values, axis=-1, keepdims=True)
    centered = values - row_mean
    inv_scale = lax.rsqrt(jnp.mean(centered * centered, axis=-1, keepdims=True) + 1e-05)
    return (centered * inv_scale, inv_scale)


def mlp_forward(inputs, w_first, w_second):
    pre_hidden = jnp.dot(inputs, w_first, preferred_element_type=jnp.float32)
    hidden = jax.nn.silu(pre_hidden).astype(jnp.bfloat16)
    pre_out = jnp.dot(hidden, w_second, preferred_element_type=jnp.float32)
    normed, _ = layer_norm(pre_out)
    return (normed, hidden, pre_hidden, pre_out)


def mlp_backward(inputs, hidden, pre_hidden, pre_out, w_first, w_second, upstream):
    normed, inv_scale = layer_norm(pre_out)
    centered_grad = (
        upstream
        - jnp.mean(upstream, axis=-1, keepdims=True)
        - normed * jnp.mean(upstream * normed, axis=-1, keepdims=True)
    )
    grad_out = (inv_scale * centered_grad).astype(jnp.bfloat16)
    grad_second = lax.dot_general(
        hidden, grad_out, (((0,), (0,)), ((), ())), preferred_element_type=jnp.float32
    )
    grad_hidden = lax.dot_general(
        grad_out, w_second, (((1,), (1,)), ((), ())), preferred_element_type=jnp.float32
    )
    sigmoid_val = jax.nn.sigmoid(pre_hidden)
    grad_pre = (grad_hidden * sigmoid_val * (1.0 + pre_hidden * (1.0 - sigmoid_val))).astype(
        jnp.bfloat16
    )
    grad_first = lax.dot_general(
        inputs, grad_pre, (((0,), (0,)), ((), ())), preferred_element_type=jnp.float32
    )
    grad_inputs = lax.dot_general(
        grad_pre, w_first, (((1,), (1,)), ((), ())), preferred_element_type=jnp.float32
    )
    return (grad_inputs, grad_first, grad_second)


def edge_inputs(edge_rows, first_rows, second_rows):
    latent = first_rows.shape[1]
    senders = jnp.stack([first_rows, second_rows], axis=1).reshape(-1, latent)
    receivers = jnp.stack([second_rows, first_rows], axis=1).reshape(-1, latent)
    return jnp.concatenate([edge_rows, senders, receivers], axis=1)


def agg_targets_order(inner_a, inner_b, cut_local, asked_flat):
    return jnp.concatenate([inner_a, inner_b, cut_local, asked_flat], axis=0)


def bit_groups(devices):
    bits = devices.bit_length() - 1
    groups = [(low, 1) for low in range(min(2, bits))]
    low = 2
    while low < bits:
        groups.append((low, min(2, bits - low)))
        low += 2
    return groups


def partner_pairs(devices, mask):
    return [(device, device ^ mask) for device in range(devices)]


def reduce_rows(rows, devices):
    me = lax.axis_index("dom")
    for low, width in bit_groups(devices):
        size = 1 << width
        place = (me >> low) & (size - 1)
        chunk = rows.shape[0] // size
        pieces = rows.reshape(size, chunk, rows.shape[1])
        total = lax.dynamic_index_in_dim(pieces, place, 0, False).astype(jnp.float32)
        for turn in range(1, size):
            sent = lax.dynamic_index_in_dim(pieces, place ^ turn, 0, False)
            total += lax.ppermute(sent, "dom", partner_pairs(devices, turn << low)).astype(
                jnp.float32
            )
        rows = total.astype(jnp.bfloat16)
    return rows


def gather_rows(rows, devices):
    me = lax.axis_index("dom")
    for low, width in bit_groups(devices)[::-1]:
        size = 1 << width
        place = (me >> low) & (size - 1)
        whole = jnp.zeros((size,) + rows.shape, rows.dtype)
        for turn in range(size):
            piece = rows
            if turn:
                piece = lax.ppermute(rows, "dom", partner_pairs(devices, turn << low))
            whole = lax.dynamic_update_index_in_dim(whole, piece, place ^ turn, 0)
        rows = whole.reshape(size * rows.shape[0], rows.shape[1])
    return rows


def shards(
    nodes,
    edges,
    inner_pairs,
    cut_local,
    cut_dest,
    cut_remote,
    w_edge_in,
    w_edge_out,
    w_node_in,
    w_node_out,
    ct_nodes,
    ct_edges,
):
    domains = lax.axis_size("dom")
    node_rows = nodes.shape[0]
    latent = nodes.shape[1]
    inner_count = inner_pairs.shape[0]
    cut_count = cut_local.shape[0]
    slot_count = max(2, 2 * cut_count // domains)
    total_slots = domains * slot_count
    target_dev = cut_dest[:, 0]
    dest_marks = (target_dev[:, None] == jnp.arange(domains, dtype=jnp.int32)[None, :]).astype(
        jnp.int32
    )
    before = jnp.cumsum(dest_marks, axis=0) - dest_marks
    slot_rank = jnp.sum(before * dest_marks, axis=1)
    position = target_dev * slot_count + slot_rank
    slot_node = jnp.zeros((total_slots,), jnp.int32).at[position].set(cut_remote)
    slot_pair = (
        jnp.zeros((total_slots,), jnp.int32)
        .at[position]
        .set(jnp.arange(cut_count, dtype=jnp.int32))
    )
    slot_used = jnp.zeros((total_slots,), jnp.int32).at[position].set(1)
    asked_ids = lax.all_to_all(
        slot_node.reshape(domains, slot_count), "dom", split_axis=0, concat_axis=0, tiled=True
    )
    fetched, asked_ids = (
        lax.all_to_all(nodes[asked_ids], "dom", split_axis=0, concat_axis=0, tiled=True),
        asked_ids,
    )
    asked_flat = asked_ids.reshape(-1)
    far_rows = fetched.reshape(total_slots, latent)[position]
    inner_a = inner_pairs[:, 0]
    inner_b = inner_pairs[:, 1]
    inner_input = edge_inputs(edges[: 2 * inner_count], nodes[inner_a], nodes[inner_b])
    cut_input = edge_inputs(edges[2 * inner_count :], nodes[cut_local], far_rows)
    edge_input = jnp.concatenate([inner_input, cut_input], axis=0)
    edge_out, edge_hidden, edge_pre_hidden, edge_pre_out = mlp_forward(
        edge_input, w_edge_in, w_edge_out
    )
    message = edge_out.astype(jnp.bfloat16)
    new_edges = (edges.astype(jnp.float32) + message.astype(jnp.float32)).astype(jnp.bfloat16)
    message_pairs = message.reshape(inner_count + cut_count, 2, latent)
    outgoing = jnp.where(
        slot_used[:, None] > 0,
        message_pairs[inner_count:, 0][slot_pair],
        jnp.zeros((), jnp.bfloat16),
    )
    incoming = lax.all_to_all(
        outgoing.reshape(domains, slot_count, latent),
        "dom",
        split_axis=0,
        concat_axis=0,
        tiled=True,
    ).reshape(total_slots, latent)
    agg_values = jnp.concatenate(
        [
            message_pairs[:inner_count, 0],
            message_pairs[:inner_count, 1],
            message_pairs[inner_count:, 1],
            incoming,
        ],
        axis=0,
    )
    agg_targets = jnp.concatenate([inner_b, inner_a, cut_local, asked_flat], axis=0)
    onehot = (jnp.arange(node_rows, dtype=jnp.int32)[:, None] == agg_targets[None, :]).astype(
        jnp.bfloat16
    )
    aggregate = jnp.dot(onehot, agg_values, preferred_element_type=jnp.float32).astype(jnp.bfloat16)
    node_input = jnp.concatenate([nodes, aggregate], axis=1)
    node_out, node_hidden, node_pre_hidden, node_pre_out = mlp_forward(
        node_input, w_node_in, w_node_out
    )
    new_nodes = (nodes.astype(jnp.float32) + node_out).astype(jnp.bfloat16)
    ct_node_f = ct_nodes.astype(jnp.float32)
    ct_edge_f = ct_edges.astype(jnp.float32)
    grad_node_input, grad_node_in, grad_node_out = mlp_backward(
        node_input, node_hidden, node_pre_hidden, node_pre_out, w_node_in, w_node_out, ct_node_f
    )
    grad_aggregate = grad_node_input[:, latent:].astype(jnp.bfloat16)
    far_grads = lax.all_to_all(
        grad_aggregate[asked_ids], "dom", split_axis=0, concat_axis=0, tiled=True
    ).reshape(total_slots, latent)[position]
    toward_second = jnp.concatenate([grad_aggregate[inner_b], far_grads], axis=0)
    toward_first = jnp.concatenate([grad_aggregate[inner_a], grad_aggregate[cut_local]], axis=0)
    receiver_grads = jnp.stack([toward_second, toward_first], axis=1).reshape(-1, latent)
    grad_message = ct_edge_f + receiver_grads.astype(jnp.float32)
    grad_edge_input, grad_edge_in, grad_edge_out = mlp_backward(
        edge_input, edge_hidden, edge_pre_hidden, edge_pre_out, w_edge_in, w_edge_out, grad_message
    )
    node_total = gather_rows(
        reduce_rows(
            jnp.concatenate([grad_node_in, grad_node_out], axis=0).astype(jnp.bfloat16), domains
        ),
        domains,
    )
    edge_total = gather_rows(
        reduce_rows(
            jnp.concatenate([grad_edge_in, grad_edge_out], axis=0).astype(jnp.bfloat16), domains
        ),
        domains,
    )
    grad_edge_in, grad_edge_out = edge_total[: 3 * latent], edge_total[3 * latent :]
    grad_node_in, grad_node_out = node_total[: 2 * latent], node_total[2 * latent :]
    grad_edges = ct_edge_f + grad_edge_input[:, :latent]
    send_grads = grad_edge_input[:, latent : 2 * latent].reshape(inner_count + cut_count, 2, latent)
    recv_grads = grad_edge_input[:, 2 * latent :].reshape(inner_count + cut_count, 2, latent)
    first_grads = send_grads[:, 0] + recv_grads[:, 1]
    used_rows = slot_used[:, None] > 0
    both_grads = jnp.stack([recv_grads[inner_count:, 0], send_grads[inner_count:, 1]], axis=1)
    outgoing_grads = jnp.where(used_rows[:, :, None], both_grads[slot_pair], 0.0)
    returned_pairs = lax.all_to_all(
        outgoing_grads.reshape(domains, slot_count, 2, latent).astype(jnp.bfloat16),
        "dom",
        split_axis=0,
        concat_axis=0,
        tiled=True,
    ).astype(jnp.float32)
    returned = (returned_pairs[:, :, 0] + returned_pairs[:, :, 1]).reshape(total_slots, latent)
    inner_second_grads = recv_grads[:inner_count, 0] + send_grads[:inner_count, 1]
    grad_values = jnp.concatenate(
        [first_grads[:inner_count], inner_second_grads, first_grads[inner_count:], returned], axis=0
    )
    grad_nodes = (
        ct_node_f
        + grad_node_input[:, :latent]
        + jax.ops.segment_sum(
            grad_values, agg_targets_order(inner_a, inner_b, cut_local, asked_flat), node_rows
        )
    )
    return (
        new_nodes,
        new_edges,
        grad_nodes,
        grad_edges,
        grad_edge_in.astype(jnp.bfloat16),
        grad_edge_out.astype(jnp.bfloat16),
        grad_node_in.astype(jnp.bfloat16),
        grad_node_out.astype(jnp.bfloat16),
    )


def solution(mesh):
    placed = (
        P(("groups", "dom"), None),
        P(("groups", "dom"), None),
        P(("groups", "dom"), None),
        P(("groups", "dom")),
        P(("groups", "dom"), None),
        P(("groups", "dom")),
        P(),
        P(),
        P(),
        P(),
        P(("groups", "dom"), None),
        P(("groups", "dom"), None),
    )
    return jax.shard_map(
        shards,
        mesh=mesh,
        in_specs=placed,
        out_specs=(
            P(("groups", "dom"), None),
            P(("groups", "dom"), None),
            P(("groups", "dom"), None),
            P(("groups", "dom"), None),
            P("groups", None),
            P("groups", None),
            P("groups", None),
            P("groups", None),
        ),
        check_vma=False,
    )
```

```python
import functools

import jax
import jax.numpy as jnp
from jax import lax
from jax.experimental import pallas as pl
from jax.experimental.pallas import tpu as pltpu
from jax.sharding import PartitionSpec as P

BF16 = jnp.bfloat16
F32 = jnp.float32
VMEM_LIMIT = 40 * 1024 * 1024


def dot(left, right):
    return jnp.dot(left, right, preferred_element_type=F32)


def dot_rows(left, right):
    return lax.dot_general(left, right, (((0,), (0,)), ((), ())), preferred_element_type=F32)


def dot_cols(left, right):
    return lax.dot_general(left, right, (((1,), (1,)), ((), ())), preferred_element_type=F32)


def iota(shape, axis):
    return lax.broadcasted_iota(jnp.int32, shape, axis)


def marks(mask):
    return jnp.where(mask, 1.0, 0.0).astype(BF16)


def onehot(column, width):
    return marks(column == iota((column.shape[0], width), 1))


def to_column(row):
    count = row.shape[1]
    square = (count, count)
    kept = jnp.where(iota(square, 0) == iota(square, 1), row.astype(F32), 0.0)
    return jnp.sum(kept, axis=1, keepdims=True)


def slot_ranks(dest, domains):
    count = dest.shape[0]
    square = (count, count)
    dest_marks = onehot(dest, domains)
    before = dot(marks(iota(square, 0) > iota(square, 1)), dest_marks)
    return dest_marks, jnp.sum(before * dest_marks.astype(F32), axis=1, keepdims=True)


def pair_marks(first, second, width):
    pairs = first.shape[0]
    shape = (2 * pairs, pairs)
    edge, pair = iota(shape, 0), iota(shape, 1)
    mine = (edge >> 1) == pair
    even = marks(mine & ((edge & 1) == 0))
    odd = marks(mine & ((edge & 1) == 1))
    first_marks, second_marks = onehot(first, width), onehot(second, width)
    senders = dot(even, first_marks) + dot(odd, second_marks)
    receivers = dot(even, second_marks) + dot(odd, first_marks)
    return senders.astype(BF16), receivers.astype(BF16)


def normalise(values):
    centered = values - jnp.mean(values, axis=1, keepdims=True)
    inv_scale = lax.rsqrt(jnp.mean(centered * centered, axis=1, keepdims=True) + 1e-05)
    return centered * inv_scale, inv_scale


def activate(pre_hidden):
    gate = jax.nn.sigmoid(pre_hidden)
    return (pre_hidden * gate).astype(BF16), gate * (1.0 + pre_hidden * (1.0 - gate))


def norm_backward(upstream, normed, inv_scale):
    centered = (
        upstream
        - jnp.mean(upstream, axis=1, keepdims=True)
        - normed * jnp.mean(upstream * normed, axis=1, keepdims=True)
    )
    return (inv_scale * centered).astype(BF16)


def ask_kernel(dest_ref, remote_ref, ask_ref):
    domains, slots = ask_ref.shape
    dest_marks, rank = slot_ranks(dest_ref[...], domains)
    rank_marks = jnp.where(rank == iota((rank.shape[0], slots), 1).astype(F32), 1.0, 0.0)
    wanted = (rank_marks * to_column(remote_ref[...])).astype(BF16)
    ask_ref[...] = dot_rows(dest_marks, wanted).astype(jnp.int32)


def reply_kernel(asked_ref, nodes_ref, reply_ref, asked_marks_ref):
    domains, slots = asked_ref.shape
    total = domains * slots
    shift = slots.bit_length() - 1
    spread = marks((iota((total, domains), 0) >> shift) == iota((total, domains), 1))
    listed = dot(spread, asked_ref[...].astype(F32).astype(BF16))
    at_slot = (iota((total, slots), 0) & (slots - 1)) == iota((total, slots), 1)
    column = jnp.sum(jnp.where(at_slot, listed, 0.0), axis=1, keepdims=True)
    node_rows = nodes_ref.shape[0]
    asked_marks = marks(column == iota((total, node_rows), 1).astype(F32))
    asked_marks_ref[...] = asked_marks
    reply_ref[...] = dot(asked_marks, nodes_ref[...]).astype(BF16)


def cut_marks_kernel(dest_ref, local_ref, dep_ref, senders_ref, receivers_ref, *, domains, slots):
    width = senders_ref.shape[1]
    base = width - domains * slots
    dest = dest_ref[...]
    _, rank = slot_ranks(dest, domains)
    second = dest * slots + rank.astype(jnp.int32) + base
    first = to_column(local_ref[...]).astype(jnp.int32)
    senders, receivers = pair_marks(first, second, width)
    senders_ref[...] = senders
    receivers_ref[...] = receivers


def edge_forward(edge, sender, receiver, w_in_ref, w_out_ref):
    latent = edge.shape[1]
    pre_hidden = (
        dot(edge, w_in_ref[:latent])
        + dot(sender, w_in_ref[latent : 2 * latent])
        + dot(receiver, w_in_ref[2 * latent :])
    )
    hidden, slope = activate(pre_hidden)
    normed, inv_scale = normalise(dot(hidden, w_out_ref[...]))
    return hidden, slope, normed, inv_scale


def inner_forward_kernel(
    pairs_ref,
    edges_ref,
    nodes_ref,
    w_in_ref,
    w_out_ref,
    dep_ref,
    senders_ref,
    receivers_ref,
    sender_ref,
    receiver_ref,
    hidden_ref,
    slope_ref,
    normed_ref,
    scale_ref,
    total_ref,
):
    pairs = pairs_ref[...]
    senders, receivers = pair_marks(pairs[:, 0:1], pairs[:, 1:2], nodes_ref.shape[0])
    senders_ref[...] = senders
    receivers_ref[...] = receivers
    nodes = nodes_ref[...]
    sender = dot(senders, nodes).astype(BF16)
    receiver = dot(receivers, nodes).astype(BF16)
    sender_ref[...] = sender
    receiver_ref[...] = receiver
    hidden, slope, normed, inv_scale = edge_forward(
        edges_ref[...], sender, receiver, w_in_ref, w_out_ref
    )
    hidden_ref[...] = hidden
    slope_ref[...] = slope
    normed_ref[...] = normed
    scale_ref[...] = inv_scale
    part = dot_rows(receivers, normed.astype(BF16))

    @pl.when(pl.program_id(0) == 0)
    def _():
        total_ref[...] = part

    @pl.when(pl.program_id(0) > 0)
    def _():
        total_ref[...] += part


def cut_forward_kernel(
    senders_ref,
    receivers_ref,
    edges_ref,
    nodes_ref,
    far_ref,
    w_in_ref,
    w_out_ref,
    inner_total_ref,
    sender_ref,
    receiver_ref,
    hidden_ref,
    slope_ref,
    normed_ref,
    scale_ref,
    total_ref,
    outgoing_ref,
):
    base = nodes_ref.shape[0]
    nodes, far = nodes_ref[...], far_ref[...]

    def rows_of(marks_ref):
        return (dot(marks_ref[:, :base], nodes) + dot(marks_ref[:, base:], far)).astype(BF16)

    sender, receiver = rows_of(senders_ref), rows_of(receivers_ref)
    sender_ref[...] = sender
    receiver_ref[...] = receiver
    hidden, slope, normed, inv_scale = edge_forward(
        edges_ref[...], sender, receiver, w_in_ref, w_out_ref
    )
    hidden_ref[...] = hidden
    slope_ref[...] = slope
    normed_ref[...] = normed
    scale_ref[...] = inv_scale
    message = normed.astype(BF16)
    total_ref[...] = inner_total_ref[...] + dot_rows(receivers_ref[:, :base], message)
    outgoing_ref[...] = dot_rows(receivers_ref[:, base:], message).astype(BF16)


def new_edges_kernel(edges_ref, inner_ref, cut_ref, dep_ref, out_ref):
    inner_rows = inner_ref.shape[0]

    def added(edge, normed):
        return (edge.astype(F32) + normed.astype(BF16).astype(F32)).astype(BF16)

    out_ref[:inner_rows] = added(edges_ref[:inner_rows], inner_ref[...])
    out_ref[inner_rows:] = added(edges_ref[inner_rows:], cut_ref[...])


def node_kernel(
    incoming_ref,
    asked_marks_ref,
    total_ref,
    nodes_ref,
    ct_ref,
    w_in_ref,
    w_out_ref,
    new_nodes_ref,
    self_grad_ref,
    agg_grad_ref,
    reply_ref,
    aggregate_ref,
    hidden_ref,
    grad_out_ref,
    grad_pre_ref,
):
    latent = nodes_ref.shape[1]
    nodes, asked_marks = nodes_ref[...], asked_marks_ref[...]
    aggregate = (total_ref[...] + dot_rows(asked_marks, incoming_ref[...])).astype(BF16)
    aggregate_ref[...] = aggregate
    pre_hidden = dot(nodes, w_in_ref[:latent]) + dot(aggregate, w_in_ref[latent:])
    hidden, slope = activate(pre_hidden)
    hidden_ref[...] = hidden
    normed, inv_scale = normalise(dot(hidden, w_out_ref[...]))
    upstream = ct_ref[...].astype(F32)
    grad_out = norm_backward(upstream, normed, inv_scale)
    grad_out_ref[...] = grad_out
    grad_pre = (dot_cols(grad_out, w_out_ref[...]) * slope).astype(BF16)
    grad_pre_ref[...] = grad_pre
    agg_grad = dot_cols(grad_pre, w_in_ref[latent:]).astype(BF16)
    agg_grad_ref[...] = agg_grad
    reply_ref[...] = dot(asked_marks, agg_grad).astype(BF16)
    self_grad_ref[...] = upstream + dot_cols(grad_pre, w_in_ref[:latent])
    new_nodes_ref[...] = (nodes.astype(F32) + normed).astype(BF16)


def node_weights_kernel(
    place_ref, nodes_ref, aggregate_ref, hidden_ref, grad_out_ref, grad_pre_ref, keep_ref, send_ref
):
    latent = nodes_ref.shape[1]
    half = latent // 2

    def fill(low_ref, high_ref):
        grad_pre, grad_out = grad_pre_ref[...], grad_out_ref[...]
        low_ref[:latent] = dot_rows(nodes_ref[...], grad_pre).astype(BF16)
        low_ref[latent:] = dot_rows(aggregate_ref[:, :half], grad_pre).astype(BF16)
        high_ref[:half] = dot_rows(aggregate_ref[:, half:], grad_pre).astype(BF16)
        high_ref[half:] = dot_rows(hidden_ref[...], grad_out).astype(BF16)

    @pl.when(place_ref[0] == 0)
    def _():
        fill(keep_ref, send_ref)

    @pl.when(place_ref[0] != 0)
    def _():
        fill(send_ref, keep_ref)


def edge_backward(ct, target_grads, normed, inv_scale, slope, w_out):
    grad_out = norm_backward(ct.astype(F32) + target_grads, normed, inv_scale)
    return grad_out, (dot_cols(grad_out, w_out) * slope).astype(BF16)


def inner_backward_kernel(
    receivers_ref,
    agg_grad_ref,
    ct_ref,
    normed_ref,
    scale_ref,
    slope_ref,
    w_out_ref,
    dep_ref,
    grad_out_ref,
    grad_pre_ref,
):
    grad_out, grad_pre = edge_backward(
        ct_ref[...],
        dot(receivers_ref[...], agg_grad_ref[...]),
        normed_ref[...],
        scale_ref[...],
        slope_ref[...],
        w_out_ref[...],
    )
    grad_out_ref[...] = grad_out
    grad_pre_ref[...] = grad_pre


def cut_backward_kernel(
    receivers_ref,
    agg_grad_ref,
    far_grad_ref,
    ct_ref,
    normed_ref,
    scale_ref,
    slope_ref,
    w_out_ref,
    grad_out_ref,
    grad_pre_ref,
):
    base = agg_grad_ref.shape[0]
    target = dot(receivers_ref[:, :base], agg_grad_ref[...]) + dot(
        receivers_ref[:, base:], far_grad_ref[...]
    )
    grad_out, grad_pre = edge_backward(
        ct_ref[...], target, normed_ref[...], scale_ref[...], slope_ref[...], w_out_ref[...]
    )
    grad_out_ref[...] = grad_out
    grad_pre_ref[...] = grad_pre


def edge_weights_kernel(
    place_ref,
    edges_ref,
    inner_sender_ref,
    cut_sender_ref,
    inner_receiver_ref,
    cut_receiver_ref,
    inner_hidden_ref,
    cut_hidden_ref,
    inner_out_ref,
    cut_out_ref,
    inner_pre_ref,
    cut_pre_ref,
    dep_ref,
    out_ref,
):
    latent = edges_ref.shape[1]
    inner_rows = inner_pre_ref.shape[0]

    @pl.when(place_ref[0] == 0)
    def _():
        inner_pre, cut_pre = inner_pre_ref[...], cut_pre_ref[...]
        out_ref[:latent] = (
            dot_rows(edges_ref[:inner_rows], inner_pre) + dot_rows(edges_ref[inner_rows:], cut_pre)
        ).astype(BF16)
        out_ref[latent:] = (
            dot_rows(inner_sender_ref[...], inner_pre) + dot_rows(cut_sender_ref[...], cut_pre)
        ).astype(BF16)

    @pl.when(place_ref[0] != 0)
    def _():
        out_ref[:latent] = (
            dot_rows(inner_receiver_ref[...], inner_pre_ref[...])
            + dot_rows(cut_receiver_ref[...], cut_pre_ref[...])
        ).astype(BF16)
        out_ref[latent:] = (
            dot_rows(inner_hidden_ref[...], inner_out_ref[...])
            + dot_rows(cut_hidden_ref[...], cut_out_ref[...])
        ).astype(BF16)


def input_grads_kernel(
    inner_senders_ref,
    inner_receivers_ref,
    cut_senders_ref,
    cut_receivers_ref,
    inner_pre_ref,
    cut_pre_ref,
    w_in_ref,
    dep_ref,
    local_ref,
    outgoing_ref,
):
    latent = inner_pre_ref.shape[1]
    base = inner_senders_ref.shape[1]
    inner_pre, cut_pre = inner_pre_ref[...], cut_pre_ref[...]
    w_sender, w_receiver = w_in_ref[latent : 2 * latent], w_in_ref[2 * latent :]

    def summed(inner_marks_ref, cut_marks_ref):
        return (
            dot_rows(inner_marks_ref[...], inner_pre) + dot_rows(cut_marks_ref[:, :base], cut_pre)
        ).astype(BF16)

    outgoing_ref[...] = (
        dot_cols(dot_rows(cut_senders_ref[:, base:], cut_pre).astype(BF16), w_sender)
        + dot_cols(dot_rows(cut_receivers_ref[:, base:], cut_pre).astype(BF16), w_receiver)
    ).astype(BF16)
    local_ref[...] = dot_cols(summed(inner_senders_ref, cut_senders_ref), w_sender) + dot_cols(
        summed(inner_receivers_ref, cut_receivers_ref), w_receiver
    )


def edge_grads_kernel(ct_ref, inner_pre_ref, cut_pre_ref, w_edge_ref, dep_ref, out_ref, *, blocks):
    inside = pl.program_id(0) < blocks

    @pl.when(inside)
    def _():
        out_ref[...] = ct_ref[...].astype(F32) + dot_cols(inner_pre_ref[...], w_edge_ref[...])

    @pl.when(jnp.logical_not(inside))
    def _():
        out_ref[...] = ct_ref[...].astype(F32) + dot_cols(cut_pre_ref[...], w_edge_ref[...])


def node_grads_kernel(self_ref, local_ref, asked_marks_ref, returned_ref, out_ref):
    out_ref[...] = (
        self_ref[...] + local_ref[...] + dot_rows(asked_marks_ref[...], returned_ref[...])
    )


VMEM = pl.BlockSpec(memory_space=pltpu.VMEM)
SMEM = pl.BlockSpec(memory_space=pltpu.SMEM)
ANY = pl.BlockSpec(memory_space=pl.ANY)


def shaped(dtype, *shape):
    return jax.ShapeDtypeStruct(shape, dtype)


def run(body, outs, ins, flops, specs=None, out_specs=None, grid=None):
    single = not isinstance(outs, (list, tuple))
    out_shape = [outs] if single else list(outs)
    moved = sum(item.size * item.dtype.itemsize for item in list(ins) + out_shape)
    extra = {} if grid is None else {"grid": grid}
    result = pl.pallas_call(
        body,
        out_shape=out_shape,
        in_specs=[VMEM] * len(ins) if specs is None else specs,
        out_specs=[VMEM] * len(out_shape) if out_specs is None else out_specs,
        compiler_params=pltpu.CompilerParams(vmem_limit_bytes=VMEM_LIMIT),
        cost_estimate=pl.CostEstimate(flops=flops, bytes_accessed=moved, transcendentals=0),
        **extra,
    )(*ins)
    return result[0] if single else result


def bit_groups(devices):
    bits = devices.bit_length() - 1
    groups = [(low, 1) for low in range(min(2, bits))]
    low = 2
    while low < bits:
        groups.append((low, min(2, bits - low)))
        low += 2
    return groups


def partner_pairs(devices, mask):
    return [(device, device ^ mask) for device in range(devices)]


def reduce_rows(keep, send, devices):
    me = lax.axis_index("dom")
    groups = bit_groups(devices)
    received = lax.ppermute(send, "dom", partner_pairs(devices, 1))
    rows = (keep.astype(F32) + received.astype(F32)).astype(BF16)
    for low, width in groups[1:]:
        size = 1 << width
        place = (me >> low) & (size - 1)
        chunk = rows.shape[0] // size
        pieces = rows.reshape(size, chunk, rows.shape[1])
        total = lax.dynamic_index_in_dim(pieces, place, 0, False).astype(F32)
        for turn in range(1, size):
            sent = lax.dynamic_index_in_dim(pieces, place ^ turn, 0, False)
            total += lax.ppermute(sent, "dom", partner_pairs(devices, turn << low)).astype(F32)
        rows = total.astype(BF16)
    return rows


def gather_rows(rows, devices):
    me = lax.axis_index("dom")
    for low, width in bit_groups(devices)[::-1]:
        size = 1 << width
        place = (me >> low) & (size - 1)
        whole = jnp.zeros((size,) + rows.shape, rows.dtype)
        for turn in range(size):
            piece = rows
            if turn:
                piece = lax.ppermute(rows, "dom", partner_pairs(devices, turn << low))
            whole = lax.dynamic_update_index_in_dim(whole, piece, place ^ turn, 0)
        rows = whole.reshape(size * rows.shape[0], rows.shape[1])
    return rows


def exchange(rows, domains):
    shape = rows.shape
    split = rows.reshape((domains, shape[0] // domains) + shape[1:])
    return lax.all_to_all(split, "dom", split_axis=0, concat_axis=0, tiled=True).reshape(shape)


def shards(
    nodes,
    edges,
    inner_pairs,
    cut_local,
    cut_dest,
    cut_remote,
    w_edge_in,
    w_edge_out,
    w_node_in,
    w_node_out,
    ct_nodes,
    ct_edges,
):
    domains = lax.axis_size("dom")
    node_rows, latent = nodes.shape
    inner_count, cut_count = inner_pairs.shape[0], cut_local.shape[0]
    inner_rows, cut_rows = 2 * inner_count, 2 * cut_count
    slots = max(2, 2 * cut_count // domains)
    total_slots = domains * slots
    table = node_rows + total_slots
    square = 2 * latent * latent
    place = lax.axis_index("dom") & 1
    mine, other = place.reshape(1), (1 - place).reshape(1)

    ask = run(
        ask_kernel, shaped(jnp.int32, domains, slots), [cut_dest, cut_remote.reshape(1, -1)], 10**7
    )
    asked = lax.all_to_all(ask, "dom", split_axis=0, concat_axis=0, tiled=True)
    cut_senders, cut_receivers = run(
        functools.partial(cut_marks_kernel, domains=domains, slots=slots),
        [shaped(BF16, cut_rows, table)] * 2,
        [cut_dest, cut_local.reshape(1, -1), ask],
        10**8,
        [VMEM, VMEM, ANY],
    )
    reply, asked_marks = run(
        reply_kernel,
        [shaped(BF16, total_slots, latent), shaped(BF16, total_slots, node_rows)],
        [asked, nodes],
        10**8,
    )
    far = exchange(reply, domains)

    block = cut_rows
    blocks = inner_rows // block

    def rows_spec(width, rows=block):
        return pl.BlockSpec((rows, width), lambda step: (step, 0))

    def all_spec(array):
        return pl.BlockSpec(array.shape, lambda step: (0, 0))

    saved_widths = [node_rows, node_rows, latent, latent, latent, latent, latent, 1]
    saved_types = [BF16, BF16, BF16, BF16, BF16, F32, F32, F32]
    (
        inner_senders,
        inner_receivers,
        inner_sender,
        inner_receiver,
        inner_hidden,
        inner_slope,
        inner_normed,
        inner_scale,
        inner_total,
    ) = run(
        inner_forward_kernel,
        [shaped(kind, inner_rows, width) for kind, width in zip(saved_types, saved_widths)]
        + [shaped(F32, node_rows, latent)],
        [inner_pairs, edges, nodes, w_edge_in, w_edge_out, reply],
        inner_rows * 4 * square,
        [
            rows_spec(2, block // 2),
            rows_spec(latent),
            all_spec(nodes),
            all_spec(w_edge_in),
            all_spec(w_edge_out),
            ANY,
        ],
        [rows_spec(width) for width in saved_widths] + [all_spec(nodes)],
        (blocks,),
    )

    def last_rows(array):
        return pl.BlockSpec((block, array.shape[1]), lambda step: (blocks, 0))

    (
        cut_sender,
        cut_receiver,
        cut_hidden,
        cut_slope,
        cut_normed,
        cut_scale,
        total,
        outgoing,
    ) = run(
        cut_forward_kernel,
        [shaped(kind, cut_rows, width) for kind, width in zip(saved_types, saved_widths)][2:]
        + [shaped(F32, node_rows, latent), shaped(BF16, total_slots, latent)],
        [
            cut_senders,
            cut_receivers,
            edges,
            nodes,
            far,
            w_edge_in,
            w_edge_out,
            inner_total,
        ],
        cut_rows * 4 * square,
        [
            all_spec(cut_senders),
            all_spec(cut_receivers),
            last_rows(edges),
            all_spec(nodes),
            all_spec(far),
            all_spec(w_edge_in),
            all_spec(w_edge_out),
            all_spec(inner_total),
        ],
        [rows_spec(width) for width in saved_widths[2:]]
        + [all_spec(nodes), rows_spec(latent, total_slots)],
        (1,),
    )
    incoming = exchange(outgoing, domains)
    new_edges = run(
        new_edges_kernel,
        shaped(BF16, *edges.shape),
        [edges, inner_normed, cut_normed, outgoing],
        10**7,
        [VMEM, VMEM, VMEM, ANY],
    )
    (
        new_nodes,
        self_grad,
        agg_grad,
        grad_reply,
        aggregate,
        node_hidden,
        node_out,
        node_pre,
    ) = run(
        node_kernel,
        [
            shaped(BF16, node_rows, latent),
            shaped(F32, node_rows, latent),
            shaped(BF16, node_rows, latent),
            shaped(BF16, total_slots, latent),
        ]
        + [shaped(BF16, node_rows, latent)] * 4,
        [incoming, asked_marks, total, nodes, ct_nodes, w_node_in, w_node_out],
        node_rows * 6 * square,
    )
    far_grad = exchange(grad_reply, domains)
    node_keep, node_send = run(
        node_weights_kernel,
        [shaped(BF16, 3 * latent // 2, latent)] * 2,
        [mine, nodes, aggregate, node_hidden, node_out, node_pre],
        node_rows * 3 * square,
        [SMEM] + [VMEM] * 5,
    )
    node_total = gather_rows(reduce_rows(node_keep, node_send, domains), domains)

    inner_out, inner_pre = run(
        inner_backward_kernel,
        [shaped(BF16, inner_rows, latent)] * 2,
        [
            inner_receivers,
            agg_grad,
            ct_edges,
            inner_normed,
            inner_scale,
            inner_slope,
            w_edge_out,
            grad_reply,
        ],
        inner_rows * square,
        [
            rows_spec(node_rows),
            all_spec(agg_grad),
            rows_spec(latent),
            rows_spec(latent),
            rows_spec(1),
            rows_spec(latent),
            all_spec(w_edge_out),
            ANY,
        ],
        [rows_spec(latent)] * 2,
        (blocks,),
    )
    cut_out, cut_pre = run(
        cut_backward_kernel,
        [shaped(BF16, cut_rows, latent)] * 2,
        [
            cut_receivers,
            agg_grad,
            far_grad,
            ct_edges,
            cut_normed,
            cut_scale,
            cut_slope,
            w_edge_out,
        ],
        cut_rows * square,
        [
            all_spec(cut_receivers),
            all_spec(agg_grad),
            all_spec(far_grad),
            last_rows(ct_edges),
            all_spec(cut_normed),
            all_spec(cut_scale),
            all_spec(cut_slope),
            all_spec(w_edge_out),
        ],
        [rows_spec(latent)] * 2,
        (1,),
    )
    factors = [
        edges,
        inner_sender,
        cut_sender,
        inner_receiver,
        cut_receiver,
        inner_hidden,
        cut_hidden,
        inner_out,
        cut_out,
        inner_pre,
        cut_pre,
    ]

    def edge_weights(half, dep):
        return run(
            edge_weights_kernel,
            shaped(BF16, 2 * latent, latent),
            [half] + factors + [dep],
            (inner_rows + cut_rows) * 2 * square,
            [SMEM] + [VMEM] * len(factors) + [ANY],
        )

    edge_send = edge_weights(other, cut_pre)
    edge_keep = edge_weights(mine, edge_send)
    edge_total = gather_rows(reduce_rows(edge_keep, edge_send, domains), domains)
    local_grad, outgoing_grad = run(
        input_grads_kernel,
        [shaped(F32, node_rows, latent), shaped(BF16, total_slots, latent)],
        [
            inner_senders,
            inner_receivers,
            cut_senders,
            cut_receivers,
            inner_pre,
            cut_pre,
            w_edge_in,
            edge_keep,
        ],
        (node_rows + total_slots) * 2 * square,
        [VMEM] * 7 + [ANY],
    )
    grad_edges = run(
        functools.partial(edge_grads_kernel, blocks=blocks),
        shaped(F32, *edges.shape),
        [ct_edges, inner_pre, cut_pre, w_edge_in, edge_keep],
        (inner_rows + cut_rows) * square,
        [
            rows_spec(latent),
            pl.BlockSpec((block, latent), lambda step: (jnp.minimum(step, blocks - 1), 0)),
            all_spec(cut_pre),
            pl.BlockSpec((latent, latent), lambda step: (0, 0)),
            ANY,
        ],
        [rows_spec(latent)],
        (blocks + 1,),
    )
    returned = exchange(outgoing_grad, domains)
    grad_nodes = run(
        node_grads_kernel,
        shaped(F32, node_rows, latent),
        [self_grad, local_grad, asked_marks, returned],
        10**8,
    )
    return (
        new_nodes,
        new_edges,
        grad_nodes,
        grad_edges,
        edge_total[: 3 * latent],
        edge_total[3 * latent :],
        node_total[: 2 * latent],
        node_total[2 * latent :],
    )


def solution(mesh):
    placed = (
        P(("groups", "dom"), None),
        P(("groups", "dom"), None),
        P(("groups", "dom"), None),
        P(("groups", "dom")),
        P(("groups", "dom"), None),
        P(("groups", "dom")),
        P(),
        P(),
        P(),
        P(),
        P(("groups", "dom"), None),
        P(("groups", "dom"), None),
    )
    return jax.shard_map(
        shards,
        mesh=mesh,
        in_specs=placed,
        out_specs=(
            P(("groups", "dom"), None),
            P(("groups", "dom"), None),
            P(("groups", "dom"), None),
            P(("groups", "dom"), None),
            P("groups", None),
            P("groups", None),
            P("groups", None),
            P("groups", None),
        ),
        check_vma=False,
    )
```

```python
import functools

import jax
import jax.numpy as jnp
from jax import lax
from jax.experimental import pallas as pl
from jax.experimental.pallas import tpu as pltpu
from jax.sharding import PartitionSpec as P

BF16 = jnp.bfloat16
F32 = jnp.float32
VMEM_LIMIT = 60 * 1024 * 1024


def dot(left, right):
    return jnp.dot(left, right, preferred_element_type=F32)


def dot_rows(left, right):
    return lax.dot_general(left, right, (((0,), (0,)), ((), ())), preferred_element_type=F32)


def dot_cols(left, right):
    return lax.dot_general(left, right, (((1,), (1,)), ((), ())), preferred_element_type=F32)


def iota(shape, axis):
    return lax.broadcasted_iota(jnp.int32, shape, axis)


def marks(mask):
    return jnp.where(mask, 1.0, 0.0).astype(BF16)


def onehot(column, width):
    return marks(column == iota((column.shape[0], width), 1))


def to_column(row):
    count = row.shape[1]
    square = (count, count)
    kept = jnp.where(iota(square, 0) == iota(square, 1), row.astype(F32), 0.0)
    return jnp.sum(kept, axis=1, keepdims=True)


def slot_ranks(dest, domains):
    count = dest.shape[0]
    square = (count, count)
    dest_marks = onehot(dest, domains)
    before = dot(marks(iota(square, 0) > iota(square, 1)), dest_marks)
    return dest_marks, jnp.sum(before * dest_marks.astype(F32), axis=1, keepdims=True)


def pair_marks(first, second, width):
    pairs = first.shape[0]
    shape = (2 * pairs, pairs)
    edge, pair = iota(shape, 0), iota(shape, 1)
    mine = (edge >> 1) == pair
    even = marks(mine & ((edge & 1) == 0))
    odd = marks(mine & ((edge & 1) == 1))
    first_marks, second_marks = onehot(first, width), onehot(second, width)
    senders = dot(even, first_marks) + dot(odd, second_marks)
    receivers = dot(even, second_marks) + dot(odd, first_marks)
    return senders.astype(BF16), receivers.astype(BF16)


def normalise(values):
    centered = values - jnp.mean(values, axis=1, keepdims=True)
    inv_scale = lax.rsqrt(jnp.mean(centered * centered, axis=1, keepdims=True) + 1e-05)
    return centered * inv_scale, inv_scale


def activate(pre_hidden):
    gate = jax.nn.sigmoid(pre_hidden)
    return (pre_hidden * gate).astype(BF16), gate * (1.0 + pre_hidden * (1.0 - gate))


def norm_backward(upstream, normed, inv_scale):
    centered = (
        upstream
        - jnp.mean(upstream, axis=1, keepdims=True)
        - normed * jnp.mean(upstream * normed, axis=1, keepdims=True)
    )
    return (inv_scale * centered).astype(BF16)


def ask_kernel(dest_ref, remote_ref, ask_ref):
    domains, slots = ask_ref.shape
    dest_marks, rank = slot_ranks(to_column(dest_ref[...]).astype(jnp.int32), domains)
    rank_marks = jnp.where(rank == iota((rank.shape[0], slots), 1).astype(F32), 1.0, 0.0)
    wanted = (rank_marks * to_column(remote_ref[...])).astype(BF16)
    ask_ref[...] = dot_rows(dest_marks, wanted).astype(jnp.int32)


def reply_kernel(asked_ref, nodes_ref, reply_ref, asked_marks_ref):
    domains, slots = asked_ref.shape
    total = domains * slots
    shift = slots.bit_length() - 1
    spread = marks((iota((total, domains), 0) >> shift) == iota((total, domains), 1))
    listed = dot(spread, asked_ref[...].astype(F32).astype(BF16))
    at_slot = (iota((total, slots), 0) & (slots - 1)) == iota((total, slots), 1)
    column = jnp.sum(jnp.where(at_slot, listed, 0.0), axis=1, keepdims=True)
    node_rows = nodes_ref.shape[0]
    asked_marks = marks(column == iota((total, node_rows), 1).astype(F32))
    asked_marks_ref[...] = asked_marks
    reply_ref[...] = dot(asked_marks, nodes_ref[...]).astype(BF16)


def cut_marks_kernel(dest_ref, local_ref, dep_ref, senders_ref, receivers_ref, *, domains, slots):
    width = senders_ref.shape[1]
    base = width - domains * slots
    dest = to_column(dest_ref[...]).astype(jnp.int32)
    _, rank = slot_ranks(dest, domains)
    second = dest * slots + rank.astype(jnp.int32) + base
    first = to_column(local_ref[...]).astype(jnp.int32)
    senders, receivers = pair_marks(first, second, width)
    senders_ref[...] = senders
    receivers_ref[...] = receivers


def edge_forward(edge, sender, receiver, w_in_ref, w_out_ref):
    latent = edge.shape[1]
    pre_hidden = (
        dot(edge, w_in_ref[:latent])
        + dot(sender, w_in_ref[latent : 2 * latent])
        + dot(receiver, w_in_ref[2 * latent :])
    )
    hidden, slope = activate(pre_hidden)
    normed, inv_scale = normalise(dot(hidden, w_out_ref[...]))
    return hidden, slope, normed, inv_scale


def inner_forward_kernel(
    pairs_ref,
    edges_ref,
    nodes_ref,
    w_in_ref,
    w_out_ref,
    dep_ref,
    senders_ref,
    receivers_ref,
    sender_ref,
    receiver_ref,
    hidden_ref,
    slope_ref,
    normed_ref,
    scale_ref,
    total_ref,
):
    first, second = (to_column(pairs_ref[side : side + 1]).astype(jnp.int32) for side in range(2))
    senders, receivers = pair_marks(first, second, nodes_ref.shape[0])
    senders_ref[...] = senders
    receivers_ref[...] = receivers
    nodes = nodes_ref[...]
    sender = dot(senders, nodes).astype(BF16)
    receiver = dot(receivers, nodes).astype(BF16)
    sender_ref[...] = sender
    receiver_ref[...] = receiver
    hidden, slope, normed, inv_scale = edge_forward(
        edges_ref[...], sender, receiver, w_in_ref, w_out_ref
    )
    hidden_ref[...] = hidden
    slope_ref[...] = slope
    normed_ref[...] = normed
    scale_ref[...] = inv_scale
    part = dot_rows(receivers, normed.astype(BF16))

    @pl.when(pl.program_id(0) == 0)
    def _():
        total_ref[...] = part

    @pl.when(pl.program_id(0) > 0)
    def _():
        total_ref[...] += part


def cut_forward_kernel(
    senders_ref,
    receivers_ref,
    edges_ref,
    nodes_ref,
    far_ref,
    w_in_ref,
    w_out_ref,
    inner_total_ref,
    sender_ref,
    receiver_ref,
    hidden_ref,
    slope_ref,
    normed_ref,
    scale_ref,
    total_ref,
    outgoing_ref,
):
    base = nodes_ref.shape[0]
    nodes, far = nodes_ref[...], far_ref[...]

    def rows_of(marks_ref):
        return (dot(marks_ref[:, :base], nodes) + dot(marks_ref[:, base:], far)).astype(BF16)

    sender, receiver = rows_of(senders_ref), rows_of(receivers_ref)
    sender_ref[...] = sender
    receiver_ref[...] = receiver
    hidden, slope, normed, inv_scale = edge_forward(
        edges_ref[...], sender, receiver, w_in_ref, w_out_ref
    )
    hidden_ref[...] = hidden
    slope_ref[...] = slope
    normed_ref[...] = normed
    scale_ref[...] = inv_scale
    message = normed.astype(BF16)
    total_ref[...] = inner_total_ref[...] + dot_rows(receivers_ref[:, :base], message)
    outgoing_ref[...] = dot_rows(receivers_ref[:, base:], message).astype(BF16)


def new_edges_kernel(edges_ref, inner_ref, cut_ref, dep_ref, out_ref):
    inner_rows = inner_ref.shape[0]

    def added(edge, normed):
        return (edge.astype(F32) + normed.astype(BF16).astype(F32)).astype(BF16)

    out_ref[:inner_rows] = added(edges_ref[:inner_rows], inner_ref[...])
    out_ref[inner_rows:] = added(edges_ref[inner_rows:], cut_ref[...])


def node_kernel(
    incoming_ref,
    asked_marks_ref,
    total_ref,
    nodes_ref,
    ct_ref,
    w_in_ref,
    w_out_ref,
    new_nodes_ref,
    self_grad_ref,
    agg_grad_ref,
    reply_ref,
    aggregate_ref,
    hidden_ref,
    grad_out_ref,
    grad_pre_ref,
):
    latent = nodes_ref.shape[1]
    nodes, asked_marks = nodes_ref[...], asked_marks_ref[...]
    aggregate = (total_ref[...] + dot_rows(asked_marks, incoming_ref[...])).astype(BF16)
    aggregate_ref[...] = aggregate
    pre_hidden = dot(nodes, w_in_ref[:latent]) + dot(aggregate, w_in_ref[latent:])
    hidden, slope = activate(pre_hidden)
    hidden_ref[...] = hidden
    normed, inv_scale = normalise(dot(hidden, w_out_ref[...]))
    upstream = ct_ref[...].astype(F32)
    grad_out = norm_backward(upstream, normed, inv_scale)
    grad_out_ref[...] = grad_out
    grad_pre = (dot_cols(grad_out, w_out_ref[...]) * slope).astype(BF16)
    grad_pre_ref[...] = grad_pre
    agg_grad = dot_cols(grad_pre, w_in_ref[latent:]).astype(BF16)
    agg_grad_ref[...] = agg_grad
    reply_ref[...] = dot(asked_marks, agg_grad).astype(BF16)
    self_grad_ref[...] = upstream + dot_cols(grad_pre, w_in_ref[:latent])
    new_nodes_ref[...] = (nodes.astype(F32) + normed).astype(BF16)


def node_weights_kernel(
    place_ref, nodes_ref, aggregate_ref, hidden_ref, grad_out_ref, grad_pre_ref, keep_ref, send_ref
):
    latent = nodes_ref.shape[1]
    half = latent // 2

    def fill(low_ref, high_ref):
        grad_pre, grad_out = grad_pre_ref[...], grad_out_ref[...]
        low_ref[:latent] = dot_rows(nodes_ref[...], grad_pre).astype(BF16)
        low_ref[latent:] = dot_rows(aggregate_ref[:, :half], grad_pre).astype(BF16)
        high_ref[:half] = dot_rows(aggregate_ref[:, half:], grad_pre).astype(BF16)
        high_ref[half:] = dot_rows(hidden_ref[...], grad_out).astype(BF16)

    @pl.when(place_ref[0] == 0)
    def _():
        fill(keep_ref, send_ref)

    @pl.when(place_ref[0] != 0)
    def _():
        fill(send_ref, keep_ref)


def edge_backward(ct, target_grads, normed, inv_scale, slope, w_out):
    grad_out = norm_backward(ct.astype(F32) + target_grads, normed, inv_scale)
    return grad_out, (dot_cols(grad_out, w_out) * slope).astype(BF16)


def inner_backward_kernel(
    receivers_ref,
    agg_grad_ref,
    ct_ref,
    normed_ref,
    scale_ref,
    slope_ref,
    w_out_ref,
    dep_ref,
    grad_out_ref,
    grad_pre_ref,
):
    grad_out, grad_pre = edge_backward(
        ct_ref[...],
        dot(receivers_ref[...], agg_grad_ref[...]),
        normed_ref[...],
        scale_ref[...],
        slope_ref[...],
        w_out_ref[...],
    )
    grad_out_ref[...] = grad_out
    grad_pre_ref[...] = grad_pre


def cut_backward_kernel(
    receivers_ref,
    agg_grad_ref,
    far_grad_ref,
    ct_ref,
    normed_ref,
    scale_ref,
    slope_ref,
    w_out_ref,
    grad_out_ref,
    grad_pre_ref,
):
    base = agg_grad_ref.shape[0]
    target = dot(receivers_ref[:, :base], agg_grad_ref[...]) + dot(
        receivers_ref[:, base:], far_grad_ref[...]
    )
    grad_out, grad_pre = edge_backward(
        ct_ref[...], target, normed_ref[...], scale_ref[...], slope_ref[...], w_out_ref[...]
    )
    grad_out_ref[...] = grad_out
    grad_pre_ref[...] = grad_pre


def edge_weights_kernel(
    place_ref,
    edges_ref,
    inner_sender_ref,
    cut_sender_ref,
    inner_receiver_ref,
    cut_receiver_ref,
    inner_hidden_ref,
    cut_hidden_ref,
    inner_out_ref,
    cut_out_ref,
    inner_pre_ref,
    cut_pre_ref,
    dep_ref,
    out_ref,
):
    latent = edges_ref.shape[1]
    inner_rows = inner_pre_ref.shape[0]

    @pl.when(place_ref[0] == 0)
    def _():
        inner_pre, cut_pre = inner_pre_ref[...], cut_pre_ref[...]
        out_ref[:latent] = (
            dot_rows(edges_ref[:inner_rows], inner_pre) + dot_rows(edges_ref[inner_rows:], cut_pre)
        ).astype(BF16)
        out_ref[latent:] = (
            dot_rows(inner_sender_ref[...], inner_pre) + dot_rows(cut_sender_ref[...], cut_pre)
        ).astype(BF16)

    @pl.when(place_ref[0] != 0)
    def _():
        out_ref[:latent] = (
            dot_rows(inner_receiver_ref[...], inner_pre_ref[...])
            + dot_rows(cut_receiver_ref[...], cut_pre_ref[...])
        ).astype(BF16)
        out_ref[latent:] = (
            dot_rows(inner_hidden_ref[...], inner_out_ref[...])
            + dot_rows(cut_hidden_ref[...], cut_out_ref[...])
        ).astype(BF16)


def input_grads_kernel(
    inner_senders_ref,
    inner_receivers_ref,
    cut_senders_ref,
    cut_receivers_ref,
    inner_pre_ref,
    cut_pre_ref,
    w_in_ref,
    dep_ref,
    local_ref,
    outgoing_ref,
):
    latent = inner_pre_ref.shape[1]
    base = inner_senders_ref.shape[1]
    inner_pre, cut_pre = inner_pre_ref[...], cut_pre_ref[...]
    w_sender, w_receiver = w_in_ref[latent : 2 * latent], w_in_ref[2 * latent :]

    def summed(inner_marks_ref, cut_marks_ref):
        return (
            dot_rows(inner_marks_ref[...], inner_pre) + dot_rows(cut_marks_ref[:, :base], cut_pre)
        ).astype(BF16)

    outgoing_ref[...] = (
        dot_cols(dot_rows(cut_senders_ref[:, base:], cut_pre).astype(BF16), w_sender)
        + dot_cols(dot_rows(cut_receivers_ref[:, base:], cut_pre).astype(BF16), w_receiver)
    ).astype(BF16)
    local_ref[...] = dot_cols(summed(inner_senders_ref, cut_senders_ref), w_sender) + dot_cols(
        summed(inner_receivers_ref, cut_receivers_ref), w_receiver
    )


def edge_grads_kernel(ct_ref, inner_pre_ref, cut_pre_ref, w_edge_ref, dep_ref, out_ref, *, blocks):
    inside = pl.program_id(0) < blocks

    @pl.when(inside)
    def _():
        out_ref[...] = ct_ref[...].astype(F32) + dot_cols(inner_pre_ref[...], w_edge_ref[...])

    @pl.when(jnp.logical_not(inside))
    def _():
        out_ref[...] = ct_ref[...].astype(F32) + dot_cols(cut_pre_ref[...], w_edge_ref[...])


def node_grads_kernel(self_ref, local_ref, asked_marks_ref, returned_ref, out_ref):
    out_ref[...] = (
        self_ref[...] + local_ref[...] + dot_rows(asked_marks_ref[...], returned_ref[...])
    )


VMEM = pl.BlockSpec(memory_space=pltpu.VMEM)
SMEM = pl.BlockSpec(memory_space=pltpu.SMEM)
ANY = pl.BlockSpec(memory_space=pl.ANY)


def shaped(dtype, *shape):
    return jax.ShapeDtypeStruct(shape, dtype)


def run(body, outs, ins, flops, specs=None, out_specs=None, grid=None):
    single = not isinstance(outs, (list, tuple))
    out_shape = [outs] if single else list(outs)
    moved = sum(item.size * item.dtype.itemsize for item in list(ins) + out_shape)
    extra = {} if grid is None else {"grid": grid}
    result = pl.pallas_call(
        body,
        out_shape=out_shape,
        in_specs=[VMEM] * len(ins) if specs is None else specs,
        out_specs=[VMEM] * len(out_shape) if out_specs is None else out_specs,
        compiler_params=pltpu.CompilerParams(vmem_limit_bytes=VMEM_LIMIT),
        cost_estimate=pl.CostEstimate(flops=flops, bytes_accessed=moved, transcendentals=0),
        **extra,
    )(*ins)
    return result[0] if single else result


def bit_groups(devices):
    bits = devices.bit_length() - 1
    groups = [(low, 1) for low in range(min(2, bits))]
    low = 2
    while low < bits:
        groups.append((low, min(2, bits - low)))
        low += 2
    return groups


def partner_pairs(devices, mask):
    return [(device, device ^ mask) for device in range(devices)]


def reduce_rows(keep, send, devices):
    me = lax.axis_index("dom")
    groups = bit_groups(devices)
    received = lax.ppermute(send, "dom", partner_pairs(devices, 1))
    rows = (keep.astype(F32) + received.astype(F32)).astype(BF16)
    for low, width in groups[1:]:
        size = 1 << width
        place = (me >> low) & (size - 1)
        chunk = rows.shape[0] // size
        pieces = rows.reshape(size, chunk, rows.shape[1])
        total = lax.dynamic_index_in_dim(pieces, place, 0, False).astype(F32)
        for turn in range(1, size):
            sent = lax.dynamic_index_in_dim(pieces, place ^ turn, 0, False)
            total += lax.ppermute(sent, "dom", partner_pairs(devices, turn << low)).astype(F32)
        rows = total.astype(BF16)
    return rows


def gather_rows(rows, devices):
    me = lax.axis_index("dom")
    for low, width in bit_groups(devices)[::-1]:
        size = 1 << width
        place = (me >> low) & (size - 1)
        whole = jnp.zeros((size,) + rows.shape, rows.dtype)
        for turn in range(size):
            piece = rows
            if turn:
                piece = lax.ppermute(rows, "dom", partner_pairs(devices, turn << low))
            whole = lax.dynamic_update_index_in_dim(whole, piece, place ^ turn, 0)
        rows = whole.reshape(size * rows.shape[0], rows.shape[1])
    return rows


def exchange(rows, domains):
    shape = rows.shape
    split = rows.reshape((domains, shape[0] // domains) + shape[1:])
    return lax.all_to_all(split, "dom", split_axis=0, concat_axis=0, tiled=True).reshape(shape)


def shards(
    nodes,
    edges,
    inner_pairs,
    cut_local,
    cut_dest,
    cut_remote,
    w_edge_in,
    w_edge_out,
    w_node_in,
    w_node_out,
    ct_nodes,
    ct_edges,
):
    domains = lax.axis_size("dom")
    node_rows, latent = nodes.shape
    inner_count, cut_count = inner_pairs.shape[0], cut_local.shape[0]
    inner_rows, cut_rows = 2 * inner_count, 2 * cut_count
    slots = max(2, 2 * cut_count // domains)
    total_slots = domains * slots
    table = node_rows + total_slots
    square = 2 * latent * latent
    place = lax.axis_index("dom") & 1
    mine, other = place.reshape(1), (1 - place).reshape(1)

    ask = run(
        ask_kernel, shaped(jnp.int32, domains, slots), [cut_dest.reshape(1, -1), cut_remote.reshape(1, -1)], 10**7
    )
    asked = lax.all_to_all(ask, "dom", split_axis=0, concat_axis=0, tiled=True)
    cut_senders, cut_receivers = run(
        functools.partial(cut_marks_kernel, domains=domains, slots=slots),
        [shaped(BF16, cut_rows, table)] * 2,
        [cut_dest.reshape(1, -1), cut_local.reshape(1, -1), ask],
        10**8,
        [VMEM, VMEM, ANY],
    )
    reply, asked_marks = run(
        reply_kernel,
        [shaped(BF16, total_slots, latent), shaped(BF16, total_slots, node_rows)],
        [asked, nodes],
        10**8,
    )
    far = exchange(reply, domains)

    block = cut_rows
    blocks = inner_rows // block

    def rows_spec(width, rows=block):
        return pl.BlockSpec((rows, width), lambda step: (step, 0))

    def all_spec(array):
        return pl.BlockSpec(array.shape, lambda step: (0, 0))

    saved_widths = [node_rows, node_rows, latent, latent, latent, latent, latent, 1]
    saved_types = [BF16, BF16, BF16, BF16, BF16, F32, F32, F32]
    (
        inner_senders,
        inner_receivers,
        inner_sender,
        inner_receiver,
        inner_hidden,
        inner_slope,
        inner_normed,
        inner_scale,
        inner_total,
    ) = run(
        inner_forward_kernel,
        [shaped(kind, inner_rows, width) for kind, width in zip(saved_types, saved_widths)]
        + [shaped(F32, node_rows, latent)],
        [inner_pairs.T, edges, nodes, w_edge_in, w_edge_out, reply],
        inner_rows * 4 * square,
        [
            pl.BlockSpec((2, block // 2), lambda step: (0, step)),
            rows_spec(latent),
            all_spec(nodes),
            all_spec(w_edge_in),
            all_spec(w_edge_out),
            ANY,
        ],
        [rows_spec(width) for width in saved_widths] + [all_spec(nodes)],
        (blocks,),
    )

    def last_rows(array):
        return pl.BlockSpec((block, array.shape[1]), lambda step: (blocks, 0))

    (
        cut_sender,
        cut_receiver,
        cut_hidden,
        cut_slope,
        cut_normed,
        cut_scale,
        total,
        outgoing,
    ) = run(
        cut_forward_kernel,
        [shaped(kind, cut_rows, width) for kind, width in zip(saved_types, saved_widths)][2:]
        + [shaped(F32, node_rows, latent), shaped(BF16, total_slots, latent)],
        [
            cut_senders,
            cut_receivers,
            edges,
            nodes,
            far,
            w_edge_in,
            w_edge_out,
            inner_total,
        ],
        cut_rows * 4 * square,
        [
            all_spec(cut_senders),
            all_spec(cut_receivers),
            last_rows(edges),
            all_spec(nodes),
            all_spec(far),
            all_spec(w_edge_in),
            all_spec(w_edge_out),
            all_spec(inner_total),
        ],
        [rows_spec(width) for width in saved_widths[2:]]
        + [all_spec(nodes), rows_spec(latent, total_slots)],
        (1,),
    )
    incoming = exchange(outgoing, domains)
    new_edges = run(
        new_edges_kernel,
        shaped(BF16, *edges.shape),
        [edges, inner_normed, cut_normed, outgoing],
        10**7,
        [VMEM, VMEM, VMEM, ANY],
    )
    (
        new_nodes,
        self_grad,
        agg_grad,
        grad_reply,
        aggregate,
        node_hidden,
        node_out,
        node_pre,
    ) = run(
        node_kernel,
        [
            shaped(BF16, node_rows, latent),
            shaped(F32, node_rows, latent),
            shaped(BF16, node_rows, latent),
            shaped(BF16, total_slots, latent),
        ]
        + [shaped(BF16, node_rows, latent)] * 4,
        [incoming, asked_marks, total, nodes, ct_nodes, w_node_in, w_node_out],
        node_rows * 6 * square,
    )
    far_grad = exchange(grad_reply, domains)
    node_keep, node_send = run(
        node_weights_kernel,
        [shaped(BF16, 3 * latent // 2, latent)] * 2,
        [mine, nodes, aggregate, node_hidden, node_out, node_pre],
        node_rows * 3 * square,
        [SMEM] + [VMEM] * 5,
    )
    node_total = gather_rows(reduce_rows(node_keep, node_send, domains), domains)

    inner_out, inner_pre = run(
        inner_backward_kernel,
        [shaped(BF16, inner_rows, latent)] * 2,
        [
            inner_receivers,
            agg_grad,
            ct_edges,
            inner_normed,
            inner_scale,
            inner_slope,
            w_edge_out,
            grad_reply,
        ],
        inner_rows * square,
        [
            rows_spec(node_rows),
            all_spec(agg_grad),
            rows_spec(latent),
            rows_spec(latent),
            rows_spec(1),
            rows_spec(latent),
            all_spec(w_edge_out),
            ANY,
        ],
        [rows_spec(latent)] * 2,
        (blocks,),
    )
    cut_out, cut_pre = run(
        cut_backward_kernel,
        [shaped(BF16, cut_rows, latent)] * 2,
        [
            cut_receivers,
            agg_grad,
            far_grad,
            ct_edges,
            cut_normed,
            cut_scale,
            cut_slope,
            w_edge_out,
        ],
        cut_rows * square,
        [
            all_spec(cut_receivers),
            all_spec(agg_grad),
            all_spec(far_grad),
            last_rows(ct_edges),
            all_spec(cut_normed),
            all_spec(cut_scale),
            all_spec(cut_slope),
            all_spec(w_edge_out),
        ],
        [rows_spec(latent)] * 2,
        (1,),
    )
    factors = [
        edges,
        inner_sender,
        cut_sender,
        inner_receiver,
        cut_receiver,
        inner_hidden,
        cut_hidden,
        inner_out,
        cut_out,
        inner_pre,
        cut_pre,
    ]

    def edge_weights(half, dep):
        return run(
            edge_weights_kernel,
            shaped(BF16, 2 * latent, latent),
            [half] + factors + [dep],
            (inner_rows + cut_rows) * 2 * square,
            [SMEM] + [VMEM] * len(factors) + [ANY],
        )

    edge_send = edge_weights(other, cut_pre)
    edge_keep = edge_weights(mine, edge_send)
    edge_total = gather_rows(reduce_rows(edge_keep, edge_send, domains), domains)
    local_grad, outgoing_grad = run(
        input_grads_kernel,
        [shaped(F32, node_rows, latent), shaped(BF16, total_slots, latent)],
        [
            inner_senders,
            inner_receivers,
            cut_senders,
            cut_receivers,
            inner_pre,
            cut_pre,
            w_edge_in,
            edge_keep,
        ],
        (node_rows + total_slots) * 2 * square,
        [VMEM] * 7 + [ANY],
    )
    grad_edges = run(
        functools.partial(edge_grads_kernel, blocks=blocks),
        shaped(F32, *edges.shape),
        [ct_edges, inner_pre, cut_pre, w_edge_in, edge_keep],
        (inner_rows + cut_rows) * square,
        [
            rows_spec(latent),
            pl.BlockSpec((block, latent), lambda step: (jnp.minimum(step, blocks - 1), 0)),
            all_spec(cut_pre),
            pl.BlockSpec((latent, latent), lambda step: (0, 0)),
            ANY,
        ],
        [rows_spec(latent)],
        (blocks + 1,),
    )
    returned = exchange(outgoing_grad, domains)
    grad_nodes = run(
        node_grads_kernel,
        shaped(F32, node_rows, latent),
        [self_grad, local_grad, asked_marks, returned],
        10**8,
    )
    return (
        new_nodes,
        new_edges,
        grad_nodes,
        grad_edges,
        edge_total[: 3 * latent],
        edge_total[3 * latent :],
        node_total[: 2 * latent],
        node_total[2 * latent :],
    )


def solution(mesh):
    placed = (
        P(("groups", "dom"), None),
        P(("groups", "dom"), None),
        P(("groups", "dom"), None),
        P(("groups", "dom")),
        P(("groups", "dom"), None),
        P(("groups", "dom")),
        P(),
        P(),
        P(),
        P(),
        P(("groups", "dom"), None),
        P(("groups", "dom"), None),
    )
    return jax.shard_map(
        shards,
        mesh=mesh,
        in_specs=placed,
        out_specs=(
            P(("groups", "dom"), None),
            P(("groups", "dom"), None),
            P(("groups", "dom"), None),
            P(("groups", "dom"), None),
            P("groups", None),
            P("groups", None),
            P("groups", None),
            P("groups", None),
        ),
        check_vma=False,
    )
```

```python
import functools

import jax
import jax.numpy as jnp
from jax import lax
from jax.experimental import pallas as pl
from jax.experimental.pallas import tpu as pltpu
from jax.sharding import PartitionSpec as P

BF16 = jnp.bfloat16
F32 = jnp.float32
VMEM_LIMIT = 60 * 1024 * 1024


def dot(left, right):
    return jnp.dot(left, right, preferred_element_type=F32)


def dot_rows(left, right):
    return lax.dot_general(left, right, (((0,), (0,)), ((), ())), preferred_element_type=F32)


def dot_cols(left, right):
    return lax.dot_general(left, right, (((1,), (1,)), ((), ())), preferred_element_type=F32)


def iota(shape, axis):
    return lax.broadcasted_iota(jnp.int32, shape, axis)


def marks(mask):
    return jnp.where(mask, 1.0, 0.0).astype(BF16)


def onehot(column, width):
    return marks(column == iota((column.shape[0], width), 1))


def to_column(row):
    count = row.shape[1]
    square = (count, count)
    kept = jnp.where(iota(square, 0) == iota(square, 1), row.astype(F32), 0.0)
    return jnp.sum(kept, axis=1, keepdims=True)


def slot_ranks(dest, domains):
    count = dest.shape[0]
    square = (count, count)
    dest_marks = onehot(dest, domains)
    before = dot(marks(iota(square, 0) > iota(square, 1)), dest_marks)
    return dest_marks, jnp.sum(before * dest_marks.astype(F32), axis=1, keepdims=True)


def pair_marks(first, second, width):
    pairs = first.shape[0]
    shape = (2 * pairs, pairs)
    edge, pair = iota(shape, 0), iota(shape, 1)
    mine = (edge >> 1) == pair
    even = marks(mine & ((edge & 1) == 0))
    odd = marks(mine & ((edge & 1) == 1))
    first_marks, second_marks = onehot(first, width), onehot(second, width)
    senders = dot(even, first_marks) + dot(odd, second_marks)
    receivers = dot(even, second_marks) + dot(odd, first_marks)
    return senders.astype(BF16), receivers.astype(BF16)


def normalise(values):
    centered = values - jnp.mean(values, axis=1, keepdims=True)
    inv_scale = lax.rsqrt(jnp.mean(centered * centered, axis=1, keepdims=True) + 1e-05)
    return centered * inv_scale, inv_scale


def activate(pre_hidden):
    gate = jax.nn.sigmoid(pre_hidden)
    return (pre_hidden * gate).astype(BF16), gate * (1.0 + pre_hidden * (1.0 - gate))


def norm_backward(upstream, normed, inv_scale):
    centered = (
        upstream
        - jnp.mean(upstream, axis=1, keepdims=True)
        - normed * jnp.mean(upstream * normed, axis=1, keepdims=True)
    )
    return (inv_scale * centered).astype(BF16)


def ask_kernel(dest_ref, remote_ref, ask_ref):
    domains, slots = ask_ref.shape
    dest_marks, rank = slot_ranks(to_column(dest_ref[...]).astype(jnp.int32), domains)
    rank_marks = jnp.where(rank == iota((rank.shape[0], slots), 1).astype(F32), 1.0, 0.0)
    wanted = (rank_marks * to_column(remote_ref[...])).astype(BF16)
    ask_ref[...] = dot_rows(dest_marks, wanted).astype(jnp.int32)


def reply_kernel(asked_ref, nodes_ref, reply_ref, asked_marks_ref):
    domains, slots = asked_ref.shape
    total = domains * slots
    shift = slots.bit_length() - 1
    spread = marks((iota((total, domains), 0) >> shift) == iota((total, domains), 1))
    listed = dot(spread, asked_ref[...].astype(F32).astype(BF16))
    at_slot = (iota((total, slots), 0) & (slots - 1)) == iota((total, slots), 1)
    column = jnp.sum(jnp.where(at_slot, listed, 0.0), axis=1, keepdims=True)
    node_rows = nodes_ref.shape[0]
    asked_marks = marks(column == iota((total, node_rows), 1).astype(F32))
    asked_marks_ref[...] = asked_marks
    reply_ref[...] = dot(asked_marks, nodes_ref[...]).astype(BF16)


def cut_marks_kernel(dest_ref, local_ref, senders_ref, receivers_ref, *, domains, slots):
    width = senders_ref.shape[1]
    base = width - domains * slots
    dest = to_column(dest_ref[...]).astype(jnp.int32)
    _, rank = slot_ranks(dest, domains)
    second = dest * slots + rank.astype(jnp.int32) + base
    first = to_column(local_ref[...]).astype(jnp.int32)
    senders, receivers = pair_marks(first, second, width)
    senders_ref[...] = senders
    receivers_ref[...] = receivers


def edge_forward(edge, sender, receiver, w_in_ref, w_out_ref):
    latent = edge.shape[1]
    pre_hidden = (
        dot(edge, w_in_ref[:latent])
        + dot(sender, w_in_ref[latent : 2 * latent])
        + dot(receiver, w_in_ref[2 * latent :])
    )
    hidden, slope = activate(pre_hidden)
    normed, inv_scale = normalise(dot(hidden, w_out_ref[...]))
    return hidden, slope, normed, inv_scale


def inner_forward_kernel(
    pairs_ref,
    edges_ref,
    nodes_ref,
    w_in_ref,
    w_out_ref,
    senders_ref,
    receivers_ref,
    sender_ref,
    receiver_ref,
    hidden_ref,
    slope_ref,
    normed_ref,
    scale_ref,
    total_ref,
):
    first, second = (to_column(pairs_ref[side : side + 1]).astype(jnp.int32) for side in range(2))
    senders, receivers = pair_marks(first, second, nodes_ref.shape[0])
    senders_ref[...] = senders
    receivers_ref[...] = receivers
    nodes = nodes_ref[...]
    sender = dot(senders, nodes).astype(BF16)
    receiver = dot(receivers, nodes).astype(BF16)
    sender_ref[...] = sender
    receiver_ref[...] = receiver
    hidden, slope, normed, inv_scale = edge_forward(
        edges_ref[...], sender, receiver, w_in_ref, w_out_ref
    )
    hidden_ref[...] = hidden
    slope_ref[...] = slope
    normed_ref[...] = normed
    scale_ref[...] = inv_scale
    part = dot_rows(receivers, normed.astype(BF16))

    @pl.when(pl.program_id(0) == 0)
    def _():
        total_ref[...] = part

    @pl.when(pl.program_id(0) > 0)
    def _():
        total_ref[...] += part


def cut_forward_kernel(
    senders_ref,
    receivers_ref,
    edges_ref,
    nodes_ref,
    far_ref,
    w_in_ref,
    w_out_ref,
    inner_total_ref,
    sender_ref,
    receiver_ref,
    hidden_ref,
    slope_ref,
    normed_ref,
    scale_ref,
    total_ref,
    outgoing_ref,
):
    base = nodes_ref.shape[0]
    nodes, far = nodes_ref[...], far_ref[...]

    def rows_of(marks_ref):
        return (dot(marks_ref[:, :base], nodes) + dot(marks_ref[:, base:], far)).astype(BF16)

    sender, receiver = rows_of(senders_ref), rows_of(receivers_ref)
    sender_ref[...] = sender
    receiver_ref[...] = receiver
    hidden, slope, normed, inv_scale = edge_forward(
        edges_ref[...], sender, receiver, w_in_ref, w_out_ref
    )
    hidden_ref[...] = hidden
    slope_ref[...] = slope
    normed_ref[...] = normed
    scale_ref[...] = inv_scale
    message = normed.astype(BF16)
    total_ref[...] = inner_total_ref[...] + dot_rows(receivers_ref[:, :base], message)
    outgoing_ref[...] = dot_rows(receivers_ref[:, base:], message).astype(BF16)


def new_edges_kernel(edges_ref, inner_ref, cut_ref, out_ref):
    inner_rows = inner_ref.shape[0]

    def added(edge, normed):
        return (edge.astype(F32) + normed.astype(BF16).astype(F32)).astype(BF16)

    out_ref[:inner_rows] = added(edges_ref[:inner_rows], inner_ref[...])
    out_ref[inner_rows:] = added(edges_ref[inner_rows:], cut_ref[...])


def node_kernel(
    incoming_ref,
    asked_marks_ref,
    total_ref,
    nodes_ref,
    ct_ref,
    w_in_ref,
    w_out_ref,
    new_nodes_ref,
    self_grad_ref,
    agg_grad_ref,
    reply_ref,
    aggregate_ref,
    hidden_ref,
    grad_out_ref,
    grad_pre_ref,
):
    latent = nodes_ref.shape[1]
    nodes, asked_marks = nodes_ref[...], asked_marks_ref[...]
    aggregate = (total_ref[...] + dot_rows(asked_marks, incoming_ref[...])).astype(BF16)
    aggregate_ref[...] = aggregate
    pre_hidden = dot(nodes, w_in_ref[:latent]) + dot(aggregate, w_in_ref[latent:])
    hidden, slope = activate(pre_hidden)
    hidden_ref[...] = hidden
    normed, inv_scale = normalise(dot(hidden, w_out_ref[...]))
    upstream = ct_ref[...].astype(F32)
    grad_out = norm_backward(upstream, normed, inv_scale)
    grad_out_ref[...] = grad_out
    grad_pre = (dot_cols(grad_out, w_out_ref[...]) * slope).astype(BF16)
    grad_pre_ref[...] = grad_pre
    agg_grad = dot_cols(grad_pre, w_in_ref[latent:]).astype(BF16)
    agg_grad_ref[...] = agg_grad
    reply_ref[...] = dot(asked_marks, agg_grad).astype(BF16)
    self_grad_ref[...] = upstream + dot_cols(grad_pre, w_in_ref[:latent])
    new_nodes_ref[...] = (nodes.astype(F32) + normed).astype(BF16)


def node_weights_kernel(
    me_ref, nodes_ref, aggregate_ref, hidden_ref, grad_out_ref, grad_pre_ref, keep_ref, send_ref
):
    latent = nodes_ref.shape[1]
    half = latent // 2

    def fill(low_ref, high_ref):
        grad_pre, grad_out = grad_pre_ref[...], grad_out_ref[...]
        low_ref[:latent] = dot_rows(nodes_ref[...], grad_pre).astype(BF16)
        low_ref[latent:] = dot_rows(aggregate_ref[:, :half], grad_pre).astype(BF16)
        high_ref[:half] = dot_rows(aggregate_ref[:, half:], grad_pre).astype(BF16)
        high_ref[half:] = dot_rows(hidden_ref[...], grad_out).astype(BF16)

    halves(me_ref, keep_ref, send_ref, fill)


def halves(me_ref, keep_ref, send_ref, fill):
    @pl.when((me_ref[0] & 1) == 0)
    def _():
        fill(keep_ref, send_ref)

    @pl.when((me_ref[0] & 1) != 0)
    def _():
        fill(send_ref, keep_ref)


def edge_weights_kernel(me_ref, *refs):
    keep_ref, send_ref = refs[-2:]
    low_inner, low_cut, high_inner, high_cut = refs[:4]
    rights = refs[4:-2]

    def fill(low_ref, high_ref):
        low_ref[...] = (
            dot_rows(low_inner[...], rights[0][...]) + dot_rows(low_cut[...], rights[1][...])
        ).astype(BF16)
        high_ref[...] = (
            dot_rows(high_inner[...], rights[-2][...]) + dot_rows(high_cut[...], rights[-1][...])
        ).astype(BF16)

    halves(me_ref, keep_ref, send_ref, fill)


def fold_kernel(me_ref, *refs, low, width, parts):
    size = 1 << width
    sources, pieces = refs[:parts], refs[parts:]
    chunk = pieces[0].shape[0]
    place = (me_ref[0] >> low) & (size - 1)
    for turn in range(size):
        start = pl.multiple_of((place ^ turn) * chunk, 16) if width else 0
        rows = pl.ds(start, chunk)
        total = sources[0][rows].astype(F32)
        for source in sources[1:]:
            total += source[rows].astype(F32)
        pieces[turn][...] = total.astype(BF16)


def place_kernel(me_ref, *refs):
    out_ref = refs[-1]
    chunk = refs[0].shape[0]
    place = (me_ref[0] >> 2) & 3
    for turn in range(4):
        start = pl.multiple_of((place ^ turn) * chunk, 16)
        out_ref[pl.ds(start, chunk)] = refs[turn][...]


def spread_kernel(me_ref, *refs, quarters):
    sources, outs = refs[: 4 * quarters], refs[4 * quarters :]
    place = (me_ref[0] & 1) * 2 + ((me_ref[0] >> 1) & 1)
    spans, top = [], 0
    for out in outs:
        spans.append((top, top + out.shape[0], out))
        top += out.shape[0]

    def put(row, source):
        height = source.shape[0]
        for start, end, out in spans:
            first, last = max(row, start), min(row + height, end)
            if first < last:
                out[first - start : last - start] = source[first - row : last - row]

    for stream in range(quarters):
        group = sources[4 * stream : 4 * stream + 4]
        near, across = group[1], group[2]
        by_distance = [group[0], across, near, group[3]]
        height = group[0].shape[0]
        base = sum(4 * sources[4 * before].shape[0] for before in range(stream))
        for mine in range(4):

            @pl.when(place == mine)
            def _():
                for quarter in range(4):
                    put(base + quarter * height, by_distance[quarter ^ mine])


def edge_backward(ct, target_grads, normed, inv_scale, slope, w_out):
    grad_out = norm_backward(ct.astype(F32) + target_grads, normed, inv_scale)
    return grad_out, (dot_cols(grad_out, w_out) * slope).astype(BF16)


def inner_backward_kernel(
    receivers_ref,
    agg_grad_ref,
    ct_ref,
    normed_ref,
    scale_ref,
    slope_ref,
    w_out_ref,
    grad_out_ref,
    grad_pre_ref,
):
    grad_out, grad_pre = edge_backward(
        ct_ref[...],
        dot(receivers_ref[...], agg_grad_ref[...]),
        normed_ref[...],
        scale_ref[...],
        slope_ref[...],
        w_out_ref[...],
    )
    grad_out_ref[...] = grad_out
    grad_pre_ref[...] = grad_pre


def cut_backward_kernel(
    receivers_ref,
    agg_grad_ref,
    far_grad_ref,
    ct_ref,
    normed_ref,
    scale_ref,
    slope_ref,
    w_out_ref,
    grad_out_ref,
    grad_pre_ref,
):
    base = agg_grad_ref.shape[0]
    target = dot(receivers_ref[:, :base], agg_grad_ref[...]) + dot(
        receivers_ref[:, base:], far_grad_ref[...]
    )
    grad_out, grad_pre = edge_backward(
        ct_ref[...], target, normed_ref[...], scale_ref[...], slope_ref[...], w_out_ref[...]
    )
    grad_out_ref[...] = grad_out
    grad_pre_ref[...] = grad_pre


def input_grads_kernel(
    inner_senders_ref,
    inner_receivers_ref,
    cut_senders_ref,
    cut_receivers_ref,
    inner_pre_ref,
    cut_pre_ref,
    w_in_ref,
    local_ref,
    outgoing_ref,
):
    latent = inner_pre_ref.shape[1]
    base = inner_senders_ref.shape[1]
    inner_pre, cut_pre = inner_pre_ref[...], cut_pre_ref[...]
    w_sender, w_receiver = w_in_ref[latent : 2 * latent], w_in_ref[2 * latent :]

    def summed(inner_marks_ref, cut_marks_ref):
        return (
            dot_rows(inner_marks_ref[...], inner_pre) + dot_rows(cut_marks_ref[:, :base], cut_pre)
        ).astype(BF16)

    outgoing_ref[...] = (
        dot_cols(dot_rows(cut_senders_ref[:, base:], cut_pre).astype(BF16), w_sender)
        + dot_cols(dot_rows(cut_receivers_ref[:, base:], cut_pre).astype(BF16), w_receiver)
    ).astype(BF16)
    local_ref[...] = dot_cols(summed(inner_senders_ref, cut_senders_ref), w_sender) + dot_cols(
        summed(inner_receivers_ref, cut_receivers_ref), w_receiver
    )


def edge_grads_kernel(ct_ref, inner_pre_ref, cut_pre_ref, w_edge_ref, out_ref, *, blocks):
    inside = pl.program_id(0) < blocks

    @pl.when(inside)
    def _():
        out_ref[...] = ct_ref[...].astype(F32) + dot_cols(inner_pre_ref[...], w_edge_ref[...])

    @pl.when(jnp.logical_not(inside))
    def _():
        out_ref[...] = ct_ref[...].astype(F32) + dot_cols(cut_pre_ref[...], w_edge_ref[...])


def node_grads_kernel(self_ref, local_ref, asked_marks_ref, returned_ref, out_ref):
    out_ref[...] = (
        self_ref[...] + local_ref[...] + dot_rows(asked_marks_ref[...], returned_ref[...])
    )


VMEM = pl.BlockSpec(memory_space=pltpu.VMEM)
SMEM = pl.BlockSpec(memory_space=pltpu.SMEM)
ANY = pl.BlockSpec(memory_space=pl.ANY)


def shaped(dtype, *shape):
    return jax.ShapeDtypeStruct(shape, dtype)


class Line:
    def __init__(self):
        self.last = None

    def run(self, body, outs, ins, flops, specs=None, out_specs=None, grid=None):
        single = not isinstance(outs, (list, tuple))
        out_shape = [outs] if single else list(outs)
        specs = [VMEM] * len(ins) if specs is None else list(specs)
        moved = sum(item.size * item.dtype.itemsize for item in list(ins) + out_shape)
        count, extra = len(ins), {} if grid is None else {"grid": grid}
        ins = list(ins)
        if self.last is not None:
            ins.append(self.last)
            specs.append(ANY)

        def ordered(*refs):
            return body(*refs[:count], *refs[len(ins) :])

        result = pl.pallas_call(
            ordered,
            out_shape=out_shape,
            in_specs=specs,
            out_specs=[VMEM] * len(out_shape) if out_specs is None else out_specs,
            compiler_params=pltpu.CompilerParams(vmem_limit_bytes=VMEM_LIMIT),
            cost_estimate=pl.CostEstimate(flops=flops, bytes_accessed=moved, transcendentals=0),
            **extra,
        )(*ins)
        self.last = result[-1]
        return result[0] if single else result


class Stream:
    def __init__(self, line, me, devices, keep, send):
        self.line, self.me, self.devices = line, me, devices
        self.keep, self.sent = keep, [send]
        self.masks = [1]

    def swap(self):
        self.got = [
            lax.ppermute(part, "dom", [(device, device ^ mask) for device in range(self.devices)])
            for part, mask in zip(self.sent, self.masks)
        ]

    def fold(self, low, width):
        size = 1 << width
        rows, latent = self.keep.shape
        chunk = rows // size
        piece = shaped(BF16, chunk, latent)
        pieces = self.line.run(
            functools.partial(fold_kernel, low=low, width=width, parts=1 + len(self.got)),
            [piece] * size,
            [self.me, self.keep] + self.got,
            rows * latent * 4,
            [SMEM] + [VMEM] * (1 + len(self.got)),
        )
        self.keep, self.sent = pieces[0], list(pieces[1:])
        self.masks = [turn << low for turn in range(1, size)]
        self.swap()

    def settle(self):
        chunk = self.line.run(
            functools.partial(fold_kernel, low=0, width=0, parts=4),
            [shaped(BF16, *self.keep.shape)],
            [self.me, self.keep] + self.got,
            self.keep.size * 4,
            [SMEM] + [VMEM] * 4,
        )[0]
        if self.devices > 16:
            alike = [list(range(low, self.devices, 16)) for low in range(16)]
            chunk = lax.psum(chunk, "dom", axis_index_groups=alike)
        self.keep, self.sent, self.masks = chunk, [chunk] * 3, [4, 8, 12]
        self.swap()

    def place(self):
        rows, latent = self.keep.shape
        column = self.line.run(
            place_kernel,
            shaped(BF16, 4 * rows, latent),
            [self.me, self.keep] + self.got,
            10**6,
            [SMEM] + [VMEM] * 4,
        )
        self.keep, self.sent, self.masks = column, [column, column], [1, 2]
        self.swap()
        near, across = self.got
        self.sent, self.masks = [across], [1]
        self.swap()
        self.quarters = [column, near, across, self.got[0]]


def exchange(rows, domains):
    shape = rows.shape
    split = rows.reshape((domains, shape[0] // domains) + shape[1:])
    return lax.all_to_all(split, "dom", split_axis=0, concat_axis=0, tiled=True).reshape(shape)


def shards(
    nodes,
    edges,
    inner_pairs,
    cut_local,
    cut_dest,
    cut_remote,
    w_edge_in,
    w_edge_out,
    w_node_in,
    w_node_out,
    ct_nodes,
    ct_edges,
):
    domains = lax.axis_size("dom")
    node_rows, latent = nodes.shape
    inner_count, cut_count = inner_pairs.shape[0], cut_local.shape[0]
    inner_rows, cut_rows = 2 * inner_count, 2 * cut_count
    slots = max(2, 2 * cut_count // domains)
    total_slots = domains * slots
    table = node_rows + total_slots
    square = 2 * latent * latent
    me = lax.axis_index("dom").reshape(1)
    line = Line()

    ask = line.run(
        ask_kernel, shaped(jnp.int32, domains, slots), [cut_dest.reshape(1, -1), cut_remote.reshape(1, -1)], 10**7
    )
    asked = lax.all_to_all(ask, "dom", split_axis=0, concat_axis=0, tiled=True)
    cut_senders, cut_receivers = line.run(
        functools.partial(cut_marks_kernel, domains=domains, slots=slots),
        [shaped(BF16, cut_rows, table)] * 2,
        [cut_dest.reshape(1, -1), cut_local.reshape(1, -1)],
        10**8,
    )
    reply, asked_marks = line.run(
        reply_kernel,
        [shaped(BF16, total_slots, latent), shaped(BF16, total_slots, node_rows)],
        [asked, nodes],
        10**8,
    )
    far = exchange(reply, domains)

    block = cut_rows
    blocks = inner_rows // block

    def rows_spec(width, rows=block):
        return pl.BlockSpec((rows, width), lambda step: (step, 0))

    def all_spec(array):
        return pl.BlockSpec(array.shape, lambda step: (0, 0))

    saved_widths = [node_rows, node_rows, latent, latent, latent, latent, latent, 1]
    saved_types = [BF16, BF16, BF16, BF16, BF16, F32, F32, F32]
    (
        inner_senders,
        inner_receivers,
        inner_sender,
        inner_receiver,
        inner_hidden,
        inner_slope,
        inner_normed,
        inner_scale,
        inner_total,
    ) = line.run(
        inner_forward_kernel,
        [shaped(kind, inner_rows, width) for kind, width in zip(saved_types, saved_widths)]
        + [shaped(F32, node_rows, latent)],
        [inner_pairs.T, edges, nodes, w_edge_in, w_edge_out],
        inner_rows * 4 * square,
        [
            pl.BlockSpec((2, block // 2), lambda step: (0, step)),
            rows_spec(latent),
            all_spec(nodes),
            all_spec(w_edge_in),
            all_spec(w_edge_out),
        ],
        [rows_spec(width) for width in saved_widths] + [all_spec(nodes)],
        (blocks,),
    )

    def last_rows(array):
        last = array.shape[0] // block - 1
        return pl.BlockSpec((block, array.shape[1]), lambda step: (last, 0))

    (
        cut_sender,
        cut_receiver,
        cut_hidden,
        cut_slope,
        cut_normed,
        cut_scale,
        total,
        outgoing,
    ) = line.run(
        cut_forward_kernel,
        [shaped(kind, cut_rows, width) for kind, width in zip(saved_types, saved_widths)][2:]
        + [shaped(F32, node_rows, latent), shaped(BF16, total_slots, latent)],
        [
            cut_senders,
            cut_receivers,
            edges,
            nodes,
            far,
            w_edge_in,
            w_edge_out,
            inner_total,
        ],
        cut_rows * 4 * square,
        [
            all_spec(cut_senders),
            all_spec(cut_receivers),
            last_rows(edges),
            all_spec(nodes),
            all_spec(far),
            all_spec(w_edge_in),
            all_spec(w_edge_out),
            all_spec(inner_total),
        ],
        [rows_spec(width) for width in saved_widths[2:]]
        + [all_spec(nodes), rows_spec(latent, total_slots)],
        (1,),
    )
    incoming = exchange(outgoing, domains)
    new_edges = line.run(
        new_edges_kernel,
        shaped(BF16, *edges.shape),
        [edges, inner_normed, cut_normed],
        10**7,
    )
    (
        new_nodes,
        self_grad,
        agg_grad,
        grad_reply,
        aggregate,
        node_hidden,
        node_out,
        node_pre,
    ) = line.run(
        node_kernel,
        [
            shaped(BF16, node_rows, latent),
            shaped(F32, node_rows, latent),
            shaped(BF16, node_rows, latent),
            shaped(BF16, total_slots, latent),
        ]
        + [shaped(BF16, node_rows, latent)] * 4,
        [incoming, asked_marks, total, nodes, ct_nodes, w_node_in, w_node_out],
        node_rows * 6 * square,
    )
    far_grad = exchange(grad_reply, domains)
    node_keep, node_send = line.run(
        node_weights_kernel,
        [shaped(BF16, 3 * latent // 2, latent)] * 2,
        [me, nodes, aggregate, node_hidden, node_out, node_pre],
        node_rows * 3 * square,
        [SMEM] + [VMEM] * 5,
    )
    node_stream = Stream(line, me, domains, node_keep, node_send)
    node_stream.swap()
    inner_out, inner_pre = line.run(
        inner_backward_kernel,
        [shaped(BF16, inner_rows, latent)] * 2,
        [
            inner_receivers,
            agg_grad,
            ct_edges,
            inner_normed,
            inner_scale,
            inner_slope,
            w_edge_out,
        ],
        inner_rows * square,
        [
            rows_spec(node_rows),
            all_spec(agg_grad),
            rows_spec(latent),
            rows_spec(latent),
            rows_spec(1),
            rows_spec(latent),
            all_spec(w_edge_out),
        ],
        [rows_spec(latent)] * 2,
        (blocks,),
    )
    node_stream.fold(1, 1)
    cut_out, cut_pre = line.run(
        cut_backward_kernel,
        [shaped(BF16, cut_rows, latent)] * 2,
        [
            cut_receivers,
            agg_grad,
            far_grad,
            ct_edges,
            cut_normed,
            cut_scale,
            cut_slope,
            w_edge_out,
        ],
        cut_rows * square,
        [
            all_spec(cut_receivers),
            all_spec(agg_grad),
            all_spec(far_grad),
            last_rows(ct_edges),
            all_spec(cut_normed),
            all_spec(cut_scale),
            all_spec(cut_slope),
            all_spec(w_edge_out),
        ],
        [rows_spec(latent)] * 2,
        (1,),
    )
    def edge_stream(low_inner, low_cut, high_inner, high_cut, rights):
        factors = [low_inner, low_cut, high_inner, high_cut] + rights
        keep, send = line.run(
            edge_weights_kernel,
            [shaped(BF16, latent, latent)] * 2,
            [me] + factors,
            (inner_rows + cut_rows) * 2 * square,
            [SMEM, rows_spec(latent, inner_rows), last_rows(low_cut)]
            + [all_spec(array) for array in factors[2:]],
            [rows_spec(latent, latent)] * 2,
            (1,),
        )
        stream = Stream(line, me, domains, keep, send)
        stream.swap()
        return stream

    first = edge_stream(edges, edges, inner_sender, cut_sender, [inner_pre, cut_pre])
    second = edge_stream(
        inner_receiver,
        cut_receiver,
        inner_hidden,
        cut_hidden,
        [inner_pre, cut_pre, inner_out, cut_out],
    )
    first.fold(1, 1)
    node_stream.fold(2, 2)
    second.fold(1, 1)
    local_grad, outgoing_grad = line.run(
        input_grads_kernel,
        [shaped(F32, node_rows, latent), shaped(BF16, total_slots, latent)],
        [
            inner_senders,
            inner_receivers,
            cut_senders,
            cut_receivers,
            inner_pre,
            cut_pre,
            w_edge_in,
        ],
        (node_rows + total_slots) * 2 * square,
    )
    returned = exchange(outgoing_grad, domains)
    first.fold(2, 2)
    node_stream.settle()
    second.fold(2, 2)
    first.settle()
    grad_edges = line.run(
        functools.partial(edge_grads_kernel, blocks=blocks),
        shaped(F32, *edges.shape),
        [ct_edges, inner_pre, cut_pre, w_edge_in],
        (inner_rows + cut_rows) * square,
        [
            rows_spec(latent),
            pl.BlockSpec((block, latent), lambda step: (jnp.minimum(step, blocks - 1), 0)),
            all_spec(cut_pre),
            pl.BlockSpec((latent, latent), lambda step: (0, 0)),
        ],
        [rows_spec(latent)],
        (blocks + 1,),
    )
    node_stream.place()
    second.settle()
    first.place()
    grad_nodes = line.run(
        node_grads_kernel,
        shaped(F32, node_rows, latent),
        [self_grad, local_grad, asked_marks, returned],
        10**8,
    )
    second.place()
    grad_node_in, grad_node_out = line.run(
        functools.partial(spread_kernel, quarters=1),
        [shaped(BF16, 2 * latent, latent), shaped(BF16, latent, latent)],
        [me] + node_stream.quarters,
        10**6,
        [SMEM] + [VMEM] * 4,
    )
    grad_edge_in, grad_edge_out = line.run(
        functools.partial(spread_kernel, quarters=2),
        [shaped(BF16, 3 * latent, latent), shaped(BF16, latent, latent)],
        [me] + first.quarters + second.quarters,
        10**6,
        [SMEM] + [VMEM] * 8,
    )
    return (
        new_nodes,
        new_edges,
        grad_nodes,
        grad_edges,
        grad_edge_in,
        grad_edge_out,
        grad_node_in,
        grad_node_out,
    )


def solution(mesh):
    placed = (
        P(("groups", "dom"), None),
        P(("groups", "dom"), None),
        P(("groups", "dom"), None),
        P(("groups", "dom")),
        P(("groups", "dom"), None),
        P(("groups", "dom")),
        P(),
        P(),
        P(),
        P(),
        P(("groups", "dom"), None),
        P(("groups", "dom"), None),
    )
    return jax.shard_map(
        shards,
        mesh=mesh,
        in_specs=placed,
        out_specs=(
            P(("groups", "dom"), None),
            P(("groups", "dom"), None),
            P(("groups", "dom"), None),
            P(("groups", "dom"), None),
            P("groups", None),
            P("groups", None),
            P("groups", None),
            P("groups", None),
        ),
        check_vma=False,
    )
```

```python
import functools

import jax
import jax.numpy as jnp
from jax import lax
from jax.experimental import pallas as pl
from jax.experimental.pallas import tpu as pltpu
from jax.sharding import PartitionSpec as P

BF16 = jnp.bfloat16
F32 = jnp.float32
VMEM_LIMIT = 60 * 1024 * 1024


def dot(left, right):
    return jnp.dot(left, right, preferred_element_type=F32)


def dot_rows(left, right):
    return lax.dot_general(left, right, (((0,), (0,)), ((), ())), preferred_element_type=F32)


def dot_cols(left, right):
    return lax.dot_general(left, right, (((1,), (1,)), ((), ())), preferred_element_type=F32)


def iota(shape, axis):
    return lax.broadcasted_iota(jnp.int32, shape, axis)


def marks(mask):
    return jnp.where(mask, 1.0, 0.0).astype(BF16)


def onehot(column, width):
    return marks(column == iota((column.shape[0], width), 1))


def to_column(row):
    count = row.shape[1]
    square = (count, count)
    kept = jnp.where(iota(square, 0) == iota(square, 1), row.astype(F32), 0.0)
    return jnp.sum(kept, axis=1, keepdims=True)


def slot_ranks(dest, domains):
    count = dest.shape[0]
    square = (count, count)
    dest_marks = onehot(dest, domains)
    before = dot(marks(iota(square, 0) > iota(square, 1)), dest_marks)
    return dest_marks, jnp.sum(before * dest_marks.astype(F32), axis=1, keepdims=True)


def pair_marks(first, second, width):
    pairs = first.shape[0]
    shape = (2 * pairs, pairs)
    edge, pair = iota(shape, 0), iota(shape, 1)
    mine = (edge >> 1) == pair
    even = marks(mine & ((edge & 1) == 0))
    odd = marks(mine & ((edge & 1) == 1))
    first_marks, second_marks = onehot(first, width), onehot(second, width)
    senders = dot(even, first_marks) + dot(odd, second_marks)
    receivers = dot(even, second_marks) + dot(odd, first_marks)
    return senders.astype(BF16), receivers.astype(BF16)


def normalise(values):
    centered = values - jnp.mean(values, axis=1, keepdims=True)
    inv_scale = lax.rsqrt(jnp.mean(centered * centered, axis=1, keepdims=True) + 1e-05)
    return centered * inv_scale, inv_scale


def activate(pre_hidden):
    gate = jax.nn.sigmoid(pre_hidden)
    return (pre_hidden * gate).astype(BF16), gate * (1.0 + pre_hidden * (1.0 - gate))


def norm_backward(upstream, normed, inv_scale):
    centered = (
        upstream
        - jnp.mean(upstream, axis=1, keepdims=True)
        - normed * jnp.mean(upstream * normed, axis=1, keepdims=True)
    )
    return (inv_scale * centered).astype(BF16)


def ask_kernel(dest_ref, remote_ref, ask_ref):
    domains, slots = ask_ref.shape
    dest_marks, rank = slot_ranks(to_column(dest_ref[...]).astype(jnp.int32), domains)
    rank_marks = jnp.where(rank == iota((rank.shape[0], slots), 1).astype(F32), 1.0, 0.0)
    wanted = (rank_marks * to_column(remote_ref[...])).astype(BF16)
    ask_ref[...] = dot_rows(dest_marks, wanted).astype(jnp.int32)


def reply_kernel(asked_ref, nodes_ref, reply_ref, asked_marks_ref):
    domains, slots = asked_ref.shape
    total = domains * slots
    shift = slots.bit_length() - 1
    spread = marks((iota((total, domains), 0) >> shift) == iota((total, domains), 1))
    listed = dot(spread, asked_ref[...].astype(F32).astype(BF16))
    at_slot = (iota((total, slots), 0) & (slots - 1)) == iota((total, slots), 1)
    column = jnp.sum(jnp.where(at_slot, listed, 0.0), axis=1, keepdims=True)
    node_rows = nodes_ref.shape[0]
    asked_marks = marks(column == iota((total, node_rows), 1).astype(F32))
    asked_marks_ref[...] = asked_marks
    reply_ref[...] = dot(asked_marks, nodes_ref[...]).astype(BF16)


def cut_marks_kernel(dest_ref, local_ref, senders_ref, receivers_ref, *, domains, slots):
    width = senders_ref.shape[1]
    base = width - domains * slots
    dest = to_column(dest_ref[...]).astype(jnp.int32)
    _, rank = slot_ranks(dest, domains)
    second = dest * slots + rank.astype(jnp.int32) + base
    first = to_column(local_ref[...]).astype(jnp.int32)
    senders, receivers = pair_marks(first, second, width)
    senders_ref[...] = senders
    receivers_ref[...] = receivers


def edge_forward(edge, sender, receiver, w_in_ref, w_out_ref):
    latent = edge.shape[1]
    pre_hidden = (
        dot(edge, w_in_ref[:latent])
        + dot(sender, w_in_ref[latent : 2 * latent])
        + dot(receiver, w_in_ref[2 * latent :])
    )
    hidden, slope = activate(pre_hidden)
    normed, inv_scale = normalise(dot(hidden, w_out_ref[...]))
    return hidden, slope, normed, inv_scale


def inner_forward_kernel(
    pairs_ref,
    edges_ref,
    nodes_ref,
    w_in_ref,
    w_out_ref,
    senders_ref,
    receivers_ref,
    sender_ref,
    receiver_ref,
    hidden_ref,
    slope_ref,
    normed_ref,
    scale_ref,
    total_ref,
):
    first, second = (to_column(pairs_ref[side : side + 1]).astype(jnp.int32) for side in range(2))
    senders, receivers = pair_marks(first, second, nodes_ref.shape[0])
    senders_ref[...] = senders
    receivers_ref[...] = receivers
    nodes = nodes_ref[...]
    sender = dot(senders, nodes).astype(BF16)
    receiver = dot(receivers, nodes).astype(BF16)
    sender_ref[...] = sender
    receiver_ref[...] = receiver
    hidden, slope, normed, inv_scale = edge_forward(
        edges_ref[...], sender, receiver, w_in_ref, w_out_ref
    )
    hidden_ref[...] = hidden
    slope_ref[...] = slope
    normed_ref[...] = normed
    scale_ref[...] = inv_scale
    part = dot_rows(receivers, normed.astype(BF16))

    @pl.when(pl.program_id(0) == 0)
    def _():
        total_ref[...] = part

    @pl.when(pl.program_id(0) > 0)
    def _():
        total_ref[...] += part


def cut_forward_kernel(
    senders_ref,
    receivers_ref,
    edges_ref,
    nodes_ref,
    far_ref,
    w_in_ref,
    w_out_ref,
    inner_total_ref,
    sender_ref,
    receiver_ref,
    hidden_ref,
    slope_ref,
    normed_ref,
    scale_ref,
    total_ref,
    outgoing_ref,
):
    base = nodes_ref.shape[0]
    nodes, far = nodes_ref[...], far_ref[...]

    def rows_of(marks_ref):
        return (dot(marks_ref[:, :base], nodes) + dot(marks_ref[:, base:], far)).astype(BF16)

    sender, receiver = rows_of(senders_ref), rows_of(receivers_ref)
    sender_ref[...] = sender
    receiver_ref[...] = receiver
    hidden, slope, normed, inv_scale = edge_forward(
        edges_ref[...], sender, receiver, w_in_ref, w_out_ref
    )
    hidden_ref[...] = hidden
    slope_ref[...] = slope
    normed_ref[...] = normed
    scale_ref[...] = inv_scale
    message = normed.astype(BF16)
    total_ref[...] = inner_total_ref[...] + dot_rows(receivers_ref[:, :base], message)
    outgoing_ref[...] = dot_rows(receivers_ref[:, base:], message).astype(BF16)


def new_edges_kernel(edges_ref, inner_ref, cut_ref, out_ref):
    inner_rows = inner_ref.shape[0]

    def added(edge, normed):
        return (edge.astype(F32) + normed.astype(BF16).astype(F32)).astype(BF16)

    out_ref[:inner_rows] = added(edges_ref[:inner_rows], inner_ref[...])
    out_ref[inner_rows:] = added(edges_ref[inner_rows:], cut_ref[...])


def node_kernel(
    incoming_ref,
    asked_marks_ref,
    total_ref,
    nodes_ref,
    ct_ref,
    w_in_ref,
    w_out_ref,
    new_nodes_ref,
    self_grad_ref,
    agg_grad_ref,
    reply_ref,
    aggregate_ref,
    hidden_ref,
    grad_out_ref,
    grad_pre_ref,
):
    latent = nodes_ref.shape[1]
    nodes, asked_marks = nodes_ref[...], asked_marks_ref[...]
    aggregate = (total_ref[...] + dot_rows(asked_marks, incoming_ref[...])).astype(BF16)
    aggregate_ref[...] = aggregate
    pre_hidden = dot(nodes, w_in_ref[:latent]) + dot(aggregate, w_in_ref[latent:])
    hidden, slope = activate(pre_hidden)
    hidden_ref[...] = hidden
    normed, inv_scale = normalise(dot(hidden, w_out_ref[...]))
    upstream = ct_ref[...].astype(F32)
    grad_out = norm_backward(upstream, normed, inv_scale)
    grad_out_ref[...] = grad_out
    grad_pre = (dot_cols(grad_out, w_out_ref[...]) * slope).astype(BF16)
    grad_pre_ref[...] = grad_pre
    agg_grad = dot_cols(grad_pre, w_in_ref[latent:]).astype(BF16)
    agg_grad_ref[...] = agg_grad
    reply_ref[...] = dot(asked_marks, agg_grad).astype(BF16)
    self_grad_ref[...] = upstream + dot_cols(grad_pre, w_in_ref[:latent])
    new_nodes_ref[...] = (nodes.astype(F32) + normed).astype(BF16)


def node_weights_kernel(
    me_ref, nodes_ref, aggregate_ref, hidden_ref, grad_out_ref, grad_pre_ref, keep_ref, send_ref
):
    latent = nodes_ref.shape[1]
    half = latent // 2

    def fill(low_ref, high_ref):
        grad_pre, grad_out = grad_pre_ref[...], grad_out_ref[...]
        low_ref[:latent] = dot_rows(nodes_ref[...], grad_pre).astype(BF16)
        low_ref[latent:] = dot_rows(aggregate_ref[:, :half], grad_pre).astype(BF16)
        high_ref[:half] = dot_rows(aggregate_ref[:, half:], grad_pre).astype(BF16)
        high_ref[half:] = dot_rows(hidden_ref[...], grad_out).astype(BF16)

    halves(me_ref, keep_ref, send_ref, fill)


def halves(me_ref, keep_ref, send_ref, fill):
    @pl.when((me_ref[0] & 1) == 0)
    def _():
        fill(keep_ref, send_ref)

    @pl.when((me_ref[0] & 1) != 0)
    def _():
        fill(send_ref, keep_ref)


def edge_backward(ct, target_grads, normed, inv_scale, slope, w_out):
    grad_out = norm_backward(ct.astype(F32) + target_grads, normed, inv_scale)
    return grad_out, (dot_cols(grad_out, w_out) * slope).astype(BF16)


def inner_backward_kernel(
    receivers_ref,
    agg_grad_ref,
    ct_ref,
    normed_ref,
    scale_ref,
    slope_ref,
    w_out_ref,
    grad_out_ref,
    grad_pre_ref,
):
    grad_out, grad_pre = edge_backward(
        ct_ref[...],
        dot(receivers_ref[...], agg_grad_ref[...]),
        normed_ref[...],
        scale_ref[...],
        slope_ref[...],
        w_out_ref[...],
    )
    grad_out_ref[...] = grad_out
    grad_pre_ref[...] = grad_pre


def cut_backward_kernel(
    receivers_ref,
    agg_grad_ref,
    far_grad_ref,
    ct_ref,
    normed_ref,
    scale_ref,
    slope_ref,
    w_out_ref,
    grad_out_ref,
    grad_pre_ref,
):
    base = agg_grad_ref.shape[0]
    target = dot(receivers_ref[:, :base], agg_grad_ref[...]) + dot(
        receivers_ref[:, base:], far_grad_ref[...]
    )
    grad_out, grad_pre = edge_backward(
        ct_ref[...], target, normed_ref[...], scale_ref[...], slope_ref[...], w_out_ref[...]
    )
    grad_out_ref[...] = grad_out
    grad_pre_ref[...] = grad_pre


def edge_weights_kernel(
    me_ref,
    edges_ref,
    inner_sender_ref,
    cut_sender_ref,
    inner_receiver_ref,
    cut_receiver_ref,
    inner_hidden_ref,
    cut_hidden_ref,
    inner_out_ref,
    cut_out_ref,
    inner_pre_ref,
    cut_pre_ref,
    out_ref,
    *,
    turned,
):
    latent = edges_ref.shape[1]
    inner_rows = inner_pre_ref.shape[0]

    @pl.when((me_ref[0] & 1) == turned)
    def _():
        inner_pre, cut_pre = inner_pre_ref[...], cut_pre_ref[...]
        out_ref[:latent] = (
            dot_rows(edges_ref[:inner_rows], inner_pre) + dot_rows(edges_ref[inner_rows:], cut_pre)
        ).astype(BF16)
        out_ref[latent:] = (
            dot_rows(inner_sender_ref[...], inner_pre) + dot_rows(cut_sender_ref[...], cut_pre)
        ).astype(BF16)

    @pl.when((me_ref[0] & 1) != turned)
    def _():
        out_ref[:latent] = (
            dot_rows(inner_receiver_ref[...], inner_pre_ref[...])
            + dot_rows(cut_receiver_ref[...], cut_pre_ref[...])
        ).astype(BF16)
        out_ref[latent:] = (
            dot_rows(inner_hidden_ref[...], inner_out_ref[...])
            + dot_rows(cut_hidden_ref[...], cut_out_ref[...])
        ).astype(BF16)


def input_grads_kernel(
    inner_senders_ref,
    inner_receivers_ref,
    cut_senders_ref,
    cut_receivers_ref,
    inner_pre_ref,
    cut_pre_ref,
    w_in_ref,
    local_ref,
    outgoing_ref,
):
    latent = inner_pre_ref.shape[1]
    base = inner_senders_ref.shape[1]
    inner_pre, cut_pre = inner_pre_ref[...], cut_pre_ref[...]
    w_sender, w_receiver = w_in_ref[latent : 2 * latent], w_in_ref[2 * latent :]

    def summed(inner_marks_ref, cut_marks_ref):
        return (
            dot_rows(inner_marks_ref[...], inner_pre) + dot_rows(cut_marks_ref[:, :base], cut_pre)
        ).astype(BF16)

    outgoing_ref[...] = (
        dot_cols(dot_rows(cut_senders_ref[:, base:], cut_pre).astype(BF16), w_sender)
        + dot_cols(dot_rows(cut_receivers_ref[:, base:], cut_pre).astype(BF16), w_receiver)
    ).astype(BF16)
    local_ref[...] = dot_cols(summed(inner_senders_ref, cut_senders_ref), w_sender) + dot_cols(
        summed(inner_receivers_ref, cut_receivers_ref), w_receiver
    )


def edge_grads_kernel(ct_ref, inner_pre_ref, cut_pre_ref, w_edge_ref, out_ref, *, blocks):
    inside = pl.program_id(0) < blocks

    @pl.when(inside)
    def _():
        out_ref[...] = ct_ref[...].astype(F32) + dot_cols(inner_pre_ref[...], w_edge_ref[...])

    @pl.when(jnp.logical_not(inside))
    def _():
        out_ref[...] = ct_ref[...].astype(F32) + dot_cols(cut_pre_ref[...], w_edge_ref[...])


def node_grads_kernel(self_ref, local_ref, asked_marks_ref, returned_ref, out_ref):
    out_ref[...] = (
        self_ref[...] + local_ref[...] + dot_rows(asked_marks_ref[...], returned_ref[...])
    )


VMEM = pl.BlockSpec(memory_space=pltpu.VMEM)
SMEM = pl.BlockSpec(memory_space=pltpu.SMEM)
ANY = pl.BlockSpec(memory_space=pl.ANY)


def shaped(dtype, *shape):
    return jax.ShapeDtypeStruct(shape, dtype)


class Line:
    def __init__(self):
        self.last = None

    def run(self, body, outs, ins, flops, specs=None, out_specs=None, grid=None):
        single = not isinstance(outs, (list, tuple))
        out_shape = [outs] if single else list(outs)
        specs = [VMEM] * len(ins) if specs is None else list(specs)
        moved = sum(item.size * item.dtype.itemsize for item in list(ins) + out_shape)
        count, extra = len(ins), {} if grid is None else {"grid": grid}
        ins = list(ins)
        if self.last is not None:
            ins.append(self.last)
            specs.append(ANY)

        def ordered(*refs):
            return body(*refs[:count], *refs[len(ins) :])

        result = pl.pallas_call(
            ordered,
            out_shape=out_shape,
            in_specs=specs,
            out_specs=[VMEM] * len(out_shape) if out_specs is None else out_specs,
            compiler_params=pltpu.CompilerParams(vmem_limit_bytes=VMEM_LIMIT),
            cost_estimate=pl.CostEstimate(flops=flops, bytes_accessed=moved, transcendentals=0),
            **extra,
        )(*ins)
        self.last = result[-1]
        return result[0] if single else result


def bit_groups(devices):
    bits = devices.bit_length() - 1
    groups = [(low, 1) for low in range(min(2, bits))]
    low = 2
    while low < bits:
        groups.append((low, min(2, bits - low)))
        low += 2
    return groups


def across(rows, devices, mask):
    return lax.ppermute(rows, "dom", [(device, device ^ mask) for device in range(devices)])


def fence(*values):
    return lax.optimization_barrier(values)


def place_of(low, size):
    return (lax.axis_index("dom") >> low) & (size - 1)


def pieces_of(rows, low, width):
    size = 1 << width
    place = place_of(low, size)
    pieces = rows.reshape(size, rows.shape[0] // size, rows.shape[1])
    return [lax.dynamic_index_in_dim(pieces, place ^ turn, 0, False) for turn in range(size)]


def traded(pieces, devices, low):
    return pieces[:1] + [
        across(piece, devices, turn << low) for turn, piece in enumerate(pieces) if turn
    ]


def handed(rows, devices, low, width):
    return traded([rows] * (1 << width), devices, low)


def added(*parts):
    return sum(part.astype(F32) for part in parts).astype(BF16)


def joined(parts, low):
    size = len(parts)
    place = place_of(low, size)
    if size == 2:
        orders = [jnp.concatenate(parts), jnp.concatenate(parts[::-1])]
        return jnp.where(place == 0, *orders)
    whole = jnp.zeros((size,) + parts[0].shape, parts[0].dtype)
    for turn, part in enumerate(parts):
        whole = lax.dynamic_update_index_in_dim(whole, part, place ^ turn, 0)
    return whole.reshape(size * parts[0].shape[0], parts[0].shape[1])


def last_step(rows, others, lower, split):
    half = rows.shape[0]
    low, high = jnp.where(lower, rows, others), jnp.where(lower, others, rows)
    return jnp.concatenate([low, high[: split - half]], axis=0), high[split - half :]


def exchange(rows, domains):
    shape = rows.shape
    split = rows.reshape((domains, shape[0] // domains) + shape[1:])
    return lax.all_to_all(split, "dom", split_axis=0, concat_axis=0, tiled=True).reshape(shape)


def shards(
    nodes,
    edges,
    inner_pairs,
    cut_local,
    cut_dest,
    cut_remote,
    w_edge_in,
    w_edge_out,
    w_node_in,
    w_node_out,
    ct_nodes,
    ct_edges,
):
    domains = lax.axis_size("dom")
    node_rows, latent = nodes.shape
    inner_count, cut_count = inner_pairs.shape[0], cut_local.shape[0]
    inner_rows, cut_rows = 2 * inner_count, 2 * cut_count
    slots = max(2, 2 * cut_count // domains)
    total_slots = domains * slots
    table = node_rows + total_slots
    square = 2 * latent * latent
    me = lax.axis_index("dom").reshape(1)
    line = Line()

    ask = line.run(
        ask_kernel, shaped(jnp.int32, domains, slots), [cut_dest.reshape(1, -1), cut_remote.reshape(1, -1)], 10**7
    )
    asked = lax.all_to_all(ask, "dom", split_axis=0, concat_axis=0, tiled=True)
    cut_senders, cut_receivers = line.run(
        functools.partial(cut_marks_kernel, domains=domains, slots=slots),
        [shaped(BF16, cut_rows, table)] * 2,
        [cut_dest.reshape(1, -1), cut_local.reshape(1, -1)],
        10**8,
    )
    reply, asked_marks = line.run(
        reply_kernel,
        [shaped(BF16, total_slots, latent), shaped(BF16, total_slots, node_rows)],
        [asked, nodes],
        10**8,
    )
    far = exchange(reply, domains)

    block = cut_rows
    blocks = inner_rows // block

    def rows_spec(width, rows=block):
        return pl.BlockSpec((rows, width), lambda step: (step, 0))

    def all_spec(array):
        return pl.BlockSpec(array.shape, lambda step: (0, 0))

    saved_widths = [node_rows, node_rows, latent, latent, latent, latent, latent, 1]
    saved_types = [BF16, BF16, BF16, BF16, BF16, F32, F32, F32]
    (
        inner_senders,
        inner_receivers,
        inner_sender,
        inner_receiver,
        inner_hidden,
        inner_slope,
        inner_normed,
        inner_scale,
        inner_total,
    ) = line.run(
        inner_forward_kernel,
        [shaped(kind, inner_rows, width) for kind, width in zip(saved_types, saved_widths)]
        + [shaped(F32, node_rows, latent)],
        [inner_pairs.T, edges, nodes, w_edge_in, w_edge_out],
        inner_rows * 4 * square,
        [
            pl.BlockSpec((2, block // 2), lambda step: (0, step)),
            rows_spec(latent),
            all_spec(nodes),
            all_spec(w_edge_in),
            all_spec(w_edge_out),
        ],
        [rows_spec(width) for width in saved_widths] + [all_spec(nodes)],
        (blocks,),
    )

    def last_rows(array):
        last = array.shape[0] // block - 1
        return pl.BlockSpec((block, array.shape[1]), lambda step: (last, 0))

    (
        cut_sender,
        cut_receiver,
        cut_hidden,
        cut_slope,
        cut_normed,
        cut_scale,
        total,
        outgoing,
    ) = line.run(
        cut_forward_kernel,
        [shaped(kind, cut_rows, width) for kind, width in zip(saved_types, saved_widths)][2:]
        + [shaped(F32, node_rows, latent), shaped(BF16, total_slots, latent)],
        [
            cut_senders,
            cut_receivers,
            edges,
            nodes,
            far,
            w_edge_in,
            w_edge_out,
            inner_total,
        ],
        cut_rows * 4 * square,
        [
            all_spec(cut_senders),
            all_spec(cut_receivers),
            last_rows(edges),
            all_spec(nodes),
            all_spec(far),
            all_spec(w_edge_in),
            all_spec(w_edge_out),
            all_spec(inner_total),
        ],
        [rows_spec(width) for width in saved_widths[2:]]
        + [all_spec(nodes), rows_spec(latent, total_slots)],
        (1,),
    )
    incoming = exchange(outgoing, domains)
    new_edges = line.run(
        new_edges_kernel,
        shaped(BF16, *edges.shape),
        [edges, inner_normed, cut_normed],
        10**7,
    )
    (
        new_nodes,
        self_grad,
        agg_grad,
        grad_reply,
        aggregate,
        node_hidden,
        node_out,
        node_pre,
    ) = line.run(
        node_kernel,
        [
            shaped(BF16, node_rows, latent),
            shaped(F32, node_rows, latent),
            shaped(BF16, node_rows, latent),
            shaped(BF16, total_slots, latent),
        ]
        + [shaped(BF16, node_rows, latent)] * 4,
        [incoming, asked_marks, total, nodes, ct_nodes, w_node_in, w_node_out],
        node_rows * 6 * square,
    )
    far_grad = exchange(grad_reply, domains)
    node_keep, node_send = line.run(
        node_weights_kernel,
        [shaped(BF16, 3 * latent // 2, latent)] * 2,
        [me, nodes, aggregate, node_hidden, node_out, node_pre],
        node_rows * 3 * square,
        [SMEM] + [VMEM] * 5,
    )
    node_sum = added(node_keep, across(node_send, domains, 1))
    inner_out, inner_pre = line.run(
        inner_backward_kernel,
        [shaped(BF16, inner_rows, latent)] * 2,
        [
            inner_receivers,
            agg_grad,
            ct_edges,
            inner_normed,
            inner_scale,
            inner_slope,
            w_edge_out,
        ],
        inner_rows * square,
        [
            rows_spec(node_rows),
            all_spec(agg_grad),
            rows_spec(latent),
            rows_spec(latent),
            rows_spec(1),
            rows_spec(latent),
            all_spec(w_edge_out),
        ],
        [rows_spec(latent)] * 2,
        (blocks,),
    )
    groups = bit_groups(domains)
    bit_one, bits_two = groups[1], groups[2]
    far_grad, node_sum, inner_pre = fence(far_grad, node_sum, inner_pre)
    node_parts = traded(pieces_of(node_sum, *bit_one), domains, bit_one[0])
    cut_out, cut_pre = line.run(
        cut_backward_kernel,
        [shaped(BF16, cut_rows, latent)] * 2,
        [
            cut_receivers,
            agg_grad,
            far_grad,
            ct_edges,
            cut_normed,
            cut_scale,
            cut_slope,
            w_edge_out,
        ],
        cut_rows * square,
        [
            all_spec(cut_receivers),
            all_spec(agg_grad),
            all_spec(far_grad),
            last_rows(ct_edges),
            all_spec(cut_normed),
            all_spec(cut_scale),
            all_spec(cut_slope),
            all_spec(w_edge_out),
        ],
        [rows_spec(latent)] * 2,
        (1,),
    )
    factors = [
        edges,
        inner_sender,
        cut_sender,
        inner_receiver,
        cut_receiver,
        inner_hidden,
        cut_hidden,
        inner_out,
        cut_out,
        inner_pre,
        cut_pre,
    ]

    def edge_weights(turned, place):
        return line.run(
            functools.partial(edge_weights_kernel, turned=turned),
            shaped(BF16, 2 * latent, latent),
            [place] + factors,
            (inner_rows + cut_rows) * 2 * square,
            [SMEM] + [VMEM] * len(factors),
        )

    edge_send, place, *node_parts = fence(edge_weights(1, me), me, *node_parts)
    edge_parts = [edge_weights(0, place), across(edge_send, domains, 1)]
    node_parts = traded(pieces_of(added(*node_parts), *bits_two), domains, bits_two[0])
    fenced = fence(*edge_parts, *node_parts, inner_pre, cut_pre)
    edge_sum, node_sum = added(*fenced[:2]), added(*fenced[2:6])
    inner_pre, cut_pre = fenced[6:]
    for low, width in groups[3:]:
        node_sum = added(*traded(pieces_of(node_sum, low, width), domains, low))
    for low, width in groups[:2:-1]:
        node_sum = joined(handed(node_sum, domains, low, width), low)
    edge_parts = traded(pieces_of(edge_sum, *bit_one), domains, bit_one[0])
    node_parts = handed(node_sum, domains, *bits_two)
    local_grad, outgoing_grad = line.run(
        input_grads_kernel,
        [shaped(F32, node_rows, latent), shaped(BF16, total_slots, latent)],
        [
            inner_senders,
            inner_receivers,
            cut_senders,
            cut_receivers,
            inner_pre,
            cut_pre,
            w_edge_in,
        ],
        (node_rows + total_slots) * 2 * square,
    )
    returned = exchange(outgoing_grad, domains)
    fenced = fence(*edge_parts, *node_parts, inner_pre, cut_pre, local_grad)
    edge_sum, node_sum = added(*fenced[:2]), joined(fenced[2:6], bits_two[0])
    inner_pre, cut_pre, local_grad = fenced[6:]
    edge_parts = traded(pieces_of(edge_sum, *bits_two), domains, bits_two[0])
    node_parts = handed(node_sum, domains, *bit_one)
    grad_edges = line.run(
        functools.partial(edge_grads_kernel, blocks=blocks),
        shaped(F32, *edges.shape),
        [ct_edges, inner_pre, cut_pre, w_edge_in],
        (inner_rows + cut_rows) * square,
        [
            rows_spec(latent),
            pl.BlockSpec((block, latent), lambda step: (jnp.minimum(step, blocks - 1), 0)),
            all_spec(cut_pre),
            pl.BlockSpec((latent, latent), lambda step: (0, 0)),
        ],
        [rows_spec(latent)],
        (blocks + 1,),
    )
    fenced = fence(*edge_parts, *node_parts, returned, grad_edges)
    edge_sum, node_sum = added(*fenced[:4]), joined(fenced[4:6], bit_one[0])
    returned, grad_edges = fenced[6:]
    for low, width in groups[3:]:
        edge_sum = added(*traded(pieces_of(edge_sum, low, width), domains, low))
    for low, width in groups[:2:-1]:
        edge_sum = joined(handed(edge_sum, domains, low, width), low)
    edge_parts = handed(edge_sum, domains, *bits_two)
    others = across(node_sum, domains, 1)
    grad_nodes = line.run(
        node_grads_kernel,
        shaped(F32, node_rows, latent),
        [self_grad, local_grad, asked_marks, returned],
        10**8,
    )
    *edge_parts, node_sum, others, grad_nodes = fence(*edge_parts, node_sum, others, grad_nodes)
    edge_parts = handed(joined(edge_parts, bits_two[0]), domains, *bit_one)
    lower = place_of(0, 2) == 0
    grad_node_in, grad_node_out = last_step(node_sum, others, lower, 2 * latent)
    *edge_parts, grad_node_in, grad_node_out = fence(*edge_parts, grad_node_in, grad_node_out)
    edge_sum = joined(edge_parts, bit_one[0])
    grad_edge_in, grad_edge_out = last_step(
        edge_sum, across(edge_sum, domains, 1), lower, 3 * latent
    )
    return (
        new_nodes,
        new_edges,
        grad_nodes,
        grad_edges,
        grad_edge_in,
        grad_edge_out,
        grad_node_in,
        grad_node_out,
    )


def solution(mesh):
    placed = (
        P(("groups", "dom"), None),
        P(("groups", "dom"), None),
        P(("groups", "dom"), None),
        P(("groups", "dom")),
        P(("groups", "dom"), None),
        P(("groups", "dom")),
        P(),
        P(),
        P(),
        P(),
        P(("groups", "dom"), None),
        P(("groups", "dom"), None),
    )
    return jax.shard_map(
        shards,
        mesh=mesh,
        in_specs=placed,
        out_specs=(
            P(("groups", "dom"), None),
            P(("groups", "dom"), None),
            P(("groups", "dom"), None),
            P(("groups", "dom"), None),
            P("groups", None),
            P("groups", None),
            P("groups", None),
            P("groups", None),
        ),
        check_vma=False,
    )
```

```python
import functools

import jax
import jax.numpy as jnp
from jax import lax
from jax.experimental import pallas as pl
from jax.experimental.pallas import tpu as pltpu
from jax.sharding import PartitionSpec as P

BF16 = jnp.bfloat16
F32 = jnp.float32
VMEM_LIMIT = 60 * 1024 * 1024


def dot(left, right):
    return jnp.dot(left, right, preferred_element_type=F32)


def dot_rows(left, right):
    return lax.dot_general(left, right, (((0,), (0,)), ((), ())), preferred_element_type=F32)


def dot_cols(left, right):
    return lax.dot_general(left, right, (((1,), (1,)), ((), ())), preferred_element_type=F32)


def iota(shape, axis):
    return lax.broadcasted_iota(jnp.int32, shape, axis)


def marks(mask):
    return jnp.where(mask, 1.0, 0.0).astype(BF16)


def onehot(column, width):
    return marks(column == iota((column.shape[0], width), 1))


def to_column(row):
    count = row.shape[1]
    square = (count, count)
    kept = jnp.where(iota(square, 0) == iota(square, 1), row.astype(F32), 0.0)
    return jnp.sum(kept, axis=1, keepdims=True)


def slot_ranks(dest, domains):
    count = dest.shape[0]
    square = (count, count)
    dest_marks = onehot(dest, domains)
    before = dot(marks(iota(square, 0) > iota(square, 1)), dest_marks)
    return dest_marks, jnp.sum(before * dest_marks.astype(F32), axis=1, keepdims=True)


def pair_marks(first, second, width):
    pairs = first.shape[0]
    shape = (2 * pairs, pairs)
    edge, pair = iota(shape, 0), iota(shape, 1)
    mine = (edge >> 1) == pair
    even = marks(mine & ((edge & 1) == 0))
    odd = marks(mine & ((edge & 1) == 1))
    first_marks, second_marks = onehot(first, width), onehot(second, width)
    senders = dot(even, first_marks) + dot(odd, second_marks)
    receivers = dot(even, second_marks) + dot(odd, first_marks)
    return senders.astype(BF16), receivers.astype(BF16)


def normalise(values):
    centered = values - jnp.mean(values, axis=1, keepdims=True)
    inv_scale = lax.rsqrt(jnp.mean(centered * centered, axis=1, keepdims=True) + 1e-05)
    return centered * inv_scale, inv_scale


def activate(pre_hidden):
    gate = jax.nn.sigmoid(pre_hidden)
    return (pre_hidden * gate).astype(BF16), gate * (1.0 + pre_hidden * (1.0 - gate))


def norm_backward(upstream, normed, inv_scale):
    centered = (
        upstream
        - jnp.mean(upstream, axis=1, keepdims=True)
        - normed * jnp.mean(upstream * normed, axis=1, keepdims=True)
    )
    return (inv_scale * centered).astype(BF16)


def ask_kernel(dest_ref, remote_ref, ask_ref):
    domains, slots = ask_ref.shape
    dest_marks, rank = slot_ranks(to_column(dest_ref[...]).astype(jnp.int32), domains)
    rank_marks = jnp.where(rank == iota((rank.shape[0], slots), 1).astype(F32), 1.0, 0.0)
    wanted = (rank_marks * to_column(remote_ref[...])).astype(BF16)
    ask_ref[...] = dot_rows(dest_marks, wanted).astype(jnp.int32)


def reply_kernel(asked_ref, nodes_ref, reply_ref, asked_marks_ref):
    domains, slots = asked_ref.shape
    total = domains * slots
    shift = slots.bit_length() - 1
    spread = marks((iota((total, domains), 0) >> shift) == iota((total, domains), 1))
    listed = dot(spread, asked_ref[...].astype(F32).astype(BF16))
    at_slot = (iota((total, slots), 0) & (slots - 1)) == iota((total, slots), 1)
    column = jnp.sum(jnp.where(at_slot, listed, 0.0), axis=1, keepdims=True)
    node_rows = nodes_ref.shape[0]
    asked_marks = marks(column == iota((total, node_rows), 1).astype(F32))
    asked_marks_ref[...] = asked_marks
    reply_ref[...] = dot(asked_marks, nodes_ref[...]).astype(BF16)


def cut_marks_kernel(dest_ref, local_ref, senders_ref, receivers_ref, *, domains, slots):
    width = senders_ref.shape[1]
    base = width - domains * slots
    dest = to_column(dest_ref[...]).astype(jnp.int32)
    _, rank = slot_ranks(dest, domains)
    second = dest * slots + rank.astype(jnp.int32) + base
    first = to_column(local_ref[...]).astype(jnp.int32)
    senders, receivers = pair_marks(first, second, width)
    senders_ref[...] = senders
    receivers_ref[...] = receivers


def edge_forward(edge, sender, receiver, w_in_ref, w_out_ref):
    latent = edge.shape[1]
    pre_hidden = (
        dot(edge, w_in_ref[:latent])
        + dot(sender, w_in_ref[latent : 2 * latent])
        + dot(receiver, w_in_ref[2 * latent :])
    )
    hidden, slope = activate(pre_hidden)
    normed, inv_scale = normalise(dot(hidden, w_out_ref[...]))
    return hidden, slope, normed, inv_scale


def inner_forward_kernel(
    pairs_ref,
    edges_ref,
    nodes_ref,
    w_in_ref,
    w_out_ref,
    senders_ref,
    receivers_ref,
    sender_ref,
    receiver_ref,
    hidden_ref,
    slope_ref,
    normed_ref,
    scale_ref,
    total_ref,
):
    first, second = (to_column(pairs_ref[side : side + 1]).astype(jnp.int32) for side in range(2))
    senders, receivers = pair_marks(first, second, nodes_ref.shape[0])
    senders_ref[...] = senders
    receivers_ref[...] = receivers
    nodes = nodes_ref[...]
    sender = dot(senders, nodes).astype(BF16)
    receiver = dot(receivers, nodes).astype(BF16)
    sender_ref[...] = sender
    receiver_ref[...] = receiver
    hidden, slope, normed, inv_scale = edge_forward(
        edges_ref[...], sender, receiver, w_in_ref, w_out_ref
    )
    hidden_ref[...] = hidden
    slope_ref[...] = slope
    normed_ref[...] = normed
    scale_ref[...] = inv_scale
    part = dot_rows(receivers, normed.astype(BF16))

    @pl.when(pl.program_id(0) == 0)
    def _():
        total_ref[...] = part

    @pl.when(pl.program_id(0) > 0)
    def _():
        total_ref[...] += part


def cut_forward_kernel(
    senders_ref,
    receivers_ref,
    edges_ref,
    nodes_ref,
    far_ref,
    w_in_ref,
    w_out_ref,
    inner_total_ref,
    sender_ref,
    receiver_ref,
    hidden_ref,
    slope_ref,
    normed_ref,
    scale_ref,
    total_ref,
    outgoing_ref,
):
    base = nodes_ref.shape[0]
    nodes, far = nodes_ref[...], far_ref[...]

    def rows_of(marks_ref):
        return (dot(marks_ref[:, :base], nodes) + dot(marks_ref[:, base:], far)).astype(BF16)

    sender, receiver = rows_of(senders_ref), rows_of(receivers_ref)
    sender_ref[...] = sender
    receiver_ref[...] = receiver
    hidden, slope, normed, inv_scale = edge_forward(
        edges_ref[...], sender, receiver, w_in_ref, w_out_ref
    )
    hidden_ref[...] = hidden
    slope_ref[...] = slope
    normed_ref[...] = normed
    scale_ref[...] = inv_scale
    message = normed.astype(BF16)
    total_ref[...] = inner_total_ref[...] + dot_rows(receivers_ref[:, :base], message)
    outgoing_ref[...] = dot_rows(receivers_ref[:, base:], message).astype(BF16)


def new_edges_kernel(edges_ref, inner_ref, cut_ref, out_ref):
    inner_rows = inner_ref.shape[0]

    def added(edge, normed):
        return (edge.astype(F32) + normed.astype(BF16).astype(F32)).astype(BF16)

    out_ref[:inner_rows] = added(edges_ref[:inner_rows], inner_ref[...])
    out_ref[inner_rows:] = added(edges_ref[inner_rows:], cut_ref[...])


def node_kernel(
    incoming_ref,
    asked_marks_ref,
    total_ref,
    nodes_ref,
    ct_ref,
    w_in_ref,
    w_out_ref,
    new_nodes_ref,
    self_grad_ref,
    agg_grad_ref,
    reply_ref,
    aggregate_ref,
    hidden_ref,
    grad_out_ref,
    grad_pre_ref,
):
    latent = nodes_ref.shape[1]
    nodes, asked_marks = nodes_ref[...], asked_marks_ref[...]
    aggregate = (total_ref[...] + dot_rows(asked_marks, incoming_ref[...])).astype(BF16)
    aggregate_ref[...] = aggregate
    pre_hidden = dot(nodes, w_in_ref[:latent]) + dot(aggregate, w_in_ref[latent:])
    hidden, slope = activate(pre_hidden)
    hidden_ref[...] = hidden
    normed, inv_scale = normalise(dot(hidden, w_out_ref[...]))
    upstream = ct_ref[...].astype(F32)
    grad_out = norm_backward(upstream, normed, inv_scale)
    grad_out_ref[...] = grad_out
    grad_pre = (dot_cols(grad_out, w_out_ref[...]) * slope).astype(BF16)
    grad_pre_ref[...] = grad_pre
    agg_grad = dot_cols(grad_pre, w_in_ref[latent:]).astype(BF16)
    agg_grad_ref[...] = agg_grad
    reply_ref[...] = dot(asked_marks, agg_grad).astype(BF16)
    self_grad_ref[...] = upstream + dot_cols(grad_pre, w_in_ref[:latent])
    new_nodes_ref[...] = (nodes.astype(F32) + normed).astype(BF16)


def node_weights_kernel(
    me_ref, nodes_ref, aggregate_ref, hidden_ref, grad_out_ref, grad_pre_ref, keep_ref, send_ref
):
    latent = nodes_ref.shape[1]
    half = latent // 2

    def fill(low_ref, high_ref):
        grad_pre, grad_out = grad_pre_ref[...], grad_out_ref[...]
        low_ref[:latent] = dot_rows(nodes_ref[...], grad_pre).astype(BF16)
        low_ref[latent:] = dot_rows(aggregate_ref[:, :half], grad_pre).astype(BF16)
        high_ref[:half] = dot_rows(aggregate_ref[:, half:], grad_pre).astype(BF16)
        high_ref[half:] = dot_rows(hidden_ref[...], grad_out).astype(BF16)

    halves(me_ref, keep_ref, send_ref, fill)


def halves(me_ref, keep_ref, send_ref, fill):
    @pl.when((me_ref[0] & 1) == 0)
    def _():
        fill(keep_ref, send_ref)

    @pl.when((me_ref[0] & 1) != 0)
    def _():
        fill(send_ref, keep_ref)


def edge_backward(ct, target_grads, normed, inv_scale, slope, w_out):
    grad_out = norm_backward(ct.astype(F32) + target_grads, normed, inv_scale)
    return grad_out, (dot_cols(grad_out, w_out) * slope).astype(BF16)


def inner_backward_kernel(
    receivers_ref,
    agg_grad_ref,
    ct_ref,
    normed_ref,
    scale_ref,
    slope_ref,
    w_out_ref,
    grad_out_ref,
    grad_pre_ref,
):
    grad_out, grad_pre = edge_backward(
        ct_ref[...],
        dot(receivers_ref[...], agg_grad_ref[...]),
        normed_ref[...],
        scale_ref[...],
        slope_ref[...],
        w_out_ref[...],
    )
    grad_out_ref[...] = grad_out
    grad_pre_ref[...] = grad_pre


def cut_backward_kernel(
    receivers_ref,
    agg_grad_ref,
    far_grad_ref,
    ct_ref,
    normed_ref,
    scale_ref,
    slope_ref,
    w_out_ref,
    grad_out_ref,
    grad_pre_ref,
):
    base = agg_grad_ref.shape[0]
    target = dot(receivers_ref[:, :base], agg_grad_ref[...]) + dot(
        receivers_ref[:, base:], far_grad_ref[...]
    )
    grad_out, grad_pre = edge_backward(
        ct_ref[...], target, normed_ref[...], scale_ref[...], slope_ref[...], w_out_ref[...]
    )
    grad_out_ref[...] = grad_out
    grad_pre_ref[...] = grad_pre


def edge_weights_kernel(
    me_ref,
    edges_ref,
    inner_sender_ref,
    cut_sender_ref,
    inner_receiver_ref,
    cut_receiver_ref,
    inner_hidden_ref,
    cut_hidden_ref,
    inner_out_ref,
    cut_out_ref,
    inner_pre_ref,
    cut_pre_ref,
    out_ref,
    *,
    turned,
):
    latent = edges_ref.shape[1]
    inner_rows = inner_pre_ref.shape[0]

    @pl.when((me_ref[0] & 1) == turned)
    def _():
        inner_pre, cut_pre = inner_pre_ref[...], cut_pre_ref[...]
        out_ref[:latent] = (
            dot_rows(edges_ref[:inner_rows], inner_pre) + dot_rows(edges_ref[inner_rows:], cut_pre)
        ).astype(BF16)
        out_ref[latent:] = (
            dot_rows(inner_sender_ref[...], inner_pre) + dot_rows(cut_sender_ref[...], cut_pre)
        ).astype(BF16)

    @pl.when((me_ref[0] & 1) != turned)
    def _():
        out_ref[:latent] = (
            dot_rows(inner_receiver_ref[...], inner_pre_ref[...])
            + dot_rows(cut_receiver_ref[...], cut_pre_ref[...])
        ).astype(BF16)
        out_ref[latent:] = (
            dot_rows(inner_hidden_ref[...], inner_out_ref[...])
            + dot_rows(cut_hidden_ref[...], cut_out_ref[...])
        ).astype(BF16)


def input_grads_kernel(
    inner_senders_ref,
    inner_receivers_ref,
    cut_senders_ref,
    cut_receivers_ref,
    inner_pre_ref,
    cut_pre_ref,
    w_in_ref,
    local_ref,
    outgoing_ref,
):
    latent = inner_pre_ref.shape[1]
    base = inner_senders_ref.shape[1]
    inner_pre, cut_pre = inner_pre_ref[...], cut_pre_ref[...]
    w_sender, w_receiver = w_in_ref[latent : 2 * latent], w_in_ref[2 * latent :]

    def summed(inner_marks_ref, cut_marks_ref):
        return (
            dot_rows(inner_marks_ref[...], inner_pre) + dot_rows(cut_marks_ref[:, :base], cut_pre)
        ).astype(BF16)

    outgoing_ref[...] = (
        dot_cols(dot_rows(cut_senders_ref[:, base:], cut_pre).astype(BF16), w_sender)
        + dot_cols(dot_rows(cut_receivers_ref[:, base:], cut_pre).astype(BF16), w_receiver)
    ).astype(BF16)
    local_ref[...] = dot_cols(summed(inner_senders_ref, cut_senders_ref), w_sender) + dot_cols(
        summed(inner_receivers_ref, cut_receivers_ref), w_receiver
    )


def edge_grads_kernel(ct_ref, inner_pre_ref, cut_pre_ref, w_edge_ref, out_ref, *, blocks):
    inside = pl.program_id(0) < blocks

    @pl.when(inside)
    def _():
        out_ref[...] = ct_ref[...].astype(F32) + dot_cols(inner_pre_ref[...], w_edge_ref[...])

    @pl.when(jnp.logical_not(inside))
    def _():
        out_ref[...] = ct_ref[...].astype(F32) + dot_cols(cut_pre_ref[...], w_edge_ref[...])


def node_grads_kernel(self_ref, local_ref, asked_marks_ref, returned_ref, out_ref):
    out_ref[...] = (
        self_ref[...] + local_ref[...] + dot_rows(asked_marks_ref[...], returned_ref[...])
    )


VMEM = pl.BlockSpec(memory_space=pltpu.VMEM)
SMEM = pl.BlockSpec(memory_space=pltpu.SMEM)
ANY = pl.BlockSpec(memory_space=pl.ANY)


def shaped(dtype, *shape):
    return jax.ShapeDtypeStruct(shape, dtype)


class Line:
    def __init__(self):
        self.last = None

    def run(self, body, outs, ins, flops, specs=None, out_specs=None, grid=None):
        single = not isinstance(outs, (list, tuple))
        out_shape = [outs] if single else list(outs)
        specs = [VMEM] * len(ins) if specs is None else list(specs)
        moved = sum(item.size * item.dtype.itemsize for item in list(ins) + out_shape)
        count, extra = len(ins), {} if grid is None else {"grid": grid}
        ins = list(ins)
        if self.last is not None:
            ins.append(self.last)
            specs.append(ANY)

        def ordered(*refs):
            return body(*refs[:count], *refs[len(ins) :])

        result = pl.pallas_call(
            ordered,
            out_shape=out_shape,
            in_specs=specs,
            out_specs=[VMEM] * len(out_shape) if out_specs is None else out_specs,
            compiler_params=pltpu.CompilerParams(vmem_limit_bytes=VMEM_LIMIT),
            cost_estimate=pl.CostEstimate(flops=flops, bytes_accessed=moved, transcendentals=0),
            **extra,
        )(*ins)
        self.last = result[-1]
        return result[0] if single else result


def bit_groups(devices):
    bits = devices.bit_length() - 1
    groups = [(low, 1) for low in range(min(2, bits))]
    low = 2
    while low < bits:
        groups.append((low, min(2, bits - low)))
        low += 2
    return groups


def across(rows, devices, mask):
    return lax.ppermute(rows, "dom", [(device, device ^ mask) for device in range(devices)])


def fence(*values):
    return lax.optimization_barrier(values)


def place_of(low, size):
    return (lax.axis_index("dom") >> low) & (size - 1)


def pieces_of(rows, low, width):
    size = 1 << width
    place = place_of(low, size)
    pieces = rows.reshape(size, rows.shape[0] // size, rows.shape[1])
    return [lax.dynamic_index_in_dim(pieces, place ^ turn, 0, False) for turn in range(size)]


def traded(pieces, devices, low):
    return pieces[:1] + [
        across(piece, devices, turn << low) for turn, piece in enumerate(pieces) if turn
    ]


def handed(rows, devices, low, width):
    return traded([rows] * (1 << width), devices, low)


def added(*parts):
    return sum(part.astype(F32) for part in parts).astype(BF16)


def joined(parts, low):
    size = len(parts)
    place = place_of(low, size)
    if size == 2:
        orders = [jnp.concatenate(parts), jnp.concatenate(parts[::-1])]
        return jnp.where(place == 0, *orders)
    whole = jnp.zeros((size,) + parts[0].shape, parts[0].dtype)
    for turn, part in enumerate(parts):
        whole = lax.dynamic_update_index_in_dim(whole, part, place ^ turn, 0)
    return whole.reshape(size * parts[0].shape[0], parts[0].shape[1])


def by_owner(rows, groups):
    sizes = [1 << width for _, width in groups]
    split = rows.reshape(sizes[::-1] + [-1, rows.shape[1]])
    turned = list(range(len(sizes)))[::-1] + [len(sizes), len(sizes) + 1]
    return split.transpose(turned).reshape(rows.shape)


def exchange(rows, domains):
    shape = rows.shape
    split = rows.reshape((domains, shape[0] // domains) + shape[1:])
    return lax.all_to_all(split, "dom", split_axis=0, concat_axis=0, tiled=True).reshape(shape)


def shards(
    nodes,
    edges,
    inner_pairs,
    cut_local,
    cut_dest,
    cut_remote,
    w_edge_in,
    w_edge_out,
    w_node_in,
    w_node_out,
    ct_nodes,
    ct_edges,
):
    domains = lax.axis_size("dom")
    node_rows, latent = nodes.shape
    inner_count, cut_count = inner_pairs.shape[0], cut_local.shape[0]
    inner_rows, cut_rows = 2 * inner_count, 2 * cut_count
    slots = max(2, 2 * cut_count // domains)
    total_slots = domains * slots
    table = node_rows + total_slots
    square = 2 * latent * latent
    me = lax.axis_index("dom").reshape(1)
    line = Line()

    ask = line.run(
        ask_kernel, shaped(jnp.int32, domains, slots), [cut_dest.reshape(1, -1), cut_remote.reshape(1, -1)], 10**7
    )
    asked = lax.all_to_all(ask, "dom", split_axis=0, concat_axis=0, tiled=True)
    cut_senders, cut_receivers = line.run(
        functools.partial(cut_marks_kernel, domains=domains, slots=slots),
        [shaped(BF16, cut_rows, table)] * 2,
        [cut_dest.reshape(1, -1), cut_local.reshape(1, -1)],
        10**8,
    )
    reply, asked_marks = line.run(
        reply_kernel,
        [shaped(BF16, total_slots, latent), shaped(BF16, total_slots, node_rows)],
        [asked, nodes],
        10**8,
    )
    far = exchange(reply, domains)

    block = cut_rows
    blocks = inner_rows // block

    def rows_spec(width, rows=block):
        return pl.BlockSpec((rows, width), lambda step: (step, 0))

    def all_spec(array):
        return pl.BlockSpec(array.shape, lambda step: (0, 0))

    saved_widths = [node_rows, node_rows, latent, latent, latent, latent, latent, 1]
    saved_types = [BF16, BF16, BF16, BF16, BF16, F32, F32, F32]
    (
        inner_senders,
        inner_receivers,
        inner_sender,
        inner_receiver,
        inner_hidden,
        inner_slope,
        inner_normed,
        inner_scale,
        inner_total,
    ) = line.run(
        inner_forward_kernel,
        [shaped(kind, inner_rows, width) for kind, width in zip(saved_types, saved_widths)]
        + [shaped(F32, node_rows, latent)],
        [inner_pairs.T, edges, nodes, w_edge_in, w_edge_out],
        inner_rows * 4 * square,
        [
            pl.BlockSpec((2, block // 2), lambda step: (0, step)),
            rows_spec(latent),
            all_spec(nodes),
            all_spec(w_edge_in),
            all_spec(w_edge_out),
        ],
        [rows_spec(width) for width in saved_widths] + [all_spec(nodes)],
        (blocks,),
    )

    def last_rows(array):
        last = array.shape[0] // block - 1
        return pl.BlockSpec((block, array.shape[1]), lambda step: (last, 0))

    (
        cut_sender,
        cut_receiver,
        cut_hidden,
        cut_slope,
        cut_normed,
        cut_scale,
        total,
        outgoing,
    ) = line.run(
        cut_forward_kernel,
        [shaped(kind, cut_rows, width) for kind, width in zip(saved_types, saved_widths)][2:]
        + [shaped(F32, node_rows, latent), shaped(BF16, total_slots, latent)],
        [
            cut_senders,
            cut_receivers,
            edges,
            nodes,
            far,
            w_edge_in,
            w_edge_out,
            inner_total,
        ],
        cut_rows * 4 * square,
        [
            all_spec(cut_senders),
            all_spec(cut_receivers),
            last_rows(edges),
            all_spec(nodes),
            all_spec(far),
            all_spec(w_edge_in),
            all_spec(w_edge_out),
            all_spec(inner_total),
        ],
        [rows_spec(width) for width in saved_widths[2:]]
        + [all_spec(nodes), rows_spec(latent, total_slots)],
        (1,),
    )
    incoming = exchange(outgoing, domains)
    new_edges = line.run(
        new_edges_kernel,
        shaped(BF16, *edges.shape),
        [edges, inner_normed, cut_normed],
        10**7,
    )
    (
        new_nodes,
        self_grad,
        agg_grad,
        grad_reply,
        aggregate,
        node_hidden,
        node_out,
        node_pre,
    ) = line.run(
        node_kernel,
        [
            shaped(BF16, node_rows, latent),
            shaped(F32, node_rows, latent),
            shaped(BF16, node_rows, latent),
            shaped(BF16, total_slots, latent),
        ]
        + [shaped(BF16, node_rows, latent)] * 4,
        [incoming, asked_marks, total, nodes, ct_nodes, w_node_in, w_node_out],
        node_rows * 6 * square,
    )
    far_grad = exchange(grad_reply, domains)
    inner_out, inner_pre = line.run(
        inner_backward_kernel,
        [shaped(BF16, inner_rows, latent)] * 2,
        [
            inner_receivers,
            agg_grad,
            ct_edges,
            inner_normed,
            inner_scale,
            inner_slope,
            w_edge_out,
        ],
        inner_rows * square,
        [
            rows_spec(node_rows),
            all_spec(agg_grad),
            rows_spec(latent),
            rows_spec(latent),
            rows_spec(1),
            rows_spec(latent),
            all_spec(w_edge_out),
        ],
        [rows_spec(latent)] * 2,
        (blocks,),
    )
    node_keep, node_send = line.run(
        node_weights_kernel,
        [shaped(BF16, 3 * latent // 2, latent)] * 2,
        [me, nodes, aggregate, node_hidden, node_out, node_pre],
        node_rows * 3 * square,
        [SMEM] + [VMEM] * 5,
    )
    node_sum = added(node_keep, across(node_send, domains, 1))
    groups = bit_groups(domains)
    bit_one, bits_two = groups[1], groups[2]
    node_parts = traded(pieces_of(node_sum, *bit_one), domains, bit_one[0])
    far_grad, node_sum, inner_pre = fence(far_grad, node_sum, inner_pre)
    cut_out, cut_pre = line.run(
        cut_backward_kernel,
        [shaped(BF16, cut_rows, latent)] * 2,
        [
            cut_receivers,
            agg_grad,
            far_grad,
            ct_edges,
            cut_normed,
            cut_scale,
            cut_slope,
            w_edge_out,
        ],
        cut_rows * square,
        [
            all_spec(cut_receivers),
            all_spec(agg_grad),
            all_spec(far_grad),
            last_rows(ct_edges),
            all_spec(cut_normed),
            all_spec(cut_scale),
            all_spec(cut_slope),
            all_spec(w_edge_out),
        ],
        [rows_spec(latent)] * 2,
        (1,),
    )
    factors = [
        edges,
        inner_sender,
        cut_sender,
        inner_receiver,
        cut_receiver,
        inner_hidden,
        cut_hidden,
        inner_out,
        cut_out,
        inner_pre,
        cut_pre,
    ]

    def edge_weights(turned, place):
        return line.run(
            functools.partial(edge_weights_kernel, turned=turned),
            shaped(BF16, 2 * latent, latent),
            [place] + factors,
            (inner_rows + cut_rows) * 2 * square,
            [SMEM] + [VMEM] * len(factors),
        )

    edge_send, place, *node_parts = fence(edge_weights(1, me), me, *node_parts)
    edge_parts = [edge_weights(0, place), across(edge_send, domains, 1)]
    fenced = fence(*edge_parts, *node_parts, inner_pre, cut_pre)
    edge_parts, node_parts, (inner_pre, cut_pre) = fenced[:2], fenced[2:4], fenced[4:]
    edge_parts = traded(pieces_of(added(*edge_parts), *bit_one), domains, bit_one[0])
    node_parts = traded(pieces_of(added(*node_parts), *bits_two), domains, bits_two[0])
    local_grad, outgoing_grad = line.run(
        input_grads_kernel,
        [shaped(F32, node_rows, latent), shaped(BF16, total_slots, latent)],
        [
            inner_senders,
            inner_receivers,
            cut_senders,
            cut_receivers,
            inner_pre,
            cut_pre,
            w_edge_in,
        ],
        (node_rows + total_slots) * 2 * square,
    )
    returned = exchange(outgoing_grad, domains)
    fenced = fence(*edge_parts, *node_parts, inner_pre, cut_pre, local_grad)
    edge_parts, node_sum = fenced[:2], added(*fenced[2:6])
    inner_pre, cut_pre, local_grad = fenced[6:]
    for low, width in groups[3:]:
        node_sum = added(*traded(pieces_of(node_sum, low, width), domains, low))
    node_total = lax.all_gather(node_sum, "dom", axis=0, tiled=True)
    edge_parts = traded(pieces_of(added(*edge_parts), *bits_two), domains, bits_two[0])
    grad_edges = line.run(
        functools.partial(edge_grads_kernel, blocks=blocks),
        shaped(F32, *edges.shape),
        [ct_edges, inner_pre, cut_pre, w_edge_in],
        (inner_rows + cut_rows) * square,
        [
            rows_spec(latent),
            pl.BlockSpec((block, latent), lambda step: (jnp.minimum(step, blocks - 1), 0)),
            all_spec(cut_pre),
            pl.BlockSpec((latent, latent), lambda step: (0, 0)),
        ],
        [rows_spec(latent)],
        (blocks + 1,),
    )
    *edge_parts, returned, grad_edges = fence(*edge_parts, returned, grad_edges)
    edge_sum = added(*edge_parts)
    for low, width in groups[3:]:
        edge_sum = added(*traded(pieces_of(edge_sum, low, width), domains, low))
    for low, width in groups[:2:-1]:
        edge_sum = joined(handed(edge_sum, domains, low, width), low)
    edge_parts = handed(edge_sum, domains, *bits_two)
    grad_nodes = line.run(
        node_grads_kernel,
        shaped(F32, node_rows, latent),
        [self_grad, local_grad, asked_marks, returned],
        10**8,
    )
    *edge_parts, grad_nodes, node_total = fence(*edge_parts, grad_nodes, node_total)
    edge_sum = joined(edge_parts, bits_two[0])
    edge_parts = handed(edge_sum, domains, *bit_one) + [across(edge_sum, domains, 1)]
    node_total = by_owner(node_total, groups)
    grad_node_in, grad_node_out = node_total[: 2 * latent], node_total[2 * latent :]
    mine, far, near, grad_node_in, grad_node_out = fence(*edge_parts, grad_node_in, grad_node_out)
    corner = across(far, domains, 1)
    lower, left = place_of(0, 2) == 0, place_of(bit_one[0], 2) == 0
    own, other = [mine, far], [near, corner]
    low_half = [jnp.where(lower, one, two) for one, two in zip(own, other)]
    high_half = [jnp.where(lower, two, one) for one, two in zip(own, other)]
    grad_edge_in = jnp.concatenate(
        [
            jnp.where(left, low_half[0], low_half[1]),
            jnp.where(left, low_half[1], low_half[0]),
            jnp.where(left, high_half[0], high_half[1]),
        ]
    )
    grad_edge_out = jnp.where(left, high_half[1], high_half[0])
    return (
        new_nodes,
        new_edges,
        grad_nodes,
        grad_edges,
        grad_edge_in,
        grad_edge_out,
        grad_node_in,
        grad_node_out,
    )


def solution(mesh):
    placed = (
        P(("groups", "dom"), None),
        P(("groups", "dom"), None),
        P(("groups", "dom"), None),
        P(("groups", "dom")),
        P(("groups", "dom"), None),
        P(("groups", "dom")),
        P(),
        P(),
        P(),
        P(),
        P(("groups", "dom"), None),
        P(("groups", "dom"), None),
    )
    return jax.shard_map(
        shards,
        mesh=mesh,
        in_specs=placed,
        out_specs=(
            P(("groups", "dom"), None),
            P(("groups", "dom"), None),
            P(("groups", "dom"), None),
            P(("groups", "dom"), None),
            P("groups", None),
            P("groups", None),
            P("groups", None),
            P("groups", None),
        ),
        check_vma=False,
    )
```

```python
import functools

import jax
import jax.numpy as jnp
from jax import lax
from jax.experimental import pallas as pl
from jax.experimental.pallas import tpu as pltpu
from jax.sharding import PartitionSpec as P

BF16 = jnp.bfloat16
F32 = jnp.float32
VMEM_LIMIT = 60 * 1024 * 1024


def dot(left, right):
    return jnp.dot(left, right, preferred_element_type=F32)


def dot_rows(left, right):
    return lax.dot_general(left, right, (((0,), (0,)), ((), ())), preferred_element_type=F32)


def dot_cols(left, right):
    return lax.dot_general(left, right, (((1,), (1,)), ((), ())), preferred_element_type=F32)


def iota(shape, axis):
    return lax.broadcasted_iota(jnp.int32, shape, axis)


def marks(mask):
    return jnp.where(mask, 1.0, 0.0).astype(BF16)


def onehot(column, width):
    return marks(column == iota((column.shape[0], width), 1))


def to_column(row):
    count = row.shape[1]
    square = (count, count)
    kept = jnp.where(iota(square, 0) == iota(square, 1), row.astype(F32), 0.0)
    return jnp.sum(kept, axis=1, keepdims=True)


def slot_ranks(dest, domains):
    count = dest.shape[0]
    square = (count, count)
    dest_marks = onehot(dest, domains)
    before = dot(marks(iota(square, 0) > iota(square, 1)), dest_marks)
    return dest_marks, jnp.sum(before * dest_marks.astype(F32), axis=1, keepdims=True)


def pair_marks(first, second, width):
    pairs = first.shape[0]
    shape = (2 * pairs, pairs)
    edge, pair = iota(shape, 0), iota(shape, 1)
    mine = (edge >> 1) == pair
    even = marks(mine & ((edge & 1) == 0))
    odd = marks(mine & ((edge & 1) == 1))
    first_marks, second_marks = onehot(first, width), onehot(second, width)
    senders = dot(even, first_marks) + dot(odd, second_marks)
    receivers = dot(even, second_marks) + dot(odd, first_marks)
    return senders.astype(BF16), receivers.astype(BF16)


def normalise(values):
    centered = values - jnp.mean(values, axis=1, keepdims=True)
    inv_scale = lax.rsqrt(jnp.mean(centered * centered, axis=1, keepdims=True) + 1e-05)
    return centered * inv_scale, inv_scale


def activate(pre_hidden):
    gate = jax.nn.sigmoid(pre_hidden)
    return (pre_hidden * gate).astype(BF16), gate * (1.0 + pre_hidden * (1.0 - gate))


def norm_backward(upstream, normed, inv_scale):
    centered = (
        upstream
        - jnp.mean(upstream, axis=1, keepdims=True)
        - normed * jnp.mean(upstream * normed, axis=1, keepdims=True)
    )
    return (inv_scale * centered).astype(BF16)


def ask_kernel(dest_ref, remote_ref, ask_ref):
    domains, slots = ask_ref.shape
    dest_marks, rank = slot_ranks(to_column(dest_ref[...]).astype(jnp.int32), domains)
    rank_marks = jnp.where(rank == iota((rank.shape[0], slots), 1).astype(F32), 1.0, 0.0)
    wanted = (rank_marks * to_column(remote_ref[...])).astype(BF16)
    ask_ref[...] = dot_rows(dest_marks, wanted).astype(jnp.int32)


def reply_kernel(asked_ref, nodes_ref, reply_ref, asked_marks_ref):
    domains, slots = asked_ref.shape
    total = domains * slots
    shift = slots.bit_length() - 1
    spread = marks((iota((total, domains), 0) >> shift) == iota((total, domains), 1))
    listed = dot(spread, asked_ref[...].astype(F32).astype(BF16))
    at_slot = (iota((total, slots), 0) & (slots - 1)) == iota((total, slots), 1)
    column = jnp.sum(jnp.where(at_slot, listed, 0.0), axis=1, keepdims=True)
    node_rows = nodes_ref.shape[0]
    asked_marks = marks(column == iota((total, node_rows), 1).astype(F32))
    asked_marks_ref[...] = asked_marks
    reply_ref[...] = dot(asked_marks, nodes_ref[...]).astype(BF16)


def cut_marks_kernel(dest_ref, local_ref, senders_ref, receivers_ref, *, domains, slots):
    width = senders_ref.shape[1]
    base = width - domains * slots
    dest = to_column(dest_ref[...]).astype(jnp.int32)
    _, rank = slot_ranks(dest, domains)
    second = dest * slots + rank.astype(jnp.int32) + base
    first = to_column(local_ref[...]).astype(jnp.int32)
    senders, receivers = pair_marks(first, second, width)
    senders_ref[...] = senders
    receivers_ref[...] = receivers


def edge_forward(edge, sender, receiver, w_in_ref, w_out_ref):
    latent = edge.shape[1]
    pre_hidden = (
        dot(edge, w_in_ref[:latent])
        + dot(sender, w_in_ref[latent : 2 * latent])
        + dot(receiver, w_in_ref[2 * latent :])
    )
    hidden, slope = activate(pre_hidden)
    normed, inv_scale = normalise(dot(hidden, w_out_ref[...]))
    return hidden, slope, normed, inv_scale


def inner_forward_kernel(
    pairs_ref,
    edges_ref,
    nodes_ref,
    w_in_ref,
    w_out_ref,
    senders_ref,
    receivers_ref,
    sender_ref,
    receiver_ref,
    hidden_ref,
    slope_ref,
    normed_ref,
    scale_ref,
    total_ref,
):
    first, second = (to_column(pairs_ref[side : side + 1]).astype(jnp.int32) for side in range(2))
    senders, receivers = pair_marks(first, second, nodes_ref.shape[0])
    senders_ref[...] = senders
    receivers_ref[...] = receivers
    nodes = nodes_ref[...]
    sender = dot(senders, nodes).astype(BF16)
    receiver = dot(receivers, nodes).astype(BF16)
    sender_ref[...] = sender
    receiver_ref[...] = receiver
    hidden, slope, normed, inv_scale = edge_forward(
        edges_ref[...], sender, receiver, w_in_ref, w_out_ref
    )
    hidden_ref[...] = hidden
    slope_ref[...] = slope
    normed_ref[...] = normed
    scale_ref[...] = inv_scale
    part = dot_rows(receivers, normed.astype(BF16))

    @pl.when(pl.program_id(0) == 0)
    def _():
        total_ref[...] = part

    @pl.when(pl.program_id(0) > 0)
    def _():
        total_ref[...] += part


def cut_forward_kernel(
    senders_ref,
    receivers_ref,
    edges_ref,
    nodes_ref,
    far_ref,
    w_in_ref,
    w_out_ref,
    inner_total_ref,
    sender_ref,
    receiver_ref,
    hidden_ref,
    slope_ref,
    normed_ref,
    scale_ref,
    total_ref,
    outgoing_ref,
):
    base = nodes_ref.shape[0]
    nodes, far = nodes_ref[...], far_ref[...]

    def rows_of(marks_ref):
        return (dot(marks_ref[:, :base], nodes) + dot(marks_ref[:, base:], far)).astype(BF16)

    sender, receiver = rows_of(senders_ref), rows_of(receivers_ref)
    sender_ref[...] = sender
    receiver_ref[...] = receiver
    hidden, slope, normed, inv_scale = edge_forward(
        edges_ref[...], sender, receiver, w_in_ref, w_out_ref
    )
    hidden_ref[...] = hidden
    slope_ref[...] = slope
    normed_ref[...] = normed
    scale_ref[...] = inv_scale
    message = normed.astype(BF16)
    total_ref[...] = inner_total_ref[...] + dot_rows(receivers_ref[:, :base], message)
    outgoing_ref[...] = dot_rows(receivers_ref[:, base:], message).astype(BF16)


def new_edges_kernel(edges_ref, inner_ref, cut_ref, out_ref):
    inner_rows = inner_ref.shape[0]

    def added(edge, normed):
        return (edge.astype(F32) + normed.astype(BF16).astype(F32)).astype(BF16)

    out_ref[:inner_rows] = added(edges_ref[:inner_rows], inner_ref[...])
    out_ref[inner_rows:] = added(edges_ref[inner_rows:], cut_ref[...])


def node_kernel(
    incoming_ref,
    asked_marks_ref,
    total_ref,
    nodes_ref,
    ct_ref,
    w_in_ref,
    w_out_ref,
    new_nodes_ref,
    self_grad_ref,
    agg_grad_ref,
    reply_ref,
    aggregate_ref,
    hidden_ref,
    grad_out_ref,
    grad_pre_ref,
):
    latent = nodes_ref.shape[1]
    nodes, asked_marks = nodes_ref[...], asked_marks_ref[...]
    aggregate = (total_ref[...] + dot_rows(asked_marks, incoming_ref[...])).astype(BF16)
    aggregate_ref[...] = aggregate
    pre_hidden = dot(nodes, w_in_ref[:latent]) + dot(aggregate, w_in_ref[latent:])
    hidden, slope = activate(pre_hidden)
    hidden_ref[...] = hidden
    normed, inv_scale = normalise(dot(hidden, w_out_ref[...]))
    upstream = ct_ref[...].astype(F32)
    grad_out = norm_backward(upstream, normed, inv_scale)
    grad_out_ref[...] = grad_out
    grad_pre = (dot_cols(grad_out, w_out_ref[...]) * slope).astype(BF16)
    grad_pre_ref[...] = grad_pre
    agg_grad = dot_cols(grad_pre, w_in_ref[latent:]).astype(BF16)
    agg_grad_ref[...] = agg_grad
    reply_ref[...] = dot(asked_marks, agg_grad).astype(BF16)
    self_grad_ref[...] = upstream + dot_cols(grad_pre, w_in_ref[:latent])
    new_nodes_ref[...] = (nodes.astype(F32) + normed).astype(BF16)


def node_weights_kernel(
    me_ref, nodes_ref, aggregate_ref, hidden_ref, grad_out_ref, grad_pre_ref, keep_ref, send_ref
):
    latent = nodes_ref.shape[1]
    half = latent // 2

    def fill(low_ref, high_ref):
        grad_pre, grad_out = grad_pre_ref[...], grad_out_ref[...]
        low_ref[:latent] = dot_rows(nodes_ref[...], grad_pre).astype(BF16)
        low_ref[latent:] = dot_rows(aggregate_ref[:, :half], grad_pre).astype(BF16)
        high_ref[:half] = dot_rows(aggregate_ref[:, half:], grad_pre).astype(BF16)
        high_ref[half:] = dot_rows(hidden_ref[...], grad_out).astype(BF16)

    halves(me_ref, keep_ref, send_ref, fill)


def halves(me_ref, keep_ref, send_ref, fill):
    @pl.when((me_ref[0] & 1) == 0)
    def _():
        fill(keep_ref, send_ref)

    @pl.when((me_ref[0] & 1) != 0)
    def _():
        fill(send_ref, keep_ref)


def edge_backward(ct, target_grads, normed, inv_scale, slope, w_out):
    grad_out = norm_backward(ct.astype(F32) + target_grads, normed, inv_scale)
    return grad_out, (dot_cols(grad_out, w_out) * slope).astype(BF16)


def inner_backward_kernel(
    receivers_ref,
    agg_grad_ref,
    ct_ref,
    normed_ref,
    scale_ref,
    slope_ref,
    w_out_ref,
    grad_out_ref,
    grad_pre_ref,
):
    grad_out, grad_pre = edge_backward(
        ct_ref[...],
        dot(receivers_ref[...], agg_grad_ref[...]),
        normed_ref[...],
        scale_ref[...],
        slope_ref[...],
        w_out_ref[...],
    )
    grad_out_ref[...] = grad_out
    grad_pre_ref[...] = grad_pre


def cut_backward_kernel(
    receivers_ref,
    agg_grad_ref,
    far_grad_ref,
    ct_ref,
    normed_ref,
    scale_ref,
    slope_ref,
    w_out_ref,
    grad_out_ref,
    grad_pre_ref,
):
    base = agg_grad_ref.shape[0]
    target = dot(receivers_ref[:, :base], agg_grad_ref[...]) + dot(
        receivers_ref[:, base:], far_grad_ref[...]
    )
    grad_out, grad_pre = edge_backward(
        ct_ref[...], target, normed_ref[...], scale_ref[...], slope_ref[...], w_out_ref[...]
    )
    grad_out_ref[...] = grad_out
    grad_pre_ref[...] = grad_pre


def edge_weights_kernel(
    me_ref,
    edges_ref,
    inner_sender_ref,
    cut_sender_ref,
    inner_receiver_ref,
    cut_receiver_ref,
    inner_hidden_ref,
    cut_hidden_ref,
    inner_out_ref,
    cut_out_ref,
    inner_pre_ref,
    cut_pre_ref,
    out_ref,
    *,
    turned,
):
    latent = edges_ref.shape[1]
    inner_rows = inner_pre_ref.shape[0]

    @pl.when((me_ref[0] & 1) == turned)
    def _():
        inner_pre, cut_pre = inner_pre_ref[...], cut_pre_ref[...]
        out_ref[:latent] = (
            dot_rows(edges_ref[:inner_rows], inner_pre) + dot_rows(edges_ref[inner_rows:], cut_pre)
        ).astype(BF16)
        out_ref[latent:] = (
            dot_rows(inner_sender_ref[...], inner_pre) + dot_rows(cut_sender_ref[...], cut_pre)
        ).astype(BF16)

    @pl.when((me_ref[0] & 1) != turned)
    def _():
        out_ref[:latent] = (
            dot_rows(inner_receiver_ref[...], inner_pre_ref[...])
            + dot_rows(cut_receiver_ref[...], cut_pre_ref[...])
        ).astype(BF16)
        out_ref[latent:] = (
            dot_rows(inner_hidden_ref[...], inner_out_ref[...])
            + dot_rows(cut_hidden_ref[...], cut_out_ref[...])
        ).astype(BF16)


def input_grads_kernel(
    inner_senders_ref,
    inner_receivers_ref,
    cut_senders_ref,
    cut_receivers_ref,
    inner_pre_ref,
    cut_pre_ref,
    w_in_ref,
    local_ref,
    outgoing_ref,
):
    latent = inner_pre_ref.shape[1]
    base = inner_senders_ref.shape[1]
    inner_pre, cut_pre = inner_pre_ref[...], cut_pre_ref[...]
    w_sender, w_receiver = w_in_ref[latent : 2 * latent], w_in_ref[2 * latent :]

    def summed(inner_marks_ref, cut_marks_ref):
        return (
            dot_rows(inner_marks_ref[...], inner_pre) + dot_rows(cut_marks_ref[:, :base], cut_pre)
        ).astype(BF16)

    outgoing_ref[...] = (
        dot_cols(dot_rows(cut_senders_ref[:, base:], cut_pre).astype(BF16), w_sender)
        + dot_cols(dot_rows(cut_receivers_ref[:, base:], cut_pre).astype(BF16), w_receiver)
    ).astype(BF16)
    local_ref[...] = dot_cols(summed(inner_senders_ref, cut_senders_ref), w_sender) + dot_cols(
        summed(inner_receivers_ref, cut_receivers_ref), w_receiver
    )


def edge_grads_kernel(ct_ref, inner_pre_ref, cut_pre_ref, w_edge_ref, out_ref, *, blocks):
    inside = pl.program_id(0) < blocks

    @pl.when(inside)
    def _():
        out_ref[...] = ct_ref[...].astype(F32) + dot_cols(inner_pre_ref[...], w_edge_ref[...])

    @pl.when(jnp.logical_not(inside))
    def _():
        out_ref[...] = ct_ref[...].astype(F32) + dot_cols(cut_pre_ref[...], w_edge_ref[...])


def node_grads_kernel(self_ref, local_ref, asked_marks_ref, returned_ref, out_ref):
    out_ref[...] = (
        self_ref[...] + local_ref[...] + dot_rows(asked_marks_ref[...], returned_ref[...])
    )


VMEM = pl.BlockSpec(memory_space=pltpu.VMEM)
SMEM = pl.BlockSpec(memory_space=pltpu.SMEM)
ANY = pl.BlockSpec(memory_space=pl.ANY)


def shaped(dtype, *shape):
    return jax.ShapeDtypeStruct(shape, dtype)


class Line:
    def __init__(self):
        self.last = None

    def run(self, body, outs, ins, flops, specs=None, out_specs=None, grid=None):
        single = not isinstance(outs, (list, tuple))
        out_shape = [outs] if single else list(outs)
        specs = [VMEM] * len(ins) if specs is None else list(specs)
        count, extra = len(ins), {} if grid is None else {"grid": grid}
        ins = list(ins)
        if self.last is not None:
            ins.append(self.last)
            specs.append(ANY)

        def ordered(*refs):
            return body(*refs[:count], *refs[len(ins) :])

        result = pl.pallas_call(
            ordered,
            out_shape=out_shape,
            in_specs=specs,
            out_specs=[VMEM] * len(out_shape) if out_specs is None else out_specs,
            compiler_params=pltpu.CompilerParams(vmem_limit_bytes=VMEM_LIMIT),
            cost_estimate=pl.CostEstimate(flops=1, bytes_accessed=1, transcendentals=0),
            **extra,
        )(*ins)
        self.last = result[-1]
        return result[0] if single else result


def bit_groups(devices):
    bits = devices.bit_length() - 1
    groups = [(low, 1) for low in range(min(2, bits))]
    low = 2
    while low < bits:
        groups.append((low, min(2, bits - low)))
        low += 2
    return groups


def across(rows, devices, mask):
    return lax.ppermute(rows, "dom", [(device, device ^ mask) for device in range(devices)])


def fence(*values):
    return lax.optimization_barrier(values)


def place_of(low, size):
    return (lax.axis_index("dom") >> low) & (size - 1)


def pieces_of(rows, low, width):
    size = 1 << width
    place = place_of(low, size)
    pieces = rows.reshape(size, rows.shape[0] // size, rows.shape[1])
    return [lax.dynamic_index_in_dim(pieces, place ^ turn, 0, False) for turn in range(size)]


def traded(pieces, devices, low):
    return pieces[:1] + [
        across(piece, devices, turn << low) for turn, piece in enumerate(pieces) if turn
    ]


def handed(rows, devices, low, width):
    return traded([rows] * (1 << width), devices, low)


def added(*parts):
    return sum(part.astype(F32) for part in parts).astype(BF16)


def joined(parts, low):
    size = len(parts)
    place = place_of(low, size)
    if size == 2:
        orders = [jnp.concatenate(parts), jnp.concatenate(parts[::-1])]
        return jnp.where(place == 0, *orders)
    whole = jnp.zeros((size,) + parts[0].shape, parts[0].dtype)
    for turn, part in enumerate(parts):
        whole = lax.dynamic_update_index_in_dim(whole, part, place ^ turn, 0)
    return whole.reshape(size * parts[0].shape[0], parts[0].shape[1])


def line_groups(devices, low, width):
    size, mask = 1 << width, ((1 << width) - 1) << low
    bases = [device for device in range(devices) if device & mask == 0]
    return [[base + (turn << low) for turn in range(size)] for base in bases]


def line_trade(rows, devices, low, width):
    groups = line_groups(devices, low, width)
    size = 1 << width
    pieces = rows.reshape(size, rows.shape[0] // size, rows.shape[1])
    return lax.all_to_all(
        pieces, "dom", split_axis=0, concat_axis=0, axis_index_groups=groups, tiled=True
    )


def line_sum(parts):
    return jnp.sum(parts.astype(F32), axis=0).astype(BF16)


def line_share(rows, devices, low, width):
    copies = jnp.broadcast_to(rows[None], (1 << width,) + rows.shape)
    return line_trade(copies.reshape(-1, rows.shape[1]), devices, low, width)


def merged(parts):
    return parts.reshape(-1, parts.shape[-1])


def exchange(rows, domains):
    shape = rows.shape
    split = rows.reshape((domains, shape[0] // domains) + shape[1:])
    return lax.all_to_all(split, "dom", split_axis=0, concat_axis=0, tiled=True).reshape(shape)


def shards(
    nodes,
    edges,
    inner_pairs,
    cut_local,
    cut_dest,
    cut_remote,
    w_edge_in,
    w_edge_out,
    w_node_in,
    w_node_out,
    ct_nodes,
    ct_edges,
):
    domains = lax.axis_size("dom")
    node_rows, latent = nodes.shape
    inner_count, cut_count = inner_pairs.shape[0], cut_local.shape[0]
    inner_rows, cut_rows = 2 * inner_count, 2 * cut_count
    slots = max(2, 2 * cut_count // domains)
    total_slots = domains * slots
    table = node_rows + total_slots
    square = 2 * latent * latent
    me = lax.axis_index("dom").reshape(1)
    line = Line()

    ask = line.run(
        ask_kernel, shaped(jnp.int32, domains, slots), [cut_dest.reshape(1, -1), cut_remote.reshape(1, -1)], 10**7
    )
    asked = lax.all_to_all(ask, "dom", split_axis=0, concat_axis=0, tiled=True)
    cut_senders, cut_receivers = line.run(
        functools.partial(cut_marks_kernel, domains=domains, slots=slots),
        [shaped(BF16, cut_rows, table)] * 2,
        [cut_dest.reshape(1, -1), cut_local.reshape(1, -1)],
        10**8,
    )
    reply, asked_marks = line.run(
        reply_kernel,
        [shaped(BF16, total_slots, latent), shaped(BF16, total_slots, node_rows)],
        [asked, nodes],
        10**8,
    )
    far = exchange(reply, domains)

    block = cut_rows
    blocks = inner_rows // block

    def rows_spec(width, rows=block):
        return pl.BlockSpec((rows, width), lambda step: (step, 0))

    def all_spec(array):
        return pl.BlockSpec(array.shape, lambda step: (0, 0))

    saved_widths = [node_rows, node_rows, latent, latent, latent, latent, latent, 1]
    saved_types = [BF16, BF16, BF16, BF16, BF16, F32, F32, F32]
    (
        inner_senders,
        inner_receivers,
        inner_sender,
        inner_receiver,
        inner_hidden,
        inner_slope,
        inner_normed,
        inner_scale,
        inner_total,
    ) = line.run(
        inner_forward_kernel,
        [shaped(kind, inner_rows, width) for kind, width in zip(saved_types, saved_widths)]
        + [shaped(F32, node_rows, latent)],
        [inner_pairs.T, edges, nodes, w_edge_in, w_edge_out],
        inner_rows * 4 * square,
        [
            pl.BlockSpec((2, block // 2), lambda step: (0, step)),
            rows_spec(latent),
            all_spec(nodes),
            all_spec(w_edge_in),
            all_spec(w_edge_out),
        ],
        [rows_spec(width) for width in saved_widths] + [all_spec(nodes)],
        (blocks,),
    )

    def last_rows(array):
        last = array.shape[0] // block - 1
        return pl.BlockSpec((block, array.shape[1]), lambda step: (last, 0))

    (
        cut_sender,
        cut_receiver,
        cut_hidden,
        cut_slope,
        cut_normed,
        cut_scale,
        total,
        outgoing,
    ) = line.run(
        cut_forward_kernel,
        [shaped(kind, cut_rows, width) for kind, width in zip(saved_types, saved_widths)][2:]
        + [shaped(F32, node_rows, latent), shaped(BF16, total_slots, latent)],
        [
            cut_senders,
            cut_receivers,
            edges,
            nodes,
            far,
            w_edge_in,
            w_edge_out,
            inner_total,
        ],
        cut_rows * 4 * square,
        [
            all_spec(cut_senders),
            all_spec(cut_receivers),
            last_rows(edges),
            all_spec(nodes),
            all_spec(far),
            all_spec(w_edge_in),
            all_spec(w_edge_out),
            all_spec(inner_total),
        ],
        [rows_spec(width) for width in saved_widths[2:]]
        + [all_spec(nodes), rows_spec(latent, total_slots)],
        (1,),
    )
    incoming = exchange(outgoing, domains)
    new_edges = line.run(
        new_edges_kernel,
        shaped(BF16, *edges.shape),
        [edges, inner_normed, cut_normed],
        10**7,
    )
    (
        new_nodes,
        self_grad,
        agg_grad,
        grad_reply,
        aggregate,
        node_hidden,
        node_out,
        node_pre,
    ) = line.run(
        node_kernel,
        [
            shaped(BF16, node_rows, latent),
            shaped(F32, node_rows, latent),
            shaped(BF16, node_rows, latent),
            shaped(BF16, total_slots, latent),
        ]
        + [shaped(BF16, node_rows, latent)] * 4,
        [incoming, asked_marks, total, nodes, ct_nodes, w_node_in, w_node_out],
        node_rows * 6 * square,
    )
    far_grad = exchange(grad_reply, domains)
    node_keep, node_send = line.run(
        node_weights_kernel,
        [shaped(BF16, 3 * latent // 2, latent)] * 2,
        [me, nodes, aggregate, node_hidden, node_out, node_pre],
        node_rows * 3 * square,
        [SMEM] + [VMEM] * 5,
    )
    node_sum = added(node_keep, across(node_send, domains, 1))
    inner_out, inner_pre = line.run(
        inner_backward_kernel,
        [shaped(BF16, inner_rows, latent)] * 2,
        [
            inner_receivers,
            agg_grad,
            ct_edges,
            inner_normed,
            inner_scale,
            inner_slope,
            w_edge_out,
        ],
        inner_rows * square,
        [
            rows_spec(node_rows),
            all_spec(agg_grad),
            rows_spec(latent),
            rows_spec(latent),
            rows_spec(1),
            rows_spec(latent),
            all_spec(w_edge_out),
        ],
        [rows_spec(latent)] * 2,
        (blocks,),
    )
    groups = bit_groups(domains)
    bit_one, bits_two = groups[1], groups[2]
    node_parts = traded(pieces_of(node_sum, *bit_one), domains, bit_one[0])
    far_grad, node_sum, inner_pre = fence(far_grad, node_sum, inner_pre)
    cut_out, cut_pre = line.run(
        cut_backward_kernel,
        [shaped(BF16, cut_rows, latent)] * 2,
        [
            cut_receivers,
            agg_grad,
            far_grad,
            ct_edges,
            cut_normed,
            cut_scale,
            cut_slope,
            w_edge_out,
        ],
        cut_rows * square,
        [
            all_spec(cut_receivers),
            all_spec(agg_grad),
            all_spec(far_grad),
            last_rows(ct_edges),
            all_spec(cut_normed),
            all_spec(cut_scale),
            all_spec(cut_slope),
            all_spec(w_edge_out),
        ],
        [rows_spec(latent)] * 2,
        (1,),
    )
    factors = [
        edges,
        inner_sender,
        cut_sender,
        inner_receiver,
        cut_receiver,
        inner_hidden,
        cut_hidden,
        inner_out,
        cut_out,
        inner_pre,
        cut_pre,
    ]

    def edge_weights(turned, place):
        return line.run(
            functools.partial(edge_weights_kernel, turned=turned),
            shaped(BF16, 2 * latent, latent),
            [place] + factors,
            (inner_rows + cut_rows) * 2 * square,
            [SMEM] + [VMEM] * len(factors),
        )

    edge_send, place, *node_parts = fence(edge_weights(1, me), me, *node_parts)
    edge_parts = [edge_weights(0, place), across(edge_send, domains, 1)]
    node_parts = line_trade(added(*node_parts), domains, *bits_two)
    *edge_parts, node_parts, inner_pre, cut_pre = fence(
        *edge_parts, node_parts, inner_pre, cut_pre
    )
    node_sum = line_sum(node_parts)
    for low, width in groups[3:]:
        node_sum = line_sum(line_trade(node_sum, domains, low, width))
    for low, width in groups[:2:-1]:
        node_sum = merged(line_share(node_sum, domains, low, width))
    edge_parts = traded(pieces_of(added(*edge_parts), *bit_one), domains, bit_one[0])
    node_parts = line_share(node_sum, domains, *bits_two)
    local_grad, outgoing_grad = line.run(
        input_grads_kernel,
        [shaped(F32, node_rows, latent), shaped(BF16, total_slots, latent)],
        [
            inner_senders,
            inner_receivers,
            cut_senders,
            cut_receivers,
            inner_pre,
            cut_pre,
            w_edge_in,
        ],
        (node_rows + total_slots) * 2 * square,
    )
    fenced = fence(*edge_parts, node_parts, inner_pre, cut_pre, local_grad)
    edge_parts, node_sum, inner_pre, cut_pre, local_grad = (fenced[:2], *fenced[2:])
    node_sum = merged(node_sum)
    edge_parts = line_trade(added(*edge_parts), domains, *bits_two)
    node_parts = handed(node_sum, domains, *bit_one)
    grad_edges = line.run(
        functools.partial(edge_grads_kernel, blocks=blocks),
        shaped(F32, *edges.shape),
        [ct_edges, inner_pre, cut_pre, w_edge_in],
        (inner_rows + cut_rows) * square,
        [
            rows_spec(latent),
            pl.BlockSpec((block, latent), lambda step: (jnp.minimum(step, blocks - 1), 0)),
            all_spec(cut_pre),
            pl.BlockSpec((latent, latent), lambda step: (0, 0)),
        ],
        [rows_spec(latent)],
        (blocks + 1,),
    )
    edge_parts, *node_parts, grad_edges = fence(edge_parts, *node_parts, grad_edges)
    edge_sum, node_sum = line_sum(edge_parts), joined(node_parts, bit_one[0])
    for low, width in groups[3:]:
        edge_sum = line_sum(line_trade(edge_sum, domains, low, width))
    for low, width in groups[:2:-1]:
        edge_sum = merged(line_share(edge_sum, domains, low, width))
    edge_parts = line_share(edge_sum, domains, *bits_two)
    others = across(node_sum, domains, 1)
    edge_parts, node_sum, others, outgoing_grad = fence(
        edge_parts, node_sum, others, outgoing_grad
    )
    edge_sum = merged(edge_parts)
    edge_parts = handed(edge_sum, domains, *bit_one) + [across(edge_sum, domains, 1)]
    returned = exchange(outgoing_grad, domains)
    lower, left = place_of(0, 2) == 0, place_of(bit_one[0], 2) == 0
    low_rows, high_rows = jnp.where(lower, node_sum, others), jnp.where(lower, others, node_sum)
    split = 2 * latent - low_rows.shape[0]
    grad_node_in = jnp.concatenate([low_rows, high_rows[:split]])
    grad_node_out = high_rows[split:]
    mine, far, near, grad_node_in, grad_node_out, returned = fence(
        *edge_parts, grad_node_in, grad_node_out, returned
    )
    corner = across(far, domains, 1)
    grad_nodes = line.run(
        node_grads_kernel,
        shaped(F32, node_rows, latent),
        [self_grad, local_grad, asked_marks, returned],
        10**8,
    )
    own, other = [mine, far], [near, corner]
    low_half = [jnp.where(lower, one, two) for one, two in zip(own, other)]
    high_half = [jnp.where(lower, two, one) for one, two in zip(own, other)]
    grad_edge_in = jnp.concatenate(
        [
            jnp.where(left, low_half[0], low_half[1]),
            jnp.where(left, low_half[1], low_half[0]),
            jnp.where(left, high_half[0], high_half[1]),
        ]
    )
    grad_edge_out = jnp.where(left, high_half[1], high_half[0])
    return (
        new_nodes,
        new_edges,
        grad_nodes,
        grad_edges,
        grad_edge_in,
        grad_edge_out,
        grad_node_in,
        grad_node_out,
    )


def solution(mesh):
    placed = (
        P(("groups", "dom"), None),
        P(("groups", "dom"), None),
        P(("groups", "dom"), None),
        P(("groups", "dom")),
        P(("groups", "dom"), None),
        P(("groups", "dom")),
        P(),
        P(),
        P(),
        P(),
        P(("groups", "dom"), None),
        P(("groups", "dom"), None),
    )
    return jax.shard_map(
        shards,
        mesh=mesh,
        in_specs=placed,
        out_specs=(
            P(("groups", "dom"), None),
            P(("groups", "dom"), None),
            P(("groups", "dom"), None),
            P(("groups", "dom"), None),
            P("groups", None),
            P("groups", None),
            P("groups", None),
            P("groups", None),
        ),
        check_vma=False,
    )
```

```python
import functools

import jax
import jax.numpy as jnp
from jax import lax
from jax.experimental import pallas as pl
from jax.experimental.pallas import tpu as pltpu
from jax.sharding import PartitionSpec as P

BF16 = jnp.bfloat16
F32 = jnp.float32
VMEM_LIMIT = 60 * 1024 * 1024


def dot(left, right):
    return jnp.dot(left, right, preferred_element_type=F32)


def dot_rows(left, right):
    return lax.dot_general(left, right, (((0,), (0,)), ((), ())), preferred_element_type=F32)


def dot_cols(left, right):
    return lax.dot_general(left, right, (((1,), (1,)), ((), ())), preferred_element_type=F32)


def iota(shape, axis):
    return lax.broadcasted_iota(jnp.int32, shape, axis)


def marks(mask):
    return jnp.where(mask, 1.0, 0.0).astype(BF16)


def onehot(column, width):
    return marks(column == iota((column.shape[0], width), 1))


def to_column(row):
    count = row.shape[1]
    square = (count, count)
    kept = jnp.where(iota(square, 0) == iota(square, 1), row.astype(F32), 0.0)
    return jnp.sum(kept, axis=1, keepdims=True)


def slot_ranks(dest, domains):
    count = dest.shape[0]
    square = (count, count)
    dest_marks = onehot(dest, domains)
    before = dot(marks(iota(square, 0) > iota(square, 1)), dest_marks)
    return dest_marks, jnp.sum(before * dest_marks.astype(F32), axis=1, keepdims=True)


def pair_marks(first, second, width):
    pairs = first.shape[0]
    shape = (2 * pairs, pairs)
    edge, pair = iota(shape, 0), iota(shape, 1)
    mine = (edge >> 1) == pair
    even = marks(mine & ((edge & 1) == 0))
    odd = marks(mine & ((edge & 1) == 1))
    first_marks, second_marks = onehot(first, width), onehot(second, width)
    senders = dot(even, first_marks) + dot(odd, second_marks)
    receivers = dot(even, second_marks) + dot(odd, first_marks)
    return senders.astype(BF16), receivers.astype(BF16)


def normalise(values):
    centered = values - jnp.mean(values, axis=1, keepdims=True)
    inv_scale = lax.rsqrt(jnp.mean(centered * centered, axis=1, keepdims=True) + 1e-05)
    return centered * inv_scale, inv_scale


def activate(pre_hidden):
    gate = jax.nn.sigmoid(pre_hidden)
    return (pre_hidden * gate).astype(BF16), gate * (1.0 + pre_hidden * (1.0 - gate))


def norm_backward(upstream, normed, inv_scale):
    centered = (
        upstream
        - jnp.mean(upstream, axis=1, keepdims=True)
        - normed * jnp.mean(upstream * normed, axis=1, keepdims=True)
    )
    return (inv_scale * centered).astype(BF16)


def ask_kernel(dest_ref, remote_ref, ask_ref):
    domains, slots = ask_ref.shape
    dest_marks, rank = slot_ranks(to_column(dest_ref[...]).astype(jnp.int32), domains)
    rank_marks = jnp.where(rank == iota((rank.shape[0], slots), 1).astype(F32), 1.0, 0.0)
    wanted = (rank_marks * to_column(remote_ref[...])).astype(BF16)
    ask_ref[...] = dot_rows(dest_marks, wanted).astype(jnp.int32)


def reply_kernel(asked_ref, nodes_ref, reply_ref, asked_marks_ref):
    domains, slots = asked_ref.shape
    total = domains * slots
    shift = slots.bit_length() - 1
    spread = marks((iota((total, domains), 0) >> shift) == iota((total, domains), 1))
    listed = dot(spread, asked_ref[...].astype(F32).astype(BF16))
    at_slot = (iota((total, slots), 0) & (slots - 1)) == iota((total, slots), 1)
    column = jnp.sum(jnp.where(at_slot, listed, 0.0), axis=1, keepdims=True)
    node_rows = nodes_ref.shape[0]
    asked_marks = marks(column == iota((total, node_rows), 1).astype(F32))
    asked_marks_ref[...] = asked_marks
    reply_ref[...] = dot(asked_marks, nodes_ref[...]).astype(BF16)


def cut_marks_kernel(dest_ref, local_ref, senders_ref, receivers_ref, *, domains, slots):
    width = senders_ref.shape[1]
    base = width - domains * slots
    dest = to_column(dest_ref[...]).astype(jnp.int32)
    _, rank = slot_ranks(dest, domains)
    second = dest * slots + rank.astype(jnp.int32) + base
    first = to_column(local_ref[...]).astype(jnp.int32)
    senders, receivers = pair_marks(first, second, width)
    senders_ref[...] = senders
    receivers_ref[...] = receivers


def edge_forward(edge, sender, receiver, w_in_ref, w_out_ref):
    latent = edge.shape[1]
    pre_hidden = (
        dot(edge, w_in_ref[:latent])
        + dot(sender, w_in_ref[latent : 2 * latent])
        + dot(receiver, w_in_ref[2 * latent :])
    )
    hidden, slope = activate(pre_hidden)
    normed, inv_scale = normalise(dot(hidden, w_out_ref[...]))
    return hidden, slope, normed, inv_scale


def inner_forward_kernel(
    pairs_ref,
    edges_ref,
    nodes_ref,
    w_in_ref,
    w_out_ref,
    senders_ref,
    receivers_ref,
    sender_ref,
    receiver_ref,
    hidden_ref,
    slope_ref,
    normed_ref,
    scale_ref,
    total_ref,
):
    first, second = (to_column(pairs_ref[side : side + 1]).astype(jnp.int32) for side in range(2))
    senders, receivers = pair_marks(first, second, nodes_ref.shape[0])
    senders_ref[...] = senders
    receivers_ref[...] = receivers
    nodes = nodes_ref[...]
    sender = dot(senders, nodes).astype(BF16)
    receiver = dot(receivers, nodes).astype(BF16)
    sender_ref[...] = sender
    receiver_ref[...] = receiver
    hidden, slope, normed, inv_scale = edge_forward(
        edges_ref[...], sender, receiver, w_in_ref, w_out_ref
    )
    hidden_ref[...] = hidden
    slope_ref[...] = slope
    normed_ref[...] = normed
    scale_ref[...] = inv_scale
    part = dot_rows(receivers, normed.astype(BF16))

    @pl.when(pl.program_id(0) == 0)
    def _():
        total_ref[...] = part

    @pl.when(pl.program_id(0) > 0)
    def _():
        total_ref[...] += part


def cut_forward_kernel(
    senders_ref,
    receivers_ref,
    edges_ref,
    nodes_ref,
    far_ref,
    w_in_ref,
    w_out_ref,
    inner_total_ref,
    sender_ref,
    receiver_ref,
    hidden_ref,
    slope_ref,
    normed_ref,
    scale_ref,
    total_ref,
    outgoing_ref,
):
    base = nodes_ref.shape[0]
    nodes, far = nodes_ref[...], far_ref[...]

    def rows_of(marks_ref):
        return (dot(marks_ref[:, :base], nodes) + dot(marks_ref[:, base:], far)).astype(BF16)

    sender, receiver = rows_of(senders_ref), rows_of(receivers_ref)
    sender_ref[...] = sender
    receiver_ref[...] = receiver
    hidden, slope, normed, inv_scale = edge_forward(
        edges_ref[...], sender, receiver, w_in_ref, w_out_ref
    )
    hidden_ref[...] = hidden
    slope_ref[...] = slope
    normed_ref[...] = normed
    scale_ref[...] = inv_scale
    message = normed.astype(BF16)
    total_ref[...] = inner_total_ref[...] + dot_rows(receivers_ref[:, :base], message)
    outgoing_ref[...] = dot_rows(receivers_ref[:, base:], message).astype(BF16)


def new_edges_kernel(edges_ref, inner_ref, cut_ref, out_ref):
    inner_rows = inner_ref.shape[0]

    def added(edge, normed):
        return (edge.astype(F32) + normed.astype(BF16).astype(F32)).astype(BF16)

    out_ref[:inner_rows] = added(edges_ref[:inner_rows], inner_ref[...])
    out_ref[inner_rows:] = added(edges_ref[inner_rows:], cut_ref[...])


def node_kernel(
    me_ref,
    incoming_ref,
    asked_marks_ref,
    total_ref,
    nodes_ref,
    ct_ref,
    w_in_ref,
    w_out_ref,
    new_nodes_ref,
    self_grad_ref,
    agg_grad_ref,
    reply_ref,
    keep_ref,
    send_ref,
):
    latent = nodes_ref.shape[1]
    half = latent // 2
    nodes, asked_marks = nodes_ref[...], asked_marks_ref[...]
    aggregate = (total_ref[...] + dot_rows(asked_marks, incoming_ref[...])).astype(BF16)
    pre_hidden = dot(nodes, w_in_ref[:latent]) + dot(aggregate, w_in_ref[latent:])
    hidden, slope = activate(pre_hidden)
    normed, inv_scale = normalise(dot(hidden, w_out_ref[...]))
    upstream = ct_ref[...].astype(F32)
    grad_out = norm_backward(upstream, normed, inv_scale)
    grad_pre = (dot_cols(grad_out, w_out_ref[...]) * slope).astype(BF16)
    agg_grad = dot_cols(grad_pre, w_in_ref[latent:]).astype(BF16)
    agg_grad_ref[...] = agg_grad
    reply_ref[...] = dot(asked_marks, agg_grad).astype(BF16)
    self_grad_ref[...] = upstream + dot_cols(grad_pre, w_in_ref[:latent])
    new_nodes_ref[...] = (nodes.astype(F32) + normed).astype(BF16)

    def fill(low_ref, high_ref):
        by_aggregate = dot_rows(aggregate, grad_pre).astype(BF16)
        low_ref[:latent] = dot_rows(nodes, grad_pre).astype(BF16)
        low_ref[latent:] = by_aggregate[:half]
        high_ref[:half] = by_aggregate[half:]
        high_ref[half:] = dot_rows(hidden, grad_out).astype(BF16)

    @pl.when((me_ref[0] & 1) == 0)
    def _():
        fill(keep_ref, send_ref)

    @pl.when((me_ref[0] & 1) != 0)
    def _():
        fill(send_ref, keep_ref)


def edge_backward(ct, target_grads, normed, inv_scale, slope, w_out):
    grad_out = norm_backward(ct.astype(F32) + target_grads, normed, inv_scale)
    return grad_out, (dot_cols(grad_out, w_out) * slope).astype(BF16)


def inner_backward_kernel(
    receivers_ref,
    agg_grad_ref,
    ct_ref,
    normed_ref,
    scale_ref,
    slope_ref,
    w_out_ref,
    grad_out_ref,
    grad_pre_ref,
):
    grad_out, grad_pre = edge_backward(
        ct_ref[...],
        dot(receivers_ref[...], agg_grad_ref[...]),
        normed_ref[...],
        scale_ref[...],
        slope_ref[...],
        w_out_ref[...],
    )
    grad_out_ref[...] = grad_out
    grad_pre_ref[...] = grad_pre


def fetch_factors(half, sources, buffers, sems, wait):
    edges, inner_sender, cut_sender, inner_receiver, cut_receiver = sources[:5]
    inner_hidden, cut_hidden, inner_out, inner_pre = sources[5:]
    inner_rows, cut_rows = inner_pre.shape[0], cut_sender.shape[0]
    inner_edges = edges.at[pl.ds(0, inner_rows)]
    cut_edges = edges.at[pl.ds(inner_rows, cut_rows)]
    low = [inner_edges, cut_edges, inner_sender, cut_sender, inner_pre, inner_pre]
    high = [inner_receiver, cut_receiver, inner_hidden, cut_hidden, inner_pre, inner_out]

    def each(parts):
        for index, (source, buffer) in enumerate(zip(parts, buffers)):
            copy = pltpu.make_async_copy(source, buffer, sems.at[index])
            if wait:
                copy.wait()
            else:
                copy.start()

    @pl.when(half == 0)
    def _():
        each(low)

    @pl.when(half != 0)
    def _():
        each(high)


def edge_rows(half, buffers, cut_pre, cut_out, out_ref):
    latent = cut_pre.shape[1]
    first, first_cut, second, second_cut, first_right, second_right = buffers
    chosen = jnp.where(half == 0, cut_pre.astype(F32), cut_out.astype(F32)).astype(BF16)
    out_ref[:latent] = (
        dot_rows(first[...], first_right[...]) + dot_rows(first_cut[...], cut_pre)
    ).astype(BF16)
    out_ref[latent:] = (
        dot_rows(second[...], second_right[...]) + dot_rows(second_cut[...], chosen)
    ).astype(BF16)


def cut_backward_kernel(
    me_ref,
    receivers_ref,
    agg_grad_ref,
    far_grad_ref,
    ct_ref,
    normed_ref,
    scale_ref,
    slope_ref,
    w_out_ref,
    *refs,
):
    sources, (grad_out_ref, grad_pre_ref, out_ref), rest = refs[:9], refs[9:12], refs[12:]
    buffers, sems = rest[:-1], rest[-1]
    half = 1 - (me_ref[0] & 1)
    fetch_factors(half, sources, buffers, sems, False)
    base = agg_grad_ref.shape[0]
    target = dot(receivers_ref[:, :base], agg_grad_ref[...]) + dot(
        receivers_ref[:, base:], far_grad_ref[...]
    )
    grad_out, grad_pre = edge_backward(
        ct_ref[...], target, normed_ref[...], scale_ref[...], slope_ref[...], w_out_ref[...]
    )
    grad_out_ref[...] = grad_out
    grad_pre_ref[...] = grad_pre
    fetch_factors(half, sources, buffers, sems, True)
    edge_rows(half, buffers, grad_pre, grad_out, out_ref)


def edge_weights_kernel(me_ref, cut_out_ref, cut_pre_ref, *refs):
    sources, out_ref, rest = refs[:9], refs[9], refs[10:]
    buffers, sems = rest[:-1], rest[-1]
    half = me_ref[0] & 1
    fetch_factors(half, sources, buffers, sems, False)
    fetch_factors(half, sources, buffers, sems, True)
    edge_rows(half, buffers, cut_pre_ref[...], cut_out_ref[...], out_ref)


def input_grads_kernel(
    inner_senders_ref,
    inner_receivers_ref,
    cut_senders_ref,
    cut_receivers_ref,
    inner_pre_ref,
    cut_pre_ref,
    w_in_ref,
    local_ref,
    outgoing_ref,
):
    latent = inner_pre_ref.shape[1]
    base = inner_senders_ref.shape[1]
    inner_pre, cut_pre = inner_pre_ref[...], cut_pre_ref[...]
    w_sender, w_receiver = w_in_ref[latent : 2 * latent], w_in_ref[2 * latent :]

    def summed(inner_marks_ref, cut_marks_ref):
        return (
            dot_rows(inner_marks_ref[...], inner_pre) + dot_rows(cut_marks_ref[:, :base], cut_pre)
        ).astype(BF16)

    outgoing_ref[...] = (
        dot_cols(dot_rows(cut_senders_ref[:, base:], cut_pre).astype(BF16), w_sender)
        + dot_cols(dot_rows(cut_receivers_ref[:, base:], cut_pre).astype(BF16), w_receiver)
    ).astype(BF16)
    local_ref[...] = dot_cols(summed(inner_senders_ref, cut_senders_ref), w_sender) + dot_cols(
        summed(inner_receivers_ref, cut_receivers_ref), w_receiver
    )


def edge_grads_kernel(ct_ref, inner_pre_ref, cut_pre_ref, w_edge_ref, out_ref, *, blocks):
    inside = pl.program_id(0) < blocks

    @pl.when(inside)
    def _():
        out_ref[...] = ct_ref[...].astype(F32) + dot_cols(inner_pre_ref[...], w_edge_ref[...])

    @pl.when(jnp.logical_not(inside))
    def _():
        out_ref[...] = ct_ref[...].astype(F32) + dot_cols(cut_pre_ref[...], w_edge_ref[...])


def node_grads_kernel(self_ref, local_ref, asked_marks_ref, returned_ref, out_ref):
    out_ref[...] = (
        self_ref[...] + local_ref[...] + dot_rows(asked_marks_ref[...], returned_ref[...])
    )


VMEM = pl.BlockSpec(memory_space=pltpu.VMEM)
SMEM = pl.BlockSpec(memory_space=pltpu.SMEM)
ANY = pl.BlockSpec(memory_space=pl.ANY)


def shaped(dtype, *shape):
    return jax.ShapeDtypeStruct(shape, dtype)


class Line:
    def __init__(self):
        self.last = None

    def run(self, body, outs, ins, specs=None, out_specs=None, grid=None, scratch=()):
        single = not isinstance(outs, (list, tuple))
        out_shape = [outs] if single else list(outs)
        specs = [VMEM] * len(ins) if specs is None else list(specs)
        count, extra = len(ins), {} if grid is None else {"grid": grid}
        ins = list(ins)
        if self.last is not None:
            ins.append(self.last)
            specs.append(ANY)

        def ordered(*refs):
            return body(*refs[:count], *refs[len(ins) :])

        result = pl.pallas_call(
            ordered,
            out_shape=out_shape,
            in_specs=specs,
            out_specs=[VMEM] * len(out_shape) if out_specs is None else out_specs,
            scratch_shapes=scratch,
            compiler_params=pltpu.CompilerParams(vmem_limit_bytes=VMEM_LIMIT),
            cost_estimate=pl.CostEstimate(flops=1, bytes_accessed=1, transcendentals=0),
            **extra,
        )(*ins)
        self.last = result[-1]
        return result[0] if single else result


def index_bits(devices):
    return list(range(devices.bit_length() - 1))


def across(rows, devices, mask):
    return lax.ppermute(rows, "dom", [(device, device ^ mask) for device in range(devices)])


def fence(*values):
    return lax.optimization_barrier(values)


def place_of(bit):
    return (lax.axis_index("dom") >> bit) & 1


def traded(rows, devices, bit):
    place = place_of(bit)
    halves = rows.reshape(2, rows.shape[0] // 2, rows.shape[1])
    own = lax.dynamic_index_in_dim(halves, place, 0, False)
    sent = lax.dynamic_index_in_dim(halves, 1 - place, 0, False)
    return own, across(sent, devices, 1 << bit)


def handed(rows, devices, bit):
    return [rows, across(rows, devices, 1 << bit)]


def added(left, right):
    return (left.astype(F32) + right.astype(F32)).astype(BF16)


def joined(parts, bit):
    orders = [jnp.concatenate(parts), jnp.concatenate(parts[::-1])]
    return jnp.where(place_of(bit) == 0, *orders)


def exchange(rows, domains):
    shape = rows.shape
    split = rows.reshape((domains, shape[0] // domains) + shape[1:])
    return lax.all_to_all(split, "dom", split_axis=0, concat_axis=0, tiled=True).reshape(shape)


def shards(
    nodes,
    edges,
    inner_pairs,
    cut_local,
    cut_dest,
    cut_remote,
    w_edge_in,
    w_edge_out,
    w_node_in,
    w_node_out,
    ct_nodes,
    ct_edges,
):
    domains = lax.axis_size("dom")
    node_rows, latent = nodes.shape
    inner_count, cut_count = inner_pairs.shape[0], cut_local.shape[0]
    inner_rows, cut_rows = 2 * inner_count, 2 * cut_count
    slots = max(2, 2 * cut_count // domains)
    total_slots = domains * slots
    table = node_rows + total_slots
    me = lax.axis_index("dom").reshape(1)
    line = Line()

    ask = line.run(
        ask_kernel, shaped(jnp.int32, domains, slots), [cut_dest.reshape(1, -1), cut_remote.reshape(1, -1)]
    )
    asked = lax.all_to_all(ask, "dom", split_axis=0, concat_axis=0, tiled=True)
    cut_senders, cut_receivers = line.run(
        functools.partial(cut_marks_kernel, domains=domains, slots=slots),
        [shaped(BF16, cut_rows, table)] * 2,
        [cut_dest.reshape(1, -1), cut_local.reshape(1, -1)],
    )
    reply, asked_marks = line.run(
        reply_kernel,
        [shaped(BF16, total_slots, latent), shaped(BF16, total_slots, node_rows)],
        [asked, nodes],
    )
    far = exchange(reply, domains)

    block = cut_rows
    blocks = inner_rows // block

    def rows_spec(width, rows=block):
        return pl.BlockSpec((rows, width), lambda step: (step, 0))

    def all_spec(array):
        return pl.BlockSpec(array.shape, lambda step: (0, 0))

    saved_widths = [node_rows, node_rows, latent, latent, latent, latent, latent, 1]
    saved_types = [BF16, BF16, BF16, BF16, BF16, F32, F32, F32]
    (
        inner_senders,
        inner_receivers,
        inner_sender,
        inner_receiver,
        inner_hidden,
        inner_slope,
        inner_normed,
        inner_scale,
        inner_total,
    ) = line.run(
        inner_forward_kernel,
        [shaped(kind, inner_rows, width) for kind, width in zip(saved_types, saved_widths)]
        + [shaped(F32, node_rows, latent)],
        [inner_pairs.T, edges, nodes, w_edge_in, w_edge_out],
        [
            pl.BlockSpec((2, block // 2), lambda step: (0, step)),
            rows_spec(latent),
            all_spec(nodes),
            all_spec(w_edge_in),
            all_spec(w_edge_out),
        ],
        [rows_spec(width) for width in saved_widths] + [all_spec(nodes)],
        (blocks,),
    )

    def last_rows(array):
        last = array.shape[0] // block - 1
        return pl.BlockSpec((block, array.shape[1]), lambda step: (last, 0))

    (
        cut_sender,
        cut_receiver,
        cut_hidden,
        cut_slope,
        cut_normed,
        cut_scale,
        total,
        outgoing,
    ) = line.run(
        cut_forward_kernel,
        [shaped(kind, cut_rows, width) for kind, width in zip(saved_types, saved_widths)][2:]
        + [shaped(F32, node_rows, latent), shaped(BF16, total_slots, latent)],
        [
            cut_senders,
            cut_receivers,
            edges,
            nodes,
            far,
            w_edge_in,
            w_edge_out,
            inner_total,
        ],
        [
            all_spec(cut_senders),
            all_spec(cut_receivers),
            last_rows(edges),
            all_spec(nodes),
            all_spec(far),
            all_spec(w_edge_in),
            all_spec(w_edge_out),
            all_spec(inner_total),
        ],
        [rows_spec(width) for width in saved_widths[2:]]
        + [all_spec(nodes), rows_spec(latent, total_slots)],
        (1,),
    )
    incoming = exchange(outgoing, domains)
    new_edges = line.run(
        new_edges_kernel,
        shaped(BF16, *edges.shape),
        [edges, inner_normed, cut_normed],
    )
    (
        new_nodes,
        self_grad,
        agg_grad,
        grad_reply,
        node_keep,
        node_send,
    ) = line.run(
        node_kernel,
        [
            shaped(BF16, node_rows, latent),
            shaped(F32, node_rows, latent),
            shaped(BF16, node_rows, latent),
            shaped(BF16, total_slots, latent),
        ]
        + [shaped(BF16, 3 * latent // 2, latent)] * 2,
        [me, incoming, asked_marks, total, nodes, ct_nodes, w_node_in, w_node_out],
        [SMEM] + [VMEM] * 7,
    )
    far_grad = exchange(grad_reply, domains)
    node_sum = added(node_keep, across(node_send, domains, 1))
    inner_out, inner_pre = line.run(
        inner_backward_kernel,
        [shaped(BF16, inner_rows, latent)] * 2,
        [
            inner_receivers,
            agg_grad,
            ct_edges,
            inner_normed,
            inner_scale,
            inner_slope,
            w_edge_out,
        ],
        [
            rows_spec(node_rows),
            all_spec(agg_grad),
            rows_spec(latent),
            rows_spec(latent),
            rows_spec(1),
            rows_spec(latent),
            all_spec(w_edge_out),
        ],
        [rows_spec(latent)] * 2,
        (blocks,),
    )
    bits = index_bits(domains)
    node_parts = traded(node_sum, domains, 1)
    far_grad, node_sum, inner_pre = fence(far_grad, node_sum, inner_pre)
    factors = [
        edges,
        inner_sender,
        cut_sender,
        inner_receiver,
        cut_receiver,
        inner_hidden,
        cut_hidden,
        inner_out,
        inner_pre,
    ]
    buffers = [pltpu.VMEM((rows, latent), BF16) for rows in (inner_rows, cut_rows) * 2]
    buffers += [pltpu.VMEM((inner_rows, latent), BF16)] * 2
    buffers.append(pltpu.SemaphoreType.DMA((len(buffers),)))
    cut_out, cut_pre, edge_send = line.run(
        cut_backward_kernel,
        [shaped(BF16, cut_rows, latent)] * 2 + [shaped(BF16, 2 * latent, latent)],
        [
            me,
            cut_receivers,
            agg_grad,
            far_grad,
            ct_edges,
            cut_normed,
            cut_scale,
            cut_slope,
            w_edge_out,
        ]
        + factors,
        [
            SMEM,
            all_spec(cut_receivers),
            all_spec(agg_grad),
            all_spec(far_grad),
            last_rows(ct_edges),
            all_spec(cut_normed),
            all_spec(cut_scale),
            all_spec(cut_slope),
            all_spec(w_edge_out),
        ]
        + [ANY] * len(factors),
        [rows_spec(latent)] * 2 + [rows_spec(latent, 2 * latent)],
        (1,),
        buffers,
    )
    edge_send, place, *node_parts = fence(edge_send, me, *node_parts)
    edge_keep = line.run(
        edge_weights_kernel,
        shaped(BF16, 2 * latent, latent),
        [place, cut_out, cut_pre] + factors,
        [SMEM, VMEM, VMEM] + [ANY] * len(factors),
        scratch=buffers,
    )
    edge_parts = [edge_keep, across(edge_send, domains, 1)]
    node_parts = traded(added(*node_parts), domains, 2)
    fenced = fence(*edge_parts, *node_parts, inner_pre, cut_pre)
    edge_sum, node_sum, (inner_pre, cut_pre) = added(*fenced[:2]), added(*fenced[2:4]), fenced[4:]
    edge_parts = traded(edge_sum, domains, 1)
    node_parts = traded(node_sum, domains, 3)
    local_grad, outgoing_grad = line.run(
        input_grads_kernel,
        [shaped(F32, node_rows, latent), shaped(BF16, total_slots, latent)],
        [
            inner_senders,
            inner_receivers,
            cut_senders,
            cut_receivers,
            inner_pre,
            cut_pre,
            w_edge_in,
        ],
    )
    fenced = fence(*edge_parts, *node_parts, inner_pre, cut_pre, local_grad)
    edge_sum, node_sum = added(*fenced[:2]), added(*fenced[2:4])
    inner_pre, cut_pre, local_grad = fenced[4:]
    for bit in bits[4:]:
        node_sum = added(*traded(node_sum, domains, bit))
    for bit in bits[:3:-1]:
        node_sum = joined(handed(node_sum, domains, bit), bit)
    edge_parts = traded(edge_sum, domains, 2)
    node_parts = handed(node_sum, domains, 3)
    fenced = fence(*edge_parts, *node_parts, inner_pre)
    edge_sum, node_sum, inner_pre = added(*fenced[:2]), joined(fenced[2:4], 3), fenced[4]
    edge_parts = traded(edge_sum, domains, 3)
    node_parts = handed(node_sum, domains, 2)
    grad_edges = line.run(
        functools.partial(edge_grads_kernel, blocks=blocks),
        shaped(F32, *edges.shape),
        [ct_edges, inner_pre, cut_pre, w_edge_in],
        [
            rows_spec(latent),
            pl.BlockSpec((block, latent), lambda step: (jnp.minimum(step, blocks - 1), 0)),
            all_spec(cut_pre),
            pl.BlockSpec((latent, latent), lambda step: (0, 0)),
        ],
        [rows_spec(latent)],
        (blocks + 1,),
    )
    fenced = fence(*edge_parts, *node_parts, grad_edges)
    edge_sum, node_sum, grad_edges = added(*fenced[:2]), joined(fenced[2:4], 2), fenced[4]
    for bit in bits[4:]:
        edge_sum = added(*traded(edge_sum, domains, bit))
    for bit in bits[:3:-1]:
        edge_sum = joined(handed(edge_sum, domains, bit), bit)
    node_parts = handed(node_sum, domains, 1)
    edge_parts = fence(*handed(edge_sum, domains, 3))
    edge_parts = handed(joined(edge_parts, 3), domains, 2)
    *edge_parts, node_sum, other_sum, outgoing_grad = fence(
        *edge_parts, *node_parts, outgoing_grad
    )
    node_sum = joined([node_sum, other_sum], 1)
    edge_sum = joined(edge_parts, 2)
    edge_parts = handed(edge_sum, domains, 1) + [across(edge_sum, domains, 1)]
    others = across(node_sum, domains, 1)
    returned = exchange(outgoing_grad, domains)
    lower, left = place_of(0) == 0, place_of(1) == 0
    low_rows, high_rows = jnp.where(lower, node_sum, others), jnp.where(lower, others, node_sum)
    split = 2 * latent - low_rows.shape[0]
    grad_node_in = jnp.concatenate([low_rows, high_rows[:split]])
    grad_node_out = high_rows[split:]
    mine, far, near, grad_node_in, grad_node_out, returned = fence(
        *edge_parts, grad_node_in, grad_node_out, returned
    )
    corner = across(far, domains, 1)
    grad_nodes = line.run(
        node_grads_kernel,
        shaped(F32, node_rows, latent),
        [self_grad, local_grad, asked_marks, returned],
    )
    own, other = [mine, far], [near, corner]
    low_half = [jnp.where(lower, one, two) for one, two in zip(own, other)]
    high_half = [jnp.where(lower, two, one) for one, two in zip(own, other)]
    grad_edge_in = jnp.concatenate(
        [
            jnp.where(left, low_half[0], low_half[1]),
            jnp.where(left, low_half[1], low_half[0]),
            jnp.where(left, high_half[0], high_half[1]),
        ]
    )
    grad_edge_out = jnp.where(left, high_half[1], high_half[0])
    return (
        new_nodes,
        new_edges,
        grad_nodes,
        grad_edges,
        grad_edge_in,
        grad_edge_out,
        grad_node_in,
        grad_node_out,
    )


def solution(mesh):
    placed = (
        P(("groups", "dom"), None),
        P(("groups", "dom"), None),
        P(("groups", "dom"), None),
        P(("groups", "dom")),
        P(("groups", "dom"), None),
        P(("groups", "dom")),
        P(),
        P(),
        P(),
        P(),
        P(("groups", "dom"), None),
        P(("groups", "dom"), None),
    )
    return jax.shard_map(
        shards,
        mesh=mesh,
        in_specs=placed,
        out_specs=(
            P(("groups", "dom"), None),
            P(("groups", "dom"), None),
            P(("groups", "dom"), None),
            P(("groups", "dom"), None),
            P("groups", None),
            P("groups", None),
            P("groups", None),
            P("groups", None),
        ),
        check_vma=False,
    )
```

```python
import functools

import jax
import jax.numpy as jnp
from jax import lax
from jax.experimental import pallas as pl
from jax.experimental.pallas import tpu as pltpu
from jax.sharding import PartitionSpec as P

BF16 = jnp.bfloat16
F32 = jnp.float32
VMEM_LIMIT = 60 * 1024 * 1024


def dot(left, right):
    return jnp.dot(left, right, preferred_element_type=F32)


def dot_rows(left, right):
    return lax.dot_general(left, right, (((0,), (0,)), ((), ())), preferred_element_type=F32)


def dot_cols(left, right):
    return lax.dot_general(left, right, (((1,), (1,)), ((), ())), preferred_element_type=F32)


def iota(shape, axis):
    return lax.broadcasted_iota(jnp.int32, shape, axis)


def marks(mask):
    return jnp.where(mask, 1.0, 0.0).astype(BF16)


def onehot(column, width):
    return marks(column == iota((column.shape[0], width), 1))


def to_column(row):
    count = row.shape[1]
    square = (count, count)
    kept = jnp.where(iota(square, 0) == iota(square, 1), row.astype(F32), 0.0)
    return jnp.sum(kept, axis=1, keepdims=True)


def slot_ranks(dest, domains):
    count = dest.shape[0]
    square = (count, count)
    dest_marks = onehot(dest, domains)
    before = dot(marks(iota(square, 0) > iota(square, 1)), dest_marks)
    return dest_marks, jnp.sum(before * dest_marks.astype(F32), axis=1, keepdims=True)


def pair_marks(first, second, width):
    pairs = first.shape[0]
    shape = (2 * pairs, pairs)
    edge, pair = iota(shape, 0), iota(shape, 1)
    mine = (edge >> 1) == pair
    even = marks(mine & ((edge & 1) == 0))
    odd = marks(mine & ((edge & 1) == 1))
    first_marks, second_marks = onehot(first, width), onehot(second, width)
    senders = dot(even, first_marks) + dot(odd, second_marks)
    receivers = dot(even, second_marks) + dot(odd, first_marks)
    return senders.astype(BF16), receivers.astype(BF16)


def normalise(values):
    centered = values - jnp.mean(values, axis=1, keepdims=True)
    inv_scale = lax.rsqrt(jnp.mean(centered * centered, axis=1, keepdims=True) + 1e-05)
    return centered * inv_scale, inv_scale


def activate(pre_hidden):
    gate = jax.nn.sigmoid(pre_hidden)
    return (pre_hidden * gate).astype(BF16), gate * (1.0 + pre_hidden * (1.0 - gate))


def norm_backward(upstream, normed, inv_scale):
    centered = (
        upstream
        - jnp.mean(upstream, axis=1, keepdims=True)
        - normed * jnp.mean(upstream * normed, axis=1, keepdims=True)
    )
    return (inv_scale * centered).astype(BF16)


def ask_kernel(dest_ref, remote_ref, ask_ref):
    domains, slots = ask_ref.shape
    dest_marks, rank = slot_ranks(to_column(dest_ref[...]).astype(jnp.int32), domains)
    rank_marks = jnp.where(rank == iota((rank.shape[0], slots), 1).astype(F32), 1.0, 0.0)
    wanted = (rank_marks * to_column(remote_ref[...])).astype(BF16)
    ask_ref[...] = dot_rows(dest_marks, wanted).astype(jnp.int32)


def reply_kernel(asked_ref, nodes_ref, reply_ref, asked_marks_ref):
    domains, slots = asked_ref.shape
    total = domains * slots
    shift = slots.bit_length() - 1
    spread = marks((iota((total, domains), 0) >> shift) == iota((total, domains), 1))
    listed = dot(spread, asked_ref[...].astype(F32).astype(BF16))
    at_slot = (iota((total, slots), 0) & (slots - 1)) == iota((total, slots), 1)
    column = jnp.sum(jnp.where(at_slot, listed, 0.0), axis=1, keepdims=True)
    node_rows = nodes_ref.shape[0]
    asked_marks = marks(column == iota((total, node_rows), 1).astype(F32))
    asked_marks_ref[...] = asked_marks
    reply_ref[...] = dot(asked_marks, nodes_ref[...]).astype(BF16)


def cut_marks_kernel(dest_ref, local_ref, senders_ref, receivers_ref, *, domains, slots):
    width = senders_ref.shape[1]
    base = width - domains * slots
    dest = to_column(dest_ref[...]).astype(jnp.int32)
    _, rank = slot_ranks(dest, domains)
    second = dest * slots + rank.astype(jnp.int32) + base
    first = to_column(local_ref[...]).astype(jnp.int32)
    senders, receivers = pair_marks(first, second, width)
    senders_ref[...] = senders
    receivers_ref[...] = receivers


def edge_forward(edge, sender, receiver, w_in_ref, w_out_ref):
    latent = edge.shape[1]
    pre_hidden = (
        dot(edge, w_in_ref[:latent])
        + dot(sender, w_in_ref[latent : 2 * latent])
        + dot(receiver, w_in_ref[2 * latent :])
    )
    hidden, slope = activate(pre_hidden)
    normed, inv_scale = normalise(dot(hidden, w_out_ref[...]))
    return hidden, slope, normed, inv_scale


def inner_forward_kernel(
    pairs_ref,
    edges_ref,
    nodes_ref,
    w_in_ref,
    w_out_ref,
    senders_ref,
    receivers_ref,
    sender_ref,
    receiver_ref,
    hidden_ref,
    slope_ref,
    normed_ref,
    scale_ref,
    total_ref,
):
    first, second = (to_column(pairs_ref[side : side + 1]).astype(jnp.int32) for side in range(2))
    senders, receivers = pair_marks(first, second, nodes_ref.shape[0])
    senders_ref[...] = senders
    receivers_ref[...] = receivers
    nodes = nodes_ref[...]
    sender = dot(senders, nodes).astype(BF16)
    receiver = dot(receivers, nodes).astype(BF16)
    sender_ref[...] = sender
    receiver_ref[...] = receiver
    hidden, slope, normed, inv_scale = edge_forward(
        edges_ref[...], sender, receiver, w_in_ref, w_out_ref
    )
    hidden_ref[...] = hidden
    slope_ref[...] = slope
    normed_ref[...] = normed
    scale_ref[...] = inv_scale
    part = dot_rows(receivers, normed.astype(BF16))

    @pl.when(pl.program_id(0) == 0)
    def _():
        total_ref[...] = part

    @pl.when(pl.program_id(0) > 0)
    def _():
        total_ref[...] += part


def cut_forward_kernel(
    senders_ref,
    receivers_ref,
    edges_ref,
    nodes_ref,
    far_ref,
    w_in_ref,
    w_out_ref,
    inner_total_ref,
    sender_ref,
    receiver_ref,
    hidden_ref,
    slope_ref,
    normed_ref,
    scale_ref,
    total_ref,
    outgoing_ref,
):
    base = nodes_ref.shape[0]
    nodes, far = nodes_ref[...], far_ref[...]

    def rows_of(marks_ref):
        return (dot(marks_ref[:, :base], nodes) + dot(marks_ref[:, base:], far)).astype(BF16)

    sender, receiver = rows_of(senders_ref), rows_of(receivers_ref)
    sender_ref[...] = sender
    receiver_ref[...] = receiver
    hidden, slope, normed, inv_scale = edge_forward(
        edges_ref[...], sender, receiver, w_in_ref, w_out_ref
    )
    hidden_ref[...] = hidden
    slope_ref[...] = slope
    normed_ref[...] = normed
    scale_ref[...] = inv_scale
    message = normed.astype(BF16)
    total_ref[...] = inner_total_ref[...] + dot_rows(receivers_ref[:, :base], message)
    outgoing_ref[...] = dot_rows(receivers_ref[:, base:], message).astype(BF16)


def new_edges_kernel(edges_ref, inner_ref, cut_ref, out_ref):
    inner_rows = inner_ref.shape[0]

    def added(edge, normed):
        return (edge.astype(F32) + normed.astype(BF16).astype(F32)).astype(BF16)

    out_ref[:inner_rows] = added(edges_ref[:inner_rows], inner_ref[...])
    out_ref[inner_rows:] = added(edges_ref[inner_rows:], cut_ref[...])


def turn_kernel(*refs):
    edges_ref, inner_refs, cut_refs, out_ref = refs[0], refs[1:4], refs[4:7], refs[7]
    latent = edges_ref.shape[1]
    inner_rows = inner_refs[0].shape[0]

    def put(index, inner, cut):
        rows = pl.ds(index % 2 * latent, latent)
        out_ref[index // 2, rows, :inner_rows] = inner.T
        out_ref[index // 2, rows, inner_rows:] = cut.T

    put(0, edges_ref[:inner_rows], edges_ref[inner_rows:])
    for index in range(3):
        put(index + 1, inner_refs[index][...], cut_refs[index][...])


def node_kernel(
    me_ref,
    incoming_ref,
    asked_marks_ref,
    total_ref,
    nodes_ref,
    ct_ref,
    w_in_ref,
    w_out_ref,
    new_nodes_ref,
    self_grad_ref,
    agg_grad_ref,
    reply_ref,
    keep_ref,
    send_ref,
):
    latent = nodes_ref.shape[1]
    half = latent // 2
    nodes, asked_marks = nodes_ref[...], asked_marks_ref[...]
    aggregate = (total_ref[...] + dot_rows(asked_marks, incoming_ref[...])).astype(BF16)
    pre_hidden = dot(nodes, w_in_ref[:latent]) + dot(aggregate, w_in_ref[latent:])
    hidden, slope = activate(pre_hidden)
    normed, inv_scale = normalise(dot(hidden, w_out_ref[...]))
    upstream = ct_ref[...].astype(F32)
    grad_out = norm_backward(upstream, normed, inv_scale)
    grad_pre = (dot_cols(grad_out, w_out_ref[...]) * slope).astype(BF16)
    agg_grad = dot_cols(grad_pre, w_in_ref[latent:]).astype(BF16)
    agg_grad_ref[...] = agg_grad
    reply_ref[...] = dot(asked_marks, agg_grad).astype(BF16)
    self_grad_ref[...] = upstream + dot_cols(grad_pre, w_in_ref[:latent])
    new_nodes_ref[...] = (nodes.astype(F32) + normed).astype(BF16)

    def fill(low_ref, high_ref):
        by_aggregate = dot_rows(aggregate, grad_pre).astype(BF16)
        low_ref[:latent] = dot_rows(nodes, grad_pre).astype(BF16)
        low_ref[latent:] = by_aggregate[:half]
        high_ref[:half] = by_aggregate[half:]
        high_ref[half:] = dot_rows(hidden, grad_out).astype(BF16)

    @pl.when((me_ref[0] & 1) == 0)
    def _():
        fill(keep_ref, send_ref)

    @pl.when((me_ref[0] & 1) != 0)
    def _():
        fill(send_ref, keep_ref)


def edge_backward(ct, target_grads, normed, inv_scale, slope, w_out):
    grad_out = norm_backward(ct.astype(F32) + target_grads, normed, inv_scale)
    return grad_out, (dot_cols(grad_out, w_out) * slope).astype(BF16)


def inner_backward_kernel(
    receivers_ref,
    agg_grad_ref,
    ct_ref,
    normed_ref,
    scale_ref,
    slope_ref,
    w_out_ref,
    grad_out_ref,
    grad_pre_ref,
):
    grad_out, grad_pre = edge_backward(
        ct_ref[...],
        dot(receivers_ref[...], agg_grad_ref[...]),
        normed_ref[...],
        scale_ref[...],
        slope_ref[...],
        w_out_ref[...],
    )
    grad_out_ref[...] = grad_out
    grad_pre_ref[...] = grad_pre


def fetch(half, sources, buffers, sems):
    lefts, inner_pre, inner_out = sources
    left, pre, out = buffers
    rows = pl.ds(0, inner_pre.shape[0])
    copies = [
        pltpu.make_async_copy(lefts.at[half], left, sems.at[0]),
        pltpu.make_async_copy(inner_pre, pre.at[rows], sems.at[1]),
        pltpu.make_async_copy(inner_out, out.at[rows], sems.at[2]),
    ]
    for copy in copies:
        copy.start()
    return copies


def weight_rows(half, copies, buffers, cut_pre, cut_out, put):
    left, pre, out = buffers
    latent = pre.shape[1]
    rows = pl.ds(pre.shape[0] - cut_pre.shape[0], cut_pre.shape[0])
    pre[rows] = cut_pre
    out[rows] = cut_out
    for copy in copies:
        copy.wait()
    put(0, dot(left[:latent], pre[...]))

    @pl.when(half == 0)
    def _():
        put(1, dot(left[latent:], pre[...]))

    @pl.when(half != 0)
    def _():
        put(1, dot(left[latent:], out[...]))


def cut_backward_kernel(
    me_ref,
    receivers_ref,
    agg_grad_ref,
    far_grad_ref,
    ct_ref,
    normed_ref,
    scale_ref,
    slope_ref,
    w_out_ref,
    lefts_ref,
    inner_pre_ref,
    inner_out_ref,
    grad_out_ref,
    grad_pre_ref,
    out_ref,
    *rest,
):
    buffers, sems = rest[:-1], rest[-1]
    latent = w_out_ref.shape[1]
    half = 1 - (me_ref[0] & 1)
    copies = fetch(half, (lefts_ref, inner_pre_ref, inner_out_ref), buffers, sems)
    base = agg_grad_ref.shape[0]
    target = dot(receivers_ref[:, :base], agg_grad_ref[...]) + dot(
        receivers_ref[:, base:], far_grad_ref[...]
    )
    grad_out, grad_pre = edge_backward(
        ct_ref[...], target, normed_ref[...], scale_ref[...], slope_ref[...], w_out_ref[...]
    )
    grad_out_ref[...] = grad_out
    grad_pre_ref[...] = grad_pre

    def put(index, value):
        out_ref[pl.ds(index * latent, latent)] = value.astype(BF16)

    weight_rows(half, copies, buffers, grad_pre, grad_out, put)


def edge_weights_kernel(
    me_ref,
    received_ref,
    cut_pre_ref,
    cut_out_ref,
    lefts_ref,
    inner_pre_ref,
    inner_out_ref,
    own_ref,
    sent_ref,
    *rest,
):
    buffers, sems = rest[:-1], rest[-1]
    latent = own_ref.shape[1]
    half = me_ref[0] & 1
    copies = fetch(half, (lefts_ref, inner_pre_ref, inner_out_ref), buffers, sems)
    place = (me_ref[0] >> 1) & 1

    def put(index, value):
        total = (value + received_ref[pl.ds(index * latent, latent)].astype(F32)).astype(BF16)

        @pl.when(place == index)
        def _():
            own_ref[...] = total

        @pl.when(place != index)
        def _():
            sent_ref[...] = total

    weight_rows(half, copies, buffers, cut_pre_ref[...], cut_out_ref[...], put)


def input_grads_kernel(
    inner_senders_ref,
    inner_receivers_ref,
    cut_senders_ref,
    cut_receivers_ref,
    inner_pre_ref,
    cut_pre_ref,
    w_in_ref,
    local_ref,
    outgoing_ref,
):
    latent = inner_pre_ref.shape[1]
    base = inner_senders_ref.shape[1]
    inner_pre, cut_pre = inner_pre_ref[...], cut_pre_ref[...]
    w_sender, w_receiver = w_in_ref[latent : 2 * latent], w_in_ref[2 * latent :]

    def summed(inner_marks_ref, cut_marks_ref):
        return (
            dot_rows(inner_marks_ref[...], inner_pre) + dot_rows(cut_marks_ref[:, :base], cut_pre)
        ).astype(BF16)

    outgoing_ref[...] = (
        dot_cols(dot_rows(cut_senders_ref[:, base:], cut_pre).astype(BF16), w_sender)
        + dot_cols(dot_rows(cut_receivers_ref[:, base:], cut_pre).astype(BF16), w_receiver)
    ).astype(BF16)
    local_ref[...] = dot_cols(summed(inner_senders_ref, cut_senders_ref), w_sender) + dot_cols(
        summed(inner_receivers_ref, cut_receivers_ref), w_receiver
    )


def edge_grads_kernel(ct_ref, inner_pre_ref, cut_pre_ref, w_edge_ref, out_ref, *, blocks):
    inside = pl.program_id(0) < blocks

    @pl.when(inside)
    def _():
        out_ref[...] = ct_ref[...].astype(F32) + dot_cols(inner_pre_ref[...], w_edge_ref[...])

    @pl.when(jnp.logical_not(inside))
    def _():
        out_ref[...] = ct_ref[...].astype(F32) + dot_cols(cut_pre_ref[...], w_edge_ref[...])


def node_grads_kernel(self_ref, local_ref, asked_marks_ref, returned_ref, out_ref):
    out_ref[...] = (
        self_ref[...] + local_ref[...] + dot_rows(asked_marks_ref[...], returned_ref[...])
    )


VMEM = pl.BlockSpec(memory_space=pltpu.VMEM)
SMEM = pl.BlockSpec(memory_space=pltpu.SMEM)
ANY = pl.BlockSpec(memory_space=pl.ANY)


def shaped(dtype, *shape):
    return jax.ShapeDtypeStruct(shape, dtype)


class Line:
    def __init__(self):
        self.last = None

    def run(self, body, outs, ins, specs=None, out_specs=None, grid=None, scratch=()):
        single = not isinstance(outs, (list, tuple))
        out_shape = [outs] if single else list(outs)
        specs = [VMEM] * len(ins) if specs is None else list(specs)
        count, extra = len(ins), {} if grid is None else {"grid": grid}
        ins = list(ins)
        if self.last is not None:
            ins.append(self.last)
            specs.append(ANY)

        def ordered(*refs):
            return body(*refs[:count], *refs[len(ins) :])

        result = pl.pallas_call(
            ordered,
            out_shape=out_shape,
            in_specs=specs,
            out_specs=[VMEM] * len(out_shape) if out_specs is None else out_specs,
            scratch_shapes=scratch,
            compiler_params=pltpu.CompilerParams(vmem_limit_bytes=VMEM_LIMIT),
            cost_estimate=pl.CostEstimate(flops=1, bytes_accessed=1, transcendentals=0),
            **extra,
        )(*ins)
        self.last = result[-1]
        return result[0] if single else result


def index_bits(devices):
    return list(range(devices.bit_length() - 1))


def across(rows, devices, mask):
    return lax.ppermute(rows, "dom", [(device, device ^ mask) for device in range(devices)])


def fence(*values):
    return lax.optimization_barrier(values)


def place_of(bit):
    return (lax.axis_index("dom") >> bit) & 1


def traded(rows, devices, bit):
    place = place_of(bit)
    halves = rows.reshape(2, rows.shape[0] // 2, rows.shape[1])
    own = lax.dynamic_index_in_dim(halves, place, 0, False)
    sent = lax.dynamic_index_in_dim(halves, 1 - place, 0, False)
    return own, across(sent, devices, 1 << bit)


def handed(rows, devices, bit):
    return [rows, across(rows, devices, 1 << bit)]


def added(left, right):
    return (left.astype(F32) + right.astype(F32)).astype(BF16)


def joined(parts, bit):
    orders = [jnp.concatenate(parts), jnp.concatenate(parts[::-1])]
    return jnp.where(place_of(bit) == 0, *orders)


def exchange(rows, domains):
    shape = rows.shape
    split = rows.reshape((domains, shape[0] // domains) + shape[1:])
    return lax.all_to_all(split, "dom", split_axis=0, concat_axis=0, tiled=True).reshape(shape)


def shards(
    nodes,
    edges,
    inner_pairs,
    cut_local,
    cut_dest,
    cut_remote,
    w_edge_in,
    w_edge_out,
    w_node_in,
    w_node_out,
    ct_nodes,
    ct_edges,
):
    domains = lax.axis_size("dom")
    node_rows, latent = nodes.shape
    inner_count, cut_count = inner_pairs.shape[0], cut_local.shape[0]
    inner_rows, cut_rows = 2 * inner_count, 2 * cut_count
    slots = max(2, 2 * cut_count // domains)
    total_slots = domains * slots
    table = node_rows + total_slots
    me = lax.axis_index("dom").reshape(1)
    line = Line()

    ask = line.run(
        ask_kernel, shaped(jnp.int32, domains, slots), [cut_dest.reshape(1, -1), cut_remote.reshape(1, -1)]
    )
    asked = lax.all_to_all(ask, "dom", split_axis=0, concat_axis=0, tiled=True)
    cut_senders, cut_receivers = line.run(
        functools.partial(cut_marks_kernel, domains=domains, slots=slots),
        [shaped(BF16, cut_rows, table)] * 2,
        [cut_dest.reshape(1, -1), cut_local.reshape(1, -1)],
    )
    reply, asked_marks = line.run(
        reply_kernel,
        [shaped(BF16, total_slots, latent), shaped(BF16, total_slots, node_rows)],
        [asked, nodes],
    )
    far = exchange(reply, domains)

    block = cut_rows
    blocks = inner_rows // block

    def rows_spec(width, rows=block):
        return pl.BlockSpec((rows, width), lambda step: (step, 0))

    def all_spec(array):
        return pl.BlockSpec(array.shape, lambda step: (0, 0))

    saved_widths = [node_rows, node_rows, latent, latent, latent, latent, latent, 1]
    saved_types = [BF16, BF16, BF16, BF16, BF16, F32, F32, F32]
    (
        inner_senders,
        inner_receivers,
        inner_sender,
        inner_receiver,
        inner_hidden,
        inner_slope,
        inner_normed,
        inner_scale,
        inner_total,
    ) = line.run(
        inner_forward_kernel,
        [shaped(kind, inner_rows, width) for kind, width in zip(saved_types, saved_widths)]
        + [shaped(F32, node_rows, latent)],
        [inner_pairs.T, edges, nodes, w_edge_in, w_edge_out],
        [
            pl.BlockSpec((2, block // 2), lambda step: (0, step)),
            rows_spec(latent),
            all_spec(nodes),
            all_spec(w_edge_in),
            all_spec(w_edge_out),
        ],
        [rows_spec(width) for width in saved_widths] + [all_spec(nodes)],
        (blocks,),
    )

    def last_rows(array):
        last = array.shape[0] // block - 1
        return pl.BlockSpec((block, array.shape[1]), lambda step: (last, 0))

    (
        cut_sender,
        cut_receiver,
        cut_hidden,
        cut_slope,
        cut_normed,
        cut_scale,
        total,
        outgoing,
    ) = line.run(
        cut_forward_kernel,
        [shaped(kind, cut_rows, width) for kind, width in zip(saved_types, saved_widths)][2:]
        + [shaped(F32, node_rows, latent), shaped(BF16, total_slots, latent)],
        [
            cut_senders,
            cut_receivers,
            edges,
            nodes,
            far,
            w_edge_in,
            w_edge_out,
            inner_total,
        ],
        [
            all_spec(cut_senders),
            all_spec(cut_receivers),
            last_rows(edges),
            all_spec(nodes),
            all_spec(far),
            all_spec(w_edge_in),
            all_spec(w_edge_out),
            all_spec(inner_total),
        ],
        [rows_spec(width) for width in saved_widths[2:]]
        + [all_spec(nodes), rows_spec(latent, total_slots)],
        (1,),
    )
    incoming = exchange(outgoing, domains)
    new_edges = line.run(
        new_edges_kernel,
        shaped(BF16, *edges.shape),
        [edges, inner_normed, cut_normed],
    )
    lefts = line.run(
        turn_kernel,
        shaped(BF16, 2, 2 * latent, inner_rows + cut_rows),
        [
            edges,
            inner_sender,
            inner_receiver,
            inner_hidden,
            cut_sender,
            cut_receiver,
            cut_hidden,
        ],
    )
    (
        new_nodes,
        self_grad,
        agg_grad,
        grad_reply,
        node_keep,
        node_send,
    ) = line.run(
        node_kernel,
        [
            shaped(BF16, node_rows, latent),
            shaped(F32, node_rows, latent),
            shaped(BF16, node_rows, latent),
            shaped(BF16, total_slots, latent),
        ]
        + [shaped(BF16, 3 * latent // 2, latent)] * 2,
        [me, incoming, asked_marks, total, nodes, ct_nodes, w_node_in, w_node_out],
        [SMEM] + [VMEM] * 7,
    )
    far_grad = exchange(grad_reply, domains)
    node_sum = added(node_keep, across(node_send, domains, 1))
    inner_out, inner_pre = line.run(
        inner_backward_kernel,
        [shaped(BF16, inner_rows, latent)] * 2,
        [
            inner_receivers,
            agg_grad,
            ct_edges,
            inner_normed,
            inner_scale,
            inner_slope,
            w_edge_out,
        ],
        [
            rows_spec(node_rows),
            all_spec(agg_grad),
            rows_spec(latent),
            rows_spec(latent),
            rows_spec(1),
            rows_spec(latent),
            all_spec(w_edge_out),
        ],
        [rows_spec(latent)] * 2,
        (blocks,),
    )
    bits = index_bits(domains)
    node_parts = traded(node_sum, domains, 1)
    far_grad, node_sum, inner_pre = fence(far_grad, node_sum, inner_pre)
    buffers = [
        pltpu.VMEM((2 * latent, inner_rows + cut_rows), BF16),
        pltpu.VMEM((inner_rows + cut_rows, latent), BF16),
        pltpu.VMEM((inner_rows + cut_rows, latent), BF16),
        pltpu.SemaphoreType.DMA((3,)),
    ]
    factors = [lefts, inner_pre, inner_out]
    cut_out, cut_pre, edge_send = line.run(
        cut_backward_kernel,
        [shaped(BF16, cut_rows, latent)] * 2 + [shaped(BF16, 2 * latent, latent)],
        [
            me,
            cut_receivers,
            agg_grad,
            far_grad,
            ct_edges,
            cut_normed,
            cut_scale,
            cut_slope,
            w_edge_out,
        ]
        + factors,
        [
            SMEM,
            all_spec(cut_receivers),
            all_spec(agg_grad),
            all_spec(far_grad),
            last_rows(ct_edges),
            all_spec(cut_normed),
            all_spec(cut_scale),
            all_spec(cut_slope),
            all_spec(w_edge_out),
        ]
        + [ANY] * len(factors),
        [rows_spec(latent)] * 2 + [rows_spec(latent, 2 * latent)],
        (1,),
        buffers,
    )
    edge_send, place, *node_parts = fence(edge_send, me, *node_parts)
    received = across(edge_send, domains, 1)
    node_parts = traded(added(*node_parts), domains, 2)
    cut_pre = fence(cut_pre, edge_send)[0]
    local_grad, outgoing_grad = line.run(
        input_grads_kernel,
        [shaped(F32, node_rows, latent), shaped(BF16, total_slots, latent)],
        [
            inner_senders,
            inner_receivers,
            cut_senders,
            cut_receivers,
            inner_pre,
            cut_pre,
            w_edge_in,
        ],
    )
    edge_own, edge_sent = line.run(
        edge_weights_kernel,
        [shaped(BF16, latent, latent)] * 2,
        [place, received, cut_pre, cut_out] + factors,
        [SMEM, VMEM, VMEM, VMEM] + [ANY] * len(factors),
        scratch=buffers,
    )
    edge_own, edge_sent, *node_parts, outgoing_grad, inner_pre, cut_pre = fence(
        edge_own, edge_sent, *node_parts, outgoing_grad, inner_pre, cut_pre
    )
    edge_got = across(edge_sent, domains, 2)
    node_sum = added(*node_parts)
    node_sum = added(*handed(node_sum, domains, 3))
    for bit in bits[4:]:
        node_sum = added(*handed(node_sum, domains, bit))
    returned = exchange(outgoing_grad, domains)
    grad_edges = line.run(
        functools.partial(edge_grads_kernel, blocks=blocks),
        shaped(F32, *edges.shape),
        [ct_edges, inner_pre, cut_pre, w_edge_in],
        [
            rows_spec(latent),
            pl.BlockSpec((block, latent), lambda step: (jnp.minimum(step, blocks - 1), 0)),
            all_spec(cut_pre),
            pl.BlockSpec((latent, latent), lambda step: (0, 0)),
        ],
        [rows_spec(latent)],
        (blocks + 1,),
    )
    edge_own, edge_got, node_sum, grad_edges, returned = fence(
        edge_own, edge_got, node_sum, grad_edges, returned
    )
    edge_sum = added(edge_own, edge_got)
    edge_parts = traded(edge_sum, domains, 2)
    node_parts = handed(node_sum, domains, 2)
    fenced = fence(*edge_parts, *node_parts)
    edge_sum, node_sum = added(*fenced[:2]), joined(fenced[2:4], 2)
    edge_parts = traded(edge_sum, domains, 3)
    node_parts = handed(node_sum, domains, 1)
    grad_nodes = line.run(
        node_grads_kernel,
        shaped(F32, node_rows, latent),
        [self_grad, local_grad, asked_marks, returned],
    )
    *edge_parts, grad_nodes = fence(*edge_parts, grad_nodes)
    edge_sum = added(*edge_parts)
    for bit in bits[4:]:
        edge_sum = added(*traded(edge_sum, domains, bit))
    for bit in bits[:3:-1]:
        edge_sum = joined(handed(edge_sum, domains, bit), bit)
    *edge_parts, node_sum, other_sum = fence(*handed(edge_sum, domains, 3), *node_parts)
    node_sum = joined([node_sum, other_sum], 1)
    others = across(node_sum, domains, 1)
    edge_parts = handed(joined(edge_parts, 3), domains, 2)
    *edge_parts, node_sum, others = fence(*edge_parts, node_sum, others)
    edge_sum = joined(edge_parts, 2)
    edge_parts = handed(edge_sum, domains, 1) + [across(edge_sum, domains, 1)]
    lower, left = place_of(0) == 0, place_of(1) == 0
    low_rows, high_rows = jnp.where(lower, node_sum, others), jnp.where(lower, others, node_sum)
    split = 2 * latent - low_rows.shape[0]
    grad_node_in = jnp.concatenate([low_rows, high_rows[:split]])
    grad_node_out = high_rows[split:]
    mine, far, near, grad_node_in, grad_node_out = fence(
        *edge_parts, grad_node_in, grad_node_out
    )
    corner = across(far, domains, 1)
    own, other = [mine, far], [near, corner]
    low_half = [jnp.where(lower, one, two) for one, two in zip(own, other)]
    high_half = [jnp.where(lower, two, one) for one, two in zip(own, other)]
    grad_edge_in = jnp.concatenate(
        [
            jnp.where(left, low_half[0], low_half[1]),
            jnp.where(left, low_half[1], low_half[0]),
            jnp.where(left, high_half[0], high_half[1]),
        ]
    )
    grad_edge_out = jnp.where(left, high_half[1], high_half[0])
    return (
        new_nodes,
        new_edges,
        grad_nodes,
        grad_edges,
        grad_edge_in,
        grad_edge_out,
        grad_node_in,
        grad_node_out,
    )


def solution(mesh):
    placed = (
        P(("groups", "dom"), None),
        P(("groups", "dom"), None),
        P(("groups", "dom"), None),
        P(("groups", "dom")),
        P(("groups", "dom"), None),
        P(("groups", "dom")),
        P(),
        P(),
        P(),
        P(),
        P(("groups", "dom"), None),
        P(("groups", "dom"), None),
    )
    return jax.shard_map(
        shards,
        mesh=mesh,
        in_specs=placed,
        out_specs=(
            P(("groups", "dom"), None),
            P(("groups", "dom"), None),
            P(("groups", "dom"), None),
            P(("groups", "dom"), None),
            P("groups", None),
            P("groups", None),
            P("groups", None),
            P("groups", None),
        ),
        check_vma=False,
    )
```

```python
import functools

import jax
import jax.numpy as jnp
from jax import lax
from jax.experimental import pallas as pl
from jax.experimental.pallas import tpu as pltpu
from jax.sharding import PartitionSpec as P

BF16 = jnp.bfloat16
F32 = jnp.float32
VMEM_LIMIT = 60 * 1024 * 1024


def dot(left, right):
    return jnp.dot(left, right, preferred_element_type=F32)


def dot_rows(left, right):
    return lax.dot_general(left, right, (((0,), (0,)), ((), ())), preferred_element_type=F32)


def dot_cols(left, right):
    return lax.dot_general(left, right, (((1,), (1,)), ((), ())), preferred_element_type=F32)


def iota(shape, axis):
    return lax.broadcasted_iota(jnp.int32, shape, axis)


def marks(mask):
    return jnp.where(mask, 1.0, 0.0).astype(BF16)


def onehot(column, width):
    return marks(column == iota((column.shape[0], width), 1))


def to_column(row):
    count = row.shape[1]
    square = (count, count)
    kept = jnp.where(iota(square, 0) == iota(square, 1), row.astype(F32), 0.0)
    return jnp.sum(kept, axis=1, keepdims=True)


def slot_ranks(dest, domains):
    count = dest.shape[0]
    square = (count, count)
    dest_marks = onehot(dest, domains)
    before = dot(marks(iota(square, 0) > iota(square, 1)), dest_marks)
    return dest_marks, jnp.sum(before * dest_marks.astype(F32), axis=1, keepdims=True)


def pair_marks(first, second, width):
    pairs = first.shape[0]
    shape = (2 * pairs, pairs)
    edge, pair = iota(shape, 0), iota(shape, 1)
    mine = (edge >> 1) == pair
    even = marks(mine & ((edge & 1) == 0))
    odd = marks(mine & ((edge & 1) == 1))
    first_marks, second_marks = onehot(first, width), onehot(second, width)
    senders = dot(even, first_marks) + dot(odd, second_marks)
    receivers = dot(even, second_marks) + dot(odd, first_marks)
    return senders.astype(BF16), receivers.astype(BF16)


def normalise(values):
    centered = values - jnp.mean(values, axis=1, keepdims=True)
    inv_scale = lax.rsqrt(jnp.mean(centered * centered, axis=1, keepdims=True) + 1e-05)
    return centered * inv_scale, inv_scale


def activate(pre_hidden):
    gate = jax.nn.sigmoid(pre_hidden)
    return (pre_hidden * gate).astype(BF16), gate * (1.0 + pre_hidden * (1.0 - gate))


def norm_backward(upstream, normed, inv_scale):
    centered = (
        upstream
        - jnp.mean(upstream, axis=1, keepdims=True)
        - normed * jnp.mean(upstream * normed, axis=1, keepdims=True)
    )
    return (inv_scale * centered).astype(BF16)


def ask_kernel(dest_ref, remote_ref, ask_ref):
    domains, slots = ask_ref.shape
    dest_marks, rank = slot_ranks(to_column(dest_ref[...]).astype(jnp.int32), domains)
    rank_marks = jnp.where(rank == iota((rank.shape[0], slots), 1).astype(F32), 1.0, 0.0)
    wanted = (rank_marks * to_column(remote_ref[...])).astype(BF16)
    ask_ref[...] = dot_rows(dest_marks, wanted).astype(jnp.int32)


def reply_kernel(asked_ref, nodes_ref, reply_ref, asked_marks_ref):
    domains, slots = asked_ref.shape
    total = domains * slots
    shift = slots.bit_length() - 1
    spread = marks((iota((total, domains), 0) >> shift) == iota((total, domains), 1))
    listed = dot(spread, asked_ref[...].astype(F32).astype(BF16))
    at_slot = (iota((total, slots), 0) & (slots - 1)) == iota((total, slots), 1)
    column = jnp.sum(jnp.where(at_slot, listed, 0.0), axis=1, keepdims=True)
    node_rows = nodes_ref.shape[0]
    asked_marks = marks(column == iota((total, node_rows), 1).astype(F32))
    asked_marks_ref[...] = asked_marks
    reply_ref[...] = dot(asked_marks, nodes_ref[...]).astype(BF16)


def cut_marks_kernel(dest_ref, local_ref, senders_ref, receivers_ref, *, domains, slots):
    width = senders_ref.shape[1]
    base = width - domains * slots
    dest = to_column(dest_ref[...]).astype(jnp.int32)
    _, rank = slot_ranks(dest, domains)
    second = dest * slots + rank.astype(jnp.int32) + base
    first = to_column(local_ref[...]).astype(jnp.int32)
    senders, receivers = pair_marks(first, second, width)
    senders_ref[...] = senders
    receivers_ref[...] = receivers


def edge_forward(edge, sender, receiver, w_in_ref, w_out_ref):
    latent = edge.shape[1]
    pre_hidden = (
        dot(edge, w_in_ref[:latent])
        + dot(sender, w_in_ref[latent : 2 * latent])
        + dot(receiver, w_in_ref[2 * latent :])
    )
    hidden, slope = activate(pre_hidden)
    normed, inv_scale = normalise(dot(hidden, w_out_ref[...]))
    return hidden, slope, normed, inv_scale


def inner_forward_kernel(
    pairs_ref,
    edges_ref,
    nodes_ref,
    w_in_ref,
    w_out_ref,
    senders_ref,
    receivers_ref,
    sender_ref,
    receiver_ref,
    hidden_ref,
    slope_ref,
    normed_ref,
    scale_ref,
    total_ref,
):
    first, second = (to_column(pairs_ref[side : side + 1]).astype(jnp.int32) for side in range(2))
    senders, receivers = pair_marks(first, second, nodes_ref.shape[0])
    senders_ref[...] = senders
    receivers_ref[...] = receivers
    nodes = nodes_ref[...]
    sender = dot(senders, nodes).astype(BF16)
    receiver = dot(receivers, nodes).astype(BF16)
    sender_ref[...] = sender
    receiver_ref[...] = receiver
    hidden, slope, normed, inv_scale = edge_forward(
        edges_ref[...], sender, receiver, w_in_ref, w_out_ref
    )
    hidden_ref[...] = hidden
    slope_ref[...] = slope
    normed_ref[...] = normed
    scale_ref[...] = inv_scale
    part = dot_rows(receivers, normed.astype(BF16))

    @pl.when(pl.program_id(0) == 0)
    def _():
        total_ref[...] = part

    @pl.when(pl.program_id(0) > 0)
    def _():
        total_ref[...] += part


def cut_forward_kernel(
    senders_ref,
    receivers_ref,
    edges_ref,
    nodes_ref,
    far_ref,
    w_in_ref,
    w_out_ref,
    inner_total_ref,
    sender_ref,
    receiver_ref,
    hidden_ref,
    slope_ref,
    normed_ref,
    scale_ref,
    total_ref,
    outgoing_ref,
):
    base = nodes_ref.shape[0]
    nodes, far = nodes_ref[...], far_ref[...]

    def rows_of(marks_ref):
        return (dot(marks_ref[:, :base], nodes) + dot(marks_ref[:, base:], far)).astype(BF16)

    sender, receiver = rows_of(senders_ref), rows_of(receivers_ref)
    sender_ref[...] = sender
    receiver_ref[...] = receiver
    hidden, slope, normed, inv_scale = edge_forward(
        edges_ref[...], sender, receiver, w_in_ref, w_out_ref
    )
    hidden_ref[...] = hidden
    slope_ref[...] = slope
    normed_ref[...] = normed
    scale_ref[...] = inv_scale
    message = normed.astype(BF16)
    total_ref[...] = inner_total_ref[...] + dot_rows(receivers_ref[:, :base], message)
    outgoing_ref[...] = dot_rows(receivers_ref[:, base:], message).astype(BF16)


def new_edges_kernel(edges_ref, inner_ref, cut_ref, out_ref):
    inner_rows = inner_ref.shape[0]

    def added(edge, normed):
        return (edge.astype(F32) + normed.astype(BF16).astype(F32)).astype(BF16)

    out_ref[:inner_rows] = added(edges_ref[:inner_rows], inner_ref[...])
    out_ref[inner_rows:] = added(edges_ref[inner_rows:], cut_ref[...])


def node_kernel(
    me_ref,
    incoming_ref,
    asked_marks_ref,
    total_ref,
    nodes_ref,
    ct_ref,
    w_in_ref,
    w_out_ref,
    new_nodes_ref,
    self_grad_ref,
    agg_grad_ref,
    reply_ref,
    keep_ref,
    send_ref,
):
    latent = nodes_ref.shape[1]
    half = latent // 2
    nodes, asked_marks = nodes_ref[...], asked_marks_ref[...]
    aggregate = (total_ref[...] + dot_rows(asked_marks, incoming_ref[...])).astype(BF16)
    pre_hidden = dot(nodes, w_in_ref[:latent]) + dot(aggregate, w_in_ref[latent:])
    hidden, slope = activate(pre_hidden)
    normed, inv_scale = normalise(dot(hidden, w_out_ref[...]))
    upstream = ct_ref[...].astype(F32)
    grad_out = norm_backward(upstream, normed, inv_scale)
    grad_pre = (dot_cols(grad_out, w_out_ref[...]) * slope).astype(BF16)
    agg_grad = dot_cols(grad_pre, w_in_ref[latent:]).astype(BF16)
    agg_grad_ref[...] = agg_grad
    reply_ref[...] = dot(asked_marks, agg_grad).astype(BF16)
    self_grad_ref[...] = upstream + dot_cols(grad_pre, w_in_ref[:latent])
    new_nodes_ref[...] = (nodes.astype(F32) + normed).astype(BF16)

    def fill(low_ref, high_ref):
        by_aggregate = dot_rows(aggregate, grad_pre).astype(BF16)
        low_ref[:latent] = dot_rows(nodes, grad_pre).astype(BF16)
        low_ref[latent:] = by_aggregate[:half]
        high_ref[:half] = by_aggregate[half:]
        high_ref[half:] = dot_rows(hidden, grad_out).astype(BF16)

    @pl.when((me_ref[0] & 1) == 0)
    def _():
        fill(keep_ref, send_ref)

    @pl.when((me_ref[0] & 1) != 0)
    def _():
        fill(send_ref, keep_ref)


def edge_backward(ct, target_grads, normed, inv_scale, slope, w_out):
    grad_out = norm_backward(ct.astype(F32) + target_grads, normed, inv_scale)
    return grad_out, (dot_cols(grad_out, w_out) * slope).astype(BF16)


def inner_backward_kernel(
    receivers_ref,
    agg_grad_ref,
    ct_ref,
    normed_ref,
    scale_ref,
    slope_ref,
    w_out_ref,
    grad_out_ref,
    grad_pre_ref,
):
    grad_out, grad_pre = edge_backward(
        ct_ref[...],
        dot(receivers_ref[...], agg_grad_ref[...]),
        normed_ref[...],
        scale_ref[...],
        slope_ref[...],
        w_out_ref[...],
    )
    grad_out_ref[...] = grad_out
    grad_pre_ref[...] = grad_pre


def fetch_factors(half, sources, buffers, sems, wait):
    edges, inner_sender, cut_sender, inner_receiver, cut_receiver = sources[:5]
    inner_hidden, cut_hidden, inner_out, inner_pre = sources[5:]
    inner_rows, cut_rows = inner_pre.shape[0], cut_sender.shape[0]
    inner_edges = edges.at[pl.ds(0, inner_rows)]
    cut_edges = edges.at[pl.ds(inner_rows, cut_rows)]
    low = [inner_edges, cut_edges, inner_sender, cut_sender, inner_pre, inner_pre]
    high = [inner_receiver, cut_receiver, inner_hidden, cut_hidden, inner_pre, inner_out]

    def each(parts):
        for index, (source, buffer) in enumerate(zip(parts, buffers)):
            copy = pltpu.make_async_copy(source, buffer, sems.at[index])
            if wait:
                copy.wait()
            else:
                copy.start()

    @pl.when(half == 0)
    def _():
        each(low)

    @pl.when(half != 0)
    def _():
        each(high)


def edge_rows(half, buffers, cut_pre, cut_out, out_ref):
    latent = cut_pre.shape[1]
    first, first_cut, second, second_cut, first_right, second_right = buffers
    chosen = jnp.where(half == 0, cut_pre.astype(F32), cut_out.astype(F32)).astype(BF16)
    out_ref[:latent] = (
        dot_rows(first[...], first_right[...]) + dot_rows(first_cut[...], cut_pre)
    ).astype(BF16)
    out_ref[latent:] = (
        dot_rows(second[...], second_right[...]) + dot_rows(second_cut[...], chosen)
    ).astype(BF16)


def cut_backward_kernel(
    me_ref,
    receivers_ref,
    agg_grad_ref,
    far_grad_ref,
    ct_ref,
    normed_ref,
    scale_ref,
    slope_ref,
    w_out_ref,
    *refs,
):
    sources, (grad_out_ref, grad_pre_ref, out_ref), rest = refs[:9], refs[9:12], refs[12:]
    buffers, sems = rest[:-1], rest[-1]
    half = 1 - (me_ref[0] & 1)
    fetch_factors(half, sources, buffers, sems, False)
    base = agg_grad_ref.shape[0]
    target = dot(receivers_ref[:, :base], agg_grad_ref[...]) + dot(
        receivers_ref[:, base:], far_grad_ref[...]
    )
    grad_out, grad_pre = edge_backward(
        ct_ref[...], target, normed_ref[...], scale_ref[...], slope_ref[...], w_out_ref[...]
    )
    grad_out_ref[...] = grad_out
    grad_pre_ref[...] = grad_pre
    fetch_factors(half, sources, buffers, sems, True)
    edge_rows(half, buffers, grad_pre, grad_out, out_ref)


def edge_weights_kernel(me_ref, cut_out_ref, cut_pre_ref, *refs):
    sources, out_ref, rest = refs[:9], refs[9], refs[10:]
    buffers, sems = rest[:-1], rest[-1]
    half = me_ref[0] & 1
    fetch_factors(half, sources, buffers, sems, False)
    fetch_factors(half, sources, buffers, sems, True)
    edge_rows(half, buffers, cut_pre_ref[...], cut_out_ref[...], out_ref)


def input_grads_kernel(
    inner_senders_ref,
    inner_receivers_ref,
    cut_senders_ref,
    cut_receivers_ref,
    inner_pre_ref,
    cut_pre_ref,
    w_in_ref,
    local_ref,
    outgoing_ref,
):
    latent = inner_pre_ref.shape[1]
    base = inner_senders_ref.shape[1]
    inner_pre, cut_pre = inner_pre_ref[...], cut_pre_ref[...]
    w_sender, w_receiver = w_in_ref[latent : 2 * latent], w_in_ref[2 * latent :]

    def summed(inner_marks_ref, cut_marks_ref):
        return (
            dot_rows(inner_marks_ref[...], inner_pre) + dot_rows(cut_marks_ref[:, :base], cut_pre)
        ).astype(BF16)

    outgoing_ref[...] = (
        dot_cols(dot_rows(cut_senders_ref[:, base:], cut_pre).astype(BF16), w_sender)
        + dot_cols(dot_rows(cut_receivers_ref[:, base:], cut_pre).astype(BF16), w_receiver)
    ).astype(BF16)
    local_ref[...] = dot_cols(summed(inner_senders_ref, cut_senders_ref), w_sender) + dot_cols(
        summed(inner_receivers_ref, cut_receivers_ref), w_receiver
    )


def edge_grads_kernel(ct_ref, inner_pre_ref, cut_pre_ref, w_edge_ref, out_ref, *, blocks):
    inside = pl.program_id(0) < blocks

    @pl.when(inside)
    def _():
        out_ref[...] = ct_ref[...].astype(F32) + dot_cols(inner_pre_ref[...], w_edge_ref[...])

    @pl.when(jnp.logical_not(inside))
    def _():
        out_ref[...] = ct_ref[...].astype(F32) + dot_cols(cut_pre_ref[...], w_edge_ref[...])


def node_grads_kernel(self_ref, local_ref, asked_marks_ref, returned_ref, out_ref):
    out_ref[...] = (
        self_ref[...] + local_ref[...] + dot_rows(asked_marks_ref[...], returned_ref[...])
    )


VMEM = pl.BlockSpec(memory_space=pltpu.VMEM)
SMEM = pl.BlockSpec(memory_space=pltpu.SMEM)
ANY = pl.BlockSpec(memory_space=pl.ANY)


def shaped(dtype, *shape):
    return jax.ShapeDtypeStruct(shape, dtype)


class Line:
    def __init__(self):
        self.last = None

    def run(self, body, outs, ins, specs=None, out_specs=None, grid=None, scratch=()):
        single = not isinstance(outs, (list, tuple))
        out_shape = [outs] if single else list(outs)
        specs = [VMEM] * len(ins) if specs is None else list(specs)
        count, extra = len(ins), {} if grid is None else {"grid": grid}
        ins = list(ins)
        if self.last is not None:
            ins.append(self.last)
            specs.append(ANY)

        def ordered(*refs):
            return body(*refs[:count], *refs[len(ins) :])

        result = pl.pallas_call(
            ordered,
            out_shape=out_shape,
            in_specs=specs,
            out_specs=[VMEM] * len(out_shape) if out_specs is None else out_specs,
            scratch_shapes=scratch,
            compiler_params=pltpu.CompilerParams(vmem_limit_bytes=VMEM_LIMIT),
            cost_estimate=pl.CostEstimate(flops=1, bytes_accessed=1, transcendentals=0),
            **extra,
        )(*ins)
        self.last = result[-1]
        return result[0] if single else result


def index_bits(devices):
    return list(range(devices.bit_length() - 1))


def across(rows, devices, mask):
    return lax.ppermute(rows, "dom", [(device, device ^ mask) for device in range(devices)])


def fence(*values):
    return lax.optimization_barrier(values)


def place_of(bit):
    return (lax.axis_index("dom") >> bit) & 1


def split(parts, bit):
    place = place_of(bit)
    halves = [part.reshape(2, part.shape[0] // 2, part.shape[1]) for part in parts]
    own = [lax.dynamic_index_in_dim(half, place, 0, False) for half in halves]
    sent = [lax.dynamic_index_in_dim(half, 1 - place, 0, False) for half in halves]
    return own, added(*sent)


def handed(rows, devices, bit):
    return [rows, across(rows, devices, 1 << bit)]


def added(*parts):
    return sum(part.astype(F32) for part in parts).astype(BF16)


def joined(parts, bit):
    orders = [jnp.concatenate(parts), jnp.concatenate(parts[::-1])]
    return jnp.where(place_of(bit) == 0, *orders)


def exchange(rows, domains):
    shape = rows.shape
    split = rows.reshape((domains, shape[0] // domains) + shape[1:])
    return lax.all_to_all(split, "dom", split_axis=0, concat_axis=0, tiled=True).reshape(shape)


def shards(
    nodes,
    edges,
    inner_pairs,
    cut_local,
    cut_dest,
    cut_remote,
    w_edge_in,
    w_edge_out,
    w_node_in,
    w_node_out,
    ct_nodes,
    ct_edges,
):
    domains = lax.axis_size("dom")
    node_rows, latent = nodes.shape
    inner_count, cut_count = inner_pairs.shape[0], cut_local.shape[0]
    inner_rows, cut_rows = 2 * inner_count, 2 * cut_count
    slots = max(2, 2 * cut_count // domains)
    total_slots = domains * slots
    table = node_rows + total_slots
    me = lax.axis_index("dom").reshape(1)
    line = Line()

    ask = line.run(
        ask_kernel, shaped(jnp.int32, domains, slots), [cut_dest.reshape(1, -1), cut_remote.reshape(1, -1)]
    )
    asked = lax.all_to_all(ask, "dom", split_axis=0, concat_axis=0, tiled=True)
    cut_senders, cut_receivers = line.run(
        functools.partial(cut_marks_kernel, domains=domains, slots=slots),
        [shaped(BF16, cut_rows, table)] * 2,
        [cut_dest.reshape(1, -1), cut_local.reshape(1, -1)],
    )
    reply, asked_marks = line.run(
        reply_kernel,
        [shaped(BF16, total_slots, latent), shaped(BF16, total_slots, node_rows)],
        [asked, nodes],
    )
    far = exchange(reply, domains)

    block = cut_rows
    blocks = inner_rows // block

    def rows_spec(width, rows=block):
        return pl.BlockSpec((rows, width), lambda step: (step, 0))

    def all_spec(array):
        return pl.BlockSpec(array.shape, lambda step: (0, 0))

    saved_widths = [node_rows, node_rows, latent, latent, latent, latent, latent, 1]
    saved_types = [BF16, BF16, BF16, BF16, BF16, F32, F32, F32]
    (
        inner_senders,
        inner_receivers,
        inner_sender,
        inner_receiver,
        inner_hidden,
        inner_slope,
        inner_normed,
        inner_scale,
        inner_total,
    ) = line.run(
        inner_forward_kernel,
        [shaped(kind, inner_rows, width) for kind, width in zip(saved_types, saved_widths)]
        + [shaped(F32, node_rows, latent)],
        [inner_pairs.T, edges, nodes, w_edge_in, w_edge_out],
        [
            pl.BlockSpec((2, block // 2), lambda step: (0, step)),
            rows_spec(latent),
            all_spec(nodes),
            all_spec(w_edge_in),
            all_spec(w_edge_out),
        ],
        [rows_spec(width) for width in saved_widths] + [all_spec(nodes)],
        (blocks,),
    )

    def last_rows(array):
        last = array.shape[0] // block - 1
        return pl.BlockSpec((block, array.shape[1]), lambda step: (last, 0))

    (
        cut_sender,
        cut_receiver,
        cut_hidden,
        cut_slope,
        cut_normed,
        cut_scale,
        total,
        outgoing,
    ) = line.run(
        cut_forward_kernel,
        [shaped(kind, cut_rows, width) for kind, width in zip(saved_types, saved_widths)][2:]
        + [shaped(F32, node_rows, latent), shaped(BF16, total_slots, latent)],
        [
            cut_senders,
            cut_receivers,
            edges,
            nodes,
            far,
            w_edge_in,
            w_edge_out,
            inner_total,
        ],
        [
            all_spec(cut_senders),
            all_spec(cut_receivers),
            last_rows(edges),
            all_spec(nodes),
            all_spec(far),
            all_spec(w_edge_in),
            all_spec(w_edge_out),
            all_spec(inner_total),
        ],
        [rows_spec(width) for width in saved_widths[2:]]
        + [all_spec(nodes), rows_spec(latent, total_slots)],
        (1,),
    )
    incoming = exchange(outgoing, domains)
    new_edges = line.run(
        new_edges_kernel,
        shaped(BF16, *edges.shape),
        [edges, inner_normed, cut_normed],
    )
    (
        new_nodes,
        self_grad,
        agg_grad,
        grad_reply,
        node_keep,
        node_send,
    ) = line.run(
        node_kernel,
        [
            shaped(BF16, node_rows, latent),
            shaped(F32, node_rows, latent),
            shaped(BF16, node_rows, latent),
            shaped(BF16, total_slots, latent),
        ]
        + [shaped(BF16, 3 * latent // 2, latent)] * 2,
        [me, incoming, asked_marks, total, nodes, ct_nodes, w_node_in, w_node_out],
        [SMEM] + [VMEM] * 7,
    )
    far_grad = exchange(grad_reply, domains)
    node_sum = added(node_keep, across(node_send, domains, 1))
    inner_out, inner_pre = line.run(
        inner_backward_kernel,
        [shaped(BF16, inner_rows, latent)] * 2,
        [
            inner_receivers,
            agg_grad,
            ct_edges,
            inner_normed,
            inner_scale,
            inner_slope,
            w_edge_out,
        ],
        [
            rows_spec(node_rows),
            all_spec(agg_grad),
            rows_spec(latent),
            rows_spec(latent),
            rows_spec(1),
            rows_spec(latent),
            all_spec(w_edge_out),
        ],
        [rows_spec(latent)] * 2,
        (blocks,),
    )
    bits = index_bits(domains)
    node_own, node_sent = split([node_sum], 1)
    node_parts = [*node_own, across(node_sent, domains, 2)]
    far_grad, node_sum, inner_pre = fence(far_grad, node_sum, inner_pre)
    factors = [
        edges,
        inner_sender,
        cut_sender,
        inner_receiver,
        cut_receiver,
        inner_hidden,
        cut_hidden,
        inner_out,
        inner_pre,
    ]
    buffers = [pltpu.VMEM((rows, latent), BF16) for rows in (inner_rows, cut_rows) * 2]
    buffers += [pltpu.VMEM((inner_rows, latent), BF16)] * 2
    buffers.append(pltpu.SemaphoreType.DMA((len(buffers),)))
    cut_out, cut_pre, edge_send = line.run(
        cut_backward_kernel,
        [shaped(BF16, cut_rows, latent)] * 2 + [shaped(BF16, 2 * latent, latent)],
        [
            me,
            cut_receivers,
            agg_grad,
            far_grad,
            ct_edges,
            cut_normed,
            cut_scale,
            cut_slope,
            w_edge_out,
        ]
        + factors,
        [
            SMEM,
            all_spec(cut_receivers),
            all_spec(agg_grad),
            all_spec(far_grad),
            last_rows(ct_edges),
            all_spec(cut_normed),
            all_spec(cut_scale),
            all_spec(cut_slope),
            all_spec(w_edge_out),
        ]
        + [ANY] * len(factors),
        [rows_spec(latent)] * 2 + [rows_spec(latent, 2 * latent)],
        (1,),
        buffers,
    )
    edge_send, place, *node_parts = fence(edge_send, me, *node_parts)
    received = across(edge_send, domains, 1)
    node_own, node_sent = split(node_parts, 2)
    node_got = across(node_sent, domains, 4)
    edge_keep = line.run(
        edge_weights_kernel,
        shaped(BF16, 2 * latent, latent),
        [place, cut_out, cut_pre] + factors,
        [SMEM, VMEM, VMEM] + [ANY] * len(factors),
        scratch=buffers,
    )
    edge_own, edge_sent = split(fence(edge_keep, received), 1)
    edge_sent, inner_pre, cut_pre = fence(edge_sent, inner_pre, cut_pre)
    node_got = fence(node_got, edge_sent)[0]
    edge_got = across(edge_sent, domains, 2)
    node_sum = added(*node_own, node_got)
    for bit in bits[3:]:
        node_sum = added(*handed(node_sum, domains, bit))
    local_grad, outgoing_grad = line.run(
        input_grads_kernel,
        [shaped(F32, node_rows, latent), shaped(BF16, total_slots, latent)],
        [
            inner_senders,
            inner_receivers,
            cut_senders,
            cut_receivers,
            inner_pre,
            cut_pre,
            w_edge_in,
        ],
    )
    edge_got, node_sum, inner_pre, cut_pre, local_grad = fence(
        edge_got, node_sum, inner_pre, cut_pre, local_grad
    )
    edge_own, edge_sent = split([*edge_own, edge_got], 2)
    edge_got, *node_parts = fence(across(edge_sent, domains, 4), *handed(node_sum, domains, 2))
    edge_own, edge_sent = split([*edge_own, edge_got], 3)
    edge_got = across(edge_sent, domains, 8)
    node_parts = handed(joined(node_parts, 2), domains, 1)
    grad_edges = line.run(
        functools.partial(edge_grads_kernel, blocks=blocks),
        shaped(F32, *edges.shape),
        [ct_edges, inner_pre, cut_pre, w_edge_in],
        [
            rows_spec(latent),
            pl.BlockSpec((block, latent), lambda step: (jnp.minimum(step, blocks - 1), 0)),
            all_spec(cut_pre),
            pl.BlockSpec((latent, latent), lambda step: (0, 0)),
        ],
        [rows_spec(latent)],
        (blocks + 1,),
    )
    edge_got, grad_edges, outgoing_grad = fence(edge_got, grad_edges, outgoing_grad)
    edge_sum = added(*edge_own, edge_got)
    for bit in bits[4:]:
        own, sent = split([edge_sum], bit)
        edge_sum = added(*own, across(sent, domains, 1 << bit))
    for bit in bits[:3:-1]:
        edge_sum = joined(handed(edge_sum, domains, bit), bit)
    returned = exchange(outgoing_grad, domains)
    *edge_parts, node_sum, other_sum = fence(*handed(edge_sum, domains, 3), *node_parts)
    edge_parts = handed(joined(edge_parts, 3), domains, 2)
    node_sum = joined([node_sum, other_sum], 1)
    others = across(node_sum, domains, 1)
    *edge_parts, node_sum, others = fence(*edge_parts, node_sum, others)
    edge_sum = joined(edge_parts, 2)
    edge_parts = handed(edge_sum, domains, 1) + [across(edge_sum, domains, 1)]
    lower, left = place_of(0) == 0, place_of(1) == 0
    low_rows, high_rows = jnp.where(lower, node_sum, others), jnp.where(lower, others, node_sum)
    cut_at = 2 * latent - low_rows.shape[0]
    grad_node_in = jnp.concatenate([low_rows, high_rows[:cut_at]])
    grad_node_out = high_rows[cut_at:]
    mine, far, near, grad_node_in, grad_node_out, returned = fence(
        *edge_parts, grad_node_in, grad_node_out, returned
    )
    corner = across(far, domains, 1)
    grad_nodes = line.run(
        node_grads_kernel,
        shaped(F32, node_rows, latent),
        [self_grad, local_grad, asked_marks, returned],
    )
    own, other = [mine, far], [near, corner]
    low_half = [jnp.where(lower, one, two) for one, two in zip(own, other)]
    high_half = [jnp.where(lower, two, one) for one, two in zip(own, other)]
    grad_edge_in = jnp.concatenate(
        [
            jnp.where(left, low_half[0], low_half[1]),
            jnp.where(left, low_half[1], low_half[0]),
            jnp.where(left, high_half[0], high_half[1]),
        ]
    )
    grad_edge_out = jnp.where(left, high_half[1], high_half[0])
    return (
        new_nodes,
        new_edges,
        grad_nodes,
        grad_edges,
        grad_edge_in,
        grad_edge_out,
        grad_node_in,
        grad_node_out,
    )


def solution(mesh):
    placed = (
        P(("groups", "dom"), None),
        P(("groups", "dom"), None),
        P(("groups", "dom"), None),
        P(("groups", "dom")),
        P(("groups", "dom"), None),
        P(("groups", "dom")),
        P(),
        P(),
        P(),
        P(),
        P(("groups", "dom"), None),
        P(("groups", "dom"), None),
    )
    return jax.shard_map(
        shards,
        mesh=mesh,
        in_specs=placed,
        out_specs=(
            P(("groups", "dom"), None),
            P(("groups", "dom"), None),
            P(("groups", "dom"), None),
            P(("groups", "dom"), None),
            P("groups", None),
            P("groups", None),
            P("groups", None),
            P("groups", None),
        ),
        check_vma=False,
    )
```

```python
import functools

import jax
import jax.numpy as jnp
from jax import lax
from jax.experimental import pallas as pl
from jax.experimental.pallas import tpu as pltpu
from jax.sharding import PartitionSpec as P

BF16 = jnp.bfloat16
F32 = jnp.float32
VMEM_LIMIT = 60 * 1024 * 1024


def dot(left, right):
    return jnp.dot(left, right, preferred_element_type=F32)


def dot_rows(left, right):
    return lax.dot_general(left, right, (((0,), (0,)), ((), ())), preferred_element_type=F32)


def dot_cols(left, right):
    return lax.dot_general(left, right, (((1,), (1,)), ((), ())), preferred_element_type=F32)


def iota(shape, axis):
    return lax.broadcasted_iota(jnp.int32, shape, axis)


def marks(mask):
    return jnp.where(mask, 1.0, 0.0).astype(BF16)


def onehot(column, width):
    return marks(column == iota((column.shape[0], width), 1))


def to_column(row):
    count = row.shape[1]
    square = (count, count)
    kept = jnp.where(iota(square, 0) == iota(square, 1), row.astype(F32), 0.0)
    return jnp.sum(kept, axis=1, keepdims=True)


def slot_ranks(dest, domains):
    count = dest.shape[0]
    square = (count, count)
    dest_marks = onehot(dest, domains)
    before = dot(marks(iota(square, 0) > iota(square, 1)), dest_marks)
    return dest_marks, jnp.sum(before * dest_marks.astype(F32), axis=1, keepdims=True)


def pair_marks(first, second, width):
    pairs = first.shape[0]
    shape = (2 * pairs, pairs)
    edge, pair = iota(shape, 0), iota(shape, 1)
    mine = (edge >> 1) == pair
    even = marks(mine & ((edge & 1) == 0))
    odd = marks(mine & ((edge & 1) == 1))
    first_marks, second_marks = onehot(first, width), onehot(second, width)
    senders = dot(even, first_marks) + dot(odd, second_marks)
    receivers = dot(even, second_marks) + dot(odd, first_marks)
    return senders.astype(BF16), receivers.astype(BF16)


def normalise(values):
    centered = values - jnp.mean(values, axis=1, keepdims=True)
    inv_scale = lax.rsqrt(jnp.mean(centered * centered, axis=1, keepdims=True) + 1e-05)
    return centered * inv_scale, inv_scale


def activate(pre_hidden):
    gate = jax.nn.sigmoid(pre_hidden)
    return (pre_hidden * gate).astype(BF16), gate * (1.0 + pre_hidden * (1.0 - gate))


def norm_backward(upstream, normed, inv_scale):
    centered = (
        upstream
        - jnp.mean(upstream, axis=1, keepdims=True)
        - normed * jnp.mean(upstream * normed, axis=1, keepdims=True)
    )
    return (inv_scale * centered).astype(BF16)


def loading(source, buffer, sem):
    copy = pltpu.make_async_copy(source, buffer, sem)
    copy.start()
    return copy


def ask_kernel(dest_ref, remote_ref, ask_ref):
    domains, slots = ask_ref.shape
    dest_marks, rank = slot_ranks(to_column(dest_ref[...]).astype(jnp.int32), domains)
    rank_marks = jnp.where(rank == iota((rank.shape[0], slots), 1).astype(F32), 1.0, 0.0)
    wanted = (rank_marks * to_column(remote_ref[...])).astype(BF16)
    ask_ref[...] = dot_rows(dest_marks, wanted).astype(jnp.int32)


def reply_kernel(asked_hbm, nodes_ref, reply_ref, asked_marks_ref, asked_ref, sem):
    loading(asked_hbm, asked_ref, sem).wait()
    domains, slots = asked_ref.shape
    total = domains * slots
    shift = slots.bit_length() - 1
    spread = marks((iota((total, domains), 0) >> shift) == iota((total, domains), 1))
    listed = dot(spread, asked_ref[...].astype(F32).astype(BF16))
    at_slot = (iota((total, slots), 0) & (slots - 1)) == iota((total, slots), 1)
    column = jnp.sum(jnp.where(at_slot, listed, 0.0), axis=1, keepdims=True)
    node_rows = nodes_ref.shape[0]
    asked_marks = marks(column == iota((total, node_rows), 1).astype(F32))
    asked_marks_ref[...] = asked_marks
    reply_ref[...] = dot(asked_marks, nodes_ref[...]).astype(BF16)


def cut_marks_kernel(dest_ref, local_ref, senders_ref, receivers_ref, *, domains, slots):
    width = senders_ref.shape[1]
    base = width - domains * slots
    dest = to_column(dest_ref[...]).astype(jnp.int32)
    _, rank = slot_ranks(dest, domains)
    second = dest * slots + rank.astype(jnp.int32) + base
    first = to_column(local_ref[...]).astype(jnp.int32)
    senders, receivers = pair_marks(first, second, width)
    senders_ref[...] = senders
    receivers_ref[...] = receivers


def edge_forward(edge, sender, receiver, w_in_ref, w_out_ref):
    latent = edge.shape[1]
    pre_hidden = (
        dot(edge, w_in_ref[:latent])
        + dot(sender, w_in_ref[latent : 2 * latent])
        + dot(receiver, w_in_ref[2 * latent :])
    )
    hidden, slope = activate(pre_hidden)
    normed, inv_scale = normalise(dot(hidden, w_out_ref[...]))
    return hidden, slope, normed, inv_scale


def inner_forward_kernel(
    pairs_ref,
    edges_ref,
    nodes_ref,
    w_in_ref,
    w_out_ref,
    senders_ref,
    receivers_ref,
    sender_ref,
    receiver_ref,
    hidden_ref,
    slope_ref,
    normed_ref,
    scale_ref,
    total_ref,
):
    first, second = (to_column(pairs_ref[side : side + 1]).astype(jnp.int32) for side in range(2))
    senders, receivers = pair_marks(first, second, nodes_ref.shape[0])
    senders_ref[...] = senders
    receivers_ref[...] = receivers
    nodes = nodes_ref[...]
    sender = dot(senders, nodes).astype(BF16)
    receiver = dot(receivers, nodes).astype(BF16)
    sender_ref[...] = sender
    receiver_ref[...] = receiver
    hidden, slope, normed, inv_scale = edge_forward(
        edges_ref[...], sender, receiver, w_in_ref, w_out_ref
    )
    hidden_ref[...] = hidden
    slope_ref[...] = slope
    normed_ref[...] = normed
    scale_ref[...] = inv_scale
    part = dot_rows(receivers, normed.astype(BF16))

    @pl.when(pl.program_id(0) == 0)
    def _():
        total_ref[...] = part

    @pl.when(pl.program_id(0) > 0)
    def _():
        total_ref[...] += part


def cut_forward_kernel(
    senders_ref,
    receivers_ref,
    edges_ref,
    nodes_ref,
    far_hbm,
    w_in_ref,
    w_out_ref,
    inner_total_ref,
    sender_ref,
    receiver_ref,
    hidden_ref,
    slope_ref,
    normed_ref,
    scale_ref,
    total_ref,
    outgoing_ref,
    far_ref,
    sem,
):
    loading(far_hbm, far_ref, sem).wait()
    base = nodes_ref.shape[0]
    nodes, far = nodes_ref[...], far_ref[...]

    def rows_of(marks_ref):
        return (dot(marks_ref[:, :base], nodes) + dot(marks_ref[:, base:], far)).astype(BF16)

    sender, receiver = rows_of(senders_ref), rows_of(receivers_ref)
    sender_ref[...] = sender
    receiver_ref[...] = receiver
    hidden, slope, normed, inv_scale = edge_forward(
        edges_ref[...], sender, receiver, w_in_ref, w_out_ref
    )
    hidden_ref[...] = hidden
    slope_ref[...] = slope
    normed_ref[...] = normed
    scale_ref[...] = inv_scale
    message = normed.astype(BF16)
    total_ref[...] = inner_total_ref[...] + dot_rows(receivers_ref[:, :base], message)
    outgoing_ref[...] = dot_rows(receivers_ref[:, base:], message).astype(BF16)


def new_edges_kernel(edges_ref, inner_ref, cut_ref, out_ref):
    inner_rows = inner_ref.shape[0]

    def added(edge, normed):
        return (edge.astype(F32) + normed.astype(BF16).astype(F32)).astype(BF16)

    out_ref[:inner_rows] = added(edges_ref[:inner_rows], inner_ref[...])
    out_ref[inner_rows:] = added(edges_ref[inner_rows:], cut_ref[...])


def node_kernel(
    me_ref,
    incoming_hbm,
    asked_marks_ref,
    total_ref,
    nodes_ref,
    ct_ref,
    w_in_ref,
    w_out_ref,
    new_nodes_ref,
    self_grad_ref,
    agg_grad_ref,
    reply_ref,
    keep_ref,
    send_ref,
    incoming_ref,
    sem,
):
    loading(incoming_hbm, incoming_ref, sem).wait()
    latent = nodes_ref.shape[1]
    half = latent // 2
    nodes, asked_marks = nodes_ref[...], asked_marks_ref[...]
    aggregate = (total_ref[...] + dot_rows(asked_marks, incoming_ref[...])).astype(BF16)
    pre_hidden = dot(nodes, w_in_ref[:latent]) + dot(aggregate, w_in_ref[latent:])
    hidden, slope = activate(pre_hidden)
    normed, inv_scale = normalise(dot(hidden, w_out_ref[...]))
    upstream = ct_ref[...].astype(F32)
    grad_out = norm_backward(upstream, normed, inv_scale)
    grad_pre = (dot_cols(grad_out, w_out_ref[...]) * slope).astype(BF16)
    agg_grad = dot_cols(grad_pre, w_in_ref[latent:]).astype(BF16)
    agg_grad_ref[...] = agg_grad
    reply_ref[...] = dot(asked_marks, agg_grad).astype(BF16)
    self_grad_ref[...] = upstream + dot_cols(grad_pre, w_in_ref[:latent])
    new_nodes_ref[...] = (nodes.astype(F32) + normed).astype(BF16)

    def fill(low_ref, high_ref):
        by_aggregate = dot_rows(aggregate, grad_pre).astype(BF16)
        low_ref[:latent] = dot_rows(nodes, grad_pre).astype(BF16)
        low_ref[latent:] = by_aggregate[:half]
        high_ref[:half] = by_aggregate[half:]
        high_ref[half:] = dot_rows(hidden, grad_out).astype(BF16)

    @pl.when((me_ref[0] & 1) == 0)
    def _():
        fill(keep_ref, send_ref)

    @pl.when((me_ref[0] & 1) != 0)
    def _():
        fill(send_ref, keep_ref)


def edge_backward(ct, target_grads, normed, inv_scale, slope, w_out):
    grad_out = norm_backward(ct.astype(F32) + target_grads, normed, inv_scale)
    return grad_out, (dot_cols(grad_out, w_out) * slope).astype(BF16)


def inner_backward_kernel(
    me_ref,
    receivers_ref,
    agg_grad_ref,
    ct_ref,
    normed_ref,
    scale_ref,
    slope_ref,
    w_out_ref,
    edges_ref,
    sender_ref,
    receiver_ref,
    hidden_ref,
    grad_out_ref,
    grad_pre_ref,
    part_ref,
):
    latent = w_out_ref.shape[1]
    grad_out, grad_pre = edge_backward(
        ct_ref[...],
        dot(receivers_ref[...], agg_grad_ref[...]),
        normed_ref[...],
        scale_ref[...],
        slope_ref[...],
        w_out_ref[...],
    )
    grad_out_ref[...] = grad_out
    grad_pre_ref[...] = grad_pre

    @pl.when(pl.program_id(0) == 0)
    def _():
        part_ref[...] = jnp.zeros_like(part_ref)

    @pl.when((me_ref[0] & 1) != 0)
    def _():
        part_ref[:latent] += dot_rows(edges_ref[...], grad_pre)
        part_ref[latent:] += dot_rows(sender_ref[...], grad_pre)

    @pl.when((me_ref[0] & 1) == 0)
    def _():
        part_ref[:latent] += dot_rows(receiver_ref[...], grad_pre)
        part_ref[latent:] += dot_rows(hidden_ref[...], grad_out)


def fetch_factors(half, sources, buffers, sems, wait):
    edges, inner_sender, cut_sender, inner_receiver, cut_receiver = sources[:5]
    inner_hidden, cut_hidden, inner_out, inner_pre = sources[5:]
    inner_rows, cut_rows = inner_pre.shape[0], cut_sender.shape[0]
    inner_edges = edges.at[pl.ds(0, inner_rows)]
    cut_edges = edges.at[pl.ds(inner_rows, cut_rows)]
    low = [inner_edges, cut_edges, inner_sender, cut_sender, inner_pre, inner_pre]
    high = [inner_receiver, cut_receiver, inner_hidden, cut_hidden, inner_pre, inner_out]

    def each(parts):
        for index, (source, buffer) in enumerate(zip(parts, buffers)):
            copy = pltpu.make_async_copy(source, buffer, sems.at[index])
            if wait:
                copy.wait()
            else:
                copy.start()

    @pl.when(half == 0)
    def _():
        each(low)

    @pl.when(half != 0)
    def _():
        each(high)


def place_rows(me_ref, index, latent):
    return pl.ds(pl.multiple_of((index ^ ((me_ref[0] >> 1) & 1)) * latent, latent), latent)


def cut_backward_kernel(
    me_ref,
    receivers_ref,
    agg_grad_ref,
    far_grad_hbm,
    ct_ref,
    normed_ref,
    scale_ref,
    slope_ref,
    w_out_ref,
    part_hbm,
    edges_ref,
    sender_ref,
    receiver_ref,
    hidden_ref,
    grad_out_ref,
    grad_pre_ref,
    out_ref,
    far_grad_ref,
    part_ref,
    sems,
):
    latent = w_out_ref.shape[1]
    far_copy = loading(far_grad_hbm, far_grad_ref, sems.at[0])
    part_copy = loading(part_hbm, part_ref, sems.at[1])
    base = agg_grad_ref.shape[0]
    near_grads = dot(receivers_ref[:, :base], agg_grad_ref[...])
    far_copy.wait()
    target = near_grads + dot(receivers_ref[:, base:], far_grad_ref[...])
    grad_out, grad_pre = edge_backward(
        ct_ref[...], target, normed_ref[...], scale_ref[...], slope_ref[...], w_out_ref[...]
    )
    grad_out_ref[...] = grad_out
    grad_pre_ref[...] = grad_pre
    part_copy.wait()

    def put(index, value):
        rows = pl.ds(index * latent, latent)
        out_ref[place_rows(me_ref, index, latent)] = (part_ref[rows] + value).astype(BF16)

    @pl.when((me_ref[0] & 1) != 0)
    def _():
        put(0, dot_rows(edges_ref[...], grad_pre))
        put(1, dot_rows(sender_ref[...], grad_pre))

    @pl.when((me_ref[0] & 1) == 0)
    def _():
        put(0, dot_rows(receiver_ref[...], grad_pre))
        put(1, dot_rows(hidden_ref[...], grad_out))


def edge_weights_kernel(me_ref, cut_out_ref, cut_pre_ref, *refs):
    sources, out_ref, rest = refs[:9], refs[9], refs[10:]
    buffers, sems = rest[:-1], rest[-1]
    half = me_ref[0] & 1
    fetch_factors(half, sources, buffers, sems, False)
    fetch_factors(half, sources, buffers, sems, True)
    cut_pre, cut_out = cut_pre_ref[...], cut_out_ref[...]
    latent = cut_pre.shape[1]
    first, first_cut, second, second_cut, first_right, second_right = buffers
    chosen = jnp.where(half == 0, cut_pre.astype(F32), cut_out.astype(F32)).astype(BF16)
    out_ref[place_rows(me_ref, 0, latent)] = (
        dot_rows(first[...], first_right[...]) + dot_rows(first_cut[...], cut_pre)
    ).astype(BF16)
    out_ref[place_rows(me_ref, 1, latent)] = (
        dot_rows(second[...], second_right[...]) + dot_rows(second_cut[...], chosen)
    ).astype(BF16)


def input_grads_kernel(
    inner_senders_ref,
    inner_receivers_ref,
    cut_senders_ref,
    cut_receivers_ref,
    inner_pre_ref,
    cut_pre_ref,
    w_in_ref,
    local_ref,
    outgoing_ref,
):
    latent = inner_pre_ref.shape[1]
    base = inner_senders_ref.shape[1]
    inner_pre, cut_pre = inner_pre_ref[...], cut_pre_ref[...]
    w_sender, w_receiver = w_in_ref[latent : 2 * latent], w_in_ref[2 * latent :]

    def summed(inner_marks_ref, cut_marks_ref):
        return (
            dot_rows(inner_marks_ref[...], inner_pre) + dot_rows(cut_marks_ref[:, :base], cut_pre)
        ).astype(BF16)

    outgoing_ref[...] = (
        dot_cols(dot_rows(cut_senders_ref[:, base:], cut_pre).astype(BF16), w_sender)
        + dot_cols(dot_rows(cut_receivers_ref[:, base:], cut_pre).astype(BF16), w_receiver)
    ).astype(BF16)
    local_ref[...] = dot_cols(summed(inner_senders_ref, cut_senders_ref), w_sender) + dot_cols(
        summed(inner_receivers_ref, cut_receivers_ref), w_receiver
    )


def edge_grads_kernel(ct_ref, inner_pre_ref, cut_pre_ref, w_edge_ref, out_ref, *, blocks):
    inside = pl.program_id(0) < blocks

    @pl.when(inside)
    def _():
        out_ref[...] = ct_ref[...].astype(F32) + dot_cols(inner_pre_ref[...], w_edge_ref[...])

    @pl.when(jnp.logical_not(inside))
    def _():
        out_ref[...] = ct_ref[...].astype(F32) + dot_cols(cut_pre_ref[...], w_edge_ref[...])


def node_grads_kernel(
    self_ref, local_ref, asked_marks_ref, returned_hbm, out_ref, returned_ref, sem
):
    loading(returned_hbm, returned_ref, sem).wait()
    out_ref[...] = (
        self_ref[...] + local_ref[...] + dot_rows(asked_marks_ref[...], returned_ref[...])
    )


VMEM = pl.BlockSpec(memory_space=pltpu.VMEM)
HBM = pl.BlockSpec(memory_space=pltpu.HBM)
SMEM = pl.BlockSpec(memory_space=pltpu.SMEM)
ANY = pl.BlockSpec(memory_space=pl.ANY)


def shaped(dtype, *shape):
    return jax.ShapeDtypeStruct(shape, dtype)


class Line:
    def __init__(self):
        self.last = None

    def run(self, body, outs, ins, specs=None, out_specs=None, grid=None, scratch=()):
        single = not isinstance(outs, (list, tuple))
        out_shape = [outs] if single else list(outs)
        specs = [VMEM] * len(ins) if specs is None else list(specs)
        count, extra = len(ins), {} if grid is None else {"grid": grid}
        ins = list(ins)
        if self.last is not None:
            ins.append(self.last)
            specs.append(ANY)

        def ordered(*refs):
            return body(*refs[:count], *refs[len(ins) :])

        result = pl.pallas_call(
            ordered,
            out_shape=out_shape,
            in_specs=specs,
            out_specs=[VMEM] * len(out_shape) if out_specs is None else out_specs,
            scratch_shapes=scratch,
            compiler_params=pltpu.CompilerParams(vmem_limit_bytes=VMEM_LIMIT),
            cost_estimate=pl.CostEstimate(flops=1, bytes_accessed=1, transcendentals=0),
            **extra,
        )(*ins)
        self.last = result[-1]
        return result[0] if single else result


def index_bits(devices):
    return list(range(devices.bit_length() - 1))


def across(rows, devices, mask):
    return lax.ppermute(rows, "dom", [(device, device ^ mask) for device in range(devices)])


def fence(*values):
    return lax.optimization_barrier(values)


def place_of(bit):
    return (lax.axis_index("dom") >> bit) & 1


def split(parts, bit):
    place = place_of(bit)
    halves = [part.reshape(2, part.shape[0] // 2, part.shape[1]) for part in parts]
    own = [lax.dynamic_index_in_dim(half, place, 0, False) for half in halves]
    sent = [lax.dynamic_index_in_dim(half, 1 - place, 0, False) for half in halves]
    return own, added(*sent)


def handed(rows, devices, bit):
    return [rows, across(rows, devices, 1 << bit)]


def added(*parts):
    return sum(part.astype(F32) for part in parts).astype(BF16)


def joined(parts, bit):
    orders = [jnp.concatenate(parts), jnp.concatenate(parts[::-1])]
    return jnp.where(place_of(bit) == 0, *orders)


def put_quarter(rows, piece, quarter):
    start = (jnp.minimum(quarter, 2) * piece.shape[0], 0)
    kept = lax.dynamic_slice(rows, start, piece.shape)
    return lax.dynamic_update_slice(rows, jnp.where(quarter < 3, piece, kept), start)


def exchange(rows, domains):
    shape = rows.shape
    split = rows.reshape((domains, shape[0] // domains) + shape[1:])
    return lax.all_to_all(split, "dom", split_axis=0, concat_axis=0, tiled=True).reshape(shape)


def shards(
    nodes,
    edges,
    inner_pairs,
    cut_local,
    cut_dest,
    cut_remote,
    w_edge_in,
    w_edge_out,
    w_node_in,
    w_node_out,
    ct_nodes,
    ct_edges,
):
    domains = lax.axis_size("dom")
    node_rows, latent = nodes.shape
    inner_count, cut_count = inner_pairs.shape[0], cut_local.shape[0]
    inner_rows, cut_rows = 2 * inner_count, 2 * cut_count
    slots = max(2, 2 * cut_count // domains)
    total_slots = domains * slots
    table = node_rows + total_slots
    me = lax.axis_index("dom").reshape(1)
    line = Line()

    ask = line.run(
        ask_kernel, shaped(jnp.int32, domains, slots), [cut_dest.reshape(1, -1), cut_remote.reshape(1, -1)]
    )
    asked = lax.all_to_all(ask, "dom", split_axis=0, concat_axis=0, tiled=True)
    cut_senders, cut_receivers = line.run(
        functools.partial(cut_marks_kernel, domains=domains, slots=slots),
        [shaped(BF16, cut_rows, table)] * 2,
        [cut_dest.reshape(1, -1), cut_local.reshape(1, -1)],
    )
    reply, asked_marks = line.run(
        reply_kernel,
        [shaped(BF16, total_slots, latent), shaped(BF16, total_slots, node_rows)],
        [asked, nodes],
        [HBM, VMEM],
        scratch=[pltpu.VMEM(asked.shape, jnp.int32), pltpu.SemaphoreType.DMA],
    )
    far = exchange(reply, domains)

    block = cut_rows
    blocks = inner_rows // block

    def rows_spec(width, rows=block):
        return pl.BlockSpec((rows, width), lambda step: (step, 0))

    def all_spec(array):
        return pl.BlockSpec(array.shape, lambda step: (0, 0))

    saved_widths = [node_rows, node_rows, latent, latent, latent, latent, latent, 1]
    saved_types = [BF16, BF16, BF16, BF16, BF16, F32, F32, F32]
    (
        inner_senders,
        inner_receivers,
        inner_sender,
        inner_receiver,
        inner_hidden,
        inner_slope,
        inner_normed,
        inner_scale,
        inner_total,
    ) = line.run(
        inner_forward_kernel,
        [shaped(kind, inner_rows, width) for kind, width in zip(saved_types, saved_widths)]
        + [shaped(F32, node_rows, latent)],
        [inner_pairs.T, edges, nodes, w_edge_in, w_edge_out],
        [
            pl.BlockSpec((2, block // 2), lambda step: (0, step)),
            rows_spec(latent),
            all_spec(nodes),
            all_spec(w_edge_in),
            all_spec(w_edge_out),
        ],
        [rows_spec(width) for width in saved_widths] + [all_spec(nodes)],
        (blocks,),
    )

    def last_rows(array):
        last = array.shape[0] // block - 1
        return pl.BlockSpec((block, array.shape[1]), lambda step: (last, 0))

    (
        cut_sender,
        cut_receiver,
        cut_hidden,
        cut_slope,
        cut_normed,
        cut_scale,
        total,
        outgoing,
    ) = line.run(
        cut_forward_kernel,
        [shaped(kind, cut_rows, width) for kind, width in zip(saved_types, saved_widths)][2:]
        + [shaped(F32, node_rows, latent), shaped(BF16, total_slots, latent)],
        [
            cut_senders,
            cut_receivers,
            edges,
            nodes,
            far,
            w_edge_in,
            w_edge_out,
            inner_total,
        ],
        [
            all_spec(cut_senders),
            all_spec(cut_receivers),
            last_rows(edges),
            all_spec(nodes),
            HBM,
            all_spec(w_edge_in),
            all_spec(w_edge_out),
            all_spec(inner_total),
        ],
        [rows_spec(width) for width in saved_widths[2:]]
        + [all_spec(nodes), rows_spec(latent, total_slots)],
        (1,),
        [pltpu.VMEM(far.shape, BF16), pltpu.SemaphoreType.DMA],
    )
    incoming = exchange(outgoing, domains)
    new_edges = line.run(
        new_edges_kernel,
        shaped(BF16, *edges.shape),
        [edges, inner_normed, cut_normed],
    )
    (
        new_nodes,
        self_grad,
        agg_grad,
        grad_reply,
        node_keep,
        node_send,
    ) = line.run(
        node_kernel,
        [
            shaped(BF16, node_rows, latent),
            shaped(F32, node_rows, latent),
            shaped(BF16, node_rows, latent),
            shaped(BF16, total_slots, latent),
        ]
        + [shaped(BF16, 3 * latent // 2, latent)] * 2,
        [me, incoming, asked_marks, total, nodes, ct_nodes, w_node_in, w_node_out],
        [SMEM, HBM] + [VMEM] * 6,
        scratch=[pltpu.VMEM(incoming.shape, BF16), pltpu.SemaphoreType.DMA],
    )
    far_grad = exchange(grad_reply, domains)
    node_sum = added(node_keep, across(node_send, domains, 1))
    inner_out, inner_pre, inner_part = line.run(
        inner_backward_kernel,
        [shaped(BF16, inner_rows, latent)] * 2 + [shaped(F32, 2 * latent, latent)],
        [
            me,
            inner_receivers,
            agg_grad,
            ct_edges,
            inner_normed,
            inner_scale,
            inner_slope,
            w_edge_out,
            edges,
            inner_sender,
            inner_receiver,
            inner_hidden,
        ],
        [
            SMEM,
            rows_spec(node_rows),
            all_spec(agg_grad),
            rows_spec(latent),
            rows_spec(latent),
            rows_spec(1),
            rows_spec(latent),
            all_spec(w_edge_out),
        ]
        + [rows_spec(latent)] * 4,
        [rows_spec(latent)] * 2
        + [pl.BlockSpec((2 * latent, latent), lambda step: (0, 0))],
        (blocks,),
    )
    bits = index_bits(domains)
    node_own, node_sent = split([node_sum], 1)
    node_parts = [*node_own, across(node_sent, domains, 2)]
    far_grad, node_sum, inner_part = fence(far_grad, node_sum, inner_part)
    factors = [
        edges,
        inner_sender,
        cut_sender,
        inner_receiver,
        cut_receiver,
        inner_hidden,
        cut_hidden,
        inner_out,
        inner_pre,
    ]
    buffers = [pltpu.VMEM((rows, latent), BF16) for rows in (inner_rows, cut_rows) * 2]
    buffers += [pltpu.VMEM((inner_rows, latent), BF16)] * 2
    buffers.append(pltpu.SemaphoreType.DMA((len(buffers),)))
    cut_out, cut_pre, edge_send = line.run(
        cut_backward_kernel,
        [shaped(BF16, cut_rows, latent)] * 2 + [shaped(BF16, 2 * latent, latent)],
        [
            me,
            cut_receivers,
            agg_grad,
            far_grad,
            ct_edges,
            cut_normed,
            cut_scale,
            cut_slope,
            w_edge_out,
            inner_part,
            edges,
            cut_sender,
            cut_receiver,
            cut_hidden,
        ],
        [
            SMEM,
            all_spec(cut_receivers),
            all_spec(agg_grad),
            HBM,
            last_rows(ct_edges),
            all_spec(cut_normed),
            all_spec(cut_scale),
            all_spec(cut_slope),
            all_spec(w_edge_out),
            HBM,
            last_rows(edges),
        ]
        + [all_spec(cut_sender)] * 3,
        [rows_spec(latent)] * 2 + [rows_spec(latent, 2 * latent)],
        (1,),
        [
            pltpu.VMEM(far_grad.shape, BF16),
            pltpu.VMEM(inner_part.shape, F32),
            pltpu.SemaphoreType.DMA((2,)),
        ],
    )
    edge_send, place, *node_parts = fence(edge_send, me, *node_parts)
    received = across(edge_send, domains, 1)
    node_own, node_sent = split(node_parts, 2)
    node_got = across(node_sent, domains, 4)
    edge_keep = line.run(
        edge_weights_kernel,
        shaped(BF16, 2 * latent, latent),
        [place, cut_out, cut_pre] + factors,
        [SMEM, VMEM, VMEM] + [ANY] * len(factors),
        scratch=buffers,
    )
    edge_keep, received = fence(edge_keep, received)
    edge_own = [edge_keep[:latent], received[:latent]]
    edge_sent = added(edge_keep[latent:], received[latent:])
    edge_sent, inner_pre, cut_pre = fence(edge_sent, inner_pre, cut_pre)
    node_got = fence(node_got, edge_sent)[0]
    edge_got = across(edge_sent, domains, 2)
    node_sum = added(*node_own, node_got)
    for bit in bits[3:]:
        node_sum = added(*handed(node_sum, domains, bit))
    local_grad, outgoing_grad = line.run(
        input_grads_kernel,
        [shaped(F32, node_rows, latent), shaped(BF16, total_slots, latent)],
        [
            inner_senders,
            inner_receivers,
            cut_senders,
            cut_receivers,
            inner_pre,
            cut_pre,
            w_edge_in,
        ],
    )
    edge_got, node_sum, inner_pre, cut_pre, local_grad = fence(
        edge_got, node_sum, inner_pre, cut_pre, local_grad
    )
    edge_own, edge_sent = split([*edge_own, edge_got], 2)
    edge_got = across(edge_sent, domains, 4)
    grad_edges = line.run(
        functools.partial(edge_grads_kernel, blocks=blocks),
        shaped(F32, *edges.shape),
        [ct_edges, inner_pre, cut_pre, w_edge_in],
        [
            rows_spec(latent),
            pl.BlockSpec((block, latent), lambda step: (jnp.minimum(step, blocks - 1), 0)),
            all_spec(cut_pre),
            pl.BlockSpec((latent, latent), lambda step: (0, 0)),
        ],
        [rows_spec(latent)],
        (blocks + 1,),
    )
    edge_got, node_sum, grad_edges = fence(edge_got, node_sum, grad_edges)
    edge_own, edge_sent = split([*edge_own, edge_got], 3)
    edge_got, *node_parts = fence(across(edge_sent, domains, 8), *handed(node_sum, domains, 2))
    edge_sum = added(*edge_own, edge_got)
    for bit in bits[4:]:
        own, sent = split([edge_sum], bit)
        edge_sum = added(*own, across(sent, domains, 1 << bit))
    for bit in bits[:3:-1]:
        edge_sum = joined(handed(edge_sum, domains, bit), bit)
    node_parts = handed(joined(node_parts, 2), domains, 1)
    edge_parts = fence(*handed(edge_sum, domains, 3))
    edge_parts = handed(joined(edge_parts, 3), domains, 2)
    *edge_parts, node_sum, other_sum, outgoing_grad = fence(
        *edge_parts, *node_parts, outgoing_grad
    )
    edge_sum = joined(edge_parts, 2)
    node_sum = joined([node_sum, other_sum], 1)
    far, near = across(edge_sum, domains, 2), across(edge_sum, domains, 1)
    others = across(node_sum, domains, 1)
    returned = exchange(outgoing_grad, domains)
    lower = place_of(0) == 0
    low_rows, high_rows = jnp.where(lower, node_sum, others), jnp.where(lower, others, node_sum)
    cut_at = 2 * latent - low_rows.shape[0]
    grad_node_in = jnp.concatenate([low_rows, high_rows[:cut_at]])
    grad_node_out = high_rows[cut_at:]
    mine = place_of(0) * 2 + place_of(1)
    rows = put_quarter(jnp.zeros((3 * latent, latent), BF16), edge_sum, mine)
    rows = put_quarter(rows, near, mine ^ 2)
    far, near, edge_sum, rows, grad_node_in, grad_node_out, returned = fence(
        far, near, edge_sum, rows, grad_node_in, grad_node_out, returned
    )
    corner = across(far, domains, 1)
    rows = put_quarter(rows, far, mine ^ 1)
    last = jnp.where(mine == 3, edge_sum, jnp.where(mine == 1, near, far))
    grad_nodes = line.run(
        node_grads_kernel,
        shaped(F32, node_rows, latent),
        [self_grad, local_grad, asked_marks, returned],
        [VMEM, VMEM, VMEM, HBM],
        scratch=[pltpu.VMEM(returned.shape, BF16), pltpu.SemaphoreType.DMA],
    )
    corner, rows, last, grad_nodes = fence(corner, rows, last, grad_nodes)
    grad_edge_in = put_quarter(rows, corner, mine ^ 3)
    grad_edge_out = jnp.where(mine == 0, corner, last)
    return (
        new_nodes,
        new_edges,
        grad_nodes,
        grad_edges,
        grad_edge_in,
        grad_edge_out,
        grad_node_in,
        grad_node_out,
    )


def solution(mesh):
    placed = (
        P(("groups", "dom"), None),
        P(("groups", "dom"), None),
        P(("groups", "dom"), None),
        P(("groups", "dom")),
        P(("groups", "dom"), None),
        P(("groups", "dom")),
        P(),
        P(),
        P(),
        P(),
        P(("groups", "dom"), None),
        P(("groups", "dom"), None),
    )
    return jax.shard_map(
        shards,
        mesh=mesh,
        in_specs=placed,
        out_specs=(
            P(("groups", "dom"), None),
            P(("groups", "dom"), None),
            P(("groups", "dom"), None),
            P(("groups", "dom"), None),
            P("groups", None),
            P("groups", None),
            P("groups", None),
            P("groups", None),
        ),
        check_vma=False,
    )
```

```python
import functools

import jax
import jax.numpy as jnp
from jax import lax
from jax.experimental import pallas as pl
from jax.experimental.pallas import tpu as pltpu
from jax.sharding import PartitionSpec as P

BF16 = jnp.bfloat16
F32 = jnp.float32
VMEM_LIMIT = 60 * 1024 * 1024


def dot(left, right):
    return jnp.dot(left, right, preferred_element_type=F32)


def dot_rows(left, right):
    return lax.dot_general(left, right, (((0,), (0,)), ((), ())), preferred_element_type=F32)


def dot_cols(left, right):
    return lax.dot_general(left, right, (((1,), (1,)), ((), ())), preferred_element_type=F32)


def iota(shape, axis):
    return lax.broadcasted_iota(jnp.int32, shape, axis)


def marks(mask):
    return jnp.where(mask, 1.0, 0.0).astype(BF16)


def onehot(column, width):
    return marks(column == iota((column.shape[0], width), 1))


def to_column(row):
    count = row.shape[1]
    square = (count, count)
    kept = jnp.where(iota(square, 0) == iota(square, 1), row.astype(F32), 0.0)
    return jnp.sum(kept, axis=1, keepdims=True)


def slot_ranks(dest, domains):
    count = dest.shape[0]
    square = (count, count)
    dest_marks = onehot(dest, domains)
    before = dot(marks(iota(square, 0) > iota(square, 1)), dest_marks)
    return dest_marks, jnp.sum(before * dest_marks.astype(F32), axis=1, keepdims=True)


def pair_marks(first, second, width):
    pairs = first.shape[0]
    shape = (2 * pairs, pairs)
    edge, pair = iota(shape, 0), iota(shape, 1)
    mine = (edge >> 1) == pair
    even = marks(mine & ((edge & 1) == 0))
    odd = marks(mine & ((edge & 1) == 1))
    first_marks, second_marks = onehot(first, width), onehot(second, width)
    senders = dot(even, first_marks) + dot(odd, second_marks)
    receivers = dot(even, second_marks) + dot(odd, first_marks)
    return senders.astype(BF16), receivers.astype(BF16)


def normalise(values):
    centered = values - jnp.mean(values, axis=1, keepdims=True)
    inv_scale = lax.rsqrt(jnp.mean(centered * centered, axis=1, keepdims=True) + 1e-05)
    return centered * inv_scale, inv_scale


def activate(pre_hidden):
    gate = jax.nn.sigmoid(pre_hidden)
    return (pre_hidden * gate).astype(BF16), gate * (1.0 + pre_hidden * (1.0 - gate))


def norm_backward(upstream, normed, inv_scale):
    centered = (
        upstream
        - jnp.mean(upstream, axis=1, keepdims=True)
        - normed * jnp.mean(upstream * normed, axis=1, keepdims=True)
    )
    return (inv_scale * centered).astype(BF16)


def ask_kernel(dest_ref, remote_ref, ask_ref):
    domains, slots = ask_ref.shape
    dest_marks, rank = slot_ranks(to_column(dest_ref[...]).astype(jnp.int32), domains)
    rank_marks = jnp.where(rank == iota((rank.shape[0], slots), 1).astype(F32), 1.0, 0.0)
    wanted = (rank_marks * to_column(remote_ref[...])).astype(BF16)
    ask_ref[...] = dot_rows(dest_marks, wanted).astype(jnp.int32)


def reply_kernel(asked_ref, nodes_ref, reply_ref, asked_marks_ref):
    domains, slots = asked_ref.shape
    total = domains * slots
    shift = slots.bit_length() - 1
    spread = marks((iota((total, domains), 0) >> shift) == iota((total, domains), 1))
    listed = dot(spread, asked_ref[...].astype(F32).astype(BF16))
    at_slot = (iota((total, slots), 0) & (slots - 1)) == iota((total, slots), 1)
    column = jnp.sum(jnp.where(at_slot, listed, 0.0), axis=1, keepdims=True)
    node_rows = nodes_ref.shape[0]
    asked_marks = marks(column == iota((total, node_rows), 1).astype(F32))
    asked_marks_ref[...] = asked_marks
    reply_ref[...] = dot(asked_marks, nodes_ref[...]).astype(BF16)


def cut_marks_kernel(dest_ref, local_ref, senders_ref, receivers_ref, *, domains, slots):
    width = senders_ref.shape[1]
    base = width - domains * slots
    dest = to_column(dest_ref[...]).astype(jnp.int32)
    _, rank = slot_ranks(dest, domains)
    second = dest * slots + rank.astype(jnp.int32) + base
    first = to_column(local_ref[...]).astype(jnp.int32)
    senders, receivers = pair_marks(first, second, width)
    senders_ref[...] = senders
    receivers_ref[...] = receivers


def edge_forward(edge, sender, receiver, w_in_ref, w_out_ref):
    latent = edge.shape[1]
    pre_hidden = (
        dot(edge, w_in_ref[:latent])
        + dot(sender, w_in_ref[latent : 2 * latent])
        + dot(receiver, w_in_ref[2 * latent :])
    )
    hidden, slope = activate(pre_hidden)
    normed, inv_scale = normalise(dot(hidden, w_out_ref[...]))
    return hidden, slope, normed, inv_scale


def inner_forward_kernel(
    pairs_ref,
    edges_ref,
    nodes_ref,
    w_in_ref,
    w_out_ref,
    senders_ref,
    receivers_ref,
    sender_ref,
    receiver_ref,
    hidden_ref,
    slope_ref,
    normed_ref,
    scale_ref,
    total_ref,
):
    first, second = (to_column(pairs_ref[side : side + 1]).astype(jnp.int32) for side in range(2))
    senders, receivers = pair_marks(first, second, nodes_ref.shape[0])
    senders_ref[...] = senders
    receivers_ref[...] = receivers
    nodes = nodes_ref[...]
    sender = dot(senders, nodes).astype(BF16)
    receiver = dot(receivers, nodes).astype(BF16)
    sender_ref[...] = sender
    receiver_ref[...] = receiver
    hidden, slope, normed, inv_scale = edge_forward(
        edges_ref[...], sender, receiver, w_in_ref, w_out_ref
    )
    hidden_ref[...] = hidden
    slope_ref[...] = slope
    normed_ref[...] = normed
    scale_ref[...] = inv_scale
    part = dot_rows(receivers, normed.astype(BF16))

    @pl.when(pl.program_id(0) == 0)
    def _():
        total_ref[...] = part

    @pl.when(pl.program_id(0) > 0)
    def _():
        total_ref[...] += part


def cut_forward_kernel(
    senders_ref,
    receivers_ref,
    edges_ref,
    nodes_ref,
    far_ref,
    w_in_ref,
    w_out_ref,
    inner_total_ref,
    sender_ref,
    receiver_ref,
    hidden_ref,
    slope_ref,
    normed_ref,
    scale_ref,
    total_ref,
    outgoing_ref,
):
    base = nodes_ref.shape[0]
    nodes, far = nodes_ref[...], far_ref[...]

    def rows_of(marks_ref):
        return (dot(marks_ref[:, :base], nodes) + dot(marks_ref[:, base:], far)).astype(BF16)

    sender, receiver = rows_of(senders_ref), rows_of(receivers_ref)
    sender_ref[...] = sender
    receiver_ref[...] = receiver
    hidden, slope, normed, inv_scale = edge_forward(
        edges_ref[...], sender, receiver, w_in_ref, w_out_ref
    )
    hidden_ref[...] = hidden
    slope_ref[...] = slope
    normed_ref[...] = normed
    scale_ref[...] = inv_scale
    message = normed.astype(BF16)
    total_ref[...] = inner_total_ref[...] + dot_rows(receivers_ref[:, :base], message)
    outgoing_ref[...] = dot_rows(receivers_ref[:, base:], message).astype(BF16)


def new_edges_kernel(edges_ref, inner_ref, cut_ref, out_ref):
    inner_rows = inner_ref.shape[0]

    def added(edge, normed):
        return (edge.astype(F32) + normed.astype(BF16).astype(F32)).astype(BF16)

    out_ref[:inner_rows] = added(edges_ref[:inner_rows], inner_ref[...])
    out_ref[inner_rows:] = added(edges_ref[inner_rows:], cut_ref[...])


def node_kernel(
    me_ref,
    incoming_ref,
    asked_marks_ref,
    total_ref,
    nodes_ref,
    ct_ref,
    w_in_ref,
    w_out_ref,
    new_nodes_ref,
    self_grad_ref,
    agg_grad_ref,
    reply_ref,
    keep_ref,
    send_ref,
):
    latent = nodes_ref.shape[1]
    half = latent // 2
    nodes, asked_marks = nodes_ref[...], asked_marks_ref[...]
    aggregate = (total_ref[...] + dot_rows(asked_marks, incoming_ref[...])).astype(BF16)
    pre_hidden = dot(nodes, w_in_ref[:latent]) + dot(aggregate, w_in_ref[latent:])
    hidden, slope = activate(pre_hidden)
    normed, inv_scale = normalise(dot(hidden, w_out_ref[...]))
    upstream = ct_ref[...].astype(F32)
    grad_out = norm_backward(upstream, normed, inv_scale)
    grad_pre = (dot_cols(grad_out, w_out_ref[...]) * slope).astype(BF16)
    agg_grad = dot_cols(grad_pre, w_in_ref[latent:]).astype(BF16)
    agg_grad_ref[...] = agg_grad
    reply_ref[...] = dot(asked_marks, agg_grad).astype(BF16)
    self_grad_ref[...] = upstream + dot_cols(grad_pre, w_in_ref[:latent])
    new_nodes_ref[...] = (nodes.astype(F32) + normed).astype(BF16)

    def fill(low_ref, high_ref):
        by_aggregate = dot_rows(aggregate, grad_pre).astype(BF16)
        low_ref[:latent] = dot_rows(nodes, grad_pre).astype(BF16)
        low_ref[latent:] = by_aggregate[:half]
        high_ref[:half] = by_aggregate[half:]
        high_ref[half:] = dot_rows(hidden, grad_out).astype(BF16)

    @pl.when((me_ref[0] & 1) == 0)
    def _():
        fill(keep_ref, send_ref)

    @pl.when((me_ref[0] & 1) != 0)
    def _():
        fill(send_ref, keep_ref)


def edge_backward(ct, target_grads, normed, inv_scale, slope, w_out):
    grad_out = norm_backward(ct.astype(F32) + target_grads, normed, inv_scale)
    return grad_out, (dot_cols(grad_out, w_out) * slope).astype(BF16)


def inner_backward_kernel(
    receivers_ref,
    agg_grad_ref,
    ct_ref,
    normed_ref,
    scale_ref,
    slope_ref,
    w_out_ref,
    grad_out_ref,
    grad_pre_ref,
):
    grad_out, grad_pre = edge_backward(
        ct_ref[...],
        dot(receivers_ref[...], agg_grad_ref[...]),
        normed_ref[...],
        scale_ref[...],
        slope_ref[...],
        w_out_ref[...],
    )
    grad_out_ref[...] = grad_out
    grad_pre_ref[...] = grad_pre


def fetch_factors(half, sources, buffers, sems, wait):
    edges, inner_sender, cut_sender, inner_receiver, cut_receiver = sources[:5]
    inner_hidden, cut_hidden, inner_out, inner_pre = sources[5:]
    inner_rows, cut_rows = inner_pre.shape[0], cut_sender.shape[0]
    inner_edges = edges.at[pl.ds(0, inner_rows)]
    cut_edges = edges.at[pl.ds(inner_rows, cut_rows)]
    low = [inner_edges, cut_edges, inner_sender, cut_sender, inner_pre, inner_pre]
    high = [inner_receiver, cut_receiver, inner_hidden, cut_hidden, inner_pre, inner_out]

    def each(parts):
        for index, (source, buffer) in enumerate(zip(parts, buffers)):
            copy = pltpu.make_async_copy(source, buffer, sems.at[index])
            if wait:
                copy.wait()
            else:
                copy.start()

    @pl.when(half == 0)
    def _():
        each(low)

    @pl.when(half != 0)
    def _():
        each(high)


def place_rows(me_ref, index, latent):
    return pl.ds(pl.multiple_of((index ^ ((me_ref[0] >> 1) & 1)) * latent, latent), latent)


def edge_rows(me_ref, half, buffers, cut_pre, cut_out, out_ref):
    latent = cut_pre.shape[1]
    first, first_cut, second, second_cut, first_right, second_right = buffers
    chosen = jnp.where(half == 0, cut_pre.astype(F32), cut_out.astype(F32)).astype(BF16)
    out_ref[place_rows(me_ref, 0, latent)] = (
        dot_rows(first[...], first_right[...]) + dot_rows(first_cut[...], cut_pre)
    ).astype(BF16)
    out_ref[place_rows(me_ref, 1, latent)] = (
        dot_rows(second[...], second_right[...]) + dot_rows(second_cut[...], chosen)
    ).astype(BF16)


def cut_backward_kernel(
    me_ref,
    receivers_ref,
    agg_grad_ref,
    far_grad_ref,
    ct_ref,
    normed_ref,
    scale_ref,
    slope_ref,
    w_out_ref,
    *refs,
):
    sources, (grad_out_ref, grad_pre_ref, out_ref), rest = refs[:9], refs[9:12], refs[12:]
    buffers, sems = rest[:-1], rest[-1]
    half = 1 - (me_ref[0] & 1)
    fetch_factors(half, sources, buffers, sems, False)
    base = agg_grad_ref.shape[0]
    target = dot(receivers_ref[:, :base], agg_grad_ref[...]) + dot(
        receivers_ref[:, base:], far_grad_ref[...]
    )
    grad_out, grad_pre = edge_backward(
        ct_ref[...], target, normed_ref[...], scale_ref[...], slope_ref[...], w_out_ref[...]
    )
    grad_out_ref[...] = grad_out
    grad_pre_ref[...] = grad_pre
    fetch_factors(half, sources, buffers, sems, True)
    edge_rows(me_ref, half, buffers, grad_pre, grad_out, out_ref)


def edge_weights_kernel(me_ref, cut_out_ref, cut_pre_ref, *refs):
    sources, out_ref, rest = refs[:9], refs[9], refs[10:]
    buffers, sems = rest[:-1], rest[-1]
    half = me_ref[0] & 1
    fetch_factors(half, sources, buffers, sems, False)
    fetch_factors(half, sources, buffers, sems, True)
    edge_rows(me_ref, half, buffers, cut_pre_ref[...], cut_out_ref[...], out_ref)


def input_grads_kernel(
    inner_senders_ref,
    inner_receivers_ref,
    cut_senders_ref,
    cut_receivers_ref,
    inner_pre_ref,
    cut_pre_ref,
    w_in_ref,
    local_ref,
    outgoing_ref,
):
    latent = inner_pre_ref.shape[1]
    base = inner_senders_ref.shape[1]
    inner_pre, cut_pre = inner_pre_ref[...], cut_pre_ref[...]
    w_sender, w_receiver = w_in_ref[latent : 2 * latent], w_in_ref[2 * latent :]

    def summed(inner_marks_ref, cut_marks_ref):
        return (
            dot_rows(inner_marks_ref[...], inner_pre) + dot_rows(cut_marks_ref[:, :base], cut_pre)
        ).astype(BF16)

    outgoing_ref[...] = (
        dot_cols(dot_rows(cut_senders_ref[:, base:], cut_pre).astype(BF16), w_sender)
        + dot_cols(dot_rows(cut_receivers_ref[:, base:], cut_pre).astype(BF16), w_receiver)
    ).astype(BF16)
    local_ref[...] = dot_cols(summed(inner_senders_ref, cut_senders_ref), w_sender) + dot_cols(
        summed(inner_receivers_ref, cut_receivers_ref), w_receiver
    )


def edge_grads_kernel(ct_ref, inner_pre_ref, cut_pre_ref, w_edge_ref, out_ref, *, blocks):
    inside = pl.program_id(0) < blocks

    @pl.when(inside)
    def _():
        out_ref[...] = ct_ref[...].astype(F32) + dot_cols(inner_pre_ref[...], w_edge_ref[...])

    @pl.when(jnp.logical_not(inside))
    def _():
        out_ref[...] = ct_ref[...].astype(F32) + dot_cols(cut_pre_ref[...], w_edge_ref[...])


def node_grads_kernel(self_ref, local_ref, asked_marks_ref, returned_ref, out_ref):
    out_ref[...] = (
        self_ref[...] + local_ref[...] + dot_rows(asked_marks_ref[...], returned_ref[...])
    )


VMEM = pl.BlockSpec(memory_space=pltpu.VMEM)
SMEM = pl.BlockSpec(memory_space=pltpu.SMEM)
ANY = pl.BlockSpec(memory_space=pl.ANY)


def shaped(dtype, *shape):
    return jax.ShapeDtypeStruct(shape, dtype)


class Line:
    def __init__(self):
        self.last = None

    def run(self, body, outs, ins, specs=None, out_specs=None, grid=None, scratch=()):
        single = not isinstance(outs, (list, tuple))
        out_shape = [outs] if single else list(outs)
        specs = [VMEM] * len(ins) if specs is None else list(specs)
        count, extra = len(ins), {} if grid is None else {"grid": grid}
        ins = list(ins)
        if self.last is not None:
            ins.append(self.last)
            specs.append(ANY)

        def ordered(*refs):
            return body(*refs[:count], *refs[len(ins) :])

        result = pl.pallas_call(
            ordered,
            out_shape=out_shape,
            in_specs=specs,
            out_specs=[VMEM] * len(out_shape) if out_specs is None else out_specs,
            scratch_shapes=scratch,
            compiler_params=pltpu.CompilerParams(vmem_limit_bytes=VMEM_LIMIT),
            cost_estimate=pl.CostEstimate(flops=1, bytes_accessed=1, transcendentals=0),
            **extra,
        )(*ins)
        self.last = result[-1]
        return result[0] if single else result


def index_bits(devices):
    return list(range(devices.bit_length() - 1))


def across(rows, devices, mask):
    return lax.ppermute(rows, "dom", [(device, device ^ mask) for device in range(devices)])


def fence(*values):
    return lax.optimization_barrier(values)


def place_of(bit):
    return (lax.axis_index("dom") >> bit) & 1


def split(parts, bit):
    place = place_of(bit)
    halves = [part.reshape(2, part.shape[0] // 2, part.shape[1]) for part in parts]
    own = [lax.dynamic_index_in_dim(half, place, 0, False) for half in halves]
    sent = [lax.dynamic_index_in_dim(half, 1 - place, 0, False) for half in halves]
    return own, added(*sent)


def handed(rows, devices, bit):
    return [rows, across(rows, devices, 1 << bit)]


def added(*parts):
    return sum(part.astype(F32) for part in parts).astype(BF16)


def joined(parts, bit):
    orders = [jnp.concatenate(parts), jnp.concatenate(parts[::-1])]
    return jnp.where(place_of(bit) == 0, *orders)


def exchange(rows, domains):
    shape = rows.shape
    split = rows.reshape((domains, shape[0] // domains) + shape[1:])
    return lax.all_to_all(split, "dom", split_axis=0, concat_axis=0, tiled=True).reshape(shape)


def shards(
    nodes,
    edges,
    inner_pairs,
    cut_local,
    cut_dest,
    cut_remote,
    w_edge_in,
    w_edge_out,
    w_node_in,
    w_node_out,
    ct_nodes,
    ct_edges,
):
    domains = lax.axis_size("dom")
    node_rows, latent = nodes.shape
    inner_count, cut_count = inner_pairs.shape[0], cut_local.shape[0]
    inner_rows, cut_rows = 2 * inner_count, 2 * cut_count
    slots = max(2, 2 * cut_count // domains)
    total_slots = domains * slots
    table = node_rows + total_slots
    me = lax.axis_index("dom").reshape(1)
    line = Line()

    ask = line.run(
        ask_kernel, shaped(jnp.int32, domains, slots), [cut_dest.reshape(1, -1), cut_remote.reshape(1, -1)]
    )
    asked = lax.all_to_all(ask, "dom", split_axis=0, concat_axis=0, tiled=True)
    cut_senders, cut_receivers = line.run(
        functools.partial(cut_marks_kernel, domains=domains, slots=slots),
        [shaped(BF16, cut_rows, table)] * 2,
        [cut_dest.reshape(1, -1), cut_local.reshape(1, -1)],
    )
    reply, asked_marks = line.run(
        reply_kernel,
        [shaped(BF16, total_slots, latent), shaped(BF16, total_slots, node_rows)],
        [asked, nodes],
    )
    far = exchange(reply, domains)

    block = cut_rows
    blocks = inner_rows // block

    def rows_spec(width, rows=block):
        return pl.BlockSpec((rows, width), lambda step: (step, 0))

    def all_spec(array):
        return pl.BlockSpec(array.shape, lambda step: (0, 0))

    saved_widths = [node_rows, node_rows, latent, latent, latent, latent, latent, 1]
    saved_types = [BF16, BF16, BF16, BF16, BF16, F32, F32, F32]
    (
        inner_senders,
        inner_receivers,
        inner_sender,
        inner_receiver,
        inner_hidden,
        inner_slope,
        inner_normed,
        inner_scale,
        inner_total,
    ) = line.run(
        inner_forward_kernel,
        [shaped(kind, inner_rows, width) for kind, width in zip(saved_types, saved_widths)]
        + [shaped(F32, node_rows, latent)],
        [inner_pairs.T, edges, nodes, w_edge_in, w_edge_out],
        [
            pl.BlockSpec((2, block // 2), lambda step: (0, step)),
            rows_spec(latent),
            all_spec(nodes),
            all_spec(w_edge_in),
            all_spec(w_edge_out),
        ],
        [rows_spec(width) for width in saved_widths] + [all_spec(nodes)],
        (blocks,),
    )

    def last_rows(array):
        last = array.shape[0] // block - 1
        return pl.BlockSpec((block, array.shape[1]), lambda step: (last, 0))

    (
        cut_sender,
        cut_receiver,
        cut_hidden,
        cut_slope,
        cut_normed,
        cut_scale,
        total,
        outgoing,
    ) = line.run(
        cut_forward_kernel,
        [shaped(kind, cut_rows, width) for kind, width in zip(saved_types, saved_widths)][2:]
        + [shaped(F32, node_rows, latent), shaped(BF16, total_slots, latent)],
        [
            cut_senders,
            cut_receivers,
            edges,
            nodes,
            far,
            w_edge_in,
            w_edge_out,
            inner_total,
        ],
        [
            all_spec(cut_senders),
            all_spec(cut_receivers),
            last_rows(edges),
            all_spec(nodes),
            all_spec(far),
            all_spec(w_edge_in),
            all_spec(w_edge_out),
            all_spec(inner_total),
        ],
        [rows_spec(width) for width in saved_widths[2:]]
        + [all_spec(nodes), rows_spec(latent, total_slots)],
        (1,),
    )
    incoming = exchange(outgoing, domains)
    new_edges = line.run(
        new_edges_kernel,
        shaped(BF16, *edges.shape),
        [edges, inner_normed, cut_normed],
    )
    (
        new_nodes,
        self_grad,
        agg_grad,
        grad_reply,
        node_keep,
        node_send,
    ) = line.run(
        node_kernel,
        [
            shaped(BF16, node_rows, latent),
            shaped(F32, node_rows, latent),
            shaped(BF16, node_rows, latent),
            shaped(BF16, total_slots, latent),
        ]
        + [shaped(BF16, 3 * latent // 2, latent)] * 2,
        [me, incoming, asked_marks, total, nodes, ct_nodes, w_node_in, w_node_out],
        [SMEM] + [VMEM] * 7,
    )
    far_grad = exchange(grad_reply, domains)
    node_sum = added(node_keep, across(node_send, domains, 1))
    inner_out, inner_pre = line.run(
        inner_backward_kernel,
        [shaped(BF16, inner_rows, latent)] * 2,
        [
            inner_receivers,
            agg_grad,
            ct_edges,
            inner_normed,
            inner_scale,
            inner_slope,
            w_edge_out,
        ],
        [
            rows_spec(node_rows),
            all_spec(agg_grad),
            rows_spec(latent),
            rows_spec(latent),
            rows_spec(1),
            rows_spec(latent),
            all_spec(w_edge_out),
        ],
        [rows_spec(latent)] * 2,
        (blocks,),
    )
    bits = index_bits(domains)
    node_own, node_sent = split([node_sum], 1)
    node_parts = [*node_own, across(node_sent, domains, 2)]
    far_grad, node_sum, inner_pre = fence(far_grad, node_sum, inner_pre)
    factors = [
        edges,
        inner_sender,
        cut_sender,
        inner_receiver,
        cut_receiver,
        inner_hidden,
        cut_hidden,
        inner_out,
        inner_pre,
    ]
    buffers = [pltpu.VMEM((rows, latent), BF16) for rows in (inner_rows, cut_rows) * 2]
    buffers += [pltpu.VMEM((inner_rows, latent), BF16)] * 2
    buffers.append(pltpu.SemaphoreType.DMA((len(buffers),)))
    cut_out, cut_pre, edge_send = line.run(
        cut_backward_kernel,
        [shaped(BF16, cut_rows, latent)] * 2 + [shaped(BF16, 2 * latent, latent)],
        [
            me,
            cut_receivers,
            agg_grad,
            far_grad,
            ct_edges,
            cut_normed,
            cut_scale,
            cut_slope,
            w_edge_out,
        ]
        + factors,
        [
            SMEM,
            all_spec(cut_receivers),
            all_spec(agg_grad),
            all_spec(far_grad),
            last_rows(ct_edges),
            all_spec(cut_normed),
            all_spec(cut_scale),
            all_spec(cut_slope),
            all_spec(w_edge_out),
        ]
        + [ANY] * len(factors),
        [rows_spec(latent)] * 2 + [rows_spec(latent, 2 * latent)],
        (1,),
        buffers,
    )
    edge_send, place, *node_parts = fence(edge_send, me, *node_parts)
    received = across(edge_send, domains, 1)
    node_own, node_sent = split(node_parts, 2)
    node_got = across(node_sent, domains, 4)
    edge_keep = line.run(
        edge_weights_kernel,
        shaped(BF16, 2 * latent, latent),
        [place, cut_out, cut_pre] + factors,
        [SMEM, VMEM, VMEM] + [ANY] * len(factors),
        scratch=buffers,
    )
    edge_keep, received = fence(edge_keep, received)
    edge_own = [edge_keep[:latent], received[:latent]]
    edge_sent = added(edge_keep[latent:], received[latent:])
    edge_sent, inner_pre, cut_pre = fence(edge_sent, inner_pre, cut_pre)
    node_got = fence(node_got, edge_sent)[0]
    edge_got = across(edge_sent, domains, 2)
    node_sum = added(*node_own, node_got)
    for bit in bits[3:]:
        node_sum = added(*handed(node_sum, domains, bit))
    local_grad, outgoing_grad = line.run(
        input_grads_kernel,
        [shaped(F32, node_rows, latent), shaped(BF16, total_slots, latent)],
        [
            inner_senders,
            inner_receivers,
            cut_senders,
            cut_receivers,
            inner_pre,
            cut_pre,
            w_edge_in,
        ],
    )
    edge_got, node_sum, inner_pre, cut_pre, local_grad = fence(
        edge_got, node_sum, inner_pre, cut_pre, local_grad
    )
    edge_own, edge_sent = split([added(*edge_own, edge_got)], 2)
    edge_got = across(edge_sent, domains, 4)
    grad_edges = line.run(
        functools.partial(edge_grads_kernel, blocks=blocks),
        shaped(F32, *edges.shape),
        [ct_edges, inner_pre, cut_pre, w_edge_in],
        [
            rows_spec(latent),
            pl.BlockSpec((block, latent), lambda step: (jnp.minimum(step, blocks - 1), 0)),
            all_spec(cut_pre),
            pl.BlockSpec((latent, latent), lambda step: (0, 0)),
        ],
        [rows_spec(latent)],
        (blocks + 1,),
    )
    edge_got, node_sum, grad_edges = fence(edge_got, node_sum, grad_edges)
    edge_own, edge_sent = split([added(*edge_own, edge_got)], 3)
    edge_sent, node_sum = fence(edge_sent, node_sum)
    edge_got, *node_parts = fence(across(edge_sent, domains, 8), *handed(node_sum, domains, 2))
    edge_sum = added(*edge_own, edge_got)
    for bit in bits[4:]:
        own, sent = split([edge_sum], bit)
        edge_sum = added(*own, across(sent, domains, 1 << bit))
    for bit in bits[:3:-1]:
        edge_sum = joined(handed(edge_sum, domains, bit), bit)
    node_parts = handed(joined(node_parts, 2), domains, 1)
    edge_parts = fence(*handed(edge_sum, domains, 3))
    edge_parts = handed(joined(edge_parts, 3), domains, 2)
    *edge_parts, node_sum, other_sum, outgoing_grad = fence(
        *edge_parts, *node_parts, outgoing_grad
    )
    edge_sum = joined(edge_parts, 2)
    node_sum = joined([node_sum, other_sum], 1)
    far, near = across(edge_sum, domains, 2), across(edge_sum, domains, 1)
    others = across(node_sum, domains, 1)
    returned = exchange(outgoing_grad, domains)
    lower, left = place_of(0) == 0, place_of(1) == 0
    low_rows, high_rows = jnp.where(lower, node_sum, others), jnp.where(lower, others, node_sum)
    cut_at = 2 * latent - low_rows.shape[0]
    grad_node_in = jnp.concatenate([low_rows, high_rows[:cut_at]])
    grad_node_out = high_rows[cut_at:]
    far, near, grad_node_in, grad_node_out, returned = fence(
        far, near, grad_node_in, grad_node_out, returned
    )
    corner = across(far, domains, 1)
    grad_nodes = line.run(
        node_grads_kernel,
        shaped(F32, node_rows, latent),
        [self_grad, local_grad, asked_marks, returned],
    )
    own, other = [edge_sum, far], [near, corner]
    low_half = [jnp.where(lower, one, two) for one, two in zip(own, other)]
    high_half = [jnp.where(lower, two, one) for one, two in zip(own, other)]
    grad_edge_in = jnp.concatenate(
        [
            jnp.where(left, low_half[0], low_half[1]),
            jnp.where(left, low_half[1], low_half[0]),
            jnp.where(left, high_half[0], high_half[1]),
        ]
    )
    grad_edge_out = jnp.where(left, high_half[1], high_half[0])
    return (
        new_nodes,
        new_edges,
        grad_nodes,
        grad_edges,
        grad_edge_in,
        grad_edge_out,
        grad_node_in,
        grad_node_out,
    )


def solution(mesh):
    placed = (
        P(("groups", "dom"), None),
        P(("groups", "dom"), None),
        P(("groups", "dom"), None),
        P(("groups", "dom")),
        P(("groups", "dom"), None),
        P(("groups", "dom")),
        P(),
        P(),
        P(),
        P(),
        P(("groups", "dom"), None),
        P(("groups", "dom"), None),
    )
    return jax.shard_map(
        shards,
        mesh=mesh,
        in_specs=placed,
        out_specs=(
            P(("groups", "dom"), None),
            P(("groups", "dom"), None),
            P(("groups", "dom"), None),
            P(("groups", "dom"), None),
            P("groups", None),
            P("groups", None),
            P("groups", None),
            P("groups", None),
        ),
        check_vma=False,
    )
```

```python
import functools

import jax
import jax.numpy as jnp
from jax import lax
from jax.experimental import pallas as pl
from jax.experimental.pallas import tpu as pltpu
from jax.sharding import PartitionSpec as P

BF16 = jnp.bfloat16
F32 = jnp.float32
VMEM_LIMIT = 60 * 1024 * 1024


def dot(left, right):
    return jnp.dot(left, right, preferred_element_type=F32)


def dot_rows(left, right):
    return lax.dot_general(left, right, (((0,), (0,)), ((), ())), preferred_element_type=F32)


def dot_cols(left, right):
    return lax.dot_general(left, right, (((1,), (1,)), ((), ())), preferred_element_type=F32)


def iota(shape, axis):
    return lax.broadcasted_iota(jnp.int32, shape, axis)


def marks(mask):
    return jnp.where(mask, 1.0, 0.0).astype(BF16)


def onehot(column, width):
    return marks(column == iota((column.shape[0], width), 1))


def to_column(row):
    count = row.shape[1]
    square = (count, count)
    kept = jnp.where(iota(square, 0) == iota(square, 1), row.astype(F32), 0.0)
    return jnp.sum(kept, axis=1, keepdims=True)


def slot_ranks(dest, domains):
    count = dest.shape[0]
    square = (count, count)
    dest_marks = onehot(dest, domains)
    before = dot(marks(iota(square, 0) > iota(square, 1)), dest_marks)
    return dest_marks, jnp.sum(before * dest_marks.astype(F32), axis=1, keepdims=True)


def pair_marks(first, second, width):
    pairs = first.shape[0]
    shape = (2 * pairs, pairs)
    edge, pair = iota(shape, 0), iota(shape, 1)
    mine = (edge >> 1) == pair
    even = marks(mine & ((edge & 1) == 0))
    odd = marks(mine & ((edge & 1) == 1))
    first_marks, second_marks = onehot(first, width), onehot(second, width)
    senders = dot(even, first_marks) + dot(odd, second_marks)
    receivers = dot(even, second_marks) + dot(odd, first_marks)
    return senders.astype(BF16), receivers.astype(BF16)


def normalise(values):
    centered = values - jnp.mean(values, axis=1, keepdims=True)
    inv_scale = lax.rsqrt(jnp.mean(centered * centered, axis=1, keepdims=True) + 1e-05)
    return centered * inv_scale, inv_scale


def activate(pre_hidden):
    gate = jax.nn.sigmoid(pre_hidden)
    return (pre_hidden * gate).astype(BF16), gate * (1.0 + pre_hidden * (1.0 - gate))


def norm_backward(upstream, normed, inv_scale):
    centered = (
        upstream
        - jnp.mean(upstream, axis=1, keepdims=True)
        - normed * jnp.mean(upstream * normed, axis=1, keepdims=True)
    )
    return (inv_scale * centered).astype(BF16)


def ask_kernel(dest_ref, remote_ref, ask_ref):
    domains, slots = ask_ref.shape
    dest_marks, rank = slot_ranks(to_column(dest_ref[...]).astype(jnp.int32), domains)
    rank_marks = jnp.where(rank == iota((rank.shape[0], slots), 1).astype(F32), 1.0, 0.0)
    wanted = (rank_marks * to_column(remote_ref[...])).astype(BF16)
    ask_ref[...] = dot_rows(dest_marks, wanted).astype(jnp.int32)


def reply_kernel(asked_ref, nodes_ref, reply_ref, asked_marks_ref):
    domains, slots = asked_ref.shape
    total = domains * slots
    shift = slots.bit_length() - 1
    spread = marks((iota((total, domains), 0) >> shift) == iota((total, domains), 1))
    listed = dot(spread, asked_ref[...].astype(F32).astype(BF16))
    at_slot = (iota((total, slots), 0) & (slots - 1)) == iota((total, slots), 1)
    column = jnp.sum(jnp.where(at_slot, listed, 0.0), axis=1, keepdims=True)
    node_rows = nodes_ref.shape[0]
    asked_marks = marks(column == iota((total, node_rows), 1).astype(F32))
    asked_marks_ref[...] = asked_marks
    reply_ref[...] = dot(asked_marks, nodes_ref[...]).astype(BF16)


def cut_marks_kernel(dest_ref, local_ref, senders_ref, receivers_ref, *, domains, slots):
    width = senders_ref.shape[1]
    base = width - domains * slots
    dest = to_column(dest_ref[...]).astype(jnp.int32)
    _, rank = slot_ranks(dest, domains)
    second = dest * slots + rank.astype(jnp.int32) + base
    first = to_column(local_ref[...]).astype(jnp.int32)
    senders, receivers = pair_marks(first, second, width)
    senders_ref[...] = senders
    receivers_ref[...] = receivers


def edge_forward(edge, sender, receiver, w_in_ref, w_out_ref):
    latent = edge.shape[1]
    pre_hidden = (
        dot(edge, w_in_ref[:latent])
        + dot(sender, w_in_ref[latent : 2 * latent])
        + dot(receiver, w_in_ref[2 * latent :])
    )
    hidden, slope = activate(pre_hidden)
    normed, inv_scale = normalise(dot(hidden, w_out_ref[...]))
    return hidden, slope, normed, inv_scale


def inner_forward_kernel(
    pairs_ref,
    edges_ref,
    nodes_ref,
    w_in_ref,
    w_out_ref,
    senders_ref,
    receivers_ref,
    sender_ref,
    receiver_ref,
    hidden_ref,
    slope_ref,
    normed_ref,
    scale_ref,
    total_ref,
):
    first, second = (to_column(pairs_ref[side : side + 1]).astype(jnp.int32) for side in range(2))
    senders, receivers = pair_marks(first, second, nodes_ref.shape[0])
    senders_ref[...] = senders
    receivers_ref[...] = receivers
    nodes = nodes_ref[...]
    sender = dot(senders, nodes).astype(BF16)
    receiver = dot(receivers, nodes).astype(BF16)
    sender_ref[...] = sender
    receiver_ref[...] = receiver
    hidden, slope, normed, inv_scale = edge_forward(
        edges_ref[...], sender, receiver, w_in_ref, w_out_ref
    )
    hidden_ref[...] = hidden
    slope_ref[...] = slope
    normed_ref[...] = normed
    scale_ref[...] = inv_scale
    part = dot_rows(receivers, normed.astype(BF16))

    @pl.when(pl.program_id(0) == 0)
    def _():
        total_ref[...] = part

    @pl.when(pl.program_id(0) > 0)
    def _():
        total_ref[...] += part


def cut_forward_kernel(
    senders_ref,
    receivers_ref,
    edges_ref,
    nodes_ref,
    far_ref,
    w_in_ref,
    w_out_ref,
    inner_total_ref,
    sender_ref,
    receiver_ref,
    hidden_ref,
    slope_ref,
    normed_ref,
    scale_ref,
    total_ref,
    outgoing_ref,
):
    base = nodes_ref.shape[0]
    nodes, far = nodes_ref[...], far_ref[...]

    def rows_of(marks_ref):
        return (dot(marks_ref[:, :base], nodes) + dot(marks_ref[:, base:], far)).astype(BF16)

    sender, receiver = rows_of(senders_ref), rows_of(receivers_ref)
    sender_ref[...] = sender
    receiver_ref[...] = receiver
    hidden, slope, normed, inv_scale = edge_forward(
        edges_ref[...], sender, receiver, w_in_ref, w_out_ref
    )
    hidden_ref[...] = hidden
    slope_ref[...] = slope
    normed_ref[...] = normed
    scale_ref[...] = inv_scale
    message = normed.astype(BF16)
    total_ref[...] = inner_total_ref[...] + dot_rows(receivers_ref[:, :base], message)
    outgoing_ref[...] = dot_rows(receivers_ref[:, base:], message).astype(BF16)


def new_edges_kernel(edges_ref, inner_ref, cut_ref, out_ref):
    inner_rows = inner_ref.shape[0]

    def added(edge, normed):
        return (edge.astype(F32) + normed.astype(BF16).astype(F32)).astype(BF16)

    out_ref[:inner_rows] = added(edges_ref[:inner_rows], inner_ref[...])
    out_ref[inner_rows:] = added(edges_ref[inner_rows:], cut_ref[...])


def node_kernel(
    me_ref,
    incoming_ref,
    asked_marks_ref,
    total_ref,
    nodes_ref,
    ct_ref,
    w_in_ref,
    w_out_ref,
    new_nodes_ref,
    self_grad_ref,
    agg_grad_ref,
    reply_ref,
    keep_ref,
    send_ref,
):
    latent = nodes_ref.shape[1]
    half = latent // 2
    nodes, asked_marks = nodes_ref[...], asked_marks_ref[...]
    aggregate = (total_ref[...] + dot_rows(asked_marks, incoming_ref[...])).astype(BF16)
    pre_hidden = dot(nodes, w_in_ref[:latent]) + dot(aggregate, w_in_ref[latent:])
    hidden, slope = activate(pre_hidden)
    normed, inv_scale = normalise(dot(hidden, w_out_ref[...]))
    upstream = ct_ref[...].astype(F32)
    grad_out = norm_backward(upstream, normed, inv_scale)
    grad_pre = (dot_cols(grad_out, w_out_ref[...]) * slope).astype(BF16)
    agg_grad = dot_cols(grad_pre, w_in_ref[latent:]).astype(BF16)
    agg_grad_ref[...] = agg_grad
    reply_ref[...] = dot(asked_marks, agg_grad).astype(BF16)
    self_grad_ref[...] = upstream + dot_cols(grad_pre, w_in_ref[:latent])
    new_nodes_ref[...] = (nodes.astype(F32) + normed).astype(BF16)

    def fill(low_ref, high_ref):
        by_aggregate = dot_rows(aggregate, grad_pre).astype(BF16)
        low_ref[:latent] = dot_rows(nodes, grad_pre).astype(BF16)
        low_ref[latent:] = by_aggregate[:half]
        high_ref[:half] = by_aggregate[half:]
        high_ref[half:] = dot_rows(hidden, grad_out).astype(BF16)

    @pl.when((me_ref[0] & 1) == 0)
    def _():
        fill(keep_ref, send_ref)

    @pl.when((me_ref[0] & 1) != 0)
    def _():
        fill(send_ref, keep_ref)


def edge_backward(ct, target_grads, normed, inv_scale, slope, w_out):
    grad_out = norm_backward(ct.astype(F32) + target_grads, normed, inv_scale)
    return grad_out, (dot_cols(grad_out, w_out) * slope).astype(BF16)


def inner_backward_kernel(
    receivers_ref,
    agg_grad_ref,
    ct_ref,
    normed_ref,
    scale_ref,
    slope_ref,
    w_out_ref,
    grad_out_ref,
    grad_pre_ref,
):
    grad_out, grad_pre = edge_backward(
        ct_ref[...],
        dot(receivers_ref[...], agg_grad_ref[...]),
        normed_ref[...],
        scale_ref[...],
        slope_ref[...],
        w_out_ref[...],
    )
    grad_out_ref[...] = grad_out
    grad_pre_ref[...] = grad_pre


def fetch_factors(half, sources, buffers, sems, wait=None):
    edges, inner_sender, cut_sender, inner_receiver, cut_receiver = sources[:5]
    inner_hidden, cut_hidden, inner_out, inner_pre = sources[5:]
    inner_rows, cut_rows = inner_pre.shape[0], cut_sender.shape[0]
    inner_edges = edges.at[pl.ds(0, inner_rows)]
    cut_edges = edges.at[pl.ds(inner_rows, cut_rows)]
    low = [inner_edges, cut_edges, inner_pre, inner_sender, cut_sender, inner_pre]
    high = [inner_receiver, cut_receiver, inner_pre, inner_hidden, cut_hidden, inner_out]

    def each(parts):
        for index, (source, buffer) in enumerate(zip(parts, buffers)):
            copy = pltpu.make_async_copy(source, buffer, sems.at[index])
            if wait is None:
                copy.start()
            elif index in wait:
                copy.wait()

    @pl.when(half == 0)
    def _():
        each(low)

    @pl.when(half != 0)
    def _():
        each(high)


def place_rows(me_ref, index, latent):
    return pl.ds(pl.multiple_of((index ^ ((me_ref[0] >> 1) & 1)) * latent, latent), latent)


def edge_rows(me_ref, half, sources, buffers, sems, cut_pre, cut_out, out_ref):
    latent = cut_pre.shape[1]
    first, first_cut, first_right, second, second_cut, second_right = buffers
    chosen = jnp.where(half == 0, cut_pre.astype(F32), cut_out.astype(F32)).astype(BF16)
    fetch_factors(half, sources, buffers, sems, (0, 1, 2))
    out_ref[place_rows(me_ref, 0, latent)] = (
        dot_rows(first[...], first_right[...]) + dot_rows(first_cut[...], cut_pre)
    ).astype(BF16)
    fetch_factors(half, sources, buffers, sems, (3, 4, 5))
    out_ref[place_rows(me_ref, 1, latent)] = (
        dot_rows(second[...], second_right[...]) + dot_rows(second_cut[...], chosen)
    ).astype(BF16)


def cut_backward_kernel(
    me_ref,
    receivers_ref,
    agg_grad_ref,
    far_grad_ref,
    ct_ref,
    normed_ref,
    scale_ref,
    slope_ref,
    w_out_ref,
    *refs,
):
    sources, (grad_out_ref, grad_pre_ref, out_ref), rest = refs[:9], refs[9:12], refs[12:]
    buffers, sems = rest[:-1], rest[-1]
    half = 1 - (me_ref[0] & 1)
    fetch_factors(half, sources, buffers, sems)
    base = agg_grad_ref.shape[0]
    target = dot(receivers_ref[:, :base], agg_grad_ref[...]) + dot(
        receivers_ref[:, base:], far_grad_ref[...]
    )
    grad_out, grad_pre = edge_backward(
        ct_ref[...], target, normed_ref[...], scale_ref[...], slope_ref[...], w_out_ref[...]
    )
    grad_out_ref[...] = grad_out
    grad_pre_ref[...] = grad_pre
    edge_rows(me_ref, half, sources, buffers, sems, grad_pre, grad_out, out_ref)


def edge_weights_kernel(me_ref, cut_out_ref, cut_pre_ref, *refs):
    sources, out_ref, rest = refs[:9], refs[9], refs[10:]
    buffers, sems = rest[:-1], rest[-1]
    half = me_ref[0] & 1
    fetch_factors(half, sources, buffers, sems)
    edge_rows(
        me_ref, half, sources, buffers, sems, cut_pre_ref[...], cut_out_ref[...], out_ref
    )


def input_grads_kernel(
    inner_senders_ref,
    inner_receivers_ref,
    cut_senders_ref,
    cut_receivers_ref,
    inner_pre_ref,
    cut_pre_ref,
    w_in_ref,
    local_ref,
    outgoing_ref,
):
    latent = inner_pre_ref.shape[1]
    base = inner_senders_ref.shape[1]
    inner_pre, cut_pre = inner_pre_ref[...], cut_pre_ref[...]
    w_sender, w_receiver = w_in_ref[latent : 2 * latent], w_in_ref[2 * latent :]

    def summed(inner_marks_ref, cut_marks_ref):
        return (
            dot_rows(inner_marks_ref[...], inner_pre) + dot_rows(cut_marks_ref[:, :base], cut_pre)
        ).astype(BF16)

    outgoing_ref[...] = (
        dot_cols(dot_rows(cut_senders_ref[:, base:], cut_pre).astype(BF16), w_sender)
        + dot_cols(dot_rows(cut_receivers_ref[:, base:], cut_pre).astype(BF16), w_receiver)
    ).astype(BF16)
    local_ref[...] = dot_cols(summed(inner_senders_ref, cut_senders_ref), w_sender) + dot_cols(
        summed(inner_receivers_ref, cut_receivers_ref), w_receiver
    )


def edge_grads_kernel(ct_ref, inner_pre_ref, cut_pre_ref, w_edge_ref, out_ref, *, blocks):
    inside = pl.program_id(0) < blocks

    @pl.when(inside)
    def _():
        out_ref[...] = ct_ref[...].astype(F32) + dot_cols(inner_pre_ref[...], w_edge_ref[...])

    @pl.when(jnp.logical_not(inside))
    def _():
        out_ref[...] = ct_ref[...].astype(F32) + dot_cols(cut_pre_ref[...], w_edge_ref[...])


def node_grads_kernel(self_ref, local_ref, asked_marks_ref, returned_ref, out_ref):
    out_ref[...] = (
        self_ref[...] + local_ref[...] + dot_rows(asked_marks_ref[...], returned_ref[...])
    )


VMEM = pl.BlockSpec(memory_space=pltpu.VMEM)
SMEM = pl.BlockSpec(memory_space=pltpu.SMEM)
ANY = pl.BlockSpec(memory_space=pl.ANY)


def shaped(dtype, *shape):
    return jax.ShapeDtypeStruct(shape, dtype)


class Line:
    def __init__(self):
        self.last = None

    def run(self, body, outs, ins, specs=None, out_specs=None, grid=None, scratch=()):
        single = not isinstance(outs, (list, tuple))
        out_shape = [outs] if single else list(outs)
        specs = [VMEM] * len(ins) if specs is None else list(specs)
        count, extra = len(ins), {} if grid is None else {"grid": grid}
        ins = list(ins)
        if self.last is not None:
            ins.append(self.last)
            specs.append(ANY)

        def ordered(*refs):
            return body(*refs[:count], *refs[len(ins) :])

        result = pl.pallas_call(
            ordered,
            out_shape=out_shape,
            in_specs=specs,
            out_specs=[VMEM] * len(out_shape) if out_specs is None else out_specs,
            scratch_shapes=scratch,
            compiler_params=pltpu.CompilerParams(vmem_limit_bytes=VMEM_LIMIT),
            cost_estimate=pl.CostEstimate(flops=1, bytes_accessed=1, transcendentals=0),
            **extra,
        )(*ins)
        self.last = result[-1]
        return result[0] if single else result


def index_bits(devices):
    return list(range(devices.bit_length() - 1))


def across(rows, devices, mask):
    return lax.ppermute(rows, "dom", [(device, device ^ mask) for device in range(devices)])


def fence(*values):
    return lax.optimization_barrier(values)


def place_of(bit):
    return (lax.axis_index("dom") >> bit) & 1


def split(parts, bit):
    place = place_of(bit)
    halves = [part.reshape(2, part.shape[0] // 2, part.shape[1]) for part in parts]
    own = [lax.dynamic_index_in_dim(half, place, 0, False) for half in halves]
    sent = [lax.dynamic_index_in_dim(half, 1 - place, 0, False) for half in halves]
    return own, added(*sent)


def handed(rows, devices, bit):
    return [rows, across(rows, devices, 1 << bit)]


def added(*parts):
    return sum(part.astype(F32) for part in parts).astype(BF16)


def joined(parts, bit):
    orders = [jnp.concatenate(parts), jnp.concatenate(parts[::-1])]
    return jnp.where(place_of(bit) == 0, *orders)


def exchange(rows, domains):
    shape = rows.shape
    split = rows.reshape((domains, shape[0] // domains) + shape[1:])
    return lax.all_to_all(split, "dom", split_axis=0, concat_axis=0, tiled=True).reshape(shape)


def shards(
    nodes,
    edges,
    inner_pairs,
    cut_local,
    cut_dest,
    cut_remote,
    w_edge_in,
    w_edge_out,
    w_node_in,
    w_node_out,
    ct_nodes,
    ct_edges,
):
    domains = lax.axis_size("dom")
    node_rows, latent = nodes.shape
    inner_count, cut_count = inner_pairs.shape[0], cut_local.shape[0]
    inner_rows, cut_rows = 2 * inner_count, 2 * cut_count
    slots = max(2, 2 * cut_count // domains)
    total_slots = domains * slots
    table = node_rows + total_slots
    me = lax.axis_index("dom").reshape(1)
    line = Line()

    ask = line.run(
        ask_kernel, shaped(jnp.int32, domains, slots), [cut_dest.reshape(1, -1), cut_remote.reshape(1, -1)]
    )
    asked = lax.all_to_all(ask, "dom", split_axis=0, concat_axis=0, tiled=True)
    cut_senders, cut_receivers = line.run(
        functools.partial(cut_marks_kernel, domains=domains, slots=slots),
        [shaped(BF16, cut_rows, table)] * 2,
        [cut_dest.reshape(1, -1), cut_local.reshape(1, -1)],
    )
    reply, asked_marks = line.run(
        reply_kernel,
        [shaped(BF16, total_slots, latent), shaped(BF16, total_slots, node_rows)],
        [asked, nodes],
    )
    far = exchange(reply, domains)

    block = cut_rows
    blocks = inner_rows // block

    def rows_spec(width, rows=block):
        return pl.BlockSpec((rows, width), lambda step: (step, 0))

    def all_spec(array):
        return pl.BlockSpec(array.shape, lambda step: (0, 0))

    saved_widths = [node_rows, node_rows, latent, latent, latent, latent, latent, 1]
    saved_types = [BF16, BF16, BF16, BF16, BF16, F32, F32, F32]
    (
        inner_senders,
        inner_receivers,
        inner_sender,
        inner_receiver,
        inner_hidden,
        inner_slope,
        inner_normed,
        inner_scale,
        inner_total,
    ) = line.run(
        inner_forward_kernel,
        [shaped(kind, inner_rows, width) for kind, width in zip(saved_types, saved_widths)]
        + [shaped(F32, node_rows, latent)],
        [inner_pairs.T, edges, nodes, w_edge_in, w_edge_out],
        [
            pl.BlockSpec((2, block // 2), lambda step: (0, step)),
            rows_spec(latent),
            all_spec(nodes),
            all_spec(w_edge_in),
            all_spec(w_edge_out),
        ],
        [rows_spec(width) for width in saved_widths] + [all_spec(nodes)],
        (blocks,),
    )

    def last_rows(array):
        last = array.shape[0] // block - 1
        return pl.BlockSpec((block, array.shape[1]), lambda step: (last, 0))

    (
        cut_sender,
        cut_receiver,
        cut_hidden,
        cut_slope,
        cut_normed,
        cut_scale,
        total,
        outgoing,
    ) = line.run(
        cut_forward_kernel,
        [shaped(kind, cut_rows, width) for kind, width in zip(saved_types, saved_widths)][2:]
        + [shaped(F32, node_rows, latent), shaped(BF16, total_slots, latent)],
        [
            cut_senders,
            cut_receivers,
            edges,
            nodes,
            far,
            w_edge_in,
            w_edge_out,
            inner_total,
        ],
        [
            all_spec(cut_senders),
            all_spec(cut_receivers),
            last_rows(edges),
            all_spec(nodes),
            all_spec(far),
            all_spec(w_edge_in),
            all_spec(w_edge_out),
            all_spec(inner_total),
        ],
        [rows_spec(width) for width in saved_widths[2:]]
        + [all_spec(nodes), rows_spec(latent, total_slots)],
        (1,),
    )
    incoming = exchange(outgoing, domains)
    new_edges = line.run(
        new_edges_kernel,
        shaped(BF16, *edges.shape),
        [edges, inner_normed, cut_normed],
    )
    (
        new_nodes,
        self_grad,
        agg_grad,
        grad_reply,
        node_keep,
        node_send,
    ) = line.run(
        node_kernel,
        [
            shaped(BF16, node_rows, latent),
            shaped(F32, node_rows, latent),
            shaped(BF16, node_rows, latent),
            shaped(BF16, total_slots, latent),
        ]
        + [shaped(BF16, 3 * latent // 2, latent)] * 2,
        [me, incoming, asked_marks, total, nodes, ct_nodes, w_node_in, w_node_out],
        [SMEM] + [VMEM] * 7,
    )
    far_grad = exchange(grad_reply, domains)
    node_sum = added(node_keep, across(node_send, domains, 1))
    inner_out, inner_pre = line.run(
        inner_backward_kernel,
        [shaped(BF16, inner_rows, latent)] * 2,
        [
            inner_receivers,
            agg_grad,
            ct_edges,
            inner_normed,
            inner_scale,
            inner_slope,
            w_edge_out,
        ],
        [
            rows_spec(node_rows),
            all_spec(agg_grad),
            rows_spec(latent),
            rows_spec(latent),
            rows_spec(1),
            rows_spec(latent),
            all_spec(w_edge_out),
        ],
        [rows_spec(latent)] * 2,
        (blocks,),
    )
    bits = index_bits(domains)
    node_own, node_sent = split([node_sum], 1)
    node_parts = [*node_own, across(node_sent, domains, 2)]
    far_grad, node_sum, inner_pre = fence(far_grad, node_sum, inner_pre)
    factors = [
        edges,
        inner_sender,
        cut_sender,
        inner_receiver,
        cut_receiver,
        inner_hidden,
        cut_hidden,
        inner_out,
        inner_pre,
    ]
    buffers = [
        pltpu.VMEM((rows, latent), BF16) for rows in (inner_rows, cut_rows, inner_rows) * 2
    ]
    buffers.append(pltpu.SemaphoreType.DMA((len(buffers),)))
    cut_out, cut_pre, edge_send = line.run(
        cut_backward_kernel,
        [shaped(BF16, cut_rows, latent)] * 2 + [shaped(BF16, 2 * latent, latent)],
        [
            me,
            cut_receivers,
            agg_grad,
            far_grad,
            ct_edges,
            cut_normed,
            cut_scale,
            cut_slope,
            w_edge_out,
        ]
        + factors,
        [
            SMEM,
            all_spec(cut_receivers),
            all_spec(agg_grad),
            all_spec(far_grad),
            last_rows(ct_edges),
            all_spec(cut_normed),
            all_spec(cut_scale),
            all_spec(cut_slope),
            all_spec(w_edge_out),
        ]
        + [ANY] * len(factors),
        [rows_spec(latent)] * 2 + [rows_spec(latent, 2 * latent)],
        (1,),
        buffers,
    )
    edge_send, place, *node_parts = fence(edge_send, me, *node_parts)
    received = across(edge_send, domains, 1)
    node_own, node_sent = split(node_parts, 2)
    node_got = across(node_sent, domains, 4)
    edge_keep = line.run(
        edge_weights_kernel,
        shaped(BF16, 2 * latent, latent),
        [place, cut_out, cut_pre] + factors,
        [SMEM, VMEM, VMEM] + [ANY] * len(factors),
        scratch=buffers,
    )
    edge_keep, received = fence(edge_keep, received)
    edge_sent = added(edge_keep[latent:], received[latent:])
    edge_sent, inner_pre, cut_pre = fence(edge_sent, inner_pre, cut_pre)
    node_got = fence(node_got, edge_sent)[0]
    edge_got = across(edge_sent, domains, 2)
    node_sum = added(*node_own, node_got)
    for bit in bits[3:]:
        node_sum = added(*handed(node_sum, domains, bit))
    edge_keep, received = fence(edge_keep, received, edge_sent)[:2]
    edge_own = added(edge_keep[:latent], received[:latent])
    local_grad, outgoing_grad = line.run(
        input_grads_kernel,
        [shaped(F32, node_rows, latent), shaped(BF16, total_slots, latent)],
        [
            inner_senders,
            inner_receivers,
            cut_senders,
            cut_receivers,
            inner_pre,
            cut_pre,
            w_edge_in,
        ],
    )
    edge_own, edge_got, node_sum, inner_pre, cut_pre, local_grad = fence(
        edge_own, edge_got, node_sum, inner_pre, cut_pre, local_grad
    )
    edge_own, edge_sent = split([added(edge_own, edge_got)], 2)
    edge_got = across(edge_sent, domains, 4)
    grad_edges = line.run(
        functools.partial(edge_grads_kernel, blocks=blocks),
        shaped(F32, *edges.shape),
        [ct_edges, inner_pre, cut_pre, w_edge_in],
        [
            rows_spec(latent),
            pl.BlockSpec((block, latent), lambda step: (jnp.minimum(step, blocks - 1), 0)),
            all_spec(cut_pre),
            pl.BlockSpec((latent, latent), lambda step: (0, 0)),
        ],
        [rows_spec(latent)],
        (blocks + 1,),
    )
    edge_got, node_sum, grad_edges = fence(edge_got, node_sum, grad_edges)
    edge_sum = added(*edge_own, edge_got)
    edge_sum, node_sum = fence(edge_sum, node_sum)
    edge_got = across(edge_sum, domains, 8)
    node_parts = handed(joined(handed(node_sum, domains, 2), 2), domains, 1)
    edge_sum = added(*fence(edge_sum, edge_got))
    for bit in bits[4:]:
        edge_sum = added(*handed(edge_sum, domains, bit))
    *edge_parts, node_sum, other_sum, outgoing_grad = fence(
        *handed(edge_sum, domains, 2), *node_parts, outgoing_grad
    )
    edge_sum = joined(edge_parts, 2)
    node_sum = joined([node_sum, other_sum], 1)
    far, near = across(edge_sum, domains, 2), across(edge_sum, domains, 1)
    others = across(node_sum, domains, 1)
    returned = exchange(outgoing_grad, domains)
    lower, left = place_of(0) == 0, place_of(1) == 0
    low_rows, high_rows = jnp.where(lower, node_sum, others), jnp.where(lower, others, node_sum)
    cut_at = 2 * latent - low_rows.shape[0]
    grad_node_in = jnp.concatenate([low_rows, high_rows[:cut_at]])
    grad_node_out = high_rows[cut_at:]
    far, near, grad_node_in, grad_node_out, returned = fence(
        far, near, grad_node_in, grad_node_out, returned
    )
    corner = across(far, domains, 1)
    grad_nodes = line.run(
        node_grads_kernel,
        shaped(F32, node_rows, latent),
        [self_grad, local_grad, asked_marks, returned],
    )
    high_half = [jnp.where(lower, near, edge_sum), jnp.where(lower, corner, far)]
    grad_edge_out = jnp.where(left, high_half[1], high_half[0])
    edge_sum, far, near, corner = fence(edge_sum, far, near, corner)
    low_half = [jnp.where(lower, edge_sum, near), jnp.where(lower, far, corner)]
    high_half = [jnp.where(lower, near, edge_sum), jnp.where(lower, corner, far)]
    grad_edge_in = jnp.concatenate(
        [
            jnp.where(left, low_half[0], low_half[1]),
            jnp.where(left, low_half[1], low_half[0]),
            jnp.where(left, high_half[0], high_half[1]),
        ]
    )
    return (
        new_nodes,
        new_edges,
        grad_nodes,
        grad_edges,
        grad_edge_in,
        grad_edge_out,
        grad_node_in,
        grad_node_out,
    )


def solution(mesh):
    placed = (
        P(("groups", "dom"), None),
        P(("groups", "dom"), None),
        P(("groups", "dom"), None),
        P(("groups", "dom")),
        P(("groups", "dom"), None),
        P(("groups", "dom")),
        P(),
        P(),
        P(),
        P(),
        P(("groups", "dom"), None),
        P(("groups", "dom"), None),
    )
    return jax.shard_map(
        shards,
        mesh=mesh,
        in_specs=placed,
        out_specs=(
            P(("groups", "dom"), None),
            P(("groups", "dom"), None),
            P(("groups", "dom"), None),
            P(("groups", "dom"), None),
            P("groups", None),
            P("groups", None),
            P("groups", None),
            P("groups", None),
        ),
        check_vma=False,
    )
```

```python
import functools

import jax
import jax.numpy as jnp
from jax import lax
from jax.experimental import pallas as pl
from jax.experimental.pallas import tpu as pltpu
from jax.sharding import PartitionSpec as P

BF16 = jnp.bfloat16
F32 = jnp.float32
VMEM_LIMIT = 60 * 1024 * 1024


def dot(left, right):
    return jnp.dot(left, right, preferred_element_type=F32)


def dot_rows(left, right):
    return lax.dot_general(left, right, (((0,), (0,)), ((), ())), preferred_element_type=F32)


def dot_cols(left, right):
    return lax.dot_general(left, right, (((1,), (1,)), ((), ())), preferred_element_type=F32)


def iota(shape, axis):
    return lax.broadcasted_iota(jnp.int32, shape, axis)


def marks(mask):
    return jnp.where(mask, 1.0, 0.0).astype(BF16)


def onehot(column, width):
    return marks(column == iota((column.shape[0], width), 1))


def to_column(row):
    count = row.shape[1]
    square = (count, count)
    kept = jnp.where(iota(square, 0) == iota(square, 1), row.astype(F32), 0.0)
    return jnp.sum(kept, axis=1, keepdims=True)


def slot_ranks(dest, domains):
    count = dest.shape[0]
    square = (count, count)
    dest_marks = onehot(dest, domains)
    before = dot(marks(iota(square, 0) > iota(square, 1)), dest_marks)
    return dest_marks, jnp.sum(before * dest_marks.astype(F32), axis=1, keepdims=True)


def pair_marks(first, second, width):
    pairs = first.shape[0]
    shape = (2 * pairs, pairs)
    edge, pair = iota(shape, 0), iota(shape, 1)
    mine = (edge >> 1) == pair
    even = marks(mine & ((edge & 1) == 0))
    odd = marks(mine & ((edge & 1) == 1))
    first_marks, second_marks = onehot(first, width), onehot(second, width)
    senders = dot(even, first_marks) + dot(odd, second_marks)
    receivers = dot(even, second_marks) + dot(odd, first_marks)
    return senders.astype(BF16), receivers.astype(BF16)


def normalise(values):
    centered = values - jnp.mean(values, axis=1, keepdims=True)
    inv_scale = lax.rsqrt(jnp.mean(centered * centered, axis=1, keepdims=True) + 1e-05)
    return centered * inv_scale, inv_scale


def activate(pre_hidden):
    gate = jax.nn.sigmoid(pre_hidden)
    return (pre_hidden * gate).astype(BF16), gate * (1.0 + pre_hidden * (1.0 - gate))


def norm_backward(upstream, normed, inv_scale):
    centered = (
        upstream
        - jnp.mean(upstream, axis=1, keepdims=True)
        - normed * jnp.mean(upstream * normed, axis=1, keepdims=True)
    )
    return (inv_scale * centered).astype(BF16)


def ask_kernel(dest_ref, remote_ref, ask_ref):
    domains, slots = ask_ref.shape
    dest_marks, rank = slot_ranks(to_column(dest_ref[...]).astype(jnp.int32), domains)
    rank_marks = jnp.where(rank == iota((rank.shape[0], slots), 1).astype(F32), 1.0, 0.0)
    wanted = (rank_marks * to_column(remote_ref[...])).astype(BF16)
    ask_ref[...] = dot_rows(dest_marks, wanted).astype(jnp.int32)


def reply_kernel(asked_ref, nodes_ref, reply_ref, asked_marks_ref):
    domains, slots = asked_ref.shape
    total = domains * slots
    shift = slots.bit_length() - 1
    spread = marks((iota((total, domains), 0) >> shift) == iota((total, domains), 1))
    listed = dot(spread, asked_ref[...].astype(F32).astype(BF16))
    at_slot = (iota((total, slots), 0) & (slots - 1)) == iota((total, slots), 1)
    column = jnp.sum(jnp.where(at_slot, listed, 0.0), axis=1, keepdims=True)
    node_rows = nodes_ref.shape[0]
    asked_marks = marks(column == iota((total, node_rows), 1).astype(F32))
    asked_marks_ref[...] = asked_marks
    reply_ref[...] = dot(asked_marks, nodes_ref[...]).astype(BF16)


def cut_marks_kernel(dest_ref, local_ref, senders_ref, receivers_ref, *, domains, slots):
    width = senders_ref.shape[1]
    base = width - domains * slots
    dest = to_column(dest_ref[...]).astype(jnp.int32)
    _, rank = slot_ranks(dest, domains)
    second = dest * slots + rank.astype(jnp.int32) + base
    first = to_column(local_ref[...]).astype(jnp.int32)
    senders, receivers = pair_marks(first, second, width)
    senders_ref[...] = senders
    receivers_ref[...] = receivers


def edge_forward(edge, sender, receiver, w_in_ref, w_out_ref):
    latent = edge.shape[1]
    pre_hidden = (
        dot(edge, w_in_ref[:latent])
        + dot(sender, w_in_ref[latent : 2 * latent])
        + dot(receiver, w_in_ref[2 * latent :])
    )
    hidden, slope = activate(pre_hidden)
    normed, inv_scale = normalise(dot(hidden, w_out_ref[...]))
    return hidden, slope, normed, inv_scale


def inner_forward_kernel(
    pairs_ref,
    edges_ref,
    nodes_ref,
    w_in_ref,
    w_out_ref,
    senders_ref,
    receivers_ref,
    sender_ref,
    receiver_ref,
    hidden_ref,
    slope_ref,
    normed_ref,
    scale_ref,
    total_ref,
):
    first, second = (to_column(pairs_ref[side : side + 1]).astype(jnp.int32) for side in range(2))
    senders, receivers = pair_marks(first, second, nodes_ref.shape[0])
    senders_ref[...] = senders
    receivers_ref[...] = receivers
    nodes = nodes_ref[...]
    sender = dot(senders, nodes).astype(BF16)
    receiver = dot(receivers, nodes).astype(BF16)
    sender_ref[...] = sender
    receiver_ref[...] = receiver
    hidden, slope, normed, inv_scale = edge_forward(
        edges_ref[...], sender, receiver, w_in_ref, w_out_ref
    )
    hidden_ref[...] = hidden
    slope_ref[...] = slope.astype(BF16)
    normed_ref[...] = normed.astype(BF16)
    scale_ref[...] = inv_scale
    part = dot_rows(receivers, normed.astype(BF16))

    @pl.when(pl.program_id(0) == 0)
    def _():
        total_ref[...] = part

    @pl.when(pl.program_id(0) > 0)
    def _():
        total_ref[...] += part


def cut_forward_kernel(
    senders_ref,
    receivers_ref,
    edges_ref,
    nodes_ref,
    far_ref,
    w_in_ref,
    w_out_ref,
    inner_total_ref,
    sender_ref,
    receiver_ref,
    hidden_ref,
    slope_ref,
    normed_ref,
    scale_ref,
    total_ref,
    outgoing_ref,
):
    base = nodes_ref.shape[0]
    nodes, far = nodes_ref[...], far_ref[...]

    def rows_of(marks_ref):
        return (dot(marks_ref[:, :base], nodes) + dot(marks_ref[:, base:], far)).astype(BF16)

    sender, receiver = rows_of(senders_ref), rows_of(receivers_ref)
    sender_ref[...] = sender
    receiver_ref[...] = receiver
    hidden, slope, normed, inv_scale = edge_forward(
        edges_ref[...], sender, receiver, w_in_ref, w_out_ref
    )
    hidden_ref[...] = hidden
    slope_ref[...] = slope.astype(BF16)
    normed_ref[...] = normed.astype(BF16)
    scale_ref[...] = inv_scale
    message = normed.astype(BF16)
    total_ref[...] = inner_total_ref[...] + dot_rows(receivers_ref[:, :base], message)
    outgoing_ref[...] = dot_rows(receivers_ref[:, base:], message).astype(BF16)


def new_edges_kernel(edges_ref, inner_ref, cut_ref, out_ref):
    inner_rows = inner_ref.shape[0]

    def added(edge, normed):
        return (edge.astype(F32) + normed.astype(F32)).astype(BF16)

    out_ref[:inner_rows] = added(edges_ref[:inner_rows], inner_ref[...])
    out_ref[inner_rows:] = added(edges_ref[inner_rows:], cut_ref[...])


def node_kernel(
    me_ref,
    incoming_ref,
    asked_marks_ref,
    total_ref,
    nodes_ref,
    ct_ref,
    w_in_ref,
    w_out_ref,
    new_nodes_ref,
    self_grad_ref,
    agg_grad_ref,
    reply_ref,
    keep_ref,
    send_ref,
):
    latent = nodes_ref.shape[1]
    half = latent // 2
    nodes, asked_marks = nodes_ref[...], asked_marks_ref[...]
    aggregate = (total_ref[...] + dot_rows(asked_marks, incoming_ref[...])).astype(BF16)
    pre_hidden = dot(nodes, w_in_ref[:latent]) + dot(aggregate, w_in_ref[latent:])
    hidden, slope = activate(pre_hidden)
    normed, inv_scale = normalise(dot(hidden, w_out_ref[...]))
    upstream = ct_ref[...].astype(F32)
    grad_out = norm_backward(upstream, normed, inv_scale)
    grad_pre = (dot_cols(grad_out, w_out_ref[...]) * slope).astype(BF16)
    agg_grad = dot_cols(grad_pre, w_in_ref[latent:]).astype(BF16)
    agg_grad_ref[...] = agg_grad
    reply_ref[...] = dot(asked_marks, agg_grad).astype(BF16)
    self_grad_ref[...] = upstream + dot_cols(grad_pre, w_in_ref[:latent])
    new_nodes_ref[...] = (nodes.astype(F32) + normed).astype(BF16)

    def fill(low_ref, high_ref):
        by_aggregate = dot_rows(aggregate, grad_pre).astype(BF16)
        low_ref[:latent] = dot_rows(nodes, grad_pre).astype(BF16)
        low_ref[latent:] = by_aggregate[:half]
        high_ref[:half] = by_aggregate[half:]
        high_ref[half:] = dot_rows(hidden, grad_out).astype(BF16)

    @pl.when((me_ref[0] & 1) == 0)
    def _():
        fill(keep_ref, send_ref)

    @pl.when((me_ref[0] & 1) != 0)
    def _():
        fill(send_ref, keep_ref)


def edge_backward(ct, target_grads, normed, inv_scale, slope, w_out):
    upstream = ct.astype(F32) + target_grads
    grad_out = norm_backward(upstream, normed.astype(F32), inv_scale)
    return grad_out, (dot_cols(grad_out, w_out) * slope.astype(F32)).astype(BF16)


def inner_backward_kernel(
    receivers_ref,
    agg_grad_ref,
    ct_ref,
    normed_ref,
    scale_ref,
    slope_ref,
    w_out_ref,
    grad_out_ref,
    grad_pre_ref,
):
    grad_out, grad_pre = edge_backward(
        ct_ref[...],
        dot(receivers_ref[...], agg_grad_ref[...]),
        normed_ref[...],
        scale_ref[...],
        slope_ref[...],
        w_out_ref[...],
    )
    grad_out_ref[...] = grad_out
    grad_pre_ref[...] = grad_pre


def fetch_factors(half, sources, buffers, sems, wait=None):
    edges, inner_sender, cut_sender, inner_receiver, cut_receiver = sources[:5]
    inner_hidden, cut_hidden, inner_out, inner_pre = sources[5:]
    inner_rows, cut_rows = inner_pre.shape[0], cut_sender.shape[0]
    inner_edges = edges.at[pl.ds(0, inner_rows)]
    cut_edges = edges.at[pl.ds(inner_rows, cut_rows)]
    low = [inner_edges, cut_edges, inner_pre, inner_sender, cut_sender, inner_pre]
    high = [inner_receiver, cut_receiver, inner_pre, inner_hidden, cut_hidden, inner_out]

    def each(parts):
        for index, (source, buffer) in enumerate(zip(parts, buffers)):
            copy = pltpu.make_async_copy(source, buffer, sems.at[index])
            if wait is None:
                copy.start()
            elif index in wait:
                copy.wait()

    @pl.when(half == 0)
    def _():
        each(low)

    @pl.when(half != 0)
    def _():
        each(high)


def place_rows(me_ref, index, latent):
    return pl.ds(pl.multiple_of((index ^ ((me_ref[0] >> 1) & 1)) * latent, latent), latent)


def edge_rows(me_ref, half, sources, buffers, sems, cut_pre, cut_out, out_ref):
    latent = cut_pre.shape[1]
    first, first_cut, first_right, second, second_cut, second_right = buffers
    chosen = jnp.where(half == 0, cut_pre.astype(F32), cut_out.astype(F32)).astype(BF16)
    fetch_factors(half, sources, buffers, sems, range(6))
    out_ref[place_rows(me_ref, 0, latent)] = (
        dot_rows(first[...], first_right[...]) + dot_rows(first_cut[...], cut_pre)
    ).astype(BF16)
    out_ref[place_rows(me_ref, 1, latent)] = (
        dot_rows(second[...], second_right[...]) + dot_rows(second_cut[...], chosen)
    ).astype(BF16)


def cut_backward_kernel(
    me_ref,
    receivers_ref,
    agg_grad_ref,
    far_grad_ref,
    ct_ref,
    normed_ref,
    scale_ref,
    slope_ref,
    w_out_ref,
    *refs,
):
    sources, (grad_out_ref, grad_pre_ref, out_ref), rest = refs[:9], refs[9:12], refs[12:]
    buffers, sems = rest[:-1], rest[-1]
    half = 1 - (me_ref[0] & 1)
    fetch_factors(half, sources, buffers, sems)
    base = agg_grad_ref.shape[0]
    target = dot(receivers_ref[:, :base], agg_grad_ref[...]) + dot(
        receivers_ref[:, base:], far_grad_ref[...]
    )
    grad_out, grad_pre = edge_backward(
        ct_ref[...], target, normed_ref[...], scale_ref[...], slope_ref[...], w_out_ref[...]
    )
    grad_out_ref[...] = grad_out
    grad_pre_ref[...] = grad_pre
    edge_rows(me_ref, half, sources, buffers, sems, grad_pre, grad_out, out_ref)


def edge_weights_kernel(me_ref, cut_out_ref, cut_pre_ref, *refs):
    sources, out_ref, rest = refs[:9], refs[9], refs[10:]
    buffers, sems = rest[:-1], rest[-1]
    half = me_ref[0] & 1
    fetch_factors(half, sources, buffers, sems)
    edge_rows(
        me_ref, half, sources, buffers, sems, cut_pre_ref[...], cut_out_ref[...], out_ref
    )


def input_grads_kernel(
    inner_senders_ref,
    inner_receivers_ref,
    cut_senders_ref,
    cut_receivers_ref,
    inner_pre_ref,
    cut_pre_ref,
    w_in_ref,
    local_ref,
    outgoing_ref,
):
    latent = inner_pre_ref.shape[1]
    base = inner_senders_ref.shape[1]
    inner_pre, cut_pre = inner_pre_ref[...], cut_pre_ref[...]
    w_sender, w_receiver = w_in_ref[latent : 2 * latent], w_in_ref[2 * latent :]

    def summed(inner_marks_ref, cut_marks_ref):
        return (
            dot_rows(inner_marks_ref[...], inner_pre) + dot_rows(cut_marks_ref[:, :base], cut_pre)
        ).astype(BF16)

    outgoing_ref[...] = (
        dot_cols(dot_rows(cut_senders_ref[:, base:], cut_pre).astype(BF16), w_sender)
        + dot_cols(dot_rows(cut_receivers_ref[:, base:], cut_pre).astype(BF16), w_receiver)
    ).astype(BF16)
    local_ref[...] = dot_cols(summed(inner_senders_ref, cut_senders_ref), w_sender) + dot_cols(
        summed(inner_receivers_ref, cut_receivers_ref), w_receiver
    )


def edge_grads_kernel(ct_ref, inner_pre_ref, cut_pre_ref, w_edge_ref, out_ref, *, blocks):
    inside = pl.program_id(0) < blocks

    @pl.when(inside)
    def _():
        out_ref[...] = ct_ref[...].astype(F32) + dot_cols(inner_pre_ref[...], w_edge_ref[...])

    @pl.when(jnp.logical_not(inside))
    def _():
        out_ref[...] = ct_ref[...].astype(F32) + dot_cols(cut_pre_ref[...], w_edge_ref[...])


def node_grads_kernel(self_ref, local_ref, asked_marks_ref, returned_ref, out_ref):
    out_ref[...] = (
        self_ref[...] + local_ref[...] + dot_rows(asked_marks_ref[...], returned_ref[...])
    )


VMEM = pl.BlockSpec(memory_space=pltpu.VMEM)
SMEM = pl.BlockSpec(memory_space=pltpu.SMEM)
ANY = pl.BlockSpec(memory_space=pl.ANY)


def shaped(dtype, *shape):
    return jax.ShapeDtypeStruct(shape, dtype)


class Line:
    def __init__(self):
        self.last = None

    def run(self, body, outs, ins, specs=None, out_specs=None, grid=None, scratch=()):
        single = not isinstance(outs, (list, tuple))
        out_shape = [outs] if single else list(outs)
        specs = [VMEM] * len(ins) if specs is None else list(specs)
        count, extra = len(ins), {} if grid is None else {"grid": grid}
        ins = list(ins)
        if self.last is not None:
            ins.append(self.last)
            specs.append(ANY)

        def ordered(*refs):
            return body(*refs[:count], *refs[len(ins) :])

        result = pl.pallas_call(
            ordered,
            out_shape=out_shape,
            in_specs=specs,
            out_specs=[VMEM] * len(out_shape) if out_specs is None else out_specs,
            scratch_shapes=scratch,
            compiler_params=pltpu.CompilerParams(vmem_limit_bytes=VMEM_LIMIT),
            cost_estimate=pl.CostEstimate(flops=1, bytes_accessed=1, transcendentals=0),
            **extra,
        )(*ins)
        self.last = result[-1]
        return result[0] if single else result


def index_bits(devices):
    return list(range(devices.bit_length() - 1))


def across(rows, devices, mask):
    return lax.ppermute(rows, "dom", [(device, device ^ mask) for device in range(devices)])


def fence(*values):
    return lax.optimization_barrier(values)


def place_of(bit):
    return (lax.axis_index("dom") >> bit) & 1


def split(parts, bit):
    place = place_of(bit)
    halves = [part.reshape(2, part.shape[0] // 2, part.shape[1]) for part in parts]
    own = [lax.dynamic_index_in_dim(half, place, 0, False) for half in halves]
    sent = [lax.dynamic_index_in_dim(half, 1 - place, 0, False) for half in halves]
    return own, added(*sent)


def handed(rows, devices, bit):
    return [rows, across(rows, devices, 1 << bit)]


def added(*parts):
    return sum(part.astype(F32) for part in parts).astype(BF16)


def joined(parts, bit):
    orders = [jnp.concatenate(parts), jnp.concatenate(parts[::-1])]
    return jnp.where(place_of(bit) == 0, *orders)


def exchange(rows, domains):
    shape = rows.shape
    split = rows.reshape((domains, shape[0] // domains) + shape[1:])
    return lax.all_to_all(split, "dom", split_axis=0, concat_axis=0, tiled=True).reshape(shape)


def shards(
    nodes,
    edges,
    inner_pairs,
    cut_local,
    cut_dest,
    cut_remote,
    w_edge_in,
    w_edge_out,
    w_node_in,
    w_node_out,
    ct_nodes,
    ct_edges,
):
    domains = lax.axis_size("dom")
    node_rows, latent = nodes.shape
    inner_count, cut_count = inner_pairs.shape[0], cut_local.shape[0]
    inner_rows, cut_rows = 2 * inner_count, 2 * cut_count
    slots = max(2, 2 * cut_count // domains)
    total_slots = domains * slots
    table = node_rows + total_slots
    me = lax.axis_index("dom").reshape(1)
    line = Line()

    ask = line.run(
        ask_kernel, shaped(jnp.int32, domains, slots), [cut_dest.reshape(1, -1), cut_remote.reshape(1, -1)]
    )
    asked = lax.all_to_all(ask, "dom", split_axis=0, concat_axis=0, tiled=True)
    cut_senders, cut_receivers = line.run(
        functools.partial(cut_marks_kernel, domains=domains, slots=slots),
        [shaped(BF16, cut_rows, table)] * 2,
        [cut_dest.reshape(1, -1), cut_local.reshape(1, -1)],
    )
    reply, asked_marks = line.run(
        reply_kernel,
        [shaped(BF16, total_slots, latent), shaped(BF16, total_slots, node_rows)],
        [asked, nodes],
    )
    far = exchange(reply, domains)

    block = cut_rows
    blocks = inner_rows // block

    def rows_spec(width, rows=block):
        return pl.BlockSpec((rows, width), lambda step: (step, 0))

    def all_spec(array):
        return pl.BlockSpec(array.shape, lambda step: (0, 0))

    saved_widths = [node_rows, node_rows, latent, latent, latent, latent, latent, 1]
    saved_types = [BF16] * 7 + [F32]
    (
        inner_senders,
        inner_receivers,
        inner_sender,
        inner_receiver,
        inner_hidden,
        inner_slope,
        inner_normed,
        inner_scale,
        inner_total,
    ) = line.run(
        inner_forward_kernel,
        [shaped(kind, inner_rows, width) for kind, width in zip(saved_types, saved_widths)]
        + [shaped(F32, node_rows, latent)],
        [inner_pairs.T, edges, nodes, w_edge_in, w_edge_out],
        [
            pl.BlockSpec((2, block // 2), lambda step: (0, step)),
            rows_spec(latent),
            all_spec(nodes),
            all_spec(w_edge_in),
            all_spec(w_edge_out),
        ],
        [rows_spec(width) for width in saved_widths] + [all_spec(nodes)],
        (blocks,),
    )

    def last_rows(array):
        last = array.shape[0] // block - 1
        return pl.BlockSpec((block, array.shape[1]), lambda step: (last, 0))

    (
        cut_sender,
        cut_receiver,
        cut_hidden,
        cut_slope,
        cut_normed,
        cut_scale,
        total,
        outgoing,
    ) = line.run(
        cut_forward_kernel,
        [shaped(kind, cut_rows, width) for kind, width in zip(saved_types, saved_widths)][2:]
        + [shaped(F32, node_rows, latent), shaped(BF16, total_slots, latent)],
        [
            cut_senders,
            cut_receivers,
            edges,
            nodes,
            far,
            w_edge_in,
            w_edge_out,
            inner_total,
        ],
        [
            all_spec(cut_senders),
            all_spec(cut_receivers),
            last_rows(edges),
            all_spec(nodes),
            all_spec(far),
            all_spec(w_edge_in),
            all_spec(w_edge_out),
            all_spec(inner_total),
        ],
        [rows_spec(width) for width in saved_widths[2:]]
        + [all_spec(nodes), rows_spec(latent, total_slots)],
        (1,),
    )
    incoming = exchange(outgoing, domains)
    new_edges = line.run(
        new_edges_kernel,
        shaped(BF16, *edges.shape),
        [edges, inner_normed, cut_normed],
    )
    (
        new_nodes,
        self_grad,
        agg_grad,
        grad_reply,
        node_keep,
        node_send,
    ) = line.run(
        node_kernel,
        [
            shaped(BF16, node_rows, latent),
            shaped(F32, node_rows, latent),
            shaped(BF16, node_rows, latent),
            shaped(BF16, total_slots, latent),
        ]
        + [shaped(BF16, 3 * latent // 2, latent)] * 2,
        [me, incoming, asked_marks, total, nodes, ct_nodes, w_node_in, w_node_out],
        [SMEM] + [VMEM] * 7,
    )
    far_grad = exchange(grad_reply, domains)
    node_sum = added(node_keep, across(node_send, domains, 1))
    inner_out, inner_pre = line.run(
        inner_backward_kernel,
        [shaped(BF16, inner_rows, latent)] * 2,
        [
            inner_receivers,
            agg_grad,
            ct_edges,
            inner_normed,
            inner_scale,
            inner_slope,
            w_edge_out,
        ],
        [
            rows_spec(node_rows),
            all_spec(agg_grad),
            rows_spec(latent),
            rows_spec(latent),
            rows_spec(1),
            rows_spec(latent),
            all_spec(w_edge_out),
        ],
        [rows_spec(latent)] * 2,
        (blocks,),
    )
    bits = index_bits(domains)
    node_own, node_sent = split([node_sum], 1)
    node_parts = [*node_own, across(node_sent, domains, 2)]
    far_grad, node_sum, inner_pre = fence(far_grad, node_sum, inner_pre)
    factors = [
        edges,
        inner_sender,
        cut_sender,
        inner_receiver,
        cut_receiver,
        inner_hidden,
        cut_hidden,
        inner_out,
        inner_pre,
    ]
    buffers = [
        pltpu.VMEM((rows, latent), BF16) for rows in (inner_rows, cut_rows, inner_rows) * 2
    ]
    buffers.append(pltpu.SemaphoreType.DMA((len(buffers),)))
    cut_out, cut_pre, edge_send = line.run(
        cut_backward_kernel,
        [shaped(BF16, cut_rows, latent)] * 2 + [shaped(BF16, 2 * latent, latent)],
        [
            me,
            cut_receivers,
            agg_grad,
            far_grad,
            ct_edges,
            cut_normed,
            cut_scale,
            cut_slope,
            w_edge_out,
        ]
        + factors,
        [
            SMEM,
            all_spec(cut_receivers),
            all_spec(agg_grad),
            all_spec(far_grad),
            last_rows(ct_edges),
            all_spec(cut_normed),
            all_spec(cut_scale),
            all_spec(cut_slope),
            all_spec(w_edge_out),
        ]
        + [ANY] * len(factors),
        [rows_spec(latent)] * 2 + [rows_spec(latent, 2 * latent)],
        (1,),
        buffers,
    )
    edge_send, place, *node_parts = fence(edge_send, me, *node_parts)
    received = across(edge_send, domains, 1)
    node_own, node_sent = split(node_parts, 2)
    node_got = across(node_sent, domains, 4)
    edge_keep = line.run(
        edge_weights_kernel,
        shaped(BF16, 2 * latent, latent),
        [place, cut_out, cut_pre] + factors,
        [SMEM, VMEM, VMEM] + [ANY] * len(factors),
        scratch=buffers,
    )
    edge_keep, received = fence(edge_keep, received)
    edge_sent = added(edge_keep[latent:], received[latent:])
    edge_sent, inner_pre, cut_pre = fence(edge_sent, inner_pre, cut_pre)
    node_got = fence(node_got, edge_sent)[0]
    edge_got = across(edge_sent, domains, 2)
    node_sum = added(*node_own, node_got)
    for bit in bits[3:]:
        node_sum = added(*handed(node_sum, domains, bit))
    edge_keep, received = fence(edge_keep, received, edge_sent)[:2]
    edge_own = added(edge_keep[:latent], received[:latent])
    local_grad, outgoing_grad = line.run(
        input_grads_kernel,
        [shaped(F32, node_rows, latent), shaped(BF16, total_slots, latent)],
        [
            inner_senders,
            inner_receivers,
            cut_senders,
            cut_receivers,
            inner_pre,
            cut_pre,
            w_edge_in,
        ],
    )
    edge_own, edge_got, node_sum, inner_pre, cut_pre, local_grad = fence(
        edge_own, edge_got, node_sum, inner_pre, cut_pre, local_grad
    )
    edge_own, edge_sent = split([added(edge_own, edge_got)], 2)
    edge_got = across(edge_sent, domains, 4)
    grad_edges = line.run(
        functools.partial(edge_grads_kernel, blocks=blocks),
        shaped(F32, *edges.shape),
        [ct_edges, inner_pre, cut_pre, w_edge_in],
        [
            rows_spec(latent),
            pl.BlockSpec((block, latent), lambda step: (jnp.minimum(step, blocks - 1), 0)),
            all_spec(cut_pre),
            pl.BlockSpec((latent, latent), lambda step: (0, 0)),
        ],
        [rows_spec(latent)],
        (blocks + 1,),
    )
    edge_got, node_sum, grad_edges = fence(edge_got, node_sum, grad_edges)
    edge_sum = added(*edge_own, edge_got)
    edge_sum, node_sum, outgoing_grad = fence(edge_sum, node_sum, outgoing_grad)
    edge_got = across(edge_sum, domains, 8)
    node_parts = handed(joined(handed(node_sum, domains, 2), 2), domains, 1)
    returned = exchange(outgoing_grad, domains)
    edge_sum, edge_got, returned = fence(edge_sum, edge_got, returned)
    edge_sum = added(edge_sum, edge_got)
    for bit in bits[4:]:
        edge_sum = added(*handed(edge_sum, domains, bit))
    grad_nodes = line.run(
        node_grads_kernel,
        shaped(F32, node_rows, latent),
        [self_grad, local_grad, asked_marks, returned],
    )
    *edge_parts, node_sum, other_sum, grad_nodes = fence(
        *handed(edge_sum, domains, 2), *node_parts, grad_nodes
    )
    edge_sum = joined(edge_parts, 2)
    node_sum = joined([node_sum, other_sum], 1)
    far, near = across(edge_sum, domains, 2), across(edge_sum, domains, 1)
    others = across(node_sum, domains, 1)
    lower, left = place_of(0) == 0, place_of(1) == 0
    low_rows, high_rows = jnp.where(lower, node_sum, others), jnp.where(lower, others, node_sum)
    cut_at = 2 * latent - low_rows.shape[0]
    grad_node_in = jnp.concatenate([low_rows, high_rows[:cut_at]])
    grad_node_out = high_rows[cut_at:]
    far, near, grad_node_in, grad_node_out = fence(far, near, grad_node_in, grad_node_out)
    corner = across(far, domains, 1)
    low_half = [jnp.where(lower, edge_sum, near), jnp.where(lower, far, corner)]
    high_half = [jnp.where(lower, near, edge_sum), jnp.where(lower, corner, far)]
    grad_edge_out = jnp.where(left, high_half[1], high_half[0])
    grad_edge_in = jnp.concatenate(
        [
            jnp.where(left, low_half[0], low_half[1]),
            jnp.where(left, low_half[1], low_half[0]),
            jnp.where(left, high_half[0], high_half[1]),
        ]
    )
    return (
        new_nodes,
        new_edges,
        grad_nodes,
        grad_edges,
        grad_edge_in,
        grad_edge_out,
        grad_node_in,
        grad_node_out,
    )


def solution(mesh):
    placed = (
        P(("groups", "dom"), None),
        P(("groups", "dom"), None),
        P(("groups", "dom"), None),
        P(("groups", "dom")),
        P(("groups", "dom"), None),
        P(("groups", "dom")),
        P(),
        P(),
        P(),
        P(),
        P(("groups", "dom"), None),
        P(("groups", "dom"), None),
    )
    return jax.shard_map(
        shards,
        mesh=mesh,
        in_specs=placed,
        out_specs=(
            P(("groups", "dom"), None),
            P(("groups", "dom"), None),
            P(("groups", "dom"), None),
            P(("groups", "dom"), None),
            P("groups", None),
            P("groups", None),
            P("groups", None),
            P("groups", None),
        ),
        check_vma=False,
    )
```

```python
import functools

import jax
import jax.numpy as jnp
from jax import lax
from jax.experimental import pallas as pl
from jax.experimental.pallas import tpu as pltpu
from jax.sharding import PartitionSpec as P

BF16 = jnp.bfloat16
F32 = jnp.float32
VMEM_LIMIT = 60 * 1024 * 1024


def dot(left, right):
    return jnp.dot(left, right, preferred_element_type=F32)


def dot_rows(left, right):
    return lax.dot_general(left, right, (((0,), (0,)), ((), ())), preferred_element_type=F32)


def dot_cols(left, right):
    return lax.dot_general(left, right, (((1,), (1,)), ((), ())), preferred_element_type=F32)


def iota(shape, axis):
    return lax.broadcasted_iota(jnp.int32, shape, axis)


def marks(mask):
    return jnp.where(mask, 1.0, 0.0).astype(BF16)


def onehot(column, width):
    return marks(column == iota((column.shape[0], width), 1))


def to_column(row):
    count = row.shape[1]
    square = (count, count)
    kept = jnp.where(iota(square, 0) == iota(square, 1), row.astype(F32), 0.0)
    return jnp.sum(kept, axis=1, keepdims=True)


def slot_ranks(dest, domains):
    count = dest.shape[0]
    square = (count, count)
    dest_marks = onehot(dest, domains)
    before = dot(marks(iota(square, 0) > iota(square, 1)), dest_marks)
    return dest_marks, jnp.sum(before * dest_marks.astype(F32), axis=1, keepdims=True)


def pair_marks(first, second, width):
    pairs = first.shape[0]
    shape = (2 * pairs, pairs)
    edge, pair = iota(shape, 0), iota(shape, 1)
    mine = (edge >> 1) == pair
    even = marks(mine & ((edge & 1) == 0))
    odd = marks(mine & ((edge & 1) == 1))
    first_marks, second_marks = onehot(first, width), onehot(second, width)
    senders = dot(even, first_marks) + dot(odd, second_marks)
    receivers = dot(even, second_marks) + dot(odd, first_marks)
    return senders.astype(BF16), receivers.astype(BF16)


def normalise(values):
    centered = values - jnp.mean(values, axis=1, keepdims=True)
    inv_scale = lax.rsqrt(jnp.mean(centered * centered, axis=1, keepdims=True) + 1e-05)
    return centered * inv_scale, inv_scale


def activate(pre_hidden):
    gate = jax.nn.sigmoid(pre_hidden)
    return (pre_hidden * gate).astype(BF16), gate * (1.0 + pre_hidden * (1.0 - gate))


def norm_backward(upstream, normed, inv_scale):
    centered = (
        upstream
        - jnp.mean(upstream, axis=1, keepdims=True)
        - normed * jnp.mean(upstream * normed, axis=1, keepdims=True)
    )
    return (inv_scale * centered).astype(BF16)


def ask_kernel(dest_ref, remote_ref, ask_ref):
    domains, slots = ask_ref.shape
    dest_marks, rank = slot_ranks(to_column(dest_ref[...]).astype(jnp.int32), domains)
    rank_marks = jnp.where(rank == iota((rank.shape[0], slots), 1).astype(F32), 1.0, 0.0)
    wanted = (rank_marks * to_column(remote_ref[...])).astype(BF16)
    ask_ref[...] = dot_rows(dest_marks, wanted).astype(jnp.int32)


def cut_marks_kernel(dest_ref, local_ref, senders_ref, receivers_ref, *, domains, slots):
    width = senders_ref.shape[1]
    base = width - domains * slots
    dest = to_column(dest_ref[...]).astype(jnp.int32)
    _, rank = slot_ranks(dest, domains)
    second = dest * slots + rank.astype(jnp.int32) + base
    first = to_column(local_ref[...]).astype(jnp.int32)
    senders, receivers = pair_marks(first, second, width)
    senders_ref[...] = senders
    receivers_ref[...] = receivers


def edge_forward(edge, sender, receiver, w_in_ref, w_out_ref):
    latent = edge.shape[1]
    pre_hidden = (
        dot(edge, w_in_ref[:latent])
        + dot(sender, w_in_ref[latent : 2 * latent])
        + dot(receiver, w_in_ref[2 * latent :])
    )
    hidden, slope = activate(pre_hidden)
    normed, inv_scale = normalise(dot(hidden, w_out_ref[...]))
    return hidden, slope, normed, inv_scale


def inner_forward_kernel(
    pairs_ref,
    edges_ref,
    nodes_ref,
    w_in_ref,
    w_out_ref,
    senders_ref,
    receivers_ref,
    sender_ref,
    receiver_ref,
    hidden_ref,
    slope_ref,
    normed_ref,
    scale_ref,
    total_ref,
):
    first, second = (to_column(pairs_ref[side : side + 1]).astype(jnp.int32) for side in range(2))
    senders, receivers = pair_marks(first, second, nodes_ref.shape[0])
    senders_ref[...] = senders
    receivers_ref[...] = receivers
    nodes = nodes_ref[...]
    sender = dot(senders, nodes).astype(BF16)
    receiver = dot(receivers, nodes).astype(BF16)
    sender_ref[...] = sender
    receiver_ref[...] = receiver
    hidden, slope, normed, inv_scale = edge_forward(
        edges_ref[...], sender, receiver, w_in_ref, w_out_ref
    )
    hidden_ref[...] = hidden
    slope_ref[...] = slope
    normed_ref[...] = normed
    scale_ref[...] = inv_scale
    part = dot_rows(receivers, normed.astype(BF16))

    @pl.when(pl.program_id(0) == 0)
    def _():
        total_ref[...] = part

    @pl.when(pl.program_id(0) > 0)
    def _():
        total_ref[...] += part


def cut_forward_kernel(
    senders_ref,
    receivers_ref,
    edges_ref,
    nodes_ref,
    far_ref,
    w_in_ref,
    w_out_ref,
    inner_total_ref,
    sender_ref,
    receiver_ref,
    hidden_ref,
    slope_ref,
    normed_ref,
    scale_ref,
    total_ref,
    outgoing_ref,
):
    base = nodes_ref.shape[0]
    nodes, far = nodes_ref[...], far_ref[...]

    def rows_of(marks_ref):
        return (dot(marks_ref[:, :base], nodes) + dot(marks_ref[:, base:], far)).astype(BF16)

    sender, receiver = rows_of(senders_ref), rows_of(receivers_ref)
    sender_ref[...] = sender
    receiver_ref[...] = receiver
    hidden, slope, normed, inv_scale = edge_forward(
        edges_ref[...], sender, receiver, w_in_ref, w_out_ref
    )
    hidden_ref[...] = hidden
    slope_ref[...] = slope
    normed_ref[...] = normed
    scale_ref[...] = inv_scale
    message = normed.astype(BF16)
    total_ref[...] = inner_total_ref[...] + dot_rows(receivers_ref[:, :base], message)
    outgoing_ref[...] = dot_rows(receivers_ref[:, base:], message).astype(BF16)


def new_edges_kernel(edges_ref, inner_ref, cut_ref, out_ref):
    inner_rows = inner_ref.shape[0]

    def added(edge, normed):
        return (edge.astype(F32) + normed.astype(BF16).astype(F32)).astype(BF16)

    out_ref[:inner_rows] = added(edges_ref[:inner_rows], inner_ref[...])
    out_ref[inner_rows:] = added(edges_ref[inner_rows:], cut_ref[...])


def node_kernel(
    me_ref,
    incoming_ref,
    asked_marks_ref,
    total_ref,
    nodes_ref,
    ct_ref,
    w_in_ref,
    w_out_ref,
    new_nodes_ref,
    self_grad_ref,
    agg_grad_ref,
    reply_ref,
    keep_ref,
    send_ref,
):
    latent = nodes_ref.shape[1]
    half = latent // 2
    nodes, asked_marks = nodes_ref[...], asked_marks_ref[...]
    aggregate = (total_ref[...] + dot_rows(asked_marks, incoming_ref[...])).astype(BF16)
    pre_hidden = dot(nodes, w_in_ref[:latent]) + dot(aggregate, w_in_ref[latent:])
    hidden, slope = activate(pre_hidden)
    normed, inv_scale = normalise(dot(hidden, w_out_ref[...]))
    upstream = ct_ref[...].astype(F32)
    grad_out = norm_backward(upstream, normed, inv_scale)
    grad_pre = (dot_cols(grad_out, w_out_ref[...]) * slope).astype(BF16)
    agg_grad = dot_cols(grad_pre, w_in_ref[latent:]).astype(BF16)
    agg_grad_ref[...] = agg_grad
    reply_ref[...] = dot(asked_marks, agg_grad).astype(BF16)
    self_grad_ref[...] = upstream + dot_cols(grad_pre, w_in_ref[:latent])
    new_nodes_ref[...] = (nodes.astype(F32) + normed).astype(BF16)

    def fill(low_ref, high_ref):
        by_aggregate = dot_rows(aggregate, grad_pre).astype(BF16)
        low_ref[:latent] = dot_rows(nodes, grad_pre).astype(BF16)
        low_ref[latent:] = by_aggregate[:half]
        high_ref[:half] = by_aggregate[half:]
        high_ref[half:] = dot_rows(hidden, grad_out).astype(BF16)

    @pl.when((me_ref[0] & 1) == 0)
    def _():
        fill(keep_ref, send_ref)

    @pl.when((me_ref[0] & 1) != 0)
    def _():
        fill(send_ref, keep_ref)


def edge_backward(ct, target_grads, normed, inv_scale, slope, w_out):
    grad_out = norm_backward(ct.astype(F32) + target_grads, normed, inv_scale)
    return grad_out, (dot_cols(grad_out, w_out) * slope).astype(BF16)


def inner_backward_kernel(
    receivers_ref,
    agg_grad_ref,
    ct_ref,
    normed_ref,
    scale_ref,
    slope_ref,
    w_out_ref,
    grad_out_ref,
    grad_pre_ref,
):
    grad_out, grad_pre = edge_backward(
        ct_ref[...],
        dot(receivers_ref[...], agg_grad_ref[...]),
        normed_ref[...],
        scale_ref[...],
        slope_ref[...],
        w_out_ref[...],
    )
    grad_out_ref[...] = grad_out
    grad_pre_ref[...] = grad_pre


def fetch_factors(half, sources, buffers, sems, wait=False):
    edges, inner_sender, cut_sender, inner_receiver, cut_receiver = sources[:5]
    inner_hidden, cut_hidden, inner_out, inner_pre = sources[5:]
    inner_rows, cut_rows = inner_pre.shape[0], cut_sender.shape[0]
    inner_edges = edges.at[pl.ds(0, inner_rows)]
    cut_edges = edges.at[pl.ds(inner_rows, cut_rows)]
    low = [inner_edges, cut_edges, inner_pre, inner_sender, cut_sender, inner_pre]
    high = [inner_receiver, cut_receiver, inner_pre, inner_hidden, cut_hidden, inner_out]

    def each(parts):
        for index, (source, buffer) in enumerate(zip(parts, buffers)):
            copy = pltpu.make_async_copy(source, buffer, sems.at[index])
            if wait:
                copy.wait()
            else:
                copy.start()

    @pl.when(half == 0)
    def _():
        each(low)

    @pl.when(half != 0)
    def _():
        each(high)


def place_rows(me_ref, index, latent):
    return pl.ds(pl.multiple_of((index ^ ((me_ref[0] >> 1) & 1)) * latent, latent), latent)


def edge_rows(me_ref, half, sources, buffers, sems, cut_pre, cut_out, out_ref):
    latent = cut_pre.shape[1]
    first, first_cut, first_right, second, second_cut, second_right = buffers
    chosen = jnp.where(half == 0, cut_pre.astype(F32), cut_out.astype(F32)).astype(BF16)
    fetch_factors(half, sources, buffers, sems, True)
    out_ref[place_rows(me_ref, 0, latent)] = (
        dot_rows(first[...], first_right[...]) + dot_rows(first_cut[...], cut_pre)
    ).astype(BF16)
    out_ref[place_rows(me_ref, 1, latent)] = (
        dot_rows(second[...], second_right[...]) + dot_rows(second_cut[...], chosen)
    ).astype(BF16)


def cut_backward_kernel(
    me_ref,
    receivers_ref,
    agg_grad_ref,
    far_grad_ref,
    ct_ref,
    normed_ref,
    scale_ref,
    slope_ref,
    w_out_ref,
    *refs,
):
    sources, (grad_out_ref, grad_pre_ref, out_ref), rest = refs[:9], refs[9:12], refs[12:]
    buffers, sems = rest[:-1], rest[-1]
    half = 1 - (me_ref[0] & 1)
    fetch_factors(half, sources, buffers, sems)
    base = agg_grad_ref.shape[0]
    target = dot(receivers_ref[:, :base], agg_grad_ref[...]) + dot(
        receivers_ref[:, base:], far_grad_ref[...]
    )
    grad_out, grad_pre = edge_backward(
        ct_ref[...], target, normed_ref[...], scale_ref[...], slope_ref[...], w_out_ref[...]
    )
    grad_out_ref[...] = grad_out
    grad_pre_ref[...] = grad_pre
    edge_rows(me_ref, half, sources, buffers, sems, grad_pre, grad_out, out_ref)


def edge_weights_kernel(me_ref, cut_out_ref, cut_pre_ref, *refs):
    sources, out_ref, rest = refs[:9], refs[9], refs[10:]
    buffers, sems = rest[:-1], rest[-1]
    half = me_ref[0] & 1
    fetch_factors(half, sources, buffers, sems)
    edge_rows(
        me_ref, half, sources, buffers, sems, cut_pre_ref[...], cut_out_ref[...], out_ref
    )


def input_grads_kernel(
    inner_senders_ref,
    inner_receivers_ref,
    cut_senders_ref,
    cut_receivers_ref,
    inner_pre_ref,
    cut_pre_ref,
    w_in_ref,
    local_ref,
    outgoing_ref,
):
    latent = inner_pre_ref.shape[1]
    base = inner_senders_ref.shape[1]
    inner_pre, cut_pre = inner_pre_ref[...], cut_pre_ref[...]
    w_sender, w_receiver = w_in_ref[latent : 2 * latent], w_in_ref[2 * latent :]

    def summed(inner_marks_ref, cut_marks_ref):
        return (
            dot_rows(inner_marks_ref[...], inner_pre) + dot_rows(cut_marks_ref[:, :base], cut_pre)
        ).astype(BF16)

    outgoing_ref[...] = (
        dot_cols(dot_rows(cut_senders_ref[:, base:], cut_pre).astype(BF16), w_sender)
        + dot_cols(dot_rows(cut_receivers_ref[:, base:], cut_pre).astype(BF16), w_receiver)
    ).astype(BF16)
    local_ref[...] = dot_cols(summed(inner_senders_ref, cut_senders_ref), w_sender) + dot_cols(
        summed(inner_receivers_ref, cut_receivers_ref), w_receiver
    )


def edge_grads_kernel(ct_ref, inner_pre_ref, cut_pre_ref, w_edge_ref, out_ref, *, blocks):
    inside = pl.program_id(0) < blocks

    @pl.when(inside)
    def _():
        out_ref[...] = ct_ref[...].astype(F32) + dot_cols(inner_pre_ref[...], w_edge_ref[...])

    @pl.when(jnp.logical_not(inside))
    def _():
        out_ref[...] = ct_ref[...].astype(F32) + dot_cols(cut_pre_ref[...], w_edge_ref[...])


VMEM = pl.BlockSpec(memory_space=pltpu.VMEM)
SMEM = pl.BlockSpec(memory_space=pltpu.SMEM)
ANY = pl.BlockSpec(memory_space=pl.ANY)


def shaped(dtype, *shape):
    return jax.ShapeDtypeStruct(shape, dtype)


class Line:
    def __init__(self):
        self.last = None

    def run(self, body, outs, ins, specs=None, out_specs=None, grid=None, scratch=()):
        single = not isinstance(outs, (list, tuple))
        out_shape = [outs] if single else list(outs)
        specs = [VMEM] * len(ins) if specs is None else list(specs)
        count, extra = len(ins), {} if grid is None else {"grid": grid}
        ins = list(ins)
        if self.last is not None:
            ins.append(self.last)
            specs.append(ANY)

        def ordered(*refs):
            return body(*refs[:count], *refs[len(ins) :])

        result = pl.pallas_call(
            ordered,
            out_shape=out_shape,
            in_specs=specs,
            out_specs=[VMEM] * len(out_shape) if out_specs is None else out_specs,
            scratch_shapes=scratch,
            compiler_params=pltpu.CompilerParams(vmem_limit_bytes=VMEM_LIMIT),
            cost_estimate=pl.CostEstimate(flops=1, bytes_accessed=1, transcendentals=0),
            **extra,
        )(*ins)
        self.last = result[-1]
        return result[0] if single else result


def index_bits(devices):
    return list(range(devices.bit_length() - 1))


def across(rows, devices, mask):
    return lax.ppermute(rows, "dom", [(device, device ^ mask) for device in range(devices)])


def fence(*values):
    return lax.optimization_barrier(values)


def place_of(bit):
    return (lax.axis_index("dom") >> bit) & 1


def split(parts, bit):
    place = place_of(bit)
    halves = [part.reshape(2, part.shape[0] // 2, part.shape[1]) for part in parts]
    own = [lax.dynamic_index_in_dim(half, place, 0, False) for half in halves]
    sent = [lax.dynamic_index_in_dim(half, 1 - place, 0, False) for half in halves]
    return own, added(*sent)


def handed(rows, devices, bit):
    return [rows, across(rows, devices, 1 << bit)]


def added(*parts):
    return sum(part.astype(F32) for part in parts).astype(BF16)


def joined(parts, bit):
    orders = [jnp.concatenate(parts), jnp.concatenate(parts[::-1])]
    return jnp.where(place_of(bit) == 0, *orders)


def exchange(rows, domains):
    shape = rows.shape
    split = rows.reshape((domains, shape[0] // domains) + shape[1:])
    return lax.all_to_all(split, "dom", split_axis=0, concat_axis=0, tiled=True).reshape(shape)


def shards(
    nodes,
    edges,
    inner_pairs,
    cut_local,
    cut_dest,
    cut_remote,
    w_edge_in,
    w_edge_out,
    w_node_in,
    w_node_out,
    ct_nodes,
    ct_edges,
):
    domains = lax.axis_size("dom")
    node_rows, latent = nodes.shape
    inner_count, cut_count = inner_pairs.shape[0], cut_local.shape[0]
    inner_rows, cut_rows = 2 * inner_count, 2 * cut_count
    slots = max(2, 2 * cut_count // domains)
    total_slots = domains * slots
    table = node_rows + total_slots
    me = lax.axis_index("dom").reshape(1)
    line = Line()

    ask = line.run(
        ask_kernel, shaped(jnp.int32, domains, slots), [cut_dest.reshape(1, -1), cut_remote.reshape(1, -1)]
    )
    asked = lax.all_to_all(ask, "dom", split_axis=0, concat_axis=0, tiled=True)
    cut_senders, cut_receivers = line.run(
        functools.partial(cut_marks_kernel, domains=domains, slots=slots),
        [shaped(BF16, cut_rows, table)] * 2,
        [cut_dest.reshape(1, -1), cut_local.reshape(1, -1)],
    )
    asked_marks = jnp.where(
        asked[:, :, None] == jnp.arange(node_rows, dtype=jnp.int32)[None, None], 1.0, 0.0
    ).astype(BF16)
    reply = lax.dot_general(asked_marks, nodes, (((2,), (0,)), ((), ())), preferred_element_type=F32)
    reply = reply.astype(BF16).reshape(total_slots, latent)
    asked_marks = asked_marks.reshape(total_slots, node_rows)
    far = exchange(reply, domains)

    block = cut_rows
    blocks = inner_rows // block

    def rows_spec(width, rows=block):
        return pl.BlockSpec((rows, width), lambda step: (step, 0))

    def all_spec(array):
        return pl.BlockSpec(array.shape, lambda step: (0, 0))

    saved_widths = [node_rows, node_rows, latent, latent, latent, latent, latent, 1]
    saved_types = [BF16, BF16, BF16, BF16, BF16, F32, F32, F32]
    (
        inner_senders,
        inner_receivers,
        inner_sender,
        inner_receiver,
        inner_hidden,
        inner_slope,
        inner_normed,
        inner_scale,
        inner_total,
    ) = line.run(
        inner_forward_kernel,
        [shaped(kind, inner_rows, width) for kind, width in zip(saved_types, saved_widths)]
        + [shaped(F32, node_rows, latent)],
        [inner_pairs.T, edges, nodes, w_edge_in, w_edge_out],
        [
            pl.BlockSpec((2, block // 2), lambda step: (0, step)),
            rows_spec(latent),
            all_spec(nodes),
            all_spec(w_edge_in),
            all_spec(w_edge_out),
        ],
        [rows_spec(width) for width in saved_widths] + [all_spec(nodes)],
        (blocks,),
    )

    def last_rows(array):
        last = array.shape[0] // block - 1
        return pl.BlockSpec((block, array.shape[1]), lambda step: (last, 0))

    (
        cut_sender,
        cut_receiver,
        cut_hidden,
        cut_slope,
        cut_normed,
        cut_scale,
        total,
        outgoing,
    ) = line.run(
        cut_forward_kernel,
        [shaped(kind, cut_rows, width) for kind, width in zip(saved_types, saved_widths)][2:]
        + [shaped(F32, node_rows, latent), shaped(BF16, total_slots, latent)],
        [
            cut_senders,
            cut_receivers,
            edges,
            nodes,
            far,
            w_edge_in,
            w_edge_out,
            inner_total,
        ],
        [
            all_spec(cut_senders),
            all_spec(cut_receivers),
            last_rows(edges),
            all_spec(nodes),
            all_spec(far),
            all_spec(w_edge_in),
            all_spec(w_edge_out),
            all_spec(inner_total),
        ],
        [rows_spec(width) for width in saved_widths[2:]]
        + [all_spec(nodes), rows_spec(latent, total_slots)],
        (1,),
    )
    incoming = exchange(outgoing, domains)
    new_edges = line.run(
        new_edges_kernel,
        shaped(BF16, *edges.shape),
        [edges, inner_normed, cut_normed],
    )
    (
        new_nodes,
        self_grad,
        agg_grad,
        grad_reply,
        node_keep,
        node_send,
    ) = line.run(
        node_kernel,
        [
            shaped(BF16, node_rows, latent),
            shaped(F32, node_rows, latent),
            shaped(BF16, node_rows, latent),
            shaped(BF16, total_slots, latent),
        ]
        + [shaped(BF16, 3 * latent // 2, latent)] * 2,
        [me, incoming, asked_marks, total, nodes, ct_nodes, w_node_in, w_node_out],
        [SMEM] + [VMEM] * 7,
    )
    far_grad = exchange(grad_reply, domains)
    node_sum = added(node_keep, across(node_send, domains, 1))
    inner_out, inner_pre = line.run(
        inner_backward_kernel,
        [shaped(BF16, inner_rows, latent)] * 2,
        [
            inner_receivers,
            agg_grad,
            ct_edges,
            inner_normed,
            inner_scale,
            inner_slope,
            w_edge_out,
        ],
        [
            rows_spec(node_rows),
            all_spec(agg_grad),
            rows_spec(latent),
            rows_spec(latent),
            rows_spec(1),
            rows_spec(latent),
            all_spec(w_edge_out),
        ],
        [rows_spec(latent)] * 2,
        (blocks,),
    )
    bits = index_bits(domains)
    node_own, node_sent = split([node_sum], 1)
    node_parts = [*node_own, across(node_sent, domains, 2)]
    far_grad, node_sum, inner_pre = fence(far_grad, node_sum, inner_pre)
    factors = [
        edges,
        inner_sender,
        cut_sender,
        inner_receiver,
        cut_receiver,
        inner_hidden,
        cut_hidden,
        inner_out,
        inner_pre,
    ]
    buffers = [
        pltpu.VMEM((rows, latent), BF16) for rows in (inner_rows, cut_rows, inner_rows) * 2
    ]
    buffers.append(pltpu.SemaphoreType.DMA((len(buffers),)))
    cut_out, cut_pre, edge_send = line.run(
        cut_backward_kernel,
        [shaped(BF16, cut_rows, latent)] * 2 + [shaped(BF16, 2 * latent, latent)],
        [
            me,
            cut_receivers,
            agg_grad,
            far_grad,
            ct_edges,
            cut_normed,
            cut_scale,
            cut_slope,
            w_edge_out,
        ]
        + factors,
        [
            SMEM,
            all_spec(cut_receivers),
            all_spec(agg_grad),
            all_spec(far_grad),
            last_rows(ct_edges),
            all_spec(cut_normed),
            all_spec(cut_scale),
            all_spec(cut_slope),
            all_spec(w_edge_out),
        ]
        + [ANY] * len(factors),
        [rows_spec(latent)] * 2 + [rows_spec(latent, 2 * latent)],
        (1,),
        buffers,
    )
    edge_send, place, *node_parts = fence(edge_send, me, *node_parts)
    received = across(edge_send, domains, 1)
    node_own, node_sent = split(node_parts, 2)
    node_got = across(node_sent, domains, 4)
    edge_keep = line.run(
        edge_weights_kernel,
        shaped(BF16, 2 * latent, latent),
        [place, cut_out, cut_pre] + factors,
        [SMEM, VMEM, VMEM] + [ANY] * len(factors),
        scratch=buffers,
    )
    edge_keep, received = fence(edge_keep, received)
    edge_sent = added(edge_keep[latent:], received[latent:])
    edge_sent, inner_pre, cut_pre = fence(edge_sent, inner_pre, cut_pre)
    node_got = fence(node_got, edge_sent)[0]
    edge_got = across(edge_sent, domains, 2)
    node_sum = added(*node_own, node_got)
    for bit in bits[3:]:
        node_sum = added(*handed(node_sum, domains, bit))
    edge_keep, received = fence(edge_keep, received, edge_sent)[:2]
    edge_own = added(edge_keep[:latent], received[:latent])
    local_grad, outgoing_grad = line.run(
        input_grads_kernel,
        [shaped(F32, node_rows, latent), shaped(BF16, total_slots, latent)],
        [
            inner_senders,
            inner_receivers,
            cut_senders,
            cut_receivers,
            inner_pre,
            cut_pre,
            w_edge_in,
        ],
    )
    edge_own, edge_got, node_sum, inner_pre, cut_pre, local_grad = fence(
        edge_own, edge_got, node_sum, inner_pre, cut_pre, local_grad
    )
    edge_own, edge_sent = split([added(edge_own, edge_got)], 2)
    edge_got = across(edge_sent, domains, 4)
    grad_edges = line.run(
        functools.partial(edge_grads_kernel, blocks=blocks),
        shaped(F32, *edges.shape),
        [ct_edges, inner_pre, cut_pre, w_edge_in],
        [
            rows_spec(latent),
            pl.BlockSpec((block, latent), lambda step: (jnp.minimum(step, blocks - 1), 0)),
            all_spec(cut_pre),
            pl.BlockSpec((latent, latent), lambda step: (0, 0)),
        ],
        [rows_spec(latent)],
        (blocks + 1,),
    )
    edge_got, node_sum, grad_edges = fence(edge_got, node_sum, grad_edges)
    edge_sum = added(*edge_own, edge_got)
    edge_sum, node_sum = fence(edge_sum, node_sum)
    edge_got = across(edge_sum, domains, 8)
    node_parts = handed(joined(handed(node_sum, domains, 2), 2), domains, 1)
    edge_sum = added(*fence(edge_sum, edge_got))
    for bit in bits[4:]:
        edge_sum = added(*handed(edge_sum, domains, bit))
    *edge_parts, node_sum, other_sum, outgoing_grad = fence(
        *handed(edge_sum, domains, 2), *node_parts, outgoing_grad
    )
    edge_sum = joined(edge_parts, 2)
    node_sum = joined([node_sum, other_sum], 1)
    far, near = across(edge_sum, domains, 2), across(edge_sum, domains, 1)
    others = across(node_sum, domains, 1)
    returned = exchange(outgoing_grad, domains)
    lower, left = place_of(0) == 0, place_of(1) == 0
    low_rows, high_rows = jnp.where(lower, node_sum, others), jnp.where(lower, others, node_sum)
    cut_at = 2 * latent - low_rows.shape[0]
    grad_node_in = jnp.concatenate([low_rows, high_rows[:cut_at]])
    grad_node_out = high_rows[cut_at:]
    far, near, grad_node_in, grad_node_out, returned = fence(
        far, near, grad_node_in, grad_node_out, returned
    )
    corner = across(far, domains, 1)
    grad_nodes = self_grad + local_grad + dot_rows(asked_marks, returned)
    low_half = [jnp.where(lower, edge_sum, near), jnp.where(lower, far, corner)]
    high_half = [jnp.where(lower, near, edge_sum), jnp.where(lower, corner, far)]
    grad_edge_out = jnp.where(left, high_half[1], high_half[0])
    grad_edge_in = jnp.concatenate(
        [
            jnp.where(left, low_half[0], low_half[1]),
            jnp.where(left, low_half[1], low_half[0]),
            jnp.where(left, high_half[0], high_half[1]),
        ]
    )
    return (
        new_nodes,
        new_edges,
        grad_nodes,
        grad_edges,
        grad_edge_in,
        grad_edge_out,
        grad_node_in,
        grad_node_out,
    )


def solution(mesh):
    placed = (
        P(("groups", "dom"), None),
        P(("groups", "dom"), None),
        P(("groups", "dom"), None),
        P(("groups", "dom")),
        P(("groups", "dom"), None),
        P(("groups", "dom")),
        P(),
        P(),
        P(),
        P(),
        P(("groups", "dom"), None),
        P(("groups", "dom"), None),
    )
    return jax.shard_map(
        shards,
        mesh=mesh,
        in_specs=placed,
        out_specs=(
            P(("groups", "dom"), None),
            P(("groups", "dom"), None),
            P(("groups", "dom"), None),
            P(("groups", "dom"), None),
            P("groups", None),
            P("groups", None),
            P("groups", None),
            P("groups", None),
        ),
        check_vma=False,
    )
```

```python
import functools

import jax
import jax.numpy as jnp
from jax import lax
from jax.experimental import pallas as pl
from jax.experimental.pallas import tpu as pltpu
from jax.sharding import PartitionSpec as P

BF16 = jnp.bfloat16
F32 = jnp.float32
VMEM_LIMIT = 60 * 1024 * 1024


def dot(left, right):
    return jnp.dot(left, right, preferred_element_type=F32)


def dot_rows(left, right):
    return lax.dot_general(left, right, (((0,), (0,)), ((), ())), preferred_element_type=F32)


def dot_cols(left, right):
    return lax.dot_general(left, right, (((1,), (1,)), ((), ())), preferred_element_type=F32)


def iota(shape, axis):
    return lax.broadcasted_iota(jnp.int32, shape, axis)


def marks(mask):
    return jnp.where(mask, 1.0, 0.0).astype(BF16)


def onehot(column, width):
    return marks(column == iota((column.shape[0], width), 1))


def to_column(row):
    count = row.shape[1]
    square = (count, count)
    kept = jnp.where(iota(square, 0) == iota(square, 1), row.astype(F32), 0.0)
    return jnp.sum(kept, axis=1, keepdims=True)


def slot_ranks(dest, domains):
    count = dest.shape[0]
    square = (count, count)
    dest_marks = onehot(dest, domains)
    before = dot(marks(iota(square, 0) > iota(square, 1)), dest_marks)
    return dest_marks, jnp.sum(before * dest_marks.astype(F32), axis=1, keepdims=True)


def pair_marks(first, second, width):
    pairs = first.shape[0]
    shape = (2 * pairs, pairs)
    edge, pair = iota(shape, 0), iota(shape, 1)
    mine = (edge >> 1) == pair
    even = marks(mine & ((edge & 1) == 0))
    odd = marks(mine & ((edge & 1) == 1))
    first_marks, second_marks = onehot(first, width), onehot(second, width)
    senders = dot(even, first_marks) + dot(odd, second_marks)
    receivers = dot(even, second_marks) + dot(odd, first_marks)
    return senders.astype(BF16), receivers.astype(BF16)


def normalise(values):
    centered = values - jnp.mean(values, axis=1, keepdims=True)
    inv_scale = lax.rsqrt(jnp.mean(centered * centered, axis=1, keepdims=True) + 1e-05)
    return centered * inv_scale, inv_scale


def activate(pre_hidden):
    gate = jax.nn.sigmoid(pre_hidden)
    return (pre_hidden * gate).astype(BF16), gate * (1.0 + pre_hidden * (1.0 - gate))


def norm_backward(upstream, normed, inv_scale):
    centered = (
        upstream
        - jnp.mean(upstream, axis=1, keepdims=True)
        - normed * jnp.mean(upstream * normed, axis=1, keepdims=True)
    )
    return (inv_scale * centered).astype(BF16)


def ask_kernel(dest_ref, remote_ref, ask_ref):
    domains, slots = ask_ref.shape
    dest_marks, rank = slot_ranks(to_column(dest_ref[...]).astype(jnp.int32), domains)
    rank_marks = jnp.where(rank == iota((rank.shape[0], slots), 1).astype(F32), 1.0, 0.0)
    wanted = (rank_marks * to_column(remote_ref[...])).astype(BF16)
    ask_ref[...] = dot_rows(dest_marks, wanted).astype(jnp.int32)


def cut_marks_kernel(dest_ref, local_ref, senders_ref, receivers_ref, *, domains, slots):
    width = senders_ref.shape[1]
    base = width - domains * slots
    dest = to_column(dest_ref[...]).astype(jnp.int32)
    _, rank = slot_ranks(dest, domains)
    second = dest * slots + rank.astype(jnp.int32) + base
    first = to_column(local_ref[...]).astype(jnp.int32)
    senders, receivers = pair_marks(first, second, width)
    senders_ref[...] = senders
    receivers_ref[...] = receivers


def edge_forward(edge, sender, receiver, w_in_ref, w_out_ref):
    latent = edge.shape[1]
    pre_hidden = (
        dot(edge, w_in_ref[:latent])
        + dot(sender, w_in_ref[latent : 2 * latent])
        + dot(receiver, w_in_ref[2 * latent :])
    )
    hidden, slope = activate(pre_hidden)
    normed, inv_scale = normalise(dot(hidden, w_out_ref[...]))
    return hidden, slope, normed, inv_scale


def inner_forward_kernel(
    pairs_ref,
    edges_ref,
    nodes_ref,
    w_in_ref,
    w_out_ref,
    senders_ref,
    receivers_ref,
    sender_ref,
    receiver_ref,
    hidden_ref,
    slope_ref,
    normed_ref,
    scale_ref,
    total_ref,
):
    first, second = (to_column(pairs_ref[side : side + 1]).astype(jnp.int32) for side in range(2))
    senders, receivers = pair_marks(first, second, nodes_ref.shape[0])
    senders_ref[...] = senders
    receivers_ref[...] = receivers
    nodes = nodes_ref[...]
    sender = dot(senders, nodes).astype(BF16)
    receiver = dot(receivers, nodes).astype(BF16)
    sender_ref[...] = sender
    receiver_ref[...] = receiver
    hidden, slope, normed, inv_scale = edge_forward(
        edges_ref[...], sender, receiver, w_in_ref, w_out_ref
    )
    hidden_ref[...] = hidden
    slope_ref[...] = slope
    normed_ref[...] = normed
    scale_ref[...] = inv_scale
    part = dot_rows(receivers, normed.astype(BF16))

    @pl.when(pl.program_id(0) == 0)
    def _():
        total_ref[...] = part

    @pl.when(pl.program_id(0) > 0)
    def _():
        total_ref[...] += part


def cut_forward_kernel(
    senders_ref,
    receivers_ref,
    edges_ref,
    nodes_ref,
    far_ref,
    w_in_ref,
    w_out_ref,
    inner_total_ref,
    sender_ref,
    receiver_ref,
    hidden_ref,
    slope_ref,
    normed_ref,
    scale_ref,
    total_ref,
    outgoing_ref,
):
    base = nodes_ref.shape[0]
    nodes, far = nodes_ref[...], far_ref[...]

    def rows_of(marks_ref):
        return (dot(marks_ref[:, :base], nodes) + dot(marks_ref[:, base:], far)).astype(BF16)

    sender, receiver = rows_of(senders_ref), rows_of(receivers_ref)
    sender_ref[...] = sender
    receiver_ref[...] = receiver
    hidden, slope, normed, inv_scale = edge_forward(
        edges_ref[...], sender, receiver, w_in_ref, w_out_ref
    )
    hidden_ref[...] = hidden
    slope_ref[...] = slope
    normed_ref[...] = normed
    scale_ref[...] = inv_scale
    message = normed.astype(BF16)
    total_ref[...] = inner_total_ref[...] + dot_rows(receivers_ref[:, :base], message)
    outgoing_ref[...] = dot_rows(receivers_ref[:, base:], message).astype(BF16)


def new_edges_kernel(edges_ref, inner_ref, cut_ref, out_ref):
    inner_rows = inner_ref.shape[0]

    def added(edge, normed):
        return (edge.astype(F32) + normed.astype(BF16).astype(F32)).astype(BF16)

    out_ref[:inner_rows] = added(edges_ref[:inner_rows], inner_ref[...])
    out_ref[inner_rows:] = added(edges_ref[inner_rows:], cut_ref[...])


def node_kernel(
    me_ref,
    incoming_ref,
    asked_marks_ref,
    total_ref,
    nodes_ref,
    ct_ref,
    w_in_ref,
    w_out_ref,
    new_nodes_ref,
    self_grad_ref,
    agg_grad_ref,
    reply_ref,
    keep_ref,
    send_ref,
):
    latent = nodes_ref.shape[1]
    half = latent // 2
    nodes, asked_marks = nodes_ref[...], asked_marks_ref[...]
    aggregate = (total_ref[...] + dot_rows(asked_marks, incoming_ref[...])).astype(BF16)
    pre_hidden = dot(nodes, w_in_ref[:latent]) + dot(aggregate, w_in_ref[latent:])
    hidden, slope = activate(pre_hidden)
    normed, inv_scale = normalise(dot(hidden, w_out_ref[...]))
    upstream = ct_ref[...].astype(F32)
    grad_out = norm_backward(upstream, normed, inv_scale)
    grad_pre = (dot_cols(grad_out, w_out_ref[...]) * slope).astype(BF16)
    agg_grad = dot_cols(grad_pre, w_in_ref[latent:]).astype(BF16)
    agg_grad_ref[...] = agg_grad
    reply_ref[...] = dot(asked_marks, agg_grad).astype(BF16)
    self_grad_ref[...] = upstream + dot_cols(grad_pre, w_in_ref[:latent])
    new_nodes_ref[...] = (nodes.astype(F32) + normed).astype(BF16)

    def fill(low_ref, high_ref):
        by_aggregate = dot_rows(aggregate, grad_pre).astype(BF16)
        low_ref[:latent] = dot_rows(nodes, grad_pre).astype(BF16)
        low_ref[latent:] = by_aggregate[:half]
        high_ref[:half] = by_aggregate[half:]
        high_ref[half:] = dot_rows(hidden, grad_out).astype(BF16)

    @pl.when((me_ref[0] & 1) == 0)
    def _():
        fill(keep_ref, send_ref)

    @pl.when((me_ref[0] & 1) != 0)
    def _():
        fill(send_ref, keep_ref)


def edge_backward(ct, target_grads, normed, inv_scale, slope, w_out):
    grad_out = norm_backward(ct.astype(F32) + target_grads, normed, inv_scale)
    return grad_out, (dot_cols(grad_out, w_out) * slope).astype(BF16)


def inner_backward_kernel(
    receivers_ref,
    agg_grad_ref,
    ct_ref,
    normed_ref,
    scale_ref,
    slope_ref,
    w_out_ref,
    grad_out_ref,
    grad_pre_ref,
):
    grad_out, grad_pre = edge_backward(
        ct_ref[...],
        dot(receivers_ref[...], agg_grad_ref[...]),
        normed_ref[...],
        scale_ref[...],
        slope_ref[...],
        w_out_ref[...],
    )
    grad_out_ref[...] = grad_out
    grad_pre_ref[...] = grad_pre


def fetch_factors(half, sources, buffers, sems, wait):
    edges, inner_sender, cut_sender, inner_receiver, cut_receiver = sources[:5]
    inner_hidden, cut_hidden, inner_out, inner_pre = sources[5:]
    inner_rows, cut_rows = inner_pre.shape[0], cut_sender.shape[0]
    inner_edges = edges.at[pl.ds(0, inner_rows)]
    cut_edges = edges.at[pl.ds(inner_rows, cut_rows)]
    low = [inner_edges, cut_edges, inner_sender, cut_sender, inner_pre, inner_pre]
    high = [inner_receiver, cut_receiver, inner_hidden, cut_hidden, inner_pre, inner_out]

    def each(parts):
        for index, (source, buffer) in enumerate(zip(parts, buffers)):
            copy = pltpu.make_async_copy(source, buffer, sems.at[index])
            if wait:
                copy.wait()
            else:
                copy.start()

    @pl.when(half == 0)
    def _():
        each(low)

    @pl.when(half != 0)
    def _():
        each(high)


def place_rows(me_ref, index, latent):
    return pl.ds(pl.multiple_of((index ^ ((me_ref[0] >> 1) & 1)) * latent, latent), latent)


def edge_rows(me_ref, half, buffers, cut_pre, cut_out, out_ref):
    latent = cut_pre.shape[1]
    first, first_cut, second, second_cut, first_right, second_right = buffers
    chosen = jnp.where(half == 0, cut_pre.astype(F32), cut_out.astype(F32)).astype(BF16)
    out_ref[place_rows(me_ref, 0, latent)] = (
        dot_rows(first[...], first_right[...]) + dot_rows(first_cut[...], cut_pre)
    ).astype(BF16)
    out_ref[place_rows(me_ref, 1, latent)] = (
        dot_rows(second[...], second_right[...]) + dot_rows(second_cut[...], chosen)
    ).astype(BF16)


def cut_backward_kernel(
    me_ref,
    receivers_ref,
    agg_grad_ref,
    far_grad_ref,
    ct_ref,
    normed_ref,
    scale_ref,
    slope_ref,
    w_out_ref,
    *refs,
):
    sources, (grad_out_ref, grad_pre_ref, out_ref), rest = refs[:9], refs[9:12], refs[12:]
    buffers, sems = rest[:-1], rest[-1]
    half = 1 - (me_ref[0] & 1)
    fetch_factors(half, sources, buffers, sems, False)
    base = agg_grad_ref.shape[0]
    target = dot(receivers_ref[:, :base], agg_grad_ref[...]) + dot(
        receivers_ref[:, base:], far_grad_ref[...]
    )
    grad_out, grad_pre = edge_backward(
        ct_ref[...], target, normed_ref[...], scale_ref[...], slope_ref[...], w_out_ref[...]
    )
    grad_out_ref[...] = grad_out
    grad_pre_ref[...] = grad_pre
    fetch_factors(half, sources, buffers, sems, True)
    edge_rows(me_ref, half, buffers, grad_pre, grad_out, out_ref)


def edge_weights_kernel(me_ref, cut_out_ref, cut_pre_ref, *refs):
    sources, out_ref, rest = refs[:9], refs[9], refs[10:]
    buffers, sems = rest[:-1], rest[-1]
    half = me_ref[0] & 1
    fetch_factors(half, sources, buffers, sems, False)
    fetch_factors(half, sources, buffers, sems, True)
    edge_rows(me_ref, half, buffers, cut_pre_ref[...], cut_out_ref[...], out_ref)


def place_quarters(me_ref, pieces, outs, sems):
    mine = (me_ref[0] & 1) * 2 + ((me_ref[0] >> 1) & 1)

    def each(wait):
        for index, (piece, distance) in enumerate(pieces):
            rows = piece.shape[0]
            for quarter in range(4):
                inside = (quarter + 1) * rows <= outs[0].shape[0]
                goal = outs[0].at[pl.ds(quarter * rows, rows)] if inside else outs[1]
                copy = pltpu.make_async_copy(piece, goal, sems.at[index])

                @pl.when((mine ^ distance) == quarter)
                def _():
                    if wait:
                        copy.wait()
                    else:
                        copy.start()

    each(False)
    each(True)


def first_quarters_kernel(me_ref, mine_ref, near_ref, in_ref, out_ref, sems):
    place_quarters(me_ref, [(mine_ref, 0), (near_ref, 2)], (in_ref, out_ref), sems)


def last_quarters_kernel(me_ref, far_ref, corner_ref, _, __, in_ref, out_ref, sems):
    place_quarters(me_ref, [(far_ref, 1), (corner_ref, 3)], (in_ref, out_ref), sems)


def input_grads_kernel(
    inner_senders_ref,
    inner_receivers_ref,
    cut_senders_ref,
    cut_receivers_ref,
    inner_pre_ref,
    cut_pre_ref,
    w_in_ref,
    local_ref,
    outgoing_ref,
):
    latent = inner_pre_ref.shape[1]
    base = inner_senders_ref.shape[1]
    inner_pre, cut_pre = inner_pre_ref[...], cut_pre_ref[...]
    w_sender, w_receiver = w_in_ref[latent : 2 * latent], w_in_ref[2 * latent :]

    def summed(inner_marks_ref, cut_marks_ref):
        return (
            dot_rows(inner_marks_ref[...], inner_pre) + dot_rows(cut_marks_ref[:, :base], cut_pre)
        ).astype(BF16)

    outgoing_ref[...] = (
        dot_cols(dot_rows(cut_senders_ref[:, base:], cut_pre).astype(BF16), w_sender)
        + dot_cols(dot_rows(cut_receivers_ref[:, base:], cut_pre).astype(BF16), w_receiver)
    ).astype(BF16)
    local_ref[...] = dot_cols(summed(inner_senders_ref, cut_senders_ref), w_sender) + dot_cols(
        summed(inner_receivers_ref, cut_receivers_ref), w_receiver
    )


def edge_grads_kernel(ct_ref, inner_pre_ref, cut_pre_ref, w_edge_ref, out_ref, *, blocks):
    inside = pl.program_id(0) < blocks

    @pl.when(inside)
    def _():
        out_ref[...] = ct_ref[...].astype(F32) + dot_cols(inner_pre_ref[...], w_edge_ref[...])

    @pl.when(jnp.logical_not(inside))
    def _():
        out_ref[...] = ct_ref[...].astype(F32) + dot_cols(cut_pre_ref[...], w_edge_ref[...])


VMEM = pl.BlockSpec(memory_space=pltpu.VMEM)
SMEM = pl.BlockSpec(memory_space=pltpu.SMEM)
ANY = pl.BlockSpec(memory_space=pl.ANY)
HBM = pl.BlockSpec(memory_space=pltpu.HBM)


def shaped(dtype, *shape):
    return jax.ShapeDtypeStruct(shape, dtype)


class Line:
    def __init__(self):
        self.last = None

    def run(
        self, body, outs, ins, specs=None, out_specs=None, grid=None, scratch=(), limit=VMEM_LIMIT, aliases=None
    ):
        single = not isinstance(outs, (list, tuple))
        out_shape = [outs] if single else list(outs)
        specs = [VMEM] * len(ins) if specs is None else list(specs)
        count, extra = len(ins), {} if grid is None else {"grid": grid}
        ins = list(ins)
        if self.last is not None:
            ins.append(self.last)
            specs.append(ANY)

        def ordered(*refs):
            return body(*refs[:count], *refs[len(ins) :])

        result = pl.pallas_call(
            ordered,
            out_shape=out_shape,
            in_specs=specs,
            out_specs=[VMEM] * len(out_shape) if out_specs is None else out_specs,
            scratch_shapes=scratch,
            input_output_aliases=aliases or {},
            compiler_params=pltpu.CompilerParams(vmem_limit_bytes=limit),
            cost_estimate=pl.CostEstimate(flops=1, bytes_accessed=1, transcendentals=0),
            **extra,
        )(*ins)
        self.last = result[-1]
        return result[0] if single else result


def index_bits(devices):
    return list(range(devices.bit_length() - 1))


def across(rows, devices, mask):
    return lax.ppermute(rows, "dom", [(device, device ^ mask) for device in range(devices)])


def fence(*values):
    return lax.optimization_barrier(values)


def place_of(bit):
    return (lax.axis_index("dom") >> bit) & 1


def split(parts, bit):
    place = place_of(bit)
    halves = [part.reshape(2, part.shape[0] // 2, part.shape[1]) for part in parts]
    own = [lax.dynamic_index_in_dim(half, place, 0, False) for half in halves]
    sent = [lax.dynamic_index_in_dim(half, 1 - place, 0, False) for half in halves]
    return own, added(*sent)


def handed(rows, devices, bit):
    return [rows, across(rows, devices, 1 << bit)]


def added(*parts):
    return sum(part.astype(F32) for part in parts).astype(BF16)


def joined(parts, bit):
    orders = [jnp.concatenate(parts), jnp.concatenate(parts[::-1])]
    return jnp.where(place_of(bit) == 0, *orders)


def exchange(rows, domains):
    shape = rows.shape
    split = rows.reshape((domains, shape[0] // domains) + shape[1:])
    return lax.all_to_all(split, "dom", split_axis=0, concat_axis=0, tiled=True).reshape(shape)


def shards(
    nodes,
    edges,
    inner_pairs,
    cut_local,
    cut_dest,
    cut_remote,
    w_edge_in,
    w_edge_out,
    w_node_in,
    w_node_out,
    ct_nodes,
    ct_edges,
):
    domains = lax.axis_size("dom")
    node_rows, latent = nodes.shape
    inner_count, cut_count = inner_pairs.shape[0], cut_local.shape[0]
    inner_rows, cut_rows = 2 * inner_count, 2 * cut_count
    slots = max(2, 2 * cut_count // domains)
    total_slots = domains * slots
    table = node_rows + total_slots
    me = lax.axis_index("dom").reshape(1)
    line = Line()

    ask = line.run(
        ask_kernel, shaped(jnp.int32, domains, slots), [cut_dest.reshape(1, -1), cut_remote.reshape(1, -1)]
    )
    asked = lax.all_to_all(ask, "dom", split_axis=0, concat_axis=0, tiled=True)
    cut_senders, cut_receivers = line.run(
        functools.partial(cut_marks_kernel, domains=domains, slots=slots),
        [shaped(BF16, cut_rows, table)] * 2,
        [cut_dest.reshape(1, -1), cut_local.reshape(1, -1)],
    )
    asked_marks = jnp.where(
        asked[:, :, None] == jnp.arange(node_rows, dtype=jnp.int32)[None, None], 1.0, 0.0
    ).astype(BF16)
    reply = lax.dot_general(asked_marks, nodes, (((2,), (0,)), ((), ())), preferred_element_type=F32)
    reply = reply.astype(BF16).reshape(total_slots, latent)
    asked_marks = asked_marks.reshape(total_slots, node_rows)
    far = exchange(reply, domains)

    block = cut_rows
    blocks = inner_rows // block

    def rows_spec(width, rows=block):
        return pl.BlockSpec((rows, width), lambda step: (step, 0))

    def all_spec(array):
        return pl.BlockSpec(array.shape, lambda step: (0, 0))

    saved_widths = [node_rows, node_rows, latent, latent, latent, latent, latent, 1]
    saved_types = [BF16, BF16, BF16, BF16, BF16, F32, F32, F32]
    (
        inner_senders,
        inner_receivers,
        inner_sender,
        inner_receiver,
        inner_hidden,
        inner_slope,
        inner_normed,
        inner_scale,
        inner_total,
    ) = line.run(
        inner_forward_kernel,
        [shaped(kind, inner_rows, width) for kind, width in zip(saved_types, saved_widths)]
        + [shaped(F32, node_rows, latent)],
        [inner_pairs.T, edges, nodes, w_edge_in, w_edge_out],
        [
            pl.BlockSpec((2, block // 2), lambda step: (0, step)),
            rows_spec(latent),
            all_spec(nodes),
            all_spec(w_edge_in),
            all_spec(w_edge_out),
        ],
        [rows_spec(width) for width in saved_widths] + [all_spec(nodes)],
        (blocks,),
    )

    def last_rows(array):
        last = array.shape[0] // block - 1
        return pl.BlockSpec((block, array.shape[1]), lambda step: (last, 0))

    (
        cut_sender,
        cut_receiver,
        cut_hidden,
        cut_slope,
        cut_normed,
        cut_scale,
        total,
        outgoing,
    ) = line.run(
        cut_forward_kernel,
        [shaped(kind, cut_rows, width) for kind, width in zip(saved_types, saved_widths)][2:]
        + [shaped(F32, node_rows, latent), shaped(BF16, total_slots, latent)],
        [
            cut_senders,
            cut_receivers,
            edges,
            nodes,
            far,
            w_edge_in,
            w_edge_out,
            inner_total,
        ],
        [
            all_spec(cut_senders),
            all_spec(cut_receivers),
            last_rows(edges),
            all_spec(nodes),
            all_spec(far),
            all_spec(w_edge_in),
            all_spec(w_edge_out),
            all_spec(inner_total),
        ],
        [rows_spec(width) for width in saved_widths[2:]]
        + [all_spec(nodes), rows_spec(latent, total_slots)],
        (1,),
    )
    incoming = exchange(outgoing, domains)
    new_edges = line.run(
        new_edges_kernel,
        shaped(BF16, *edges.shape),
        [edges, inner_normed, cut_normed],
    )
    (
        new_nodes,
        self_grad,
        agg_grad,
        grad_reply,
        node_keep,
        node_send,
    ) = line.run(
        node_kernel,
        [
            shaped(BF16, node_rows, latent),
            shaped(F32, node_rows, latent),
            shaped(BF16, node_rows, latent),
            shaped(BF16, total_slots, latent),
        ]
        + [shaped(BF16, 3 * latent // 2, latent)] * 2,
        [me, incoming, asked_marks, total, nodes, ct_nodes, w_node_in, w_node_out],
        [SMEM] + [VMEM] * 7,
    )
    far_grad = exchange(grad_reply, domains)
    node_sum = added(node_keep, across(node_send, domains, 1))
    inner_out, inner_pre = line.run(
        inner_backward_kernel,
        [shaped(BF16, inner_rows, latent)] * 2,
        [
            inner_receivers,
            agg_grad,
            ct_edges,
            inner_normed,
            inner_scale,
            inner_slope,
            w_edge_out,
        ],
        [
            rows_spec(node_rows),
            all_spec(agg_grad),
            rows_spec(latent),
            rows_spec(latent),
            rows_spec(1),
            rows_spec(latent),
            all_spec(w_edge_out),
        ],
        [rows_spec(latent)] * 2,
        (blocks,),
    )
    bits = index_bits(domains)
    node_own, node_sent = split([node_sum], 1)
    node_parts = [*node_own, across(node_sent, domains, 2)]
    far_grad, node_sum, inner_pre = fence(far_grad, node_sum, inner_pre)
    factors = [
        edges,
        inner_sender,
        cut_sender,
        inner_receiver,
        cut_receiver,
        inner_hidden,
        cut_hidden,
        inner_out,
        inner_pre,
    ]
    buffers = [pltpu.VMEM((rows, latent), BF16) for rows in (inner_rows, cut_rows) * 2]
    buffers += [pltpu.VMEM((inner_rows, latent), BF16)] * 2
    buffers.append(pltpu.SemaphoreType.DMA((len(buffers),)))
    cut_out, cut_pre, edge_send = line.run(
        cut_backward_kernel,
        [shaped(BF16, cut_rows, latent)] * 2 + [shaped(BF16, 2 * latent, latent)],
        [
            me,
            cut_receivers,
            agg_grad,
            far_grad,
            ct_edges,
            cut_normed,
            cut_scale,
            cut_slope,
            w_edge_out,
        ]
        + factors,
        [
            SMEM,
            all_spec(cut_receivers),
            all_spec(agg_grad),
            all_spec(far_grad),
            last_rows(ct_edges),
            all_spec(cut_normed),
            all_spec(cut_scale),
            all_spec(cut_slope),
            all_spec(w_edge_out),
        ]
        + [ANY] * len(factors),
        [rows_spec(latent)] * 2 + [rows_spec(latent, 2 * latent)],
        (1,),
        buffers,
    )
    edge_send, place, *node_parts = fence(edge_send, me, *node_parts)
    received = across(edge_send, domains, 1)
    node_own, node_sent = split(node_parts, 2)
    node_got = across(node_sent, domains, 4)
    edge_keep = line.run(
        edge_weights_kernel,
        shaped(BF16, 2 * latent, latent),
        [place, cut_out, cut_pre] + factors,
        [SMEM, VMEM, VMEM] + [ANY] * len(factors),
        scratch=buffers,
    )
    edge_keep, received = fence(edge_keep, received)
    edge_sent = added(edge_keep[latent:], received[latent:])
    edge_sent, inner_pre, cut_pre = fence(edge_sent, inner_pre, cut_pre)
    node_got = fence(node_got, edge_sent)[0]
    edge_got = across(edge_sent, domains, 2)
    node_sum = added(*node_own, node_got)
    for bit in bits[3:]:
        node_sum = added(*handed(node_sum, domains, bit))
    edge_keep, received = fence(edge_keep, received, edge_sent)[:2]
    edge_own = added(edge_keep[:latent], received[:latent])
    local_grad, outgoing_grad = line.run(
        input_grads_kernel,
        [shaped(F32, node_rows, latent), shaped(BF16, total_slots, latent)],
        [
            inner_senders,
            inner_receivers,
            cut_senders,
            cut_receivers,
            inner_pre,
            cut_pre,
            w_edge_in,
        ],
    )
    edge_own, edge_got, node_sum, inner_pre, cut_pre, local_grad = fence(
        edge_own, edge_got, node_sum, inner_pre, cut_pre, local_grad
    )
    edge_own, edge_sent = split([added(edge_own, edge_got)], 2)
    edge_got = across(edge_sent, domains, 4)
    grad_edges = line.run(
        functools.partial(edge_grads_kernel, blocks=blocks),
        shaped(F32, *edges.shape),
        [ct_edges, inner_pre, cut_pre, w_edge_in],
        [
            rows_spec(latent),
            pl.BlockSpec((block, latent), lambda step: (jnp.minimum(step, blocks - 1), 0)),
            all_spec(cut_pre),
            pl.BlockSpec((latent, latent), lambda step: (0, 0)),
        ],
        [rows_spec(latent)],
        (blocks + 1,),
    )
    edge_got, node_sum, grad_edges = fence(edge_got, node_sum, grad_edges)
    edge_sum = added(*edge_own, edge_got)
    edge_sum, node_sum = fence(edge_sum, node_sum)
    edge_got = across(edge_sum, domains, 8)
    node_parts = handed(joined(handed(node_sum, domains, 2), 2), domains, 1)
    edge_sum = added(*fence(edge_sum, edge_got))
    for bit in bits[4:]:
        edge_sum = added(*handed(edge_sum, domains, bit))
    *edge_parts, node_sum, other_sum, outgoing_grad = fence(
        *handed(edge_sum, domains, 2), *node_parts, outgoing_grad
    )
    edge_sum = joined(edge_parts, 2)
    node_sum = joined([node_sum, other_sum], 1)
    far, near = across(edge_sum, domains, 2), across(edge_sum, domains, 1)
    others = across(node_sum, domains, 1)
    returned = exchange(outgoing_grad, domains)
    lower = place_of(0) == 0
    low_rows, high_rows = jnp.where(lower, node_sum, others), jnp.where(lower, others, node_sum)
    cut_at = 2 * latent - low_rows.shape[0]
    grad_node_in = jnp.concatenate([low_rows, high_rows[:cut_at]])
    grad_node_out = high_rows[cut_at:]
    quarters = [shaped(BF16, 3 * latent, latent), shaped(BF16, latent, latent)]
    copies = dict(out_specs=[HBM] * 2, scratch=[pltpu.SemaphoreType.DMA((2,))], limit=2**20)
    grad_edge_in, grad_edge_out = line.run(
        first_quarters_kernel, quarters, [me, edge_sum, near], [SMEM, ANY, ANY], **copies
    )
    far, grad_edge_in, grad_edge_out, grad_node_in, grad_node_out, returned = fence(
        far, grad_edge_in, grad_edge_out, grad_node_in, grad_node_out, returned
    )
    corner = across(far, domains, 1)
    grad_nodes = self_grad + local_grad + dot_rows(asked_marks, returned)
    corner, grad_nodes = fence(corner, grad_nodes)
    grad_edge_in, grad_edge_out = Line().run(
        last_quarters_kernel,
        quarters,
        [me, far, corner, grad_edge_in, grad_edge_out],
        [SMEM, ANY, ANY, HBM, HBM],
        aliases={3: 0, 4: 1},
        **copies,
    )
    return (
        new_nodes,
        new_edges,
        grad_nodes,
        grad_edges,
        grad_edge_in,
        grad_edge_out,
        grad_node_in,
        grad_node_out,
    )


def solution(mesh):
    placed = (
        P(("groups", "dom"), None),
        P(("groups", "dom"), None),
        P(("groups", "dom"), None),
        P(("groups", "dom")),
        P(("groups", "dom"), None),
        P(("groups", "dom")),
        P(),
        P(),
        P(),
        P(),
        P(("groups", "dom"), None),
        P(("groups", "dom"), None),
    )
    return jax.shard_map(
        shards,
        mesh=mesh,
        in_specs=placed,
        out_specs=(
            P(("groups", "dom"), None),
            P(("groups", "dom"), None),
            P(("groups", "dom"), None),
            P(("groups", "dom"), None),
            P("groups", None),
            P("groups", None),
            P("groups", None),
            P("groups", None),
        ),
        check_vma=False,
    )
```

```python
import functools

import jax
import jax.numpy as jnp
from jax import lax
from jax.experimental import pallas as pl
from jax.experimental.pallas import tpu as pltpu
from jax.sharding import PartitionSpec as P

BF16 = jnp.bfloat16
F32 = jnp.float32
VMEM_LIMIT = 60 * 1024 * 1024


def dot(left, right):
    return jnp.dot(left, right, preferred_element_type=F32)


def dot_rows(left, right):
    return lax.dot_general(left, right, (((0,), (0,)), ((), ())), preferred_element_type=F32)


def dot_cols(left, right):
    return lax.dot_general(left, right, (((1,), (1,)), ((), ())), preferred_element_type=F32)


def iota(shape, axis):
    return lax.broadcasted_iota(jnp.int32, shape, axis)


def marks(mask):
    return jnp.where(mask, 1.0, 0.0).astype(BF16)


def onehot(column, width):
    return marks(column == iota((column.shape[0], width), 1))


def to_column(row):
    count = row.shape[1]
    square = (count, count)
    kept = jnp.where(iota(square, 0) == iota(square, 1), row.astype(F32), 0.0)
    return jnp.sum(kept, axis=1, keepdims=True)


def slot_ranks(dest, domains):
    count = dest.shape[0]
    square = (count, count)
    dest_marks = onehot(dest, domains)
    before = dot(marks(iota(square, 0) > iota(square, 1)), dest_marks)
    return dest_marks, jnp.sum(before * dest_marks.astype(F32), axis=1, keepdims=True)


def pair_marks(first, second, width):
    pairs = first.shape[0]
    shape = (2 * pairs, pairs)
    edge, pair = iota(shape, 0), iota(shape, 1)
    mine = (edge >> 1) == pair
    even = marks(mine & ((edge & 1) == 0))
    odd = marks(mine & ((edge & 1) == 1))
    first_marks, second_marks = onehot(first, width), onehot(second, width)
    senders = dot(even, first_marks) + dot(odd, second_marks)
    receivers = dot(even, second_marks) + dot(odd, first_marks)
    return senders.astype(BF16), receivers.astype(BF16)


def normalise(values):
    centered = values - jnp.mean(values, axis=1, keepdims=True)
    inv_scale = lax.rsqrt(jnp.mean(centered * centered, axis=1, keepdims=True) + 1e-05)
    return centered * inv_scale, inv_scale


def activate(pre_hidden):
    gate = jax.nn.sigmoid(pre_hidden)
    return (pre_hidden * gate).astype(BF16), gate * (1.0 + pre_hidden * (1.0 - gate))


def norm_backward(upstream, normed, inv_scale):
    centered = (
        upstream
        - jnp.mean(upstream, axis=1, keepdims=True)
        - normed * jnp.mean(upstream * normed, axis=1, keepdims=True)
    )
    return (inv_scale * centered).astype(BF16)


def ask_kernel(dest_ref, remote_ref, ask_ref):
    domains, slots = ask_ref.shape
    dest_marks, rank = slot_ranks(to_column(dest_ref[...]).astype(jnp.int32), domains)
    rank_marks = jnp.where(rank == iota((rank.shape[0], slots), 1).astype(F32), 1.0, 0.0)
    wanted = (rank_marks * to_column(remote_ref[...])).astype(BF16)
    ask_ref[...] = dot_rows(dest_marks, wanted).astype(jnp.int32)


def cut_marks_kernel(dest_ref, local_ref, senders_ref, receivers_ref, *, domains, slots):
    width = senders_ref.shape[1]
    base = width - domains * slots
    dest = to_column(dest_ref[...]).astype(jnp.int32)
    _, rank = slot_ranks(dest, domains)
    second = dest * slots + rank.astype(jnp.int32) + base
    first = to_column(local_ref[...]).astype(jnp.int32)
    senders, receivers = pair_marks(first, second, width)
    senders_ref[...] = senders
    receivers_ref[...] = receivers


def edge_forward(edge, sender, receiver, w_in_ref, w_out_ref):
    latent = edge.shape[1]
    pre_hidden = (
        dot(edge, w_in_ref[:latent])
        + dot(sender, w_in_ref[latent : 2 * latent])
        + dot(receiver, w_in_ref[2 * latent :])
    )
    hidden, slope = activate(pre_hidden)
    normed, inv_scale = normalise(dot(hidden, w_out_ref[...]))
    return hidden, slope, normed, inv_scale


def inner_forward_kernel(
    pairs_ref,
    edges_ref,
    nodes_ref,
    w_in_ref,
    w_out_ref,
    senders_ref,
    receivers_ref,
    sender_ref,
    receiver_ref,
    hidden_ref,
    slope_ref,
    normed_ref,
    scale_ref,
    total_ref,
):
    first, second = (to_column(pairs_ref[side : side + 1]).astype(jnp.int32) for side in range(2))
    senders, receivers = pair_marks(first, second, nodes_ref.shape[0])
    senders_ref[...] = senders
    receivers_ref[...] = receivers
    nodes = nodes_ref[...]
    sender = dot(senders, nodes).astype(BF16)
    receiver = dot(receivers, nodes).astype(BF16)
    sender_ref[...] = sender
    receiver_ref[...] = receiver
    hidden, slope, normed, inv_scale = edge_forward(
        edges_ref[...], sender, receiver, w_in_ref, w_out_ref
    )
    hidden_ref[...] = hidden
    slope_ref[...] = slope
    normed_ref[...] = normed
    scale_ref[...] = inv_scale
    part = dot_rows(receivers, normed.astype(BF16))

    @pl.when(pl.program_id(0) == 0)
    def _():
        total_ref[...] = part

    @pl.when(pl.program_id(0) > 0)
    def _():
        total_ref[...] += part


def cut_forward_kernel(
    senders_ref,
    receivers_ref,
    edges_ref,
    nodes_ref,
    far_ref,
    w_in_ref,
    w_out_ref,
    inner_total_ref,
    sender_ref,
    receiver_ref,
    hidden_ref,
    slope_ref,
    normed_ref,
    scale_ref,
    total_ref,
    outgoing_ref,
):
    base = nodes_ref.shape[0]
    nodes, far = nodes_ref[...], far_ref[...]

    def rows_of(marks_ref):
        return (dot(marks_ref[:, :base], nodes) + dot(marks_ref[:, base:], far)).astype(BF16)

    sender, receiver = rows_of(senders_ref), rows_of(receivers_ref)
    sender_ref[...] = sender
    receiver_ref[...] = receiver
    hidden, slope, normed, inv_scale = edge_forward(
        edges_ref[...], sender, receiver, w_in_ref, w_out_ref
    )
    hidden_ref[...] = hidden
    slope_ref[...] = slope
    normed_ref[...] = normed
    scale_ref[...] = inv_scale
    message = normed.astype(BF16)
    total_ref[...] = inner_total_ref[...] + dot_rows(receivers_ref[:, :base], message)
    outgoing_ref[...] = dot_rows(receivers_ref[:, base:], message).astype(BF16)


def new_edges_kernel(edges_ref, inner_ref, cut_ref, out_ref):
    inner_rows = inner_ref.shape[0]

    def added(edge, normed):
        return (edge.astype(F32) + normed.astype(BF16).astype(F32)).astype(BF16)

    out_ref[:inner_rows] = added(edges_ref[:inner_rows], inner_ref[...])
    out_ref[inner_rows:] = added(edges_ref[inner_rows:], cut_ref[...])


def node_kernel(
    me_ref,
    incoming_ref,
    asked_marks_ref,
    total_ref,
    nodes_ref,
    ct_ref,
    w_in_ref,
    w_out_ref,
    new_nodes_ref,
    self_grad_ref,
    agg_grad_ref,
    reply_ref,
    keep_ref,
    send_ref,
):
    latent = nodes_ref.shape[1]
    half = latent // 2
    nodes, asked_marks = nodes_ref[...], asked_marks_ref[...]
    aggregate = (total_ref[...] + dot_rows(asked_marks, incoming_ref[...])).astype(BF16)
    pre_hidden = dot(nodes, w_in_ref[:latent]) + dot(aggregate, w_in_ref[latent:])
    hidden, slope = activate(pre_hidden)
    normed, inv_scale = normalise(dot(hidden, w_out_ref[...]))
    upstream = ct_ref[...].astype(F32)
    grad_out = norm_backward(upstream, normed, inv_scale)
    grad_pre = (dot_cols(grad_out, w_out_ref[...]) * slope).astype(BF16)
    agg_grad = dot_cols(grad_pre, w_in_ref[latent:]).astype(BF16)
    agg_grad_ref[...] = agg_grad
    reply_ref[...] = dot(asked_marks, agg_grad).astype(BF16)
    self_grad_ref[...] = upstream + dot_cols(grad_pre, w_in_ref[:latent])
    new_nodes_ref[...] = (nodes.astype(F32) + normed).astype(BF16)

    def fill(low_ref, high_ref):
        by_aggregate = dot_rows(aggregate, grad_pre).astype(BF16)
        low_ref[:latent] = dot_rows(nodes, grad_pre).astype(BF16)
        low_ref[latent:] = by_aggregate[:half]
        high_ref[:half] = by_aggregate[half:]
        high_ref[half:] = dot_rows(hidden, grad_out).astype(BF16)

    @pl.when((me_ref[0] & 1) == 0)
    def _():
        fill(keep_ref, send_ref)

    @pl.when((me_ref[0] & 1) != 0)
    def _():
        fill(send_ref, keep_ref)


def edge_backward(ct, target_grads, normed, inv_scale, slope, w_out):
    grad_out = norm_backward(ct.astype(F32) + target_grads, normed, inv_scale)
    return grad_out, (dot_cols(grad_out, w_out) * slope).astype(BF16)


def inner_backward_kernel(
    receivers_ref,
    agg_grad_ref,
    ct_ref,
    normed_ref,
    scale_ref,
    slope_ref,
    w_out_ref,
    grad_out_ref,
    grad_pre_ref,
):
    grad_out, grad_pre = edge_backward(
        ct_ref[...],
        dot(receivers_ref[...], agg_grad_ref[...]),
        normed_ref[...],
        scale_ref[...],
        slope_ref[...],
        w_out_ref[...],
    )
    grad_out_ref[...] = grad_out
    grad_pre_ref[...] = grad_pre


def fetch_factors(half, sources, buffers, sems, wait):
    edges, inner_sender, cut_sender, inner_receiver, cut_receiver = sources[:5]
    inner_hidden, cut_hidden, inner_out, inner_pre = sources[5:]
    inner_rows, cut_rows = inner_pre.shape[0], cut_sender.shape[0]
    inner_edges = edges.at[pl.ds(0, inner_rows)]
    cut_edges = edges.at[pl.ds(inner_rows, cut_rows)]
    low = [inner_edges, cut_edges, inner_sender, cut_sender, inner_pre, inner_pre]
    high = [inner_receiver, cut_receiver, inner_hidden, cut_hidden, inner_pre, inner_out]

    def each(parts):
        for index, (source, buffer) in enumerate(zip(parts, buffers)):
            copy = pltpu.make_async_copy(source, buffer, sems.at[index])
            if wait:
                copy.wait()
            else:
                copy.start()

    @pl.when(half == 0)
    def _():
        each(low)

    @pl.when(half != 0)
    def _():
        each(high)


def place_rows(me_ref, index, latent):
    return pl.ds(pl.multiple_of((index ^ ((me_ref[0] >> 1) & 1)) * latent, latent), latent)


def edge_rows(me_ref, half, buffers, cut_pre, cut_out, out_ref):
    latent = cut_pre.shape[1]
    first, first_cut, second, second_cut, first_right, second_right = buffers
    chosen = jnp.where(half == 0, cut_pre.astype(F32), cut_out.astype(F32)).astype(BF16)
    out_ref[place_rows(me_ref, 0, latent)] = (
        dot_rows(first[...], first_right[...]) + dot_rows(first_cut[...], cut_pre)
    ).astype(BF16)
    out_ref[place_rows(me_ref, 1, latent)] = (
        dot_rows(second[...], second_right[...]) + dot_rows(second_cut[...], chosen)
    ).astype(BF16)


def cut_backward_kernel(
    me_ref,
    receivers_ref,
    agg_grad_ref,
    far_grad_ref,
    ct_ref,
    normed_ref,
    scale_ref,
    slope_ref,
    w_out_ref,
    *refs,
):
    sources, (grad_out_ref, grad_pre_ref, out_ref), rest = refs[:9], refs[9:12], refs[12:]
    buffers, sems = rest[:-1], rest[-1]
    half = 1 - (me_ref[0] & 1)
    fetch_factors(half, sources, buffers, sems, False)
    base = agg_grad_ref.shape[0]
    target = dot(receivers_ref[:, :base], agg_grad_ref[...]) + dot(
        receivers_ref[:, base:], far_grad_ref[...]
    )
    grad_out, grad_pre = edge_backward(
        ct_ref[...], target, normed_ref[...], scale_ref[...], slope_ref[...], w_out_ref[...]
    )
    grad_out_ref[...] = grad_out
    grad_pre_ref[...] = grad_pre
    fetch_factors(half, sources, buffers, sems, True)
    edge_rows(me_ref, half, buffers, grad_pre, grad_out, out_ref)


def edge_weights_kernel(me_ref, cut_out_ref, cut_pre_ref, *refs):
    sources, out_ref, rest = refs[:9], refs[9], refs[10:]
    buffers, sems = rest[:-1], rest[-1]
    half = me_ref[0] & 1
    fetch_factors(half, sources, buffers, sems, False)
    fetch_factors(half, sources, buffers, sems, True)
    edge_rows(me_ref, half, buffers, cut_pre_ref[...], cut_out_ref[...], out_ref)


def place_quarters(me_ref, pieces, outs, sems):
    mine = (me_ref[0] & 1) * 2 + ((me_ref[0] >> 1) & 1)
    tops = (0, outs[0].shape[0])

    def each(wait):
        for index, (piece, distance) in enumerate(pieces):
            rows = piece.shape[0]
            for quarter in range(4):

                @pl.when((mine ^ distance) == quarter)
                def _():
                    for side, (out, top) in enumerate(zip(outs, tops)):
                        first = max(quarter * rows, top)
                        count = min((quarter + 1) * rows, top + out.shape[0]) - first
                        if count > 0:
                            copy = pltpu.make_async_copy(
                                piece.at[pl.ds(first - quarter * rows, count)],
                                out.at[pl.ds(first - top, count)],
                                sems.at[2 * index + side],
                            )
                            if wait:
                                copy.wait()
                            else:
                                copy.start()

    each(False)
    each(True)


def first_quarters_kernel(me_ref, mine_ref, near_ref, in_ref, out_ref, sems):
    place_quarters(me_ref, [(mine_ref, 0), (near_ref, 2)], (in_ref, out_ref), sems)


def last_quarters_kernel(me_ref, far_ref, corner_ref, _, __, in_ref, out_ref, sems):
    place_quarters(me_ref, [(far_ref, 1), (corner_ref, 3)], (in_ref, out_ref), sems)


def all_quarters_kernel(me_ref, mine_ref, far_ref, near_ref, corner_ref, in_ref, out_ref, sems):
    pieces = [(mine_ref, 0), (far_ref, 1), (near_ref, 2), (corner_ref, 3)]
    place_quarters(me_ref, pieces, (in_ref, out_ref), sems)


def input_grads_kernel(
    inner_senders_ref,
    inner_receivers_ref,
    cut_senders_ref,
    cut_receivers_ref,
    inner_pre_ref,
    cut_pre_ref,
    w_in_ref,
    local_ref,
    outgoing_ref,
):
    latent = inner_pre_ref.shape[1]
    base = inner_senders_ref.shape[1]
    inner_pre, cut_pre = inner_pre_ref[...], cut_pre_ref[...]
    w_sender, w_receiver = w_in_ref[latent : 2 * latent], w_in_ref[2 * latent :]

    def summed(inner_marks_ref, cut_marks_ref):
        return (
            dot_rows(inner_marks_ref[...], inner_pre) + dot_rows(cut_marks_ref[:, :base], cut_pre)
        ).astype(BF16)

    outgoing_ref[...] = (
        dot_cols(dot_rows(cut_senders_ref[:, base:], cut_pre).astype(BF16), w_sender)
        + dot_cols(dot_rows(cut_receivers_ref[:, base:], cut_pre).astype(BF16), w_receiver)
    ).astype(BF16)
    local_ref[...] = dot_cols(summed(inner_senders_ref, cut_senders_ref), w_sender) + dot_cols(
        summed(inner_receivers_ref, cut_receivers_ref), w_receiver
    )


def edge_grads_kernel(ct_ref, inner_pre_ref, cut_pre_ref, w_edge_ref, out_ref, *, blocks):
    inside = pl.program_id(0) < blocks

    @pl.when(inside)
    def _():
        out_ref[...] = ct_ref[...].astype(F32) + dot_cols(inner_pre_ref[...], w_edge_ref[...])

    @pl.when(jnp.logical_not(inside))
    def _():
        out_ref[...] = ct_ref[...].astype(F32) + dot_cols(cut_pre_ref[...], w_edge_ref[...])


VMEM = pl.BlockSpec(memory_space=pltpu.VMEM)
SMEM = pl.BlockSpec(memory_space=pltpu.SMEM)
ANY = pl.BlockSpec(memory_space=pl.ANY)
HBM = pl.BlockSpec(memory_space=pltpu.HBM)


def shaped(dtype, *shape):
    return jax.ShapeDtypeStruct(shape, dtype)


class Line:
    def __init__(self):
        self.last = None

    def run(
        self, body, outs, ins, specs=None, out_specs=None, grid=None, scratch=(), limit=VMEM_LIMIT, aliases=None
    ):
        single = not isinstance(outs, (list, tuple))
        out_shape = [outs] if single else list(outs)
        specs = [VMEM] * len(ins) if specs is None else list(specs)
        count, extra = len(ins), {} if grid is None else {"grid": grid}
        ins = list(ins)
        if self.last is not None:
            ins.append(self.last)
            specs.append(ANY)

        def ordered(*refs):
            return body(*refs[:count], *refs[len(ins) :])

        result = pl.pallas_call(
            ordered,
            out_shape=out_shape,
            in_specs=specs,
            out_specs=[VMEM] * len(out_shape) if out_specs is None else out_specs,
            scratch_shapes=scratch,
            input_output_aliases=aliases or {},
            compiler_params=pltpu.CompilerParams(vmem_limit_bytes=limit),
            cost_estimate=pl.CostEstimate(flops=1, bytes_accessed=1, transcendentals=0),
            **extra,
        )(*ins)
        self.last = result[-1]
        return result[0] if single else result


def index_bits(devices):
    return list(range(devices.bit_length() - 1))


def across(rows, devices, mask):
    return lax.ppermute(rows, "dom", [(device, device ^ mask) for device in range(devices)])


def fence(*values):
    return lax.optimization_barrier(values)


def place_of(bit):
    return (lax.axis_index("dom") >> bit) & 1


def split(parts, bit):
    place = place_of(bit)
    halves = [part.reshape(2, part.shape[0] // 2, part.shape[1]) for part in parts]
    own = [lax.dynamic_index_in_dim(half, place, 0, False) for half in halves]
    sent = [lax.dynamic_index_in_dim(half, 1 - place, 0, False) for half in halves]
    return own, added(*sent)


def handed(rows, devices, bit):
    return [rows, across(rows, devices, 1 << bit)]


def added(*parts):
    return sum(part.astype(F32) for part in parts).astype(BF16)


def joined(parts, bit):
    orders = [jnp.concatenate(parts), jnp.concatenate(parts[::-1])]
    return jnp.where(place_of(bit) == 0, *orders)


def exchange(rows, domains):
    shape = rows.shape
    split = rows.reshape((domains, shape[0] // domains) + shape[1:])
    return lax.all_to_all(split, "dom", split_axis=0, concat_axis=0, tiled=True).reshape(shape)


def shards(
    nodes,
    edges,
    inner_pairs,
    cut_local,
    cut_dest,
    cut_remote,
    w_edge_in,
    w_edge_out,
    w_node_in,
    w_node_out,
    ct_nodes,
    ct_edges,
):
    domains = lax.axis_size("dom")
    node_rows, latent = nodes.shape
    inner_count, cut_count = inner_pairs.shape[0], cut_local.shape[0]
    inner_rows, cut_rows = 2 * inner_count, 2 * cut_count
    slots = max(2, 2 * cut_count // domains)
    total_slots = domains * slots
    table = node_rows + total_slots
    me = lax.axis_index("dom").reshape(1)
    line = Line()

    ask = line.run(
        ask_kernel, shaped(jnp.int32, domains, slots), [cut_dest.reshape(1, -1), cut_remote.reshape(1, -1)]
    )
    asked = lax.all_to_all(ask, "dom", split_axis=0, concat_axis=0, tiled=True)
    cut_senders, cut_receivers = line.run(
        functools.partial(cut_marks_kernel, domains=domains, slots=slots),
        [shaped(BF16, cut_rows, table)] * 2,
        [cut_dest.reshape(1, -1), cut_local.reshape(1, -1)],
    )
    asked_marks = jnp.where(
        asked[:, :, None] == jnp.arange(node_rows, dtype=jnp.int32)[None, None], 1.0, 0.0
    ).astype(BF16)
    reply = lax.dot_general(asked_marks, nodes, (((2,), (0,)), ((), ())), preferred_element_type=F32)
    reply = reply.astype(BF16).reshape(total_slots, latent)
    asked_marks = asked_marks.reshape(total_slots, node_rows)
    far = exchange(reply, domains)

    block = cut_rows
    blocks = inner_rows // block

    def rows_spec(width, rows=block):
        return pl.BlockSpec((rows, width), lambda step: (step, 0))

    def all_spec(array):
        return pl.BlockSpec(array.shape, lambda step: (0, 0))

    saved_widths = [node_rows, node_rows, latent, latent, latent, latent, latent, 1]
    saved_types = [BF16, BF16, BF16, BF16, BF16, F32, F32, F32]
    (
        inner_senders,
        inner_receivers,
        inner_sender,
        inner_receiver,
        inner_hidden,
        inner_slope,
        inner_normed,
        inner_scale,
        inner_total,
    ) = line.run(
        inner_forward_kernel,
        [shaped(kind, inner_rows, width) for kind, width in zip(saved_types, saved_widths)]
        + [shaped(F32, node_rows, latent)],
        [inner_pairs.T, edges, nodes, w_edge_in, w_edge_out],
        [
            pl.BlockSpec((2, block // 2), lambda step: (0, step)),
            rows_spec(latent),
            all_spec(nodes),
            all_spec(w_edge_in),
            all_spec(w_edge_out),
        ],
        [rows_spec(width) for width in saved_widths] + [all_spec(nodes)],
        (blocks,),
    )

    def last_rows(array):
        last = array.shape[0] // block - 1
        return pl.BlockSpec((block, array.shape[1]), lambda step: (last, 0))

    (
        cut_sender,
        cut_receiver,
        cut_hidden,
        cut_slope,
        cut_normed,
        cut_scale,
        total,
        outgoing,
    ) = line.run(
        cut_forward_kernel,
        [shaped(kind, cut_rows, width) for kind, width in zip(saved_types, saved_widths)][2:]
        + [shaped(F32, node_rows, latent), shaped(BF16, total_slots, latent)],
        [
            cut_senders,
            cut_receivers,
            edges,
            nodes,
            far,
            w_edge_in,
            w_edge_out,
            inner_total,
        ],
        [
            all_spec(cut_senders),
            all_spec(cut_receivers),
            last_rows(edges),
            all_spec(nodes),
            all_spec(far),
            all_spec(w_edge_in),
            all_spec(w_edge_out),
            all_spec(inner_total),
        ],
        [rows_spec(width) for width in saved_widths[2:]]
        + [all_spec(nodes), rows_spec(latent, total_slots)],
        (1,),
    )
    incoming = exchange(outgoing, domains)
    new_edges = line.run(
        new_edges_kernel,
        shaped(BF16, *edges.shape),
        [edges, inner_normed, cut_normed],
    )
    (
        new_nodes,
        self_grad,
        agg_grad,
        grad_reply,
        node_keep,
        node_send,
    ) = line.run(
        node_kernel,
        [
            shaped(BF16, node_rows, latent),
            shaped(F32, node_rows, latent),
            shaped(BF16, node_rows, latent),
            shaped(BF16, total_slots, latent),
        ]
        + [shaped(BF16, 3 * latent // 2, latent)] * 2,
        [me, incoming, asked_marks, total, nodes, ct_nodes, w_node_in, w_node_out],
        [SMEM] + [VMEM] * 7,
    )
    far_grad = exchange(grad_reply, domains)
    node_sum = added(node_keep, across(node_send, domains, 1))
    inner_out, inner_pre = line.run(
        inner_backward_kernel,
        [shaped(BF16, inner_rows, latent)] * 2,
        [
            inner_receivers,
            agg_grad,
            ct_edges,
            inner_normed,
            inner_scale,
            inner_slope,
            w_edge_out,
        ],
        [
            rows_spec(node_rows),
            all_spec(agg_grad),
            rows_spec(latent),
            rows_spec(latent),
            rows_spec(1),
            rows_spec(latent),
            all_spec(w_edge_out),
        ],
        [rows_spec(latent)] * 2,
        (blocks,),
    )
    bits = index_bits(domains)
    node_own, node_sent = split([node_sum], 1)
    node_parts = [*node_own, across(node_sent, domains, 2)]
    far_grad, node_sum, inner_pre = fence(far_grad, node_sum, inner_pre)
    factors = [
        edges,
        inner_sender,
        cut_sender,
        inner_receiver,
        cut_receiver,
        inner_hidden,
        cut_hidden,
        inner_out,
        inner_pre,
    ]
    buffers = [pltpu.VMEM((rows, latent), BF16) for rows in (inner_rows, cut_rows) * 2]
    buffers += [pltpu.VMEM((inner_rows, latent), BF16)] * 2
    buffers.append(pltpu.SemaphoreType.DMA((len(buffers),)))
    cut_out, cut_pre, edge_send = line.run(
        cut_backward_kernel,
        [shaped(BF16, cut_rows, latent)] * 2 + [shaped(BF16, 2 * latent, latent)],
        [
            me,
            cut_receivers,
            agg_grad,
            far_grad,
            ct_edges,
            cut_normed,
            cut_scale,
            cut_slope,
            w_edge_out,
        ]
        + factors,
        [
            SMEM,
            all_spec(cut_receivers),
            all_spec(agg_grad),
            all_spec(far_grad),
            last_rows(ct_edges),
            all_spec(cut_normed),
            all_spec(cut_scale),
            all_spec(cut_slope),
            all_spec(w_edge_out),
        ]
        + [ANY] * len(factors),
        [rows_spec(latent)] * 2 + [rows_spec(latent, 2 * latent)],
        (1,),
        buffers,
    )
    edge_send, place, *node_parts = fence(edge_send, me, *node_parts)
    received = across(edge_send, domains, 1)
    node_own, node_sent = split(node_parts, 2)
    node_got = across(node_sent, domains, 4)
    edge_keep = line.run(
        edge_weights_kernel,
        shaped(BF16, 2 * latent, latent),
        [place, cut_out, cut_pre] + factors,
        [SMEM, VMEM, VMEM] + [ANY] * len(factors),
        scratch=buffers,
    )
    edge_keep, received = fence(edge_keep, received)
    edge_sent = added(edge_keep[latent:], received[latent:])
    edge_sent, inner_pre, cut_pre = fence(edge_sent, inner_pre, cut_pre)
    node_got = fence(node_got, edge_sent)[0]
    edge_got = across(edge_sent, domains, 2)
    node_sum = added(*node_own, node_got)
    for bit in bits[3:]:
        node_sum = added(*handed(node_sum, domains, bit))
    edge_keep, received = fence(edge_keep, received, edge_sent)[:2]
    edge_own = added(edge_keep[:latent], received[:latent])
    local_grad, outgoing_grad = line.run(
        input_grads_kernel,
        [shaped(F32, node_rows, latent), shaped(BF16, total_slots, latent)],
        [
            inner_senders,
            inner_receivers,
            cut_senders,
            cut_receivers,
            inner_pre,
            cut_pre,
            w_edge_in,
        ],
    )
    edge_own, edge_got, node_sum, inner_pre, cut_pre, local_grad = fence(
        edge_own, edge_got, node_sum, inner_pre, cut_pre, local_grad
    )
    edge_own, edge_sent = split([added(edge_own, edge_got)], 2)
    edge_got = across(edge_sent, domains, 4)
    grad_edges = line.run(
        functools.partial(edge_grads_kernel, blocks=blocks),
        shaped(F32, *edges.shape),
        [ct_edges, inner_pre, cut_pre, w_edge_in],
        [
            rows_spec(latent),
            pl.BlockSpec((block, latent), lambda step: (jnp.minimum(step, blocks - 1), 0)),
            all_spec(cut_pre),
            pl.BlockSpec((latent, latent), lambda step: (0, 0)),
        ],
        [rows_spec(latent)],
        (blocks + 1,),
    )
    edge_got, node_sum, grad_edges = fence(edge_got, node_sum, grad_edges)
    edge_sum = added(*edge_own, edge_got)
    edge_sum, node_sum = fence(edge_sum, node_sum)
    edge_got = across(edge_sum, domains, 8)
    node_parts = handed(joined(handed(node_sum, domains, 2), 2), domains, 1)
    edge_sum = added(*fence(edge_sum, edge_got))
    for bit in bits[4:]:
        edge_sum = added(*handed(edge_sum, domains, bit))
    *edge_parts, node_near, node_far, outgoing_grad = fence(
        *handed(edge_sum, domains, 2), *node_parts, outgoing_grad
    )
    edge_sum = joined(edge_parts, 2)
    far, near = across(edge_sum, domains, 2), across(edge_sum, domains, 1)
    node_parts = [node_near, node_far]
    node_parts += [across(part, domains, 1) for part in node_parts]
    returned = exchange(outgoing_grad, domains)
    quarters = [shaped(BF16, 3 * latent, latent), shaped(BF16, latent, latent)]
    copies = dict(out_specs=[HBM] * 2, scratch=[pltpu.SemaphoreType.DMA((8,))], limit=2**20)
    grad_edge_in, grad_edge_out = line.run(
        first_quarters_kernel, quarters, [me, edge_sum, near], [SMEM, ANY, ANY], **copies
    )
    grad_node_in, grad_node_out = line.run(
        all_quarters_kernel,
        [shaped(BF16, 2 * latent, latent), shaped(BF16, latent, latent)],
        [me] + node_parts,
        [SMEM] + [ANY] * 4,
        **copies,
    )
    far, grad_edge_in, grad_edge_out, grad_node_in, grad_node_out, returned = fence(
        far, grad_edge_in, grad_edge_out, grad_node_in, grad_node_out, returned
    )
    corner = across(far, domains, 1)
    grad_nodes = self_grad + local_grad + dot_rows(asked_marks, returned)
    corner, grad_nodes = fence(corner, grad_nodes)
    grad_edge_in, grad_edge_out = Line().run(
        last_quarters_kernel,
        quarters,
        [me, far, corner, grad_edge_in, grad_edge_out],
        [SMEM, ANY, ANY, HBM, HBM],
        aliases={3: 0, 4: 1},
        **copies,
    )
    return (
        new_nodes,
        new_edges,
        grad_nodes,
        grad_edges,
        grad_edge_in,
        grad_edge_out,
        grad_node_in,
        grad_node_out,
    )


def solution(mesh):
    placed = (
        P(("groups", "dom"), None),
        P(("groups", "dom"), None),
        P(("groups", "dom"), None),
        P(("groups", "dom")),
        P(("groups", "dom"), None),
        P(("groups", "dom")),
        P(),
        P(),
        P(),
        P(),
        P(("groups", "dom"), None),
        P(("groups", "dom"), None),
    )
    return jax.shard_map(
        shards,
        mesh=mesh,
        in_specs=placed,
        out_specs=(
            P(("groups", "dom"), None),
            P(("groups", "dom"), None),
            P(("groups", "dom"), None),
            P(("groups", "dom"), None),
            P("groups", None),
            P("groups", None),
            P("groups", None),
            P("groups", None),
        ),
        check_vma=False,
    )
```

```python
import functools

import jax
import jax.numpy as jnp
from jax import lax
from jax.experimental import pallas as pl
from jax.experimental.pallas import tpu as pltpu
from jax.sharding import PartitionSpec as P

BF16 = jnp.bfloat16
F32 = jnp.float32
VMEM_LIMIT = 60 * 1024 * 1024


def dot(left, right):
    return jnp.dot(left, right, preferred_element_type=F32)


def dot_rows(left, right):
    return lax.dot_general(left, right, (((0,), (0,)), ((), ())), preferred_element_type=F32)


def dot_cols(left, right):
    return lax.dot_general(left, right, (((1,), (1,)), ((), ())), preferred_element_type=F32)


def iota(shape, axis):
    return lax.broadcasted_iota(jnp.int32, shape, axis)


def marks(mask):
    return jnp.where(mask, 1.0, 0.0).astype(BF16)


def onehot(column, width):
    return marks(column == iota((column.shape[0], width), 1))


def to_column(row):
    count = row.shape[1]
    square = (count, count)
    kept = jnp.where(iota(square, 0) == iota(square, 1), row.astype(F32), 0.0)
    return jnp.sum(kept, axis=1, keepdims=True)


def slot_ranks(dest, domains):
    count = dest.shape[0]
    square = (count, count)
    dest_marks = onehot(dest, domains)
    before = dot(marks(iota(square, 0) > iota(square, 1)), dest_marks)
    return dest_marks, jnp.sum(before * dest_marks.astype(F32), axis=1, keepdims=True)


def pair_marks(first, second, width):
    pairs = first.shape[0]
    shape = (2 * pairs, pairs)
    edge, pair = iota(shape, 0), iota(shape, 1)
    mine = (edge >> 1) == pair
    even = marks(mine & ((edge & 1) == 0))
    odd = marks(mine & ((edge & 1) == 1))
    first_marks, second_marks = onehot(first, width), onehot(second, width)
    senders = dot(even, first_marks) + dot(odd, second_marks)
    receivers = dot(even, second_marks) + dot(odd, first_marks)
    return senders.astype(BF16), receivers.astype(BF16)


def normalise(values):
    centered = values - jnp.mean(values, axis=1, keepdims=True)
    inv_scale = lax.rsqrt(jnp.mean(centered * centered, axis=1, keepdims=True) + 1e-05)
    return centered * inv_scale, inv_scale


def activate(pre_hidden):
    gate = jax.nn.sigmoid(pre_hidden)
    return (pre_hidden * gate).astype(BF16), gate * (1.0 + pre_hidden * (1.0 - gate))


def norm_backward(upstream, normed, inv_scale):
    centered = (
        upstream
        - jnp.mean(upstream, axis=1, keepdims=True)
        - normed * jnp.mean(upstream * normed, axis=1, keepdims=True)
    )
    return (inv_scale * centered).astype(BF16)


def ask_kernel(dest_ref, remote_ref, ask_ref):
    domains, slots = ask_ref.shape
    dest_marks, rank = slot_ranks(to_column(dest_ref[...]).astype(jnp.int32), domains)
    rank_marks = jnp.where(rank == iota((rank.shape[0], slots), 1).astype(F32), 1.0, 0.0)
    wanted = (rank_marks * to_column(remote_ref[...])).astype(BF16)
    ask_ref[...] = dot_rows(dest_marks, wanted).astype(jnp.int32)


def cut_marks_kernel(dest_ref, local_ref, senders_ref, receivers_ref, *, domains, slots):
    width = senders_ref.shape[1]
    base = width - domains * slots
    dest = to_column(dest_ref[...]).astype(jnp.int32)
    _, rank = slot_ranks(dest, domains)
    second = dest * slots + rank.astype(jnp.int32) + base
    first = to_column(local_ref[...]).astype(jnp.int32)
    senders, receivers = pair_marks(first, second, width)
    senders_ref[...] = senders
    receivers_ref[...] = receivers


def edge_forward(edge, sender, receiver, w_in_ref, w_out_ref):
    latent = edge.shape[1]
    pre_hidden = (
        dot(edge, w_in_ref[:latent])
        + dot(sender, w_in_ref[latent : 2 * latent])
        + dot(receiver, w_in_ref[2 * latent :])
    )
    hidden, slope = activate(pre_hidden)
    normed, inv_scale = normalise(dot(hidden, w_out_ref[...]))
    return hidden, slope, normed, inv_scale


def inner_forward_kernel(
    pairs_ref,
    edges_ref,
    nodes_ref,
    w_in_ref,
    w_out_ref,
    senders_ref,
    receivers_ref,
    sender_ref,
    receiver_ref,
    hidden_ref,
    slope_ref,
    normed_ref,
    scale_ref,
    total_ref,
):
    first, second = (to_column(pairs_ref[side : side + 1]).astype(jnp.int32) for side in range(2))
    senders, receivers = pair_marks(first, second, nodes_ref.shape[0])
    senders_ref[...] = senders
    receivers_ref[...] = receivers
    nodes = nodes_ref[...]
    sender = dot(senders, nodes).astype(BF16)
    receiver = dot(receivers, nodes).astype(BF16)
    sender_ref[...] = sender
    receiver_ref[...] = receiver
    hidden, slope, normed, inv_scale = edge_forward(
        edges_ref[...], sender, receiver, w_in_ref, w_out_ref
    )
    hidden_ref[...] = hidden
    slope_ref[...] = slope
    normed_ref[...] = normed
    scale_ref[...] = inv_scale
    part = dot_rows(receivers, normed.astype(BF16))

    @pl.when(pl.program_id(0) == 0)
    def _():
        total_ref[...] = part

    @pl.when(pl.program_id(0) > 0)
    def _():
        total_ref[...] += part


def cut_forward_kernel(
    senders_ref,
    receivers_ref,
    edges_ref,
    nodes_ref,
    far_ref,
    w_in_ref,
    w_out_ref,
    inner_total_ref,
    sender_ref,
    receiver_ref,
    hidden_ref,
    slope_ref,
    normed_ref,
    scale_ref,
    total_ref,
    outgoing_ref,
):
    base = nodes_ref.shape[0]
    nodes, far = nodes_ref[...], far_ref[...]

    def rows_of(marks_ref):
        return (dot(marks_ref[:, :base], nodes) + dot(marks_ref[:, base:], far)).astype(BF16)

    sender, receiver = rows_of(senders_ref), rows_of(receivers_ref)
    sender_ref[...] = sender
    receiver_ref[...] = receiver
    hidden, slope, normed, inv_scale = edge_forward(
        edges_ref[...], sender, receiver, w_in_ref, w_out_ref
    )
    hidden_ref[...] = hidden
    slope_ref[...] = slope
    normed_ref[...] = normed
    scale_ref[...] = inv_scale
    message = normed.astype(BF16)
    total_ref[...] = inner_total_ref[...] + dot_rows(receivers_ref[:, :base], message)
    outgoing_ref[...] = dot_rows(receivers_ref[:, base:], message).astype(BF16)


def new_edges_kernel(edges_ref, inner_ref, cut_ref, out_ref):
    inner_rows = inner_ref.shape[0]

    def added(edge, normed):
        return (edge.astype(F32) + normed.astype(BF16).astype(F32)).astype(BF16)

    out_ref[:inner_rows] = added(edges_ref[:inner_rows], inner_ref[...])
    out_ref[inner_rows:] = added(edges_ref[inner_rows:], cut_ref[...])


def node_kernel(
    me_ref,
    incoming_ref,
    asked_marks_ref,
    total_ref,
    nodes_ref,
    ct_ref,
    w_in_ref,
    w_out_ref,
    new_nodes_ref,
    self_grad_ref,
    agg_grad_ref,
    reply_ref,
    keep_ref,
    send_ref,
):
    latent = nodes_ref.shape[1]
    half = latent // 2
    nodes, asked_marks = nodes_ref[...], asked_marks_ref[...]
    aggregate = (total_ref[...] + dot_rows(asked_marks, incoming_ref[...])).astype(BF16)
    pre_hidden = dot(nodes, w_in_ref[:latent]) + dot(aggregate, w_in_ref[latent:])
    hidden, slope = activate(pre_hidden)
    normed, inv_scale = normalise(dot(hidden, w_out_ref[...]))
    upstream = ct_ref[...].astype(F32)
    grad_out = norm_backward(upstream, normed, inv_scale)
    grad_pre = (dot_cols(grad_out, w_out_ref[...]) * slope).astype(BF16)
    agg_grad = dot_cols(grad_pre, w_in_ref[latent:]).astype(BF16)
    agg_grad_ref[...] = agg_grad
    reply_ref[...] = dot(asked_marks, agg_grad).astype(BF16)
    self_grad_ref[...] = upstream + dot_cols(grad_pre, w_in_ref[:latent])
    new_nodes_ref[...] = (nodes.astype(F32) + normed).astype(BF16)

    def fill(low_ref, high_ref):
        by_aggregate = dot_rows(aggregate, grad_pre).astype(BF16)
        low_ref[:latent] = dot_rows(nodes, grad_pre).astype(BF16)
        low_ref[latent:] = by_aggregate[:half]
        high_ref[:half] = by_aggregate[half:]
        high_ref[half:] = dot_rows(hidden, grad_out).astype(BF16)

    @pl.when((me_ref[0] & 1) == 0)
    def _():
        fill(keep_ref, send_ref)

    @pl.when((me_ref[0] & 1) != 0)
    def _():
        fill(send_ref, keep_ref)


def edge_backward(ct, target_grads, normed, inv_scale, slope, w_out):
    grad_out = norm_backward(ct.astype(F32) + target_grads, normed, inv_scale)
    return grad_out, (dot_cols(grad_out, w_out) * slope).astype(BF16)


def inner_backward_kernel(
    receivers_ref,
    agg_grad_ref,
    ct_ref,
    normed_ref,
    scale_ref,
    slope_ref,
    w_out_ref,
    grad_out_ref,
    grad_pre_ref,
):
    grad_out, grad_pre = edge_backward(
        ct_ref[...],
        dot(receivers_ref[...], agg_grad_ref[...]),
        normed_ref[...],
        scale_ref[...],
        slope_ref[...],
        w_out_ref[...],
    )
    grad_out_ref[...] = grad_out
    grad_pre_ref[...] = grad_pre


def fetch_factors(half, sources, buffers, sems, wait):
    edges, inner_sender, cut_sender, inner_receiver, cut_receiver = sources[:5]
    inner_hidden, cut_hidden, inner_out, inner_pre = sources[5:]
    inner_rows, cut_rows = inner_pre.shape[0], cut_sender.shape[0]
    inner_edges = edges.at[pl.ds(0, inner_rows)]
    cut_edges = edges.at[pl.ds(inner_rows, cut_rows)]
    low = [inner_edges, cut_edges, inner_sender, cut_sender, inner_pre, inner_pre]
    high = [inner_receiver, cut_receiver, inner_hidden, cut_hidden, inner_pre, inner_out]

    def each(parts):
        for index, (source, buffer) in enumerate(zip(parts, buffers)):
            copy = pltpu.make_async_copy(source, buffer, sems.at[index])
            if wait:
                copy.wait()
            else:
                copy.start()

    @pl.when(half == 0)
    def _():
        each(low)

    @pl.when(half != 0)
    def _():
        each(high)


def place_rows(me_ref, index, latent):
    return pl.ds(pl.multiple_of((index ^ ((me_ref[0] >> 1) & 1)) * latent, latent), latent)


def edge_rows(me_ref, half, buffers, cut_pre, cut_out, out_ref):
    latent = cut_pre.shape[1]
    first, first_cut, second, second_cut, first_right, second_right = buffers
    chosen = jnp.where(half == 0, cut_pre.astype(F32), cut_out.astype(F32)).astype(BF16)
    out_ref[place_rows(me_ref, 0, latent)] = (
        dot_rows(first[...], first_right[...]) + dot_rows(first_cut[...], cut_pre)
    ).astype(BF16)
    out_ref[place_rows(me_ref, 1, latent)] = (
        dot_rows(second[...], second_right[...]) + dot_rows(second_cut[...], chosen)
    ).astype(BF16)


def cut_backward_kernel(
    me_ref,
    receivers_ref,
    agg_grad_ref,
    far_grad_ref,
    ct_ref,
    normed_ref,
    scale_ref,
    slope_ref,
    w_out_ref,
    *refs,
):
    sources, (grad_out_ref, grad_pre_ref, out_ref), rest = refs[:9], refs[9:12], refs[12:]
    buffers, sems = rest[:-1], rest[-1]
    half = 1 - (me_ref[0] & 1)
    fetch_factors(half, sources, buffers, sems, False)
    base = agg_grad_ref.shape[0]
    target = dot(receivers_ref[:, :base], agg_grad_ref[...]) + dot(
        receivers_ref[:, base:], far_grad_ref[...]
    )
    grad_out, grad_pre = edge_backward(
        ct_ref[...], target, normed_ref[...], scale_ref[...], slope_ref[...], w_out_ref[...]
    )
    grad_out_ref[...] = grad_out
    grad_pre_ref[...] = grad_pre
    fetch_factors(half, sources, buffers, sems, True)
    edge_rows(me_ref, half, buffers, grad_pre, grad_out, out_ref)


def edge_weights_kernel(me_ref, cut_out_ref, cut_pre_ref, *refs):
    sources, out_ref, rest = refs[:9], refs[9], refs[10:]
    buffers, sems = rest[:-1], rest[-1]
    half = me_ref[0] & 1
    fetch_factors(half, sources, buffers, sems, False)
    fetch_factors(half, sources, buffers, sems, True)
    edge_rows(me_ref, half, buffers, cut_pre_ref[...], cut_out_ref[...], out_ref)


def place_quarters(me_ref, pieces, outs, sems):
    mine = (me_ref[0] & 1) * 2 + ((me_ref[0] >> 1) & 1)
    tops = (0, outs[0].shape[0])

    def each(wait):
        for index, (piece, distance) in enumerate(pieces):
            rows = piece.shape[0]
            for quarter in range(4):

                @pl.when((mine ^ distance) == quarter)
                def _():
                    for side, (out, top) in enumerate(zip(outs, tops)):
                        first = max(quarter * rows, top)
                        count = min((quarter + 1) * rows, top + out.shape[0]) - first
                        if count > 0:
                            copy = pltpu.make_async_copy(
                                piece.at[pl.ds(first - quarter * rows, count)],
                                out.at[pl.ds(first - top, count)],
                                sems.at[2 * index + side],
                            )
                            if wait:
                                copy.wait()
                            else:
                                copy.start()

    each(False)
    each(True)


def first_quarters_kernel(me_ref, mine_ref, near_ref, in_ref, out_ref, sems):
    place_quarters(me_ref, [(mine_ref, 0), (near_ref, 2)], (in_ref, out_ref), sems)


def last_quarters_kernel(me_ref, far_ref, corner_ref, _, __, in_ref, out_ref, sems):
    place_quarters(me_ref, [(far_ref, 1), (corner_ref, 3)], (in_ref, out_ref), sems)


def all_quarters_kernel(me_ref, mine_ref, far_ref, near_ref, corner_ref, in_ref, out_ref, sems):
    pieces = [(mine_ref, 0), (far_ref, 1), (near_ref, 2), (corner_ref, 3)]
    place_quarters(me_ref, pieces, (in_ref, out_ref), sems)


def input_grads_kernel(
    inner_senders_ref,
    inner_receivers_ref,
    cut_senders_ref,
    cut_receivers_ref,
    inner_pre_ref,
    cut_pre_ref,
    w_in_ref,
    local_ref,
    outgoing_ref,
):
    latent = inner_pre_ref.shape[1]
    base = inner_senders_ref.shape[1]
    inner_pre, cut_pre = inner_pre_ref[...], cut_pre_ref[...]
    w_sender, w_receiver = w_in_ref[latent : 2 * latent], w_in_ref[2 * latent :]

    def summed(inner_marks_ref, cut_marks_ref):
        return (
            dot_rows(inner_marks_ref[...], inner_pre) + dot_rows(cut_marks_ref[:, :base], cut_pre)
        ).astype(BF16)

    outgoing_ref[...] = (
        dot_cols(dot_rows(cut_senders_ref[:, base:], cut_pre).astype(BF16), w_sender)
        + dot_cols(dot_rows(cut_receivers_ref[:, base:], cut_pre).astype(BF16), w_receiver)
    ).astype(BF16)
    local_ref[...] = dot_cols(summed(inner_senders_ref, cut_senders_ref), w_sender) + dot_cols(
        summed(inner_receivers_ref, cut_receivers_ref), w_receiver
    )


def edge_grads_kernel(ct_ref, inner_pre_ref, cut_pre_ref, w_edge_ref, out_ref, *, blocks):
    inside = pl.program_id(0) < blocks

    @pl.when(inside)
    def _():
        out_ref[...] = ct_ref[...].astype(F32) + dot_cols(inner_pre_ref[...], w_edge_ref[...])

    @pl.when(jnp.logical_not(inside))
    def _():
        out_ref[...] = ct_ref[...].astype(F32) + dot_cols(cut_pre_ref[...], w_edge_ref[...])


VMEM = pl.BlockSpec(memory_space=pltpu.VMEM)
SMEM = pl.BlockSpec(memory_space=pltpu.SMEM)
ANY = pl.BlockSpec(memory_space=pl.ANY)
HBM = pl.BlockSpec(memory_space=pltpu.HBM)


def shaped(dtype, *shape):
    return jax.ShapeDtypeStruct(shape, dtype)


class Line:
    def __init__(self):
        self.last = None

    def run(
        self, body, outs, ins, specs=None, out_specs=None, grid=None, scratch=(), limit=VMEM_LIMIT, aliases=None
    ):
        single = not isinstance(outs, (list, tuple))
        out_shape = [outs] if single else list(outs)
        specs = [VMEM] * len(ins) if specs is None else list(specs)
        count, extra = len(ins), {} if grid is None else {"grid": grid}
        ins = list(ins)
        if self.last is not None:
            ins.append(self.last)
            specs.append(ANY)

        def ordered(*refs):
            return body(*refs[:count], *refs[len(ins) :])

        result = pl.pallas_call(
            ordered,
            out_shape=out_shape,
            in_specs=specs,
            out_specs=[VMEM] * len(out_shape) if out_specs is None else out_specs,
            scratch_shapes=scratch,
            input_output_aliases=aliases or {},
            compiler_params=pltpu.CompilerParams(vmem_limit_bytes=limit),
            cost_estimate=pl.CostEstimate(flops=1, bytes_accessed=1, transcendentals=0),
            **extra,
        )(*ins)
        self.last = result[-1]
        return result[0] if single else result


def index_bits(devices):
    return list(range(devices.bit_length() - 1))


def across(rows, devices, mask):
    return lax.ppermute(rows, "dom", [(device, device ^ mask) for device in range(devices)])


def fence(*values):
    return lax.optimization_barrier(values)


def place_of(bit):
    return (lax.axis_index("dom") >> bit) & 1


def split(parts, bit):
    place = place_of(bit)
    halves = [part.reshape(2, part.shape[0] // 2, part.shape[1]) for part in parts]
    own = [lax.dynamic_index_in_dim(half, place, 0, False) for half in halves]
    sent = [lax.dynamic_index_in_dim(half, 1 - place, 0, False) for half in halves]
    return own, added(*sent)


def handed(rows, devices, bit):
    return [rows, across(rows, devices, 1 << bit)]


def added(*parts):
    return sum(part.astype(F32) for part in parts).astype(BF16)


def joined(parts, bit):
    orders = [jnp.concatenate(parts), jnp.concatenate(parts[::-1])]
    return jnp.where(place_of(bit) == 0, *orders)


def exchange(rows, domains):
    shape = rows.shape
    split = rows.reshape((domains, shape[0] // domains) + shape[1:])
    return lax.all_to_all(split, "dom", split_axis=0, concat_axis=0, tiled=True).reshape(shape)


def shards(
    nodes,
    edges,
    inner_pairs,
    cut_local,
    cut_dest,
    cut_remote,
    w_edge_in,
    w_edge_out,
    w_node_in,
    w_node_out,
    ct_nodes,
    ct_edges,
):
    domains = lax.axis_size("dom")
    node_rows, latent = nodes.shape
    inner_count, cut_count = inner_pairs.shape[0], cut_local.shape[0]
    inner_rows, cut_rows = 2 * inner_count, 2 * cut_count
    slots = max(2, 2 * cut_count // domains)
    total_slots = domains * slots
    table = node_rows + total_slots
    me = lax.axis_index("dom").reshape(1)
    line = Line()

    ask = line.run(
        ask_kernel, shaped(jnp.int32, domains, slots), [cut_dest.reshape(1, -1), cut_remote.reshape(1, -1)]
    )
    asked = lax.all_to_all(ask, "dom", split_axis=0, concat_axis=0, tiled=True)
    cut_senders, cut_receivers = line.run(
        functools.partial(cut_marks_kernel, domains=domains, slots=slots),
        [shaped(BF16, cut_rows, table)] * 2,
        [cut_dest.reshape(1, -1), cut_local.reshape(1, -1)],
    )
    asked_marks = jnp.where(
        asked[:, :, None] == jnp.arange(node_rows, dtype=jnp.int32)[None, None], 1.0, 0.0
    ).astype(BF16)
    reply = lax.dot_general(asked_marks, nodes, (((2,), (0,)), ((), ())), preferred_element_type=F32)
    reply = reply.astype(BF16).reshape(total_slots, latent)
    asked_marks = asked_marks.reshape(total_slots, node_rows)
    far = exchange(reply, domains)

    block = cut_rows
    blocks = inner_rows // block

    def rows_spec(width, rows=block):
        return pl.BlockSpec((rows, width), lambda step: (step, 0))

    def all_spec(array):
        return pl.BlockSpec(array.shape, lambda step: (0, 0))

    saved_widths = [node_rows, node_rows, latent, latent, latent, latent, latent, 1]
    saved_types = [BF16, BF16, BF16, BF16, BF16, F32, F32, F32]
    (
        inner_senders,
        inner_receivers,
        inner_sender,
        inner_receiver,
        inner_hidden,
        inner_slope,
        inner_normed,
        inner_scale,
        inner_total,
    ) = line.run(
        inner_forward_kernel,
        [shaped(kind, inner_rows, width) for kind, width in zip(saved_types, saved_widths)]
        + [shaped(F32, node_rows, latent)],
        [inner_pairs.T, edges, nodes, w_edge_in, w_edge_out],
        [
            pl.BlockSpec((2, block // 2), lambda step: (0, step)),
            rows_spec(latent),
            all_spec(nodes),
            all_spec(w_edge_in),
            all_spec(w_edge_out),
        ],
        [rows_spec(width) for width in saved_widths] + [all_spec(nodes)],
        (blocks,),
    )

    def last_rows(array):
        last = array.shape[0] // block - 1
        return pl.BlockSpec((block, array.shape[1]), lambda step: (last, 0))

    (
        cut_sender,
        cut_receiver,
        cut_hidden,
        cut_slope,
        cut_normed,
        cut_scale,
        total,
        outgoing,
    ) = line.run(
        cut_forward_kernel,
        [shaped(kind, cut_rows, width) for kind, width in zip(saved_types, saved_widths)][2:]
        + [shaped(F32, node_rows, latent), shaped(BF16, total_slots, latent)],
        [
            cut_senders,
            cut_receivers,
            edges,
            nodes,
            far,
            w_edge_in,
            w_edge_out,
            inner_total,
        ],
        [
            all_spec(cut_senders),
            all_spec(cut_receivers),
            last_rows(edges),
            all_spec(nodes),
            all_spec(far),
            all_spec(w_edge_in),
            all_spec(w_edge_out),
            all_spec(inner_total),
        ],
        [rows_spec(width) for width in saved_widths[2:]]
        + [all_spec(nodes), rows_spec(latent, total_slots)],
        (1,),
    )
    incoming = exchange(outgoing, domains)
    new_edges = line.run(
        new_edges_kernel,
        shaped(BF16, *edges.shape),
        [edges, inner_normed, cut_normed],
    )
    (
        new_nodes,
        self_grad,
        agg_grad,
        grad_reply,
        node_keep,
        node_send,
    ) = line.run(
        node_kernel,
        [
            shaped(BF16, node_rows, latent),
            shaped(F32, node_rows, latent),
            shaped(BF16, node_rows, latent),
            shaped(BF16, total_slots, latent),
        ]
        + [shaped(BF16, 3 * latent // 2, latent)] * 2,
        [me, incoming, asked_marks, total, nodes, ct_nodes, w_node_in, w_node_out],
        [SMEM] + [VMEM] * 7,
    )
    far_grad = exchange(grad_reply, domains)
    node_sum = added(node_keep, across(node_send, domains, 1))
    inner_out, inner_pre = line.run(
        inner_backward_kernel,
        [shaped(BF16, inner_rows, latent)] * 2,
        [
            inner_receivers,
            agg_grad,
            ct_edges,
            inner_normed,
            inner_scale,
            inner_slope,
            w_edge_out,
        ],
        [
            rows_spec(node_rows),
            all_spec(agg_grad),
            rows_spec(latent),
            rows_spec(latent),
            rows_spec(1),
            rows_spec(latent),
            all_spec(w_edge_out),
        ],
        [rows_spec(latent)] * 2,
        (blocks,),
    )
    bits = index_bits(domains)
    node_own, node_sent = split([node_sum], 1)
    node_parts = [*node_own, across(node_sent, domains, 2)]
    far_grad, node_sum, inner_pre = fence(far_grad, node_sum, inner_pre)
    factors = [
        edges,
        inner_sender,
        cut_sender,
        inner_receiver,
        cut_receiver,
        inner_hidden,
        cut_hidden,
        inner_out,
        inner_pre,
    ]
    buffers = [pltpu.VMEM((rows, latent), BF16) for rows in (inner_rows, cut_rows) * 2]
    buffers += [pltpu.VMEM((inner_rows, latent), BF16)] * 2
    buffers.append(pltpu.SemaphoreType.DMA((len(buffers),)))
    cut_out, cut_pre, edge_send = line.run(
        cut_backward_kernel,
        [shaped(BF16, cut_rows, latent)] * 2 + [shaped(BF16, 2 * latent, latent)],
        [
            me,
            cut_receivers,
            agg_grad,
            far_grad,
            ct_edges,
            cut_normed,
            cut_scale,
            cut_slope,
            w_edge_out,
        ]
        + factors,
        [
            SMEM,
            all_spec(cut_receivers),
            all_spec(agg_grad),
            all_spec(far_grad),
            last_rows(ct_edges),
            all_spec(cut_normed),
            all_spec(cut_scale),
            all_spec(cut_slope),
            all_spec(w_edge_out),
        ]
        + [ANY] * len(factors),
        [rows_spec(latent)] * 2 + [rows_spec(latent, 2 * latent)],
        (1,),
        buffers,
    )
    edge_send, place, *node_parts = fence(edge_send, me, *node_parts)
    received = across(edge_send, domains, 1)
    node_own, node_sent = split(node_parts, 2)
    node_got = across(node_sent, domains, 4)
    edge_keep = line.run(
        edge_weights_kernel,
        shaped(BF16, 2 * latent, latent),
        [place, cut_out, cut_pre] + factors,
        [SMEM, VMEM, VMEM] + [ANY] * len(factors),
        scratch=buffers,
    )
    edge_keep, received = fence(edge_keep, received)
    edge_sent = added(edge_keep[latent:], received[latent:])
    edge_sent, inner_pre, cut_pre = fence(edge_sent, inner_pre, cut_pre)
    node_got = fence(node_got, edge_sent)[0]
    edge_got = across(edge_sent, domains, 2)
    node_sum = added(*node_own, node_got)
    for bit in bits[3:]:
        node_sum = added(*handed(node_sum, domains, bit))
    edge_keep, received = fence(edge_keep, received, edge_sent)[:2]
    edge_own = added(edge_keep[:latent], received[:latent])
    local_grad, outgoing_grad = line.run(
        input_grads_kernel,
        [shaped(F32, node_rows, latent), shaped(BF16, total_slots, latent)],
        [
            inner_senders,
            inner_receivers,
            cut_senders,
            cut_receivers,
            inner_pre,
            cut_pre,
            w_edge_in,
        ],
    )
    edge_own, edge_got, node_sum, inner_pre, cut_pre, local_grad = fence(
        edge_own, edge_got, node_sum, inner_pre, cut_pre, local_grad
    )
    edge_own, edge_sent = split([added(edge_own, edge_got)], 2)
    edge_got = across(edge_sent, domains, 4)
    grad_edges = line.run(
        functools.partial(edge_grads_kernel, blocks=blocks),
        shaped(F32, *edges.shape),
        [ct_edges, inner_pre, cut_pre, w_edge_in],
        [
            rows_spec(latent),
            pl.BlockSpec((block, latent), lambda step: (jnp.minimum(step, blocks - 1), 0)),
            all_spec(cut_pre),
            pl.BlockSpec((latent, latent), lambda step: (0, 0)),
        ],
        [rows_spec(latent)],
        (blocks + 1,),
    )
    edge_got, node_sum, grad_edges = fence(edge_got, node_sum, grad_edges)
    edge_sum = added(*edge_own, edge_got)
    edge_sum, node_sum = fence(edge_sum, node_sum)
    edge_got = across(edge_sum, domains, 8)
    node_parts = handed(joined(handed(node_sum, domains, 2), 2), domains, 1)
    edge_sum = added(*fence(edge_sum, edge_got))
    for bit in bits[4:]:
        edge_sum = added(*handed(edge_sum, domains, bit))
    *edge_parts, node_near, node_far, outgoing_grad = fence(
        *handed(edge_sum, domains, 2), *node_parts, outgoing_grad
    )
    edge_sum = joined(edge_parts, 2)
    far, near = across(edge_sum, domains, 2), across(edge_sum, domains, 1)
    node_parts = [node_near, node_far]
    node_parts += [across(part, domains, 1) for part in node_parts]
    returned = exchange(outgoing_grad, domains)
    quarters = [shaped(BF16, 3 * latent, latent), shaped(BF16, latent, latent)]
    copies = dict(out_specs=[HBM] * 2, scratch=[pltpu.SemaphoreType.DMA((8,))], limit=2**20)
    grad_edge_in, grad_edge_out = line.run(
        first_quarters_kernel, quarters, [me, edge_sum, near], [SMEM, ANY, ANY], **copies
    )
    grad_node_in, grad_node_out = line.run(
        all_quarters_kernel,
        [shaped(BF16, 2 * latent, latent), shaped(BF16, latent, latent)],
        [me] + node_parts,
        [SMEM] + [VMEM] * 4,
        **(copies | {"limit": VMEM_LIMIT}),
    )
    far, grad_edge_in, grad_edge_out, grad_node_in, grad_node_out, returned = fence(
        far, grad_edge_in, grad_edge_out, grad_node_in, grad_node_out, returned
    )
    corner = across(far, domains, 1)
    grad_nodes = self_grad + local_grad + dot_rows(asked_marks, returned)
    corner, grad_nodes = fence(corner, grad_nodes)
    grad_edge_in, grad_edge_out = Line().run(
        last_quarters_kernel,
        quarters,
        [me, far, corner, grad_edge_in, grad_edge_out],
        [SMEM, ANY, ANY, HBM, HBM],
        aliases={3: 0, 4: 1},
        **copies,
    )
    return (
        new_nodes,
        new_edges,
        grad_nodes,
        grad_edges,
        grad_edge_in,
        grad_edge_out,
        grad_node_in,
        grad_node_out,
    )


def solution(mesh):
    placed = (
        P(("groups", "dom"), None),
        P(("groups", "dom"), None),
        P(("groups", "dom"), None),
        P(("groups", "dom")),
        P(("groups", "dom"), None),
        P(("groups", "dom")),
        P(),
        P(),
        P(),
        P(),
        P(("groups", "dom"), None),
        P(("groups", "dom"), None),
    )
    return jax.shard_map(
        shards,
        mesh=mesh,
        in_specs=placed,
        out_specs=(
            P(("groups", "dom"), None),
            P(("groups", "dom"), None),
            P(("groups", "dom"), None),
            P(("groups", "dom"), None),
            P("groups", None),
            P("groups", None),
            P("groups", None),
            P("groups", None),
        ),
        check_vma=False,
    )
```

```python
import functools

import jax
import jax.numpy as jnp
from jax import lax
from jax.experimental import pallas as pl
from jax.experimental.pallas import tpu as pltpu
from jax.sharding import PartitionSpec as P

BF16 = jnp.bfloat16
F32 = jnp.float32
VMEM_LIMIT = 60 * 1024 * 1024


def dot(left, right):
    return jnp.dot(left, right, preferred_element_type=F32)


def dot_rows(left, right):
    return lax.dot_general(left, right, (((0,), (0,)), ((), ())), preferred_element_type=F32)


def dot_cols(left, right):
    return lax.dot_general(left, right, (((1,), (1,)), ((), ())), preferred_element_type=F32)


def iota(shape, axis):
    return lax.broadcasted_iota(jnp.int32, shape, axis)


def marks(mask):
    return jnp.where(mask, 1.0, 0.0).astype(BF16)


def onehot(column, width):
    return marks(column == iota((column.shape[0], width), 1))


def to_column(row):
    count = row.shape[1]
    square = (count, count)
    kept = jnp.where(iota(square, 0) == iota(square, 1), row.astype(F32), 0.0)
    return jnp.sum(kept, axis=1, keepdims=True)


def slot_ranks(dest, domains):
    count = dest.shape[0]
    square = (count, count)
    dest_marks = onehot(dest, domains)
    before = dot(marks(iota(square, 0) > iota(square, 1)), dest_marks)
    return dest_marks, jnp.sum(before * dest_marks.astype(F32), axis=1, keepdims=True)


def pair_marks(first, second, width):
    pairs = first.shape[0]
    shape = (2 * pairs, pairs)
    edge, pair = iota(shape, 0), iota(shape, 1)
    mine = (edge >> 1) == pair
    even = marks(mine & ((edge & 1) == 0))
    odd = marks(mine & ((edge & 1) == 1))
    first_marks, second_marks = onehot(first, width), onehot(second, width)
    senders = dot(even, first_marks) + dot(odd, second_marks)
    receivers = dot(even, second_marks) + dot(odd, first_marks)
    return senders.astype(BF16), receivers.astype(BF16)


def normalise(values):
    centered = values - jnp.mean(values, axis=1, keepdims=True)
    inv_scale = lax.rsqrt(jnp.mean(centered * centered, axis=1, keepdims=True) + 1e-05)
    return centered * inv_scale, inv_scale


def activate(pre_hidden):
    gate = jax.nn.sigmoid(pre_hidden)
    return (pre_hidden * gate).astype(BF16), gate * (1.0 + pre_hidden * (1.0 - gate))


def norm_backward(upstream, normed, inv_scale):
    centered = (
        upstream
        - jnp.mean(upstream, axis=1, keepdims=True)
        - normed * jnp.mean(upstream * normed, axis=1, keepdims=True)
    )
    return (inv_scale * centered).astype(BF16)


def ask_kernel(dest_ref, remote_ref, ask_ref):
    domains, slots = ask_ref.shape
    dest_marks, rank = slot_ranks(to_column(dest_ref[...]).astype(jnp.int32), domains)
    rank_marks = jnp.where(rank == iota((rank.shape[0], slots), 1).astype(F32), 1.0, 0.0)
    wanted = (rank_marks * to_column(remote_ref[...])).astype(BF16)
    ask_ref[...] = dot_rows(dest_marks, wanted).astype(jnp.int32)


def reply_kernel(asked_ref, nodes_ref, reply_ref, asked_marks_ref):
    domains, slots = asked_ref.shape
    total = domains * slots
    shift = slots.bit_length() - 1
    spread = marks((iota((total, domains), 0) >> shift) == iota((total, domains), 1))
    listed = dot(spread, asked_ref[...].astype(F32).astype(BF16))
    at_slot = (iota((total, slots), 0) & (slots - 1)) == iota((total, slots), 1)
    column = jnp.sum(jnp.where(at_slot, listed, 0.0), axis=1, keepdims=True)
    node_rows = nodes_ref.shape[0]
    asked_marks = marks(column == iota((total, node_rows), 1).astype(F32))
    asked_marks_ref[...] = asked_marks
    reply_ref[...] = dot(asked_marks, nodes_ref[...]).astype(BF16)


def cut_marks_kernel(dest_ref, local_ref, senders_ref, receivers_ref, *, domains, slots):
    width = senders_ref.shape[1]
    base = width - domains * slots
    dest = to_column(dest_ref[...]).astype(jnp.int32)
    _, rank = slot_ranks(dest, domains)
    second = dest * slots + rank.astype(jnp.int32) + base
    first = to_column(local_ref[...]).astype(jnp.int32)
    senders, receivers = pair_marks(first, second, width)
    senders_ref[...] = senders
    receivers_ref[...] = receivers


def edge_forward(edge, sender, receiver, w_in_ref, w_out_ref):
    latent = edge.shape[1]
    pre_hidden = (
        dot(edge, w_in_ref[:latent])
        + dot(sender, w_in_ref[latent : 2 * latent])
        + dot(receiver, w_in_ref[2 * latent :])
    )
    hidden, slope = activate(pre_hidden)
    normed, inv_scale = normalise(dot(hidden, w_out_ref[...]))
    return hidden, slope, normed, inv_scale


def inner_forward_kernel(
    pairs_ref,
    edges_ref,
    nodes_ref,
    w_in_ref,
    w_out_ref,
    senders_ref,
    receivers_ref,
    sender_ref,
    receiver_ref,
    hidden_ref,
    slope_ref,
    normed_ref,
    scale_ref,
    total_ref,
):
    first, second = (to_column(pairs_ref[side : side + 1]).astype(jnp.int32) for side in range(2))
    senders, receivers = pair_marks(first, second, nodes_ref.shape[0])
    senders_ref[...] = senders
    receivers_ref[...] = receivers
    nodes = nodes_ref[...]
    sender = dot(senders, nodes).astype(BF16)
    receiver = dot(receivers, nodes).astype(BF16)
    sender_ref[...] = sender
    receiver_ref[...] = receiver
    hidden, slope, normed, inv_scale = edge_forward(
        edges_ref[...], sender, receiver, w_in_ref, w_out_ref
    )
    hidden_ref[...] = hidden
    slope_ref[...] = slope
    normed_ref[...] = normed
    scale_ref[...] = inv_scale
    part = dot_rows(receivers, normed.astype(BF16))

    @pl.when(pl.program_id(0) == 0)
    def _():
        total_ref[...] = part

    @pl.when(pl.program_id(0) > 0)
    def _():
        total_ref[...] += part


def cut_forward_kernel(
    senders_ref,
    receivers_ref,
    edges_ref,
    nodes_ref,
    far_ref,
    w_in_ref,
    w_out_ref,
    inner_total_ref,
    sender_ref,
    receiver_ref,
    hidden_ref,
    slope_ref,
    normed_ref,
    scale_ref,
    total_ref,
    outgoing_ref,
):
    base = nodes_ref.shape[0]
    nodes, far = nodes_ref[...], far_ref[...]

    def rows_of(marks_ref):
        return (dot(marks_ref[:, :base], nodes) + dot(marks_ref[:, base:], far)).astype(BF16)

    sender, receiver = rows_of(senders_ref), rows_of(receivers_ref)
    sender_ref[...] = sender
    receiver_ref[...] = receiver
    hidden, slope, normed, inv_scale = edge_forward(
        edges_ref[...], sender, receiver, w_in_ref, w_out_ref
    )
    hidden_ref[...] = hidden
    slope_ref[...] = slope
    normed_ref[...] = normed
    scale_ref[...] = inv_scale
    message = normed.astype(BF16)
    total_ref[...] = inner_total_ref[...] + dot_rows(receivers_ref[:, :base], message)
    outgoing_ref[...] = dot_rows(receivers_ref[:, base:], message).astype(BF16)


def new_edges_kernel(edges_ref, inner_ref, cut_ref, out_ref):
    inner_rows = inner_ref.shape[0]

    def added(edge, normed):
        return (edge.astype(F32) + normed.astype(BF16).astype(F32)).astype(BF16)

    out_ref[:inner_rows] = added(edges_ref[:inner_rows], inner_ref[...])
    out_ref[inner_rows:] = added(edges_ref[inner_rows:], cut_ref[...])


def node_kernel(
    me_ref,
    incoming_ref,
    asked_marks_ref,
    total_ref,
    nodes_ref,
    ct_ref,
    w_in_ref,
    w_out_ref,
    new_nodes_ref,
    self_grad_ref,
    agg_grad_ref,
    reply_ref,
    keep_ref,
    send_ref,
):
    latent = nodes_ref.shape[1]
    half = latent // 2
    nodes, asked_marks = nodes_ref[...], asked_marks_ref[...]
    aggregate = (total_ref[...] + dot_rows(asked_marks, incoming_ref[...])).astype(BF16)
    pre_hidden = dot(nodes, w_in_ref[:latent]) + dot(aggregate, w_in_ref[latent:])
    hidden, slope = activate(pre_hidden)
    normed, inv_scale = normalise(dot(hidden, w_out_ref[...]))
    upstream = ct_ref[...].astype(F32)
    grad_out = norm_backward(upstream, normed, inv_scale)
    grad_pre = (dot_cols(grad_out, w_out_ref[...]) * slope).astype(BF16)
    agg_grad = dot_cols(grad_pre, w_in_ref[latent:]).astype(BF16)
    agg_grad_ref[...] = agg_grad
    reply_ref[...] = dot(asked_marks, agg_grad).astype(BF16)
    self_grad_ref[...] = upstream + dot_cols(grad_pre, w_in_ref[:latent])
    new_nodes_ref[...] = (nodes.astype(F32) + normed).astype(BF16)

    def fill(low_ref, high_ref):
        by_aggregate = dot_rows(aggregate, grad_pre).astype(BF16)
        low_ref[:latent] = dot_rows(nodes, grad_pre).astype(BF16)
        low_ref[latent:] = by_aggregate[:half]
        high_ref[:half] = by_aggregate[half:]
        high_ref[half:] = dot_rows(hidden, grad_out).astype(BF16)

    @pl.when((me_ref[0] & 1) == 0)
    def _():
        fill(keep_ref, send_ref)

    @pl.when((me_ref[0] & 1) != 0)
    def _():
        fill(send_ref, keep_ref)


def edge_backward(ct, target_grads, normed, inv_scale, slope, w_out):
    grad_out = norm_backward(ct.astype(F32) + target_grads, normed, inv_scale)
    return grad_out, (dot_cols(grad_out, w_out) * slope).astype(BF16)


def inner_backward_kernel(
    receivers_ref,
    agg_grad_ref,
    ct_ref,
    normed_ref,
    scale_ref,
    slope_ref,
    w_out_ref,
    grad_out_ref,
    grad_pre_ref,
):
    grad_out, grad_pre = edge_backward(
        ct_ref[...],
        dot(receivers_ref[...], agg_grad_ref[...]),
        normed_ref[...],
        scale_ref[...],
        slope_ref[...],
        w_out_ref[...],
    )
    grad_out_ref[...] = grad_out
    grad_pre_ref[...] = grad_pre


def fetch_factors(half, sources, buffers, sems, wait):
    edges, inner_sender, cut_sender, inner_receiver, cut_receiver = sources[:5]
    inner_hidden, cut_hidden, inner_out, inner_pre = sources[5:]
    inner_rows, cut_rows = inner_pre.shape[0], cut_sender.shape[0]
    inner_edges = edges.at[pl.ds(0, inner_rows)]
    cut_edges = edges.at[pl.ds(inner_rows, cut_rows)]
    low = [inner_edges, cut_edges, inner_sender, cut_sender, inner_pre, inner_pre]
    high = [inner_receiver, cut_receiver, inner_hidden, cut_hidden, inner_pre, inner_out]

    def each(parts):
        for index, (source, buffer) in enumerate(zip(parts, buffers)):
            copy = pltpu.make_async_copy(source, buffer, sems.at[index])
            if wait:
                copy.wait()
            else:
                copy.start()

    @pl.when(half == 0)
    def _():
        each(low)

    @pl.when(half != 0)
    def _():
        each(high)


def place_rows(me_ref, index, latent):
    return pl.ds(pl.multiple_of((index ^ ((me_ref[0] >> 1) & 1)) * latent, latent), latent)


def edge_rows(me_ref, half, buffers, cut_pre, cut_out, out_ref):
    latent = cut_pre.shape[1]
    first, first_cut, second, second_cut, first_right, second_right = buffers
    chosen = jnp.where(half == 0, cut_pre.astype(F32), cut_out.astype(F32)).astype(BF16)
    out_ref[place_rows(me_ref, 0, latent)] = (
        dot_rows(first[...], first_right[...]) + dot_rows(first_cut[...], cut_pre)
    ).astype(BF16)
    out_ref[place_rows(me_ref, 1, latent)] = (
        dot_rows(second[...], second_right[...]) + dot_rows(second_cut[...], chosen)
    ).astype(BF16)


def cut_backward_kernel(
    me_ref,
    receivers_ref,
    agg_grad_ref,
    far_grad_ref,
    ct_ref,
    normed_ref,
    scale_ref,
    slope_ref,
    w_out_ref,
    *refs,
):
    sources, (grad_out_ref, grad_pre_ref, out_ref), rest = refs[:9], refs[9:12], refs[12:]
    buffers, sems = rest[:-1], rest[-1]
    half = 1 - (me_ref[0] & 1)
    fetch_factors(half, sources, buffers, sems, False)
    base = agg_grad_ref.shape[0]
    target = dot(receivers_ref[:, :base], agg_grad_ref[...]) + dot(
        receivers_ref[:, base:], far_grad_ref[...]
    )
    grad_out, grad_pre = edge_backward(
        ct_ref[...], target, normed_ref[...], scale_ref[...], slope_ref[...], w_out_ref[...]
    )
    grad_out_ref[...] = grad_out
    grad_pre_ref[...] = grad_pre
    fetch_factors(half, sources, buffers, sems, True)
    edge_rows(me_ref, half, buffers, grad_pre, grad_out, out_ref)


def edge_weights_kernel(me_ref, cut_out_ref, cut_pre_ref, *refs):
    sources, out_ref, rest = refs[:9], refs[9], refs[10:]
    buffers, sems = rest[:-1], rest[-1]
    half = me_ref[0] & 1
    fetch_factors(half, sources, buffers, sems, False)
    fetch_factors(half, sources, buffers, sems, True)
    edge_rows(me_ref, half, buffers, cut_pre_ref[...], cut_out_ref[...], out_ref)


def place_quarters(me_ref, pieces, outs, sems):
    mine = (me_ref[0] & 1) * 2 + ((me_ref[0] >> 1) & 1)
    tops = (0, outs[0].shape[0])

    def each(wait):
        for index, (piece, distance) in enumerate(pieces):
            rows = piece.shape[0]
            for quarter in range(4):

                @pl.when((mine ^ distance) == quarter)
                def _():
                    for side, (out, top) in enumerate(zip(outs, tops)):
                        first = max(quarter * rows, top)
                        count = min((quarter + 1) * rows, top + out.shape[0]) - first
                        if count > 0:
                            copy = pltpu.make_async_copy(
                                piece.at[pl.ds(first - quarter * rows, count)],
                                out.at[pl.ds(first - top, count)],
                                sems.at[2 * index + side],
                            )
                            if wait:
                                copy.wait()
                            else:
                                copy.start()

    each(False)
    each(True)


def first_quarters_kernel(me_ref, mine_ref, near_ref, in_ref, out_ref, sems):
    place_quarters(me_ref, [(mine_ref, 0), (near_ref, 2)], (in_ref, out_ref), sems)


def last_quarters_kernel(me_ref, far_ref, corner_ref, _, __, in_ref, out_ref, sems):
    place_quarters(me_ref, [(far_ref, 1), (corner_ref, 3)], (in_ref, out_ref), sems)


def all_quarters_kernel(me_ref, mine_ref, far_ref, near_ref, corner_ref, in_ref, out_ref, sems):
    pieces = [(mine_ref, 0), (far_ref, 1), (near_ref, 2), (corner_ref, 3)]
    place_quarters(me_ref, pieces, (in_ref, out_ref), sems)


def input_grads_kernel(
    inner_senders_ref,
    inner_receivers_ref,
    cut_senders_ref,
    cut_receivers_ref,
    inner_pre_ref,
    cut_pre_ref,
    w_in_ref,
    local_ref,
    outgoing_ref,
):
    latent = inner_pre_ref.shape[1]
    base = inner_senders_ref.shape[1]
    inner_pre, cut_pre = inner_pre_ref[...], cut_pre_ref[...]
    w_sender, w_receiver = w_in_ref[latent : 2 * latent], w_in_ref[2 * latent :]

    def summed(inner_marks_ref, cut_marks_ref):
        return (
            dot_rows(inner_marks_ref[...], inner_pre) + dot_rows(cut_marks_ref[:, :base], cut_pre)
        ).astype(BF16)

    outgoing_ref[...] = (
        dot_cols(dot_rows(cut_senders_ref[:, base:], cut_pre).astype(BF16), w_sender)
        + dot_cols(dot_rows(cut_receivers_ref[:, base:], cut_pre).astype(BF16), w_receiver)
    ).astype(BF16)
    local_ref[...] = dot_cols(summed(inner_senders_ref, cut_senders_ref), w_sender) + dot_cols(
        summed(inner_receivers_ref, cut_receivers_ref), w_receiver
    )


def edge_grads_kernel(ct_ref, inner_pre_ref, cut_pre_ref, w_edge_ref, out_ref, *, blocks):
    inside = pl.program_id(0) < blocks

    @pl.when(inside)
    def _():
        out_ref[...] = ct_ref[...].astype(F32) + dot_cols(inner_pre_ref[...], w_edge_ref[...])

    @pl.when(jnp.logical_not(inside))
    def _():
        out_ref[...] = ct_ref[...].astype(F32) + dot_cols(cut_pre_ref[...], w_edge_ref[...])


VMEM = pl.BlockSpec(memory_space=pltpu.VMEM)
SMEM = pl.BlockSpec(memory_space=pltpu.SMEM)
ANY = pl.BlockSpec(memory_space=pl.ANY)
HBM = pl.BlockSpec(memory_space=pltpu.HBM)


def shaped(dtype, *shape):
    return jax.ShapeDtypeStruct(shape, dtype)


class Line:
    def __init__(self):
        self.last = None

    def run(
        self, body, outs, ins, specs=None, out_specs=None, grid=None, scratch=(), limit=VMEM_LIMIT, aliases=None
    ):
        single = not isinstance(outs, (list, tuple))
        out_shape = [outs] if single else list(outs)
        specs = [VMEM] * len(ins) if specs is None else list(specs)
        count, extra = len(ins), {} if grid is None else {"grid": grid}
        ins = list(ins)
        if self.last is not None:
            ins.append(self.last)
            specs.append(ANY)

        def ordered(*refs):
            return body(*refs[:count], *refs[len(ins) :])

        result = pl.pallas_call(
            ordered,
            out_shape=out_shape,
            in_specs=specs,
            out_specs=[VMEM] * len(out_shape) if out_specs is None else out_specs,
            scratch_shapes=scratch,
            input_output_aliases=aliases or {},
            compiler_params=pltpu.CompilerParams(vmem_limit_bytes=limit),
            cost_estimate=pl.CostEstimate(flops=1, bytes_accessed=1, transcendentals=0),
            **extra,
        )(*ins)
        self.last = result[-1]
        return result[0] if single else result


def index_bits(devices):
    return list(range(devices.bit_length() - 1))


def across(rows, devices, mask):
    return lax.ppermute(rows, "dom", [(device, device ^ mask) for device in range(devices)])


def fence(*values):
    return lax.optimization_barrier(values)


def place_of(bit):
    return (lax.axis_index("dom") >> bit) & 1


def split(parts, bit):
    place = place_of(bit)
    halves = [part.reshape(2, part.shape[0] // 2, part.shape[1]) for part in parts]
    own = [lax.dynamic_index_in_dim(half, place, 0, False) for half in halves]
    sent = [lax.dynamic_index_in_dim(half, 1 - place, 0, False) for half in halves]
    return own, added(*sent)


def handed(rows, devices, bit):
    return [rows, across(rows, devices, 1 << bit)]


def added(*parts):
    return sum(part.astype(F32) for part in parts).astype(BF16)


def joined(parts, bit):
    orders = [jnp.concatenate(parts), jnp.concatenate(parts[::-1])]
    return jnp.where(place_of(bit) == 0, *orders)


def exchange(rows, domains):
    shape = rows.shape
    split = rows.reshape((domains, shape[0] // domains) + shape[1:])
    return lax.all_to_all(split, "dom", split_axis=0, concat_axis=0, tiled=True).reshape(shape)


def shards(
    nodes,
    edges,
    inner_pairs,
    cut_local,
    cut_dest,
    cut_remote,
    w_edge_in,
    w_edge_out,
    w_node_in,
    w_node_out,
    ct_nodes,
    ct_edges,
):
    domains = lax.axis_size("dom")
    node_rows, latent = nodes.shape
    inner_count, cut_count = inner_pairs.shape[0], cut_local.shape[0]
    inner_rows, cut_rows = 2 * inner_count, 2 * cut_count
    slots = max(2, 2 * cut_count // domains)
    total_slots = domains * slots
    table = node_rows + total_slots
    me = lax.axis_index("dom").reshape(1)
    line = Line()

    ask = line.run(
        ask_kernel, shaped(jnp.int32, domains, slots), [cut_dest.reshape(1, -1), cut_remote.reshape(1, -1)]
    )
    asked = lax.all_to_all(ask, "dom", split_axis=0, concat_axis=0, tiled=True)
    cut_senders, cut_receivers = line.run(
        functools.partial(cut_marks_kernel, domains=domains, slots=slots),
        [shaped(BF16, cut_rows, table)] * 2,
        [cut_dest.reshape(1, -1), cut_local.reshape(1, -1)],
    )
    reply, asked_marks = line.run(
        reply_kernel,
        [shaped(BF16, total_slots, latent), shaped(BF16, total_slots, node_rows)],
        [asked, nodes],
        limit=2**22,
    )
    far = exchange(reply, domains)

    block = cut_rows
    blocks = inner_rows // block

    def rows_spec(width, rows=block):
        return pl.BlockSpec((rows, width), lambda step: (step, 0))

    def all_spec(array):
        return pl.BlockSpec(array.shape, lambda step: (0, 0))

    saved_widths = [node_rows, node_rows, latent, latent, latent, latent, latent, 1]
    saved_types = [BF16, BF16, BF16, BF16, BF16, F32, F32, F32]
    (
        inner_senders,
        inner_receivers,
        inner_sender,
        inner_receiver,
        inner_hidden,
        inner_slope,
        inner_normed,
        inner_scale,
        inner_total,
    ) = line.run(
        inner_forward_kernel,
        [shaped(kind, inner_rows, width) for kind, width in zip(saved_types, saved_widths)]
        + [shaped(F32, node_rows, latent)],
        [inner_pairs.T, edges, nodes, w_edge_in, w_edge_out],
        [
            pl.BlockSpec((2, block // 2), lambda step: (0, step)),
            rows_spec(latent),
            all_spec(nodes),
            all_spec(w_edge_in),
            all_spec(w_edge_out),
        ],
        [rows_spec(width) for width in saved_widths] + [all_spec(nodes)],
        (blocks,),
    )

    def last_rows(array):
        last = array.shape[0] // block - 1
        return pl.BlockSpec((block, array.shape[1]), lambda step: (last, 0))

    (
        cut_sender,
        cut_receiver,
        cut_hidden,
        cut_slope,
        cut_normed,
        cut_scale,
        total,
        outgoing,
    ) = line.run(
        cut_forward_kernel,
        [shaped(kind, cut_rows, width) for kind, width in zip(saved_types, saved_widths)][2:]
        + [shaped(F32, node_rows, latent), shaped(BF16, total_slots, latent)],
        [
            cut_senders,
            cut_receivers,
            edges,
            nodes,
            far,
            w_edge_in,
            w_edge_out,
            inner_total,
        ],
        [
            all_spec(cut_senders),
            all_spec(cut_receivers),
            last_rows(edges),
            all_spec(nodes),
            all_spec(far),
            all_spec(w_edge_in),
            all_spec(w_edge_out),
            all_spec(inner_total),
        ],
        [rows_spec(width) for width in saved_widths[2:]]
        + [all_spec(nodes), rows_spec(latent, total_slots)],
        (1,),
    )
    incoming = exchange(outgoing, domains)
    new_edges = line.run(
        new_edges_kernel,
        shaped(BF16, *edges.shape),
        [edges, inner_normed, cut_normed],
    )
    (
        new_nodes,
        self_grad,
        agg_grad,
        grad_reply,
        node_keep,
        node_send,
    ) = line.run(
        node_kernel,
        [
            shaped(BF16, node_rows, latent),
            shaped(F32, node_rows, latent),
            shaped(BF16, node_rows, latent),
            shaped(BF16, total_slots, latent),
        ]
        + [shaped(BF16, 3 * latent // 2, latent)] * 2,
        [me, incoming, asked_marks, total, nodes, ct_nodes, w_node_in, w_node_out],
        [SMEM] + [VMEM] * 7,
    )
    far_grad = exchange(grad_reply, domains)
    node_sum = added(node_keep, across(node_send, domains, 1))
    inner_out, inner_pre = line.run(
        inner_backward_kernel,
        [shaped(BF16, inner_rows, latent)] * 2,
        [
            inner_receivers,
            agg_grad,
            ct_edges,
            inner_normed,
            inner_scale,
            inner_slope,
            w_edge_out,
        ],
        [
            rows_spec(node_rows),
            all_spec(agg_grad),
            rows_spec(latent),
            rows_spec(latent),
            rows_spec(1),
            rows_spec(latent),
            all_spec(w_edge_out),
        ],
        [rows_spec(latent)] * 2,
        (blocks,),
    )
    bits = index_bits(domains)
    node_own, node_sent = split([node_sum], 1)
    node_parts = [*node_own, across(node_sent, domains, 2)]
    far_grad, node_sum, inner_pre = fence(far_grad, node_sum, inner_pre)
    factors = [
        edges,
        inner_sender,
        cut_sender,
        inner_receiver,
        cut_receiver,
        inner_hidden,
        cut_hidden,
        inner_out,
        inner_pre,
    ]
    buffers = [pltpu.VMEM((rows, latent), BF16) for rows in (inner_rows, cut_rows) * 2]
    buffers += [pltpu.VMEM((inner_rows, latent), BF16)] * 2
    buffers.append(pltpu.SemaphoreType.DMA((len(buffers),)))
    cut_out, cut_pre, edge_send = line.run(
        cut_backward_kernel,
        [shaped(BF16, cut_rows, latent)] * 2 + [shaped(BF16, 2 * latent, latent)],
        [
            me,
            cut_receivers,
            agg_grad,
            far_grad,
            ct_edges,
            cut_normed,
            cut_scale,
            cut_slope,
            w_edge_out,
        ]
        + factors,
        [
            SMEM,
            all_spec(cut_receivers),
            all_spec(agg_grad),
            all_spec(far_grad),
            last_rows(ct_edges),
            all_spec(cut_normed),
            all_spec(cut_scale),
            all_spec(cut_slope),
            all_spec(w_edge_out),
        ]
        + [ANY] * len(factors),
        [rows_spec(latent)] * 2 + [rows_spec(latent, 2 * latent)],
        (1,),
        buffers,
    )
    edge_send, place, *node_parts = fence(edge_send, me, *node_parts)
    received = across(edge_send, domains, 1)
    node_own, node_sent = split(node_parts, 2)
    node_got = across(node_sent, domains, 4)
    edge_keep = line.run(
        edge_weights_kernel,
        shaped(BF16, 2 * latent, latent),
        [place, cut_out, cut_pre] + factors,
        [SMEM, VMEM, VMEM] + [ANY] * len(factors),
        scratch=buffers,
    )
    edge_keep, received = fence(edge_keep, received)
    edge_sent = added(edge_keep[latent:], received[latent:])
    edge_sent, inner_pre, cut_pre = fence(edge_sent, inner_pre, cut_pre)
    node_got = fence(node_got, edge_sent)[0]
    edge_got = across(edge_sent, domains, 2)
    node_sum = added(*node_own, node_got)
    for bit in bits[3:]:
        node_sum = added(*handed(node_sum, domains, bit))
    edge_keep, received = fence(edge_keep, received, edge_sent)[:2]
    edge_own = added(edge_keep[:latent], received[:latent])
    local_grad, outgoing_grad = line.run(
        input_grads_kernel,
        [shaped(F32, node_rows, latent), shaped(BF16, total_slots, latent)],
        [
            inner_senders,
            inner_receivers,
            cut_senders,
            cut_receivers,
            inner_pre,
            cut_pre,
            w_edge_in,
        ],
    )
    edge_own, edge_got, node_sum, inner_pre, cut_pre, local_grad = fence(
        edge_own, edge_got, node_sum, inner_pre, cut_pre, local_grad
    )
    edge_own, edge_sent = split([added(edge_own, edge_got)], 2)
    edge_got = across(edge_sent, domains, 4)
    grad_edges = line.run(
        functools.partial(edge_grads_kernel, blocks=blocks),
        shaped(F32, *edges.shape),
        [ct_edges, inner_pre, cut_pre, w_edge_in],
        [
            rows_spec(latent),
            pl.BlockSpec((block, latent), lambda step: (jnp.minimum(step, blocks - 1), 0)),
            all_spec(cut_pre),
            pl.BlockSpec((latent, latent), lambda step: (0, 0)),
        ],
        [rows_spec(latent)],
        (blocks + 1,),
    )
    edge_got, node_sum, grad_edges = fence(edge_got, node_sum, grad_edges)
    edge_sum = added(*edge_own, edge_got)
    edge_sum, node_sum = fence(edge_sum, node_sum)
    edge_got = across(edge_sum, domains, 8)
    node_parts = handed(joined(handed(node_sum, domains, 2), 2), domains, 1)
    edge_sum = added(*fence(edge_sum, edge_got))
    for bit in bits[4:]:
        edge_sum = added(*handed(edge_sum, domains, bit))
    *edge_parts, node_near, node_far, outgoing_grad = fence(
        *handed(edge_sum, domains, 2), *node_parts, outgoing_grad
    )
    edge_sum = joined(edge_parts, 2)
    far, near = across(edge_sum, domains, 2), across(edge_sum, domains, 1)
    node_parts = [node_near, node_far]
    node_parts += [across(part, domains, 1) for part in node_parts]
    returned = exchange(outgoing_grad, domains)
    quarters = [shaped(BF16, 3 * latent, latent), shaped(BF16, latent, latent)]
    copies = dict(out_specs=[HBM] * 2, scratch=[pltpu.SemaphoreType.DMA((8,))], limit=2**20)
    grad_edge_in, grad_edge_out = line.run(
        first_quarters_kernel, quarters, [me, edge_sum, near], [SMEM, ANY, ANY], **copies
    )
    grad_node_in, grad_node_out = line.run(
        all_quarters_kernel,
        [shaped(BF16, 2 * latent, latent), shaped(BF16, latent, latent)],
        [me] + node_parts,
        [SMEM] + [VMEM] * 4,
        **(copies | {"limit": VMEM_LIMIT}),
    )
    far, grad_edge_in, grad_edge_out, grad_node_in, grad_node_out, returned = fence(
        far, grad_edge_in, grad_edge_out, grad_node_in, grad_node_out, returned
    )
    corner = across(far, domains, 1)
    grad_nodes = self_grad + local_grad + dot_rows(asked_marks, returned)
    corner, grad_nodes = fence(corner, grad_nodes)
    grad_edge_in, grad_edge_out = Line().run(
        last_quarters_kernel,
        quarters,
        [me, far, corner, grad_edge_in, grad_edge_out],
        [SMEM, ANY, ANY, HBM, HBM],
        aliases={3: 0, 4: 1},
        **copies,
    )
    return (
        new_nodes,
        new_edges,
        grad_nodes,
        grad_edges,
        grad_edge_in,
        grad_edge_out,
        grad_node_in,
        grad_node_out,
    )


def solution(mesh):
    placed = (
        P(("groups", "dom"), None),
        P(("groups", "dom"), None),
        P(("groups", "dom"), None),
        P(("groups", "dom")),
        P(("groups", "dom"), None),
        P(("groups", "dom")),
        P(),
        P(),
        P(),
        P(),
        P(("groups", "dom"), None),
        P(("groups", "dom"), None),
    )
    return jax.shard_map(
        shards,
        mesh=mesh,
        in_specs=placed,
        out_specs=(
            P(("groups", "dom"), None),
            P(("groups", "dom"), None),
            P(("groups", "dom"), None),
            P(("groups", "dom"), None),
            P("groups", None),
            P("groups", None),
            P("groups", None),
            P("groups", None),
        ),
        check_vma=False,
    )
```

```python
import functools

import jax
import jax.numpy as jnp
from jax import lax
from jax.experimental import pallas as pl
from jax.experimental.pallas import tpu as pltpu
from jax.sharding import PartitionSpec as P

BF16 = jnp.bfloat16
F32 = jnp.float32
VMEM_LIMIT = 60 * 1024 * 1024


def dot(left, right):
    return jnp.dot(left, right, preferred_element_type=F32)


def dot_rows(left, right):
    return lax.dot_general(left, right, (((0,), (0,)), ((), ())), preferred_element_type=F32)


def dot_cols(left, right):
    return lax.dot_general(left, right, (((1,), (1,)), ((), ())), preferred_element_type=F32)


def iota(shape, axis):
    return lax.broadcasted_iota(jnp.int32, shape, axis)


def marks(mask):
    return jnp.where(mask, 1.0, 0.0).astype(BF16)


def onehot(column, width):
    return marks(column == iota((column.shape[0], width), 1))


def to_column(row):
    count = row.shape[1]
    square = (count, count)
    kept = jnp.where(iota(square, 0) == iota(square, 1), row.astype(F32), 0.0)
    return jnp.sum(kept, axis=1, keepdims=True)


def slot_ranks(dest, domains):
    count = dest.shape[0]
    square = (count, count)
    dest_marks = onehot(dest, domains)
    before = dot(marks(iota(square, 0) > iota(square, 1)), dest_marks)
    return dest_marks, jnp.sum(before * dest_marks.astype(F32), axis=1, keepdims=True)


def pair_marks(first, second, width):
    pairs = first.shape[0]
    shape = (2 * pairs, pairs)
    edge, pair = iota(shape, 0), iota(shape, 1)
    mine = (edge >> 1) == pair
    even = marks(mine & ((edge & 1) == 0))
    odd = marks(mine & ((edge & 1) == 1))
    first_marks, second_marks = onehot(first, width), onehot(second, width)
    senders = dot(even, first_marks) + dot(odd, second_marks)
    receivers = dot(even, second_marks) + dot(odd, first_marks)
    return senders.astype(BF16), receivers.astype(BF16)


def normalise(values):
    centered = values - jnp.mean(values, axis=1, keepdims=True)
    inv_scale = lax.rsqrt(jnp.mean(centered * centered, axis=1, keepdims=True) + 1e-05)
    return centered * inv_scale, inv_scale


def activate(pre_hidden):
    gate = jax.nn.sigmoid(pre_hidden)
    return (pre_hidden * gate).astype(BF16), gate * (1.0 + pre_hidden * (1.0 - gate))


def norm_backward(upstream, normed, inv_scale):
    centered = (
        upstream
        - jnp.mean(upstream, axis=1, keepdims=True)
        - normed * jnp.mean(upstream * normed, axis=1, keepdims=True)
    )
    return (inv_scale * centered).astype(BF16)


def ask_kernel(dest_ref, remote_ref, ask_ref):
    domains, slots = ask_ref.shape
    dest_marks, rank = slot_ranks(to_column(dest_ref[...]).astype(jnp.int32), domains)
    rank_marks = jnp.where(rank == iota((rank.shape[0], slots), 1).astype(F32), 1.0, 0.0)
    wanted = (rank_marks * to_column(remote_ref[...])).astype(BF16)
    ask_ref[...] = dot_rows(dest_marks, wanted).astype(jnp.int32)


def cut_marks_kernel(dest_ref, local_ref, senders_ref, receivers_ref, *, domains, slots):
    width = senders_ref.shape[1]
    base = width - domains * slots
    dest = to_column(dest_ref[...]).astype(jnp.int32)
    _, rank = slot_ranks(dest, domains)
    second = dest * slots + rank.astype(jnp.int32) + base
    first = to_column(local_ref[...]).astype(jnp.int32)
    senders, receivers = pair_marks(first, second, width)
    senders_ref[...] = senders
    receivers_ref[...] = receivers


def edge_forward(edge, sender, receiver, w_in_ref, w_out_ref):
    latent = edge.shape[1]
    pre_hidden = (
        dot(edge, w_in_ref[:latent])
        + dot(sender, w_in_ref[latent : 2 * latent])
        + dot(receiver, w_in_ref[2 * latent :])
    )
    hidden, slope = activate(pre_hidden)
    normed, inv_scale = normalise(dot(hidden, w_out_ref[...]))
    return hidden, slope, normed, inv_scale


def inner_forward_kernel(
    pairs_ref,
    edges_ref,
    nodes_ref,
    w_in_ref,
    w_out_ref,
    senders_ref,
    receivers_ref,
    sender_ref,
    receiver_ref,
    hidden_ref,
    slope_ref,
    normed_ref,
    scale_ref,
    total_ref,
):
    first, second = (to_column(pairs_ref[side : side + 1]).astype(jnp.int32) for side in range(2))
    senders, receivers = pair_marks(first, second, nodes_ref.shape[0])
    senders_ref[...] = senders
    receivers_ref[...] = receivers
    nodes = nodes_ref[...]
    sender = dot(senders, nodes).astype(BF16)
    receiver = dot(receivers, nodes).astype(BF16)
    sender_ref[...] = sender
    receiver_ref[...] = receiver
    hidden, slope, normed, inv_scale = edge_forward(
        edges_ref[...], sender, receiver, w_in_ref, w_out_ref
    )
    hidden_ref[...] = hidden
    slope_ref[...] = slope
    normed_ref[...] = normed
    scale_ref[...] = inv_scale
    part = dot_rows(receivers, normed.astype(BF16))

    @pl.when(pl.program_id(0) == 0)
    def _():
        total_ref[...] = part

    @pl.when(pl.program_id(0) > 0)
    def _():
        total_ref[...] += part


def cut_forward_kernel(
    senders_ref,
    receivers_ref,
    edges_ref,
    nodes_ref,
    far_ref,
    w_in_ref,
    w_out_ref,
    inner_total_ref,
    sender_ref,
    receiver_ref,
    hidden_ref,
    slope_ref,
    normed_ref,
    scale_ref,
    total_ref,
    outgoing_ref,
):
    base = nodes_ref.shape[0]
    nodes, far = nodes_ref[...], far_ref[...]

    def rows_of(marks_ref):
        return (dot(marks_ref[:, :base], nodes) + dot(marks_ref[:, base:], far)).astype(BF16)

    sender, receiver = rows_of(senders_ref), rows_of(receivers_ref)
    sender_ref[...] = sender
    receiver_ref[...] = receiver
    hidden, slope, normed, inv_scale = edge_forward(
        edges_ref[...], sender, receiver, w_in_ref, w_out_ref
    )
    hidden_ref[...] = hidden
    slope_ref[...] = slope
    normed_ref[...] = normed
    scale_ref[...] = inv_scale
    message = normed.astype(BF16)
    total_ref[...] = inner_total_ref[...] + dot_rows(receivers_ref[:, :base], message)
    outgoing_ref[...] = dot_rows(receivers_ref[:, base:], message).astype(BF16)


def new_edges_kernel(edges_ref, inner_ref, cut_ref, out_ref):
    inner_rows = inner_ref.shape[0]

    def added(edge, normed):
        return (edge.astype(F32) + normed.astype(BF16).astype(F32)).astype(BF16)

    out_ref[:inner_rows] = added(edges_ref[:inner_rows], inner_ref[...])
    out_ref[inner_rows:] = added(edges_ref[inner_rows:], cut_ref[...])


def node_kernel(
    me_ref,
    incoming_ref,
    asked_marks_ref,
    total_ref,
    nodes_ref,
    ct_ref,
    w_in_ref,
    w_out_ref,
    new_nodes_ref,
    self_grad_ref,
    agg_grad_ref,
    reply_ref,
    keep_ref,
    send_ref,
):
    latent = nodes_ref.shape[1]
    half = latent // 2
    nodes, asked_marks = nodes_ref[...], asked_marks_ref[...]
    aggregate = (total_ref[...] + dot_rows(asked_marks, incoming_ref[...])).astype(BF16)
    pre_hidden = dot(nodes, w_in_ref[:latent]) + dot(aggregate, w_in_ref[latent:])
    hidden, slope = activate(pre_hidden)
    normed, inv_scale = normalise(dot(hidden, w_out_ref[...]))
    upstream = ct_ref[...].astype(F32)
    grad_out = norm_backward(upstream, normed, inv_scale)
    grad_pre = (dot_cols(grad_out, w_out_ref[...]) * slope).astype(BF16)
    agg_grad = dot_cols(grad_pre, w_in_ref[latent:]).astype(BF16)
    agg_grad_ref[...] = agg_grad
    reply_ref[...] = dot(asked_marks, agg_grad).astype(BF16)
    self_grad_ref[...] = upstream + dot_cols(grad_pre, w_in_ref[:latent])
    new_nodes_ref[...] = (nodes.astype(F32) + normed).astype(BF16)

    def fill(low_ref, high_ref):
        by_aggregate = dot_rows(aggregate, grad_pre).astype(BF16)
        low_ref[:latent] = dot_rows(nodes, grad_pre).astype(BF16)
        low_ref[latent:] = by_aggregate[:half]
        high_ref[:half] = by_aggregate[half:]
        high_ref[half:] = dot_rows(hidden, grad_out).astype(BF16)

    @pl.when((me_ref[0] & 1) == 0)
    def _():
        fill(keep_ref, send_ref)

    @pl.when((me_ref[0] & 1) != 0)
    def _():
        fill(send_ref, keep_ref)


def edge_backward(ct, target_grads, normed, inv_scale, slope, w_out):
    grad_out = norm_backward(ct.astype(F32) + target_grads, normed, inv_scale)
    return grad_out, (dot_cols(grad_out, w_out) * slope).astype(BF16)


def inner_backward_kernel(
    receivers_ref,
    agg_grad_ref,
    ct_ref,
    normed_ref,
    scale_ref,
    slope_ref,
    w_out_ref,
    grad_out_ref,
    grad_pre_ref,
):
    grad_out, grad_pre = edge_backward(
        ct_ref[...],
        dot(receivers_ref[...], agg_grad_ref[...]),
        normed_ref[...],
        scale_ref[...],
        slope_ref[...],
        w_out_ref[...],
    )
    grad_out_ref[...] = grad_out
    grad_pre_ref[...] = grad_pre


def fetch_factors(half, sources, buffers, sems, wait):
    edges, inner_sender, cut_sender, inner_receiver, cut_receiver = sources[:5]
    inner_hidden, cut_hidden, inner_out, inner_pre = sources[5:]
    inner_rows, cut_rows = inner_pre.shape[0], cut_sender.shape[0]
    inner_edges = edges.at[pl.ds(0, inner_rows)]
    cut_edges = edges.at[pl.ds(inner_rows, cut_rows)]
    low = [inner_edges, cut_edges, inner_sender, cut_sender, inner_pre, inner_pre]
    high = [inner_receiver, cut_receiver, inner_hidden, cut_hidden, inner_pre, inner_out]

    def each(parts):
        for index, (source, buffer) in enumerate(zip(parts, buffers)):
            copy = pltpu.make_async_copy(source, buffer, sems.at[index])
            if wait:
                copy.wait()
            else:
                copy.start()

    @pl.when(half == 0)
    def _():
        each(low)

    @pl.when(half != 0)
    def _():
        each(high)


def place_rows(me_ref, index, latent):
    return pl.ds(pl.multiple_of((index ^ ((me_ref[0] >> 1) & 1)) * latent, latent), latent)


def edge_rows(half, buffers, cut_pre, cut_out, put):
    latent = cut_pre.shape[1]
    first, first_cut, second, second_cut, first_right, second_right = buffers
    chosen = jnp.where(half == 0, cut_pre.astype(F32), cut_out.astype(F32)).astype(BF16)
    put(0, dot_rows(first[...], first_right[...]) + dot_rows(first_cut[...], cut_pre))
    put(1, dot_rows(second[...], second_right[...]) + dot_rows(second_cut[...], chosen))


def cut_backward_kernel(
    me_ref,
    receivers_ref,
    agg_grad_ref,
    far_grad_ref,
    ct_ref,
    normed_ref,
    scale_ref,
    slope_ref,
    w_out_ref,
    *refs,
):
    sources, (grad_out_ref, grad_pre_ref, out_ref), rest = refs[:9], refs[9:12], refs[12:]
    buffers, sems = rest[:-1], rest[-1]
    half = 1 - (me_ref[0] & 1)
    fetch_factors(half, sources, buffers, sems, False)
    base = agg_grad_ref.shape[0]
    target = dot(receivers_ref[:, :base], agg_grad_ref[...]) + dot(
        receivers_ref[:, base:], far_grad_ref[...]
    )
    grad_out, grad_pre = edge_backward(
        ct_ref[...], target, normed_ref[...], scale_ref[...], slope_ref[...], w_out_ref[...]
    )
    grad_out_ref[...] = grad_out
    grad_pre_ref[...] = grad_pre
    fetch_factors(half, sources, buffers, sems, True)

    def put(index, value):
        out_ref[place_rows(me_ref, index, value.shape[1])] = value.astype(BF16)

    edge_rows(half, buffers, grad_pre, grad_out, put)


def edge_weights_kernel(me_ref, cut_out_ref, cut_pre_ref, *refs):
    sources, (own_ref, sent_ref), rest = refs[:9], refs[9:11], refs[11:]
    buffers, sems = rest[:-1], rest[-1]
    half = me_ref[0] & 1
    fetch_factors(half, sources, buffers, sems, False)
    fetch_factors(half, sources, buffers, sems, True)
    place = (me_ref[0] >> 1) & 1

    def put(index, value):
        @pl.when(place == index)
        def _():
            own_ref[...] = value.astype(BF16)

        @pl.when(place != index)
        def _():
            sent_ref[...] = value.astype(BF16)

    edge_rows(half, buffers, cut_pre_ref[...], cut_out_ref[...], put)


def place_quarters(me_ref, pieces, outs, sems):
    mine = (me_ref[0] & 1) * 2 + ((me_ref[0] >> 1) & 1)
    tops = (0, outs[0].shape[0])

    def each(wait):
        for index, (piece, distance) in enumerate(pieces):
            rows = piece.shape[0]
            for quarter in range(4):

                @pl.when((mine ^ distance) == quarter)
                def _():
                    for side, (out, top) in enumerate(zip(outs, tops)):
                        first = max(quarter * rows, top)
                        count = min((quarter + 1) * rows, top + out.shape[0]) - first
                        if count > 0:
                            copy = pltpu.make_async_copy(
                                piece.at[pl.ds(first - quarter * rows, count)],
                                out.at[pl.ds(first - top, count)],
                                sems.at[2 * index + side],
                            )
                            if wait:
                                copy.wait()
                            else:
                                copy.start()

    each(False)
    each(True)


def first_quarters_kernel(me_ref, mine_ref, near_ref, in_ref, out_ref, sems):
    place_quarters(me_ref, [(mine_ref, 0), (near_ref, 2)], (in_ref, out_ref), sems)


def last_quarters_kernel(me_ref, far_ref, corner_ref, _, __, in_ref, out_ref, sems):
    place_quarters(me_ref, [(far_ref, 1), (corner_ref, 3)], (in_ref, out_ref), sems)


def all_quarters_kernel(me_ref, mine_ref, far_ref, near_ref, corner_ref, in_ref, out_ref, sems):
    pieces = [(mine_ref, 0), (far_ref, 1), (near_ref, 2), (corner_ref, 3)]
    place_quarters(me_ref, pieces, (in_ref, out_ref), sems)


def input_grads_kernel(
    inner_senders_ref,
    inner_receivers_ref,
    cut_senders_ref,
    cut_receivers_ref,
    inner_pre_ref,
    cut_pre_ref,
    w_in_ref,
    local_ref,
    outgoing_ref,
):
    latent = inner_pre_ref.shape[1]
    base = inner_senders_ref.shape[1]
    inner_pre, cut_pre = inner_pre_ref[...], cut_pre_ref[...]
    w_sender, w_receiver = w_in_ref[latent : 2 * latent], w_in_ref[2 * latent :]

    def summed(inner_marks_ref, cut_marks_ref):
        return (
            dot_rows(inner_marks_ref[...], inner_pre) + dot_rows(cut_marks_ref[:, :base], cut_pre)
        ).astype(BF16)

    outgoing_ref[...] = (
        dot_cols(dot_rows(cut_senders_ref[:, base:], cut_pre).astype(BF16), w_sender)
        + dot_cols(dot_rows(cut_receivers_ref[:, base:], cut_pre).astype(BF16), w_receiver)
    ).astype(BF16)
    local_ref[...] = dot_cols(summed(inner_senders_ref, cut_senders_ref), w_sender) + dot_cols(
        summed(inner_receivers_ref, cut_receivers_ref), w_receiver
    )


def edge_grads_kernel(ct_ref, inner_pre_ref, cut_pre_ref, w_edge_ref, out_ref, *, blocks):
    inside = pl.program_id(0) < blocks

    @pl.when(inside)
    def _():
        out_ref[...] = ct_ref[...].astype(F32) + dot_cols(inner_pre_ref[...], w_edge_ref[...])

    @pl.when(jnp.logical_not(inside))
    def _():
        out_ref[...] = ct_ref[...].astype(F32) + dot_cols(cut_pre_ref[...], w_edge_ref[...])


VMEM = pl.BlockSpec(memory_space=pltpu.VMEM)
SMEM = pl.BlockSpec(memory_space=pltpu.SMEM)
ANY = pl.BlockSpec(memory_space=pl.ANY)
HBM = pl.BlockSpec(memory_space=pltpu.HBM)


def shaped(dtype, *shape):
    return jax.ShapeDtypeStruct(shape, dtype)


class Line:
    def __init__(self):
        self.last = None

    def run(
        self, body, outs, ins, specs=None, out_specs=None, grid=None, scratch=(), limit=VMEM_LIMIT, aliases=None
    ):
        single = not isinstance(outs, (list, tuple))
        out_shape = [outs] if single else list(outs)
        specs = [VMEM] * len(ins) if specs is None else list(specs)
        count, extra = len(ins), {} if grid is None else {"grid": grid}
        ins = list(ins)
        if self.last is not None:
            ins.append(self.last)
            specs.append(ANY)

        def ordered(*refs):
            return body(*refs[:count], *refs[len(ins) :])

        result = pl.pallas_call(
            ordered,
            out_shape=out_shape,
            in_specs=specs,
            out_specs=[VMEM] * len(out_shape) if out_specs is None else out_specs,
            scratch_shapes=scratch,
            input_output_aliases=aliases or {},
            compiler_params=pltpu.CompilerParams(vmem_limit_bytes=limit),
            cost_estimate=pl.CostEstimate(flops=1, bytes_accessed=1, transcendentals=0),
            **extra,
        )(*ins)
        self.last = result[-1]
        return result[0] if single else result


def index_bits(devices):
    return list(range(devices.bit_length() - 1))


def across(rows, devices, mask):
    return lax.ppermute(rows, "dom", [(device, device ^ mask) for device in range(devices)])


def fence(*values):
    return lax.optimization_barrier(values)


def place_of(bit):
    return (lax.axis_index("dom") >> bit) & 1


def split(parts, bit):
    place = place_of(bit)
    halves = [part.reshape(2, part.shape[0] // 2, part.shape[1]) for part in parts]
    own = [lax.dynamic_index_in_dim(half, place, 0, False) for half in halves]
    sent = [lax.dynamic_index_in_dim(half, 1 - place, 0, False) for half in halves]
    return own, added(*sent)


def handed(rows, devices, bit):
    return [rows, across(rows, devices, 1 << bit)]


def added(*parts):
    return sum(part.astype(F32) for part in parts).astype(BF16)


def joined(parts, bit):
    orders = [jnp.concatenate(parts), jnp.concatenate(parts[::-1])]
    return jnp.where(place_of(bit) == 0, *orders)


def exchange(rows, domains):
    shape = rows.shape
    split = rows.reshape((domains, shape[0] // domains) + shape[1:])
    return lax.all_to_all(split, "dom", split_axis=0, concat_axis=0, tiled=True).reshape(shape)


def shards(
    nodes,
    edges,
    inner_pairs,
    cut_local,
    cut_dest,
    cut_remote,
    w_edge_in,
    w_edge_out,
    w_node_in,
    w_node_out,
    ct_nodes,
    ct_edges,
):
    domains = lax.axis_size("dom")
    node_rows, latent = nodes.shape
    inner_count, cut_count = inner_pairs.shape[0], cut_local.shape[0]
    inner_rows, cut_rows = 2 * inner_count, 2 * cut_count
    slots = max(2, 2 * cut_count // domains)
    total_slots = domains * slots
    table = node_rows + total_slots
    me = lax.axis_index("dom").reshape(1)
    line = Line()

    ask = line.run(
        ask_kernel, shaped(jnp.int32, domains, slots), [cut_dest.reshape(1, -1), cut_remote.reshape(1, -1)]
    )
    asked = lax.all_to_all(ask, "dom", split_axis=0, concat_axis=0, tiled=True)
    cut_senders, cut_receivers = line.run(
        functools.partial(cut_marks_kernel, domains=domains, slots=slots),
        [shaped(BF16, cut_rows, table)] * 2,
        [cut_dest.reshape(1, -1), cut_local.reshape(1, -1)],
    )
    asked_marks = jnp.where(
        asked[:, :, None] == jnp.arange(node_rows, dtype=jnp.int32)[None, None], 1.0, 0.0
    ).astype(BF16)
    reply = lax.dot_general(asked_marks, nodes, (((2,), (0,)), ((), ())), preferred_element_type=F32)
    reply = reply.astype(BF16).reshape(total_slots, latent)
    asked_marks = asked_marks.reshape(total_slots, node_rows)
    far = exchange(reply, domains)

    block = cut_rows
    blocks = inner_rows // block

    def rows_spec(width, rows=block):
        return pl.BlockSpec((rows, width), lambda step: (step, 0))

    def all_spec(array):
        return pl.BlockSpec(array.shape, lambda step: (0, 0))

    saved_widths = [node_rows, node_rows, latent, latent, latent, latent, latent, 1]
    saved_types = [BF16, BF16, BF16, BF16, BF16, F32, F32, F32]
    (
        inner_senders,
        inner_receivers,
        inner_sender,
        inner_receiver,
        inner_hidden,
        inner_slope,
        inner_normed,
        inner_scale,
        inner_total,
    ) = line.run(
        inner_forward_kernel,
        [shaped(kind, inner_rows, width) for kind, width in zip(saved_types, saved_widths)]
        + [shaped(F32, node_rows, latent)],
        [inner_pairs.T, edges, nodes, w_edge_in, w_edge_out],
        [
            pl.BlockSpec((2, block // 2), lambda step: (0, step)),
            rows_spec(latent),
            all_spec(nodes),
            all_spec(w_edge_in),
            all_spec(w_edge_out),
        ],
        [rows_spec(width) for width in saved_widths] + [all_spec(nodes)],
        (blocks,),
    )

    def last_rows(array):
        last = array.shape[0] // block - 1
        return pl.BlockSpec((block, array.shape[1]), lambda step: (last, 0))

    (
        cut_sender,
        cut_receiver,
        cut_hidden,
        cut_slope,
        cut_normed,
        cut_scale,
        total,
        outgoing,
    ) = line.run(
        cut_forward_kernel,
        [shaped(kind, cut_rows, width) for kind, width in zip(saved_types, saved_widths)][2:]
        + [shaped(F32, node_rows, latent), shaped(BF16, total_slots, latent)],
        [
            cut_senders,
            cut_receivers,
            edges,
            nodes,
            far,
            w_edge_in,
            w_edge_out,
            inner_total,
        ],
        [
            all_spec(cut_senders),
            all_spec(cut_receivers),
            last_rows(edges),
            all_spec(nodes),
            all_spec(far),
            all_spec(w_edge_in),
            all_spec(w_edge_out),
            all_spec(inner_total),
        ],
        [rows_spec(width) for width in saved_widths[2:]]
        + [all_spec(nodes), rows_spec(latent, total_slots)],
        (1,),
    )
    incoming = exchange(outgoing, domains)
    new_edges = line.run(
        new_edges_kernel,
        shaped(BF16, *edges.shape),
        [edges, inner_normed, cut_normed],
    )
    (
        new_nodes,
        self_grad,
        agg_grad,
        grad_reply,
        node_keep,
        node_send,
    ) = line.run(
        node_kernel,
        [
            shaped(BF16, node_rows, latent),
            shaped(F32, node_rows, latent),
            shaped(BF16, node_rows, latent),
            shaped(BF16, total_slots, latent),
        ]
        + [shaped(BF16, 3 * latent // 2, latent)] * 2,
        [me, incoming, asked_marks, total, nodes, ct_nodes, w_node_in, w_node_out],
        [SMEM] + [VMEM] * 7,
    )
    far_grad = exchange(grad_reply, domains)
    node_sum = added(node_keep, across(node_send, domains, 1))
    inner_out, inner_pre = line.run(
        inner_backward_kernel,
        [shaped(BF16, inner_rows, latent)] * 2,
        [
            inner_receivers,
            agg_grad,
            ct_edges,
            inner_normed,
            inner_scale,
            inner_slope,
            w_edge_out,
        ],
        [
            rows_spec(node_rows),
            all_spec(agg_grad),
            rows_spec(latent),
            rows_spec(latent),
            rows_spec(1),
            rows_spec(latent),
            all_spec(w_edge_out),
        ],
        [rows_spec(latent)] * 2,
        (blocks,),
    )
    bits = index_bits(domains)
    node_own, node_sent = split([node_sum], 1)
    node_parts = [*node_own, across(node_sent, domains, 2)]
    far_grad, node_sum, inner_pre = fence(far_grad, node_sum, inner_pre)
    factors = [
        edges,
        inner_sender,
        cut_sender,
        inner_receiver,
        cut_receiver,
        inner_hidden,
        cut_hidden,
        inner_out,
        inner_pre,
    ]
    buffers = [pltpu.VMEM((rows, latent), BF16) for rows in (inner_rows, cut_rows) * 2]
    buffers += [pltpu.VMEM((inner_rows, latent), BF16)] * 2
    buffers.append(pltpu.SemaphoreType.DMA((len(buffers),)))
    cut_out, cut_pre, edge_send = line.run(
        cut_backward_kernel,
        [shaped(BF16, cut_rows, latent)] * 2 + [shaped(BF16, 2 * latent, latent)],
        [
            me,
            cut_receivers,
            agg_grad,
            far_grad,
            ct_edges,
            cut_normed,
            cut_scale,
            cut_slope,
            w_edge_out,
        ]
        + factors,
        [
            SMEM,
            all_spec(cut_receivers),
            all_spec(agg_grad),
            all_spec(far_grad),
            last_rows(ct_edges),
            all_spec(cut_normed),
            all_spec(cut_scale),
            all_spec(cut_slope),
            all_spec(w_edge_out),
        ]
        + [ANY] * len(factors),
        [rows_spec(latent)] * 2 + [rows_spec(latent, 2 * latent)],
        (1,),
        buffers,
    )
    edge_send, place, *node_parts = fence(edge_send, me, *node_parts)
    received = across(edge_send, domains, 1)
    node_own, node_sent = split(node_parts, 2)
    node_got = across(node_sent, domains, 4)
    own_keep, sent_keep = line.run(
        edge_weights_kernel,
        [shaped(BF16, latent, latent)] * 2,
        [place, cut_out, cut_pre] + factors,
        [SMEM, VMEM, VMEM] + [ANY] * len(factors),
        scratch=buffers,
    )
    own_keep, sent_keep, received = fence(own_keep, sent_keep, received)
    edge_sent = added(sent_keep, received[latent:])
    edge_sent, inner_pre, cut_pre = fence(edge_sent, inner_pre, cut_pre)
    node_got = fence(node_got, edge_sent)[0]
    edge_got = across(edge_sent, domains, 2)
    node_sum = added(*node_own, node_got)
    for bit in bits[3:]:
        node_sum = added(*handed(node_sum, domains, bit))
    own_keep, received = fence(own_keep, received, edge_sent)[:2]
    edge_own = added(own_keep, received[:latent])
    local_grad, outgoing_grad = line.run(
        input_grads_kernel,
        [shaped(F32, node_rows, latent), shaped(BF16, total_slots, latent)],
        [
            inner_senders,
            inner_receivers,
            cut_senders,
            cut_receivers,
            inner_pre,
            cut_pre,
            w_edge_in,
        ],
    )
    edge_own, edge_got, node_sum, inner_pre, cut_pre, local_grad = fence(
        edge_own, edge_got, node_sum, inner_pre, cut_pre, local_grad
    )
    edge_own, edge_sent = split([added(edge_own, edge_got)], 2)
    edge_got = across(edge_sent, domains, 4)
    grad_edges = line.run(
        functools.partial(edge_grads_kernel, blocks=blocks),
        shaped(F32, *edges.shape),
        [ct_edges, inner_pre, cut_pre, w_edge_in],
        [
            rows_spec(latent),
            pl.BlockSpec((block, latent), lambda step: (jnp.minimum(step, blocks - 1), 0)),
            all_spec(cut_pre),
            pl.BlockSpec((latent, latent), lambda step: (0, 0)),
        ],
        [rows_spec(latent)],
        (blocks + 1,),
    )
    edge_got, node_sum, grad_edges = fence(edge_got, node_sum, grad_edges)
    edge_sum = added(*edge_own, edge_got)
    edge_sum, node_sum = fence(edge_sum, node_sum)
    edge_got = across(edge_sum, domains, 8)
    node_parts = handed(joined(handed(node_sum, domains, 2), 2), domains, 1)
    edge_sum = added(*fence(edge_sum, edge_got))
    for bit in bits[4:]:
        edge_sum = added(*handed(edge_sum, domains, bit))
    *edge_parts, node_near, node_far, outgoing_grad = fence(
        *handed(edge_sum, domains, 2), *node_parts, outgoing_grad
    )
    edge_sum = joined(edge_parts, 2)
    far, near = across(edge_sum, domains, 2), across(edge_sum, domains, 1)
    node_parts = [node_near, node_far]
    node_parts += [across(part, domains, 1) for part in node_parts]
    returned = exchange(outgoing_grad, domains)
    quarters = [shaped(BF16, 3 * latent, latent), shaped(BF16, latent, latent)]
    copies = dict(out_specs=[HBM] * 2, scratch=[pltpu.SemaphoreType.DMA((8,))], limit=2**20)
    grad_edge_in, grad_edge_out = line.run(
        first_quarters_kernel, quarters, [me, edge_sum, near], [SMEM, ANY, ANY], **copies
    )
    grad_node_in, grad_node_out = line.run(
        all_quarters_kernel,
        [shaped(BF16, 2 * latent, latent), shaped(BF16, latent, latent)],
        [me] + node_parts,
        [SMEM] + [VMEM] * 4,
        **(copies | {"limit": VMEM_LIMIT}),
    )
    far, grad_edge_in, grad_edge_out, grad_node_in, grad_node_out, returned = fence(
        far, grad_edge_in, grad_edge_out, grad_node_in, grad_node_out, returned
    )
    corner = across(far, domains, 1)
    grad_nodes = self_grad + local_grad + dot_rows(asked_marks, returned)
    corner, grad_nodes = fence(corner, grad_nodes)
    grad_edge_in, grad_edge_out = Line().run(
        last_quarters_kernel,
        quarters,
        [me, far, corner, grad_edge_in, grad_edge_out],
        [SMEM, ANY, ANY, HBM, HBM],
        aliases={3: 0, 4: 1},
        **copies,
    )
    return (
        new_nodes,
        new_edges,
        grad_nodes,
        grad_edges,
        grad_edge_in,
        grad_edge_out,
        grad_node_in,
        grad_node_out,
    )


def solution(mesh):
    placed = (
        P(("groups", "dom"), None),
        P(("groups", "dom"), None),
        P(("groups", "dom"), None),
        P(("groups", "dom")),
        P(("groups", "dom"), None),
        P(("groups", "dom")),
        P(),
        P(),
        P(),
        P(),
        P(("groups", "dom"), None),
        P(("groups", "dom"), None),
    )
    return jax.shard_map(
        shards,
        mesh=mesh,
        in_specs=placed,
        out_specs=(
            P(("groups", "dom"), None),
            P(("groups", "dom"), None),
            P(("groups", "dom"), None),
            P(("groups", "dom"), None),
            P("groups", None),
            P("groups", None),
            P("groups", None),
            P("groups", None),
        ),
        check_vma=False,
    )
```
